128 devices in a mesh: gx: 16 (over z, x), gy: 8 (over y, core).
Axes of the slice: x: 4, y: 4, z: 4, core: 2. Of those that a mesh axis runs over, the one named last changes fastest.
Arguments:
- state: float32 [40, 72, 16384], P(None, None, ('gx', 'gy')), may hold values from -6 to 6
- prev_tendency: bfloat16 [40, 72, 16384], P(None, None, ('gx', 'gy')), may hold values from -6 to 6
- wind: float32 [2, 72, 16384], P(None, None, ('gx', 'gy')), may hold values from -3 to 3
- edge_links: int32 [2, 4, 1024], P(None, None, ('gx', 'gy')), may hold values from 0 to 1023, as said below
- swap_slot: int32 [16384], P(('gx', 'gy')), may hold values from 0 to 16383, as said below
- inverse: float32 [1024, 72, 72], P(('gx', 'gy'))
Outputs:
- state_out: float32 [40, 72, 16384], P(None, None, ('gx', 'gy'))
- tendency: bfloat16 [40, 72, 16384], P(None, None, ('gx', 'gy'))
The draws below stay inside these ranges and needn't reach their ends.
Inputs may be any that keep to these rules, and one draw needn't show every extreme that they name: `edge_links`: every neighbour lies within 2 elements of its element along the element order, taken cyclically, and that distance is reached; the second row holds edge numbers 0 to 3. `swap_slot`: A permutation of the columns. A column either keeps a slot of its own device (slots 128 d to 128 d + 127 for device d along gx+gy) or takes a slot of the device half of all devices away along gx+gy; two such partners hand each other equally many columns, at most 64, and some pair hands exactly 64.
All inputs are finite; a program needn't handle non-finite values.
Results may differ from the reference program's by a relative error of at most 0.0045.
Values may be sent and summed in bfloat16 or wider, within the bound.
No kernel may reach another device: no remote copies, remote signals or barrier semaphores. Data moves between devices by JAX's collectives and lax.ppermute only.
A program may use at most 128 MiB of HBM per device.

```python
import math
import jax
import jax.numpy as jnp
import numpy as np
from jax import lax

E_DEV = 8
LEV = 72
NQ = 40
RIM = 2
PCOL = 16
SUBSTEPS = 4
COLUMNS = 16384
GROUPS = 1024
N_GX = 16
N_GY = 8


def draw_edge_links(key, part):
    key = jax.random.fold_in(key, 11)
    key_reach, key_sign, key_edge = jax.random.split(key, 3)
    elements = E_DEV * N_GX * N_GY
    distance = jax.random.randint(key_reach, (4, elements), 1, RIM + 1)
    direction_sign = 2 * jax.random.randint(key_sign, (4, elements), 0, 2) - 1
    offsets = (distance * direction_sign).at[0, 0].set(RIM).at[1, 0].set(-RIM)
    neighbour = (jnp.arange(elements)[None, :] + offsets) % elements
    far_edge = jax.random.randint(key_edge, (4, elements), 0, 4)
    return jnp.stack([neighbour, far_edge]).astype(jnp.int32)


def draw_swap_slot(key, part):
    key = jax.random.fold_in(key, 23)
    key_perm, key_count, key_busy, key_shift = jax.random.split(key, 4)
    devices = N_GX * N_GY
    halfway = devices // 2
    columns_here = E_DEV * 16
    capacity = E_DEV * 8
    shuffles = jax.vmap(lambda single: jax.random.permutation(single, columns_here))(jax.random.split(key_perm, devices))
    counts = jax.random.randint(key_count, (halfway,), capacity // 2, capacity + 1)
    busiest = jax.random.randint(key_busy, (), 0, halfway)
    counts = jnp.where(jnp.arange(halfway) == busiest, capacity, counts)
    device = jnp.arange(devices)
    moving = counts[device % halfway]
    ranking = jnp.zeros((devices, columns_here), jnp.int32).at[device[:, None], shuffles].set(jnp.broadcast_to(jnp.arange(columns_here, dtype=jnp.int32), (devices, columns_here)))
    partner = jnp.bitwise_xor(device, halfway)
    moving_out = ranking < moving[:, None]
    slot_there = jnp.take_along_axis(shuffles[partner], ranking, axis=1)
    free_count = columns_here - moving
    shift = 1 + jax.random.randint(key_shift, (devices,), 0, 1 << 20) % (free_count - 1)
    stay_rank = moving[:, None] + (ranking - moving[:, None] + shift[:, None]) % free_count[:, None]
    stay_rank = jnp.where(moving_out, 0, stay_rank).astype(jnp.int32)
    slot_here = jnp.take_along_axis(shuffles, stay_rank, axis=1)
    target = jnp.where(moving_out, partner[:, None] * columns_here + slot_there, device[:, None] * columns_here + slot_here)
    return target.reshape(-1).astype(jnp.int32)


def draw_inverse(key, part):
    key = jax.random.fold_in(key, 37)
    key_diag, key_cross = jax.random.split(key)
    group_count = E_DEV * 16 * N_GX * N_GY // PCOL
    diagonal = jax.random.uniform(key_diag, (group_count, LEV), jnp.float32, 0.75, 1.25)
    coupling = jax.random.normal(key_cross, (group_count, LEV, LEV), jnp.float32) * (0.6 / math.sqrt(LEV))
    identity = jnp.eye(LEV, dtype=jnp.float32)
    return coupling * (1.0 - identity) + diagonal[:, :, None] * identity


def block_scale(rng, dims, cuts, smallest, high):
    gain, own = 1.0, jax.random.fold_in(rng, 6)
    for axis_at, shards_of in cuts:
        draws = jnp.exp(jax.random.uniform(jax.random.fold_in(own, axis_at), (shards_of,), jnp.float32, smallest / len(cuts), high / len(cuts)))
        gain = gain * jnp.repeat(draws, dims[axis_at] // shards_of).reshape([-1 if axis == axis_at else 1 for axis in range(len(dims))])
    return gain


def bell_draw(key, extent, deviation, reach, shards=(), held_as=jnp.bfloat16):
    drawn = deviation * jax.random.normal(key, extent, jnp.float32)
    if shards:
        drawn = drawn * block_scale(key, extent, shards, -0.22, 0.18)
    return jnp.clip(drawn, -reach, reach).astype(held_as)


def setup_inputs(seed: int = 0) -> dict:
    splits = jax.random.split(jax.random.key(seed), 7)
    return {
        "state": bell_draw(splits[0], (NQ, LEV, COLUMNS), 1.0, 6.0, ((2, 128),), jnp.float32),
        "prev_tendency": bell_draw(splits[1], (NQ, LEV, COLUMNS), 1.0, 6.0, ((2, 128),)),
        "wind": bell_draw(splits[2], (2, LEV, COLUMNS), 0.5, 3.0, ((2, 128),), jnp.float32),
        "edge_links": draw_edge_links(jax.random.fold_in(splits[6], 71), 0),
        "swap_slot": draw_swap_slot(jax.random.fold_in(splits[6], 71), 0),
        "inverse": draw_inverse(jax.random.fold_in(splits[6], 71), 0),
    }


time_step = 0.2
edge_points = ((0, 1, 2, 3), (3, 7, 11, 15), (15, 14, 13, 12), (12, 8, 4, 0))

def point_tables():
    edge_of = np.zeros((2, 16), np.int32)
    spot_of = np.zeros((2, 16), np.int32)
    weight_of = np.zeros((2, 16), np.float32)
    filled = np.zeros(16, np.int32)
    for k in range(4):
        for m in range(4):
            p = edge_points[k][m]
            s = filled[p]
            edge_of[s, p] = k
            spot_of[s, p] = m
            weight_of[s, p] = 1.0
            filled[p] = s + 1
    return (edge_of, spot_of, weight_of)

def gll_matrices():
    gll_nodes = np.array([-1.0, -1.0 / np.sqrt(5.0), 1.0 / np.sqrt(5.0), 1.0])
    factors = np.array([np.prod([gll_nodes[i] - gll_nodes[k] for k in range(4) if k != i]) for i in range(4)])
    derivative = np.zeros((4, 4))
    for i in range(4):
        for k in range(4):
            if i != k:
                derivative[i, k] = factors[i] / (factors[k] * (gll_nodes[i] - gll_nodes[k]))
            else:
                derivative[i, k] = sum((1.0 / (gll_nodes[i] - gll_nodes[j]) for j in range(4) if j != i))
    deriv_x = np.kron(derivative, np.eye(4))
    deriv_y = np.kron(np.eye(4), derivative)
    return (jnp.asarray(deriv_x, jnp.float32), jnp.asarray(deriv_y, jnp.float32))

def hermite(substep):
    instant = (substep + 1.0) / SUBSTEPS
    square = instant * instant
    cube = square * instant
    h00 = 2.0 * cube - 3.0 * square + 1.0
    h01 = -2.0 * cube + 3.0 * square
    slope = cube - 2.0 * square + instant + (cube - square)
    return (h00 - slope, h01 + slope)

def gather_table(edge_table, anchor, element_count):
    edge_of, spot_of, weight_of = point_tables()
    neighbour = (edge_table[0] - anchor) % element_count
    far_edge = edge_table[1]
    edge_array = jnp.asarray(np.array(edge_points, np.int32))
    near_elem = neighbour[jnp.asarray(edge_of)]
    far_side = far_edge[jnp.asarray(edge_of)]
    far_point = edge_array[far_side, jnp.asarray(3 - spot_of)[:, :, None]]
    column = near_elem * 16 + far_point
    lookup = jnp.transpose(column, (0, 2, 1)).reshape(2, -1).astype(jnp.int32)
    weight = jnp.tile(jnp.asarray(weight_of, jnp.float32), (1, edge_table.shape[2]))
    return (lookup, weight)

def advect(tracers, wind):
    deriv_x, deriv_y = gll_matrices()
    shaped = tracers.reshape(tracers.shape[:-1] + (-1, 16))
    along_x = jnp.einsum('...ep,rp->...er', shaped, deriv_x, precision=lax.Precision.HIGHEST).reshape(tracers.shape)
    along_y = jnp.einsum('...ep,rp->...er', shaped, deriv_y, precision=lax.Precision.HIGHEST).reshape(tracers.shape)
    return -(wind[0] * along_x + wind[1] * along_y)

def edge_sum(widened, own, lookup, weight):
    gathered = own + weight[0] * jnp.take(widened, lookup[0], axis=-1) + weight[1] * jnp.take(widened, lookup[1], axis=-1)
    return gathered / (1.0 + weight[0] + weight[1])

def reference(state, prev_tendency, wind, edge_links, swap_slot, inverse):
    element_count = edge_links.shape[2]
    lookup, weight = gather_table(edge_links, 0, element_count)

    def one_tracer(tracer_pair):
        tracers, earlier_tend = tracer_pair
        grouped = jnp.zeros_like(tracers).at[:, swap_slot].set(tracers)
        blocks = grouped.reshape(LEV, GROUPS, PCOL)
        relaxed = jnp.einsum('cab,bcp->acp', inverse, blocks, precision=lax.Precision.HIGHEST).reshape(tracers.shape)
        new_group = (relaxed - grouped).astype(jnp.bfloat16)
        tendency = new_group[:, swap_slot]
        earlier = earlier_tend.astype(jnp.float32)
        current = tendency.astype(jnp.float32)
        for substep in range(SUBSTEPS):
            early_weight, late_weight = hermite(substep)
            motion = advect(tracers, wind)
            tracers = tracers + time_step * (edge_sum(motion, motion, lookup, weight) + early_weight * earlier + late_weight * current)
        return (tracers, tendency)
    state_out, tendency = lax.map(one_tracer, (state, prev_tendency))
    return (state_out, tendency)
```

```python
import jax
import jax.numpy as jnp
import numpy as np
from jax import lax
from jax.experimental import pallas as pl
from jax.experimental.pallas import tpu as pltpu
from jax.sharding import PartitionSpec as P

SUBSTEPS = 4
AXES = ("gx", "gy")
LANES = 128
PARTS = 4
VMEM = 48 * 1024 * 1024

time_step = 0.2
edge_points = ((0, 1, 2, 3), (3, 7, 11, 15), (15, 14, 13, 12), (12, 8, 4, 0))


def point_tables():
    edge_of = np.zeros((2, 16), np.int32)
    spot_of = np.zeros((2, 16), np.int32)
    weight_of = np.zeros((2, 16), np.float32)
    filled = np.zeros(16, np.int32)
    for k in range(4):
        for m in range(4):
            p = edge_points[k][m]
            s = filled[p]
            edge_of[s, p] = k
            spot_of[s, p] = m
            weight_of[s, p] = 1.0
            filled[p] = s + 1
    return (edge_of, spot_of, weight_of)


def gll_derivative():
    gll_nodes = np.array([-1.0, -1.0 / np.sqrt(5.0), 1.0 / np.sqrt(5.0), 1.0])
    factors = np.array(
        [np.prod([gll_nodes[i] - gll_nodes[k] for k in range(4) if k != i]) for i in range(4)]
    )
    derivative = np.zeros((4, 4))
    for i in range(4):
        for k in range(4):
            if i != k:
                derivative[i, k] = factors[i] / (factors[k] * (gll_nodes[i] - gll_nodes[k]))
            else:
                derivative[i, k] = sum(
                    (1.0 / (gll_nodes[i] - gll_nodes[j]) for j in range(4) if j != i)
                )
    return derivative


def derivative_matrix():
    derivative = gll_derivative()
    eye_block = np.eye(8)
    both = np.concatenate(
        [
            np.kron(eye_block, np.kron(derivative, np.eye(4)).T),
            np.kron(eye_block, np.kron(np.eye(4), derivative).T),
        ],
        axis=1,
    )
    high = both.astype(jnp.bfloat16)
    low = (both - high.astype(np.float64)).astype(jnp.bfloat16)
    return np.concatenate([high, low], axis=0)


def hermite(substep):
    instant = (substep + 1.0) / SUBSTEPS
    square = instant * instant
    cube = square * instant
    h00 = 2.0 * cube - 3.0 * square + 1.0
    h01 = -2.0 * cube + 3.0 * square
    slope = cube - 2.0 * square + instant + (cube - square)
    return (h00 - slope, h01 + slope)


def edge_targets(edge_links, first_elem, element_count):
    edge_of, spot_of, _ = point_tables()
    elements = edge_links.shape[2]
    own = first_elem + jnp.arange(elements, dtype=jnp.int32)
    apart = (edge_links[0] - own[None, :] + 2) % element_count
    apart = jnp.broadcast_to(apart[:, :, None], (4, elements, 16)).reshape(4, -1)
    far = jnp.broadcast_to(edge_links[1][:, :, None], (4, elements, 16)).reshape(4, -1)
    pick = np.tile(np.arange(4)[None, :, None] == edge_of[:, None, :], (1, 1, elements))
    pick = jnp.asarray(pick.astype(np.int32))
    apart = jnp.sum(pick * apart[None], axis=1)
    far = jnp.sum(pick * far[None], axis=1)
    spot = jnp.asarray(np.tile(spot_of, (1, elements)))
    point = jnp.where(
        far == 0, 3 - spot, jnp.where(far == 1, 15 - 4 * spot, jnp.where(far == 2, 12 + spot, 4 * spot))
    )
    start = jnp.asarray((np.arange(elements * 16) // 16 * 16).astype(np.int32))
    return (start[None, :] + 16 * apart + point).astype(jnp.float32)


def lane_ids(rows):
    return lax.broadcasted_iota(jnp.int32, (rows, LANES), 1)


def pack_kernel(state_ref, prev_ref, wind_ref, target_ref, right_ref, left_ref):
    rows = state_ref.shape[1]
    for k in range(PARTS):
        part = state_ref[k].astype(jnp.bfloat16)
        right_ref[k, :rows] = part
        left_ref[k, :rows] = part
    low = lane_ids(rows) < 64
    for k in range(2):
        near = prev_ref[k].astype(jnp.float32)
        away = pltpu.roll(prev_ref[k + 2].astype(jnp.float32), 64, 1)
        right_ref[4 + k, :rows] = jnp.where(low, away, near).astype(jnp.bfloat16)
        left_ref[4 + k, :rows] = jnp.where(low, near, away).astype(jnp.bfloat16)
    for k in range(3):
        piece = wind_ref[pl.ds(48 * k, 48), :].astype(jnp.bfloat16)
        right_ref[k, rows : rows + 48] = piece
        left_ref[k, rows : rows + 48] = piece
    piece = jnp.concatenate([target_ref[...], jnp.zeros((40, LANES), jnp.float32)], axis=0)
    piece = piece.astype(jnp.bfloat16)
    for k in range(3, 6):
        right_ref[k, rows : rows + 48] = piece
        left_ref[k, rows : rows + 48] = piece


def physics_kernel(state_ref, prev_ref, own_ref, far_ref, group_ref, tend_ref, right_ref, left_ref):
    lev = 72
    group = group_ref[0:1, :]
    group = jnp.concatenate([group, group], axis=1)
    picks = [jnp.broadcast_to(group == c, (lev, 2 * LANES)) for c in range(16)]
    matrices = jnp.concatenate([own_ref[...], far_ref[...]], axis=0)
    matrices = jnp.concatenate([matrices, matrices], axis=1)
    blank = jnp.zeros((LANES - lev, 2 * LANES), jnp.float32)
    early, late = hermite(0)
    tend = []
    for k in range(PARTS):
        pair = state_ref[k]
        pair = jnp.concatenate([pair[:lev], pair[lev:]], axis=1)
        high = pair.astype(jnp.bfloat16).astype(jnp.float32)
        column = jnp.concatenate([high, blank, pair - high, blank], axis=0).astype(jnp.bfloat16)
        product = jnp.dot(matrices, column, preferred_element_type=jnp.float32)
        chosen = product[:lev]
        for c in range(1, 16):
            chosen = jnp.where(picks[c], product[c * lev : (c + 1) * lev], chosen)
        chosen = jnp.concatenate([chosen[:, :LANES], chosen[:, LANES:]], axis=0)
        chosen = chosen.astype(jnp.bfloat16)
        tend_ref[k] = chosen
        tend.append(chosen.astype(jnp.float32))
    rows = 2 * lev
    low = lane_ids(rows) < 64
    for k in range(2):
        away = pltpu.roll(tend[k + 2], 64, 1)
        right_ref[k] = jnp.where(low, away, tend[k]).astype(jnp.bfloat16)
        left_ref[k] = jnp.where(low, tend[k], away).astype(jnp.bfloat16)
    place = lane_ids(rows) // 32
    to_right = jnp.zeros((rows, LANES), jnp.float32)
    to_left = to_right
    for k in range(PARTS):
        force = time_step * (early * prev_ref[k].astype(jnp.float32) + late * tend[k])
        to_right = jnp.where(place == k, pltpu.roll(force, (32 * (k - 1)) % LANES, 1), to_right)
        to_left = jnp.where(place == k, pltpu.roll(force, (32 * (k - 2)) % LANES, 1), to_left)
    right_ref[2] = to_right.astype(jnp.bfloat16)
    left_ref[2] = to_left.astype(jnp.bfloat16)


def advance_kernel(
    state_ref,
    prev_ref,
    tend_ref,
    wind_ref,
    target_ref,
    slope_ref,
    left_ref,
    right_ref,
    left_extra_ref,
    right_extra_ref,
    left_tend_ref,
    right_tend_ref,
    out_ref,
    sum_ref,
    blow_ref,
):
    lev = 72
    pair = 2 * lev
    rows = PARTS * pair
    lane = lax.broadcasted_iota(jnp.int32, (1, LANES), 1)
    point = lane % 16
    across = (point // 4 == 0) | (point // 4 == 3)
    along = (point % 4 == 0) | (point % 4 == 3)
    slots = (across | along, across & along)
    share = jnp.where(slots[1], 1.0 / 3.0, jnp.where(slots[0], 0.5, 1.0)).astype(jnp.float32)
    low = lane < 64

    @pl.when(pl.program_id(0) == 0)
    def _():
        own_t = target_ref[0:8, :].astype(jnp.int32) - 32
        left_t = left_extra_ref[3, 0:16].astype(jnp.float32).astype(jnp.int32)[0:8] - 32 - LANES
        right_t = right_extra_ref[3, 0:16].astype(jnp.float32).astype(jnp.int32)[0:8] - 32 + LANES
        targets = (own_t, jnp.where(low, right_t, left_t), jnp.where(low, left_t, right_t))
        row = lax.broadcasted_iota(jnp.int32, (LANES, LANES), 0)
        col = lax.broadcasted_iota(jnp.int32, (LANES, LANES), 1)
        inner, outer = row < 64, jnp.where(row < 64, row - LANES, row + LANES)
        near = jnp.where(inner, row + LANES, row - LANES)
        coords = (row, near, outer)

        def block(source, result):
            total = jnp.zeros((LANES, LANES), jnp.float32)
            if source == result:
                total = (row == col).astype(jnp.float32)
            for s in range(2):
                hit = (coords[source] == targets[result][s : s + 1]) & slots[s]
                total = total + hit.astype(jnp.float32)
            return total.astype(jnp.bfloat16)

        sum_ref[0, :LANES, :LANES] = block(0, 0)
        sum_ref[0, LANES:, :LANES] = block(1, 0)
        sum_ref[0, :LANES, LANES:] = block(0, 1)
        sum_ref[0, LANES:, LANES:] = block(1, 1)
        sum_ref[1, :LANES, :LANES] = block(2, 1)
        sum_ref[1, LANES:, :LANES] = jnp.zeros((LANES, LANES), jnp.bfloat16)
        sum_ref[1, :LANES, LANES:] = block(2, 2)
        sum_ref[1, LANES:, LANES:] = block(1, 2)

        def winds(ref):
            whole = jnp.concatenate([ref[k].astype(jnp.float32) for k in range(3)], axis=0)
            return whole[:lev], whole[lev:]

        left_w, right_w = winds(left_extra_ref), winds(right_extra_ref)
        for d in range(2):
            blow_ref[0, d] = -time_step * wind_ref[d]
            blow_ref[1, d] = -time_step * jnp.where(low, right_w[d], left_w[d])
            blow_ref[2, d] = -time_step * jnp.where(low, left_w[d], right_w[d])

    slope = slope_ref[...]

    def advect(value, unit):
        value = value.astype(jnp.bfloat16)
        both = jnp.dot(
            jnp.concatenate([value, value], axis=1), slope, preferred_element_type=jnp.float32
        )
        both = both.reshape(rows // lev, lev, 2 * LANES)
        motion = both[..., :LANES] * blow_ref[unit, 0] + both[..., LANES:] * blow_ref[unit, 1]
        return motion.reshape(rows, LANES).astype(jnp.bfloat16)

    def wide(ref, count):
        return ref[:count].astype(jnp.float32)

    def halves(left, right):
        direct = jnp.where(low, right, left)
        turned = jnp.where(low, left, right).reshape(2 * pair, LANES)
        turned = pltpu.roll(turned, 64, 1)
        return jnp.concatenate([direct.reshape(2 * pair, LANES), turned], axis=0)

    left_s, right_s = wide(left_ref, 4), wide(right_ref, 4)
    own = state_ref[...].reshape(rows, LANES)
    near = jnp.where(low, right_s, left_s).reshape(rows, LANES)
    outer = jnp.where(low, left_s, right_s).reshape(rows, LANES)
    own_prev = wide(prev_ref, 4).reshape(rows, LANES)
    own_tend = wide(tend_ref, 4).reshape(rows, LANES)
    near_prev = halves(left_ref[4:6].astype(jnp.float32), right_ref[4:6].astype(jnp.float32))
    near_tend = halves(wide(left_tend_ref, 2), wide(right_tend_ref, 2))
    left_f, right_f = left_tend_ref[2].astype(jnp.float32), right_tend_ref[2].astype(jnp.float32)
    outer_force = jnp.concatenate(
        [
            jnp.where(
                low,
                pltpu.roll(left_f, (-32 * (k - 1)) % LANES, 1),
                pltpu.roll(right_f, (-32 * (k - 2)) % LANES, 1),
            )
            for k in range(PARTS)
        ],
        axis=0,
    )
    both_sum, outer_sum = sum_ref[0], sum_ref[1]
    weights = [tuple(time_step * w for w in hermite(s)) for s in range(SUBSTEPS)]

    def gather(pieces, matrix):
        return jnp.dot(
            jnp.concatenate(pieces, axis=1), matrix, preferred_element_type=jnp.float32
        )

    for s in range(SUBSTEPS):
        early, late = weights[s]
        own_force = early * own_prev + late * own_tend
        own_move, near_move = advect(own, 0), advect(near, 1)
        if s == SUBSTEPS - 1:
            total = gather([own_move, near_move], both_sum[:, :LANES])
            out_ref[...] = (own + total * share + own_force).reshape(PARTS, pair, LANES)
            break
        near_force = early * near_prev + late * near_tend
        total = gather([own_move, near_move], both_sum)
        own = own + total[:, :LANES] * share + own_force
        near_total = total[:, LANES:]
        if s == 0:
            outer_move = advect(outer, 2)
            beyond = gather([outer_move, near_move], outer_sum)
            near_total = near_total + beyond[:, :LANES]
            outer = outer + beyond[:, LANES:] * share + outer_force
        elif s == 1:
            outer_move = advect(outer, 2)
            near_total = near_total + jnp.dot(
                outer_move, outer_sum[:LANES, :LANES], preferred_element_type=jnp.float32
            )
        near = near + near_total * share + near_force


def shifted(value, by):
    count = lax.axis_size(AXES)
    return lax.ppermute(value, AXES, [(i, (i + by) % count) for i in range(count)])


def per_device(state, prev_tendency, wind, edge_links, swap_slot, inverse):
    devices = lax.axis_size(AXES)
    position = lax.axis_index(AXES)
    shape = state.shape
    lev = shape[1]
    rows = shape[0] * lev // PARTS
    steps = rows // (2 * lev)
    elements = shape[2] // 16
    params = pltpu.CompilerParams(vmem_limit_bytes=VMEM)
    bf16 = jnp.bfloat16

    state4 = state.reshape(PARTS, rows, LANES)
    prev4 = prev_tendency.reshape(PARTS, rows, LANES)
    targets = edge_targets(edge_links, position * elements, elements * devices)
    targets = jnp.concatenate([targets, jnp.zeros((6, LANES), jnp.float32)], axis=0)
    message = jax.ShapeDtypeStruct((6, rows + 48, LANES), bf16)
    to_right, to_left = pl.pallas_call(
        pack_kernel, out_shape=(message, message), compiler_params=params, name="pack"
    )(state4, prev4, wind.reshape(2 * lev, LANES), targets)
    from_left, from_right = shifted(to_right, 1), shifted(to_left, -1)

    matrices = (inverse - jnp.eye(lev, dtype=jnp.float32)).astype(bf16)
    matrices = jnp.pad(matrices, ((0, 0), (0, 0), (0, LANES - lev))).reshape(-1, LANES)
    far_matrices = lax.ppermute(matrices, AXES, [(i, i ^ (devices // 2)) for i in range(devices)])
    group = (swap_slot % LANES) // 16 + jnp.where(swap_slot // LANES == position, 0, 8)
    group = jnp.broadcast_to(group[None, :], (8, LANES))

    def chunk(count, block_rows=2 * lev):
        return pl.BlockSpec((count, block_rows, LANES), lambda j: (0, j, 0))

    def whole(array):
        return pl.BlockSpec(array.shape, lambda j, n=array.ndim: (0,) * n)

    answer = jax.ShapeDtypeStruct((3, rows, LANES), bf16)
    tend4, tend_right, tend_left = pl.pallas_call(
        physics_kernel,
        grid=(steps,),
        in_specs=[chunk(4), chunk(4), whole(matrices), whole(far_matrices), whole(group)],
        out_specs=[chunk(4), chunk(3), chunk(3)],
        out_shape=(jax.ShapeDtypeStruct((PARTS, rows, LANES), bf16), answer, answer),
        compiler_params=params,
        name="physics",
    )(state4, prev4, matrices, far_matrices, group)
    tend_from_left, tend_from_right = shifted(tend_right, 1), shifted(tend_left, -1)

    slope = jnp.asarray(derivative_matrix())
    extra = pl.BlockSpec((6, 48, LANES), lambda j: (0, rows // 48, 0))
    out4 = pl.pallas_call(
        advance_kernel,
        grid=(steps,),
        in_specs=[
            chunk(4),
            chunk(4),
            chunk(4),
            whole(wind),
            whole(targets),
            whole(slope),
            chunk(6),
            chunk(6),
            extra,
            extra,
            chunk(3),
            chunk(3),
        ],
        out_specs=chunk(4),
        out_shape=jax.ShapeDtypeStruct((PARTS, rows, LANES), jnp.float32),
        scratch_shapes=[
            pltpu.VMEM((2, 2 * LANES, 2 * LANES), bf16),
            pltpu.VMEM((3, 2, lev, LANES), jnp.float32),
        ],
        compiler_params=params,
        name="advance",
    )(
        state4,
        prev4,
        tend4,
        wind,
        targets,
        slope,
        from_left,
        from_right,
        from_left,
        from_right,
        tend_from_left,
        tend_from_right,
    )
    return (out4.reshape(shape), tend4.reshape(shape))


def solution(mesh):
    columns = P(None, None, AXES)
    return jax.shard_map(
        per_device,
        mesh=mesh,
        in_specs=(columns, columns, columns, columns, P(AXES), P(AXES, None, None)),
        out_specs=(columns, columns),
        check_vma=False,
    )
```

```python
import math

import jax
import jax.numpy as jnp
import numpy as np
from jax import lax
from jax.experimental import pallas as pl
from jax.experimental.pallas import tpu as pltpu
from jax.sharding import PartitionSpec as P

SUBSTEPS = 4
AXES = ("gx", "gy")
LANES = 128
PARTS = 4
VMEM = 16 * 1024 * 1024

time_step = 0.2
edge_points = ((0, 1, 2, 3), (3, 7, 11, 15), (15, 14, 13, 12), (12, 8, 4, 0))


def point_tables():
    edge_of = np.zeros((2, 16), np.int32)
    spot_of = np.zeros((2, 16), np.int32)
    weight_of = np.zeros((2, 16), np.float32)
    filled = np.zeros(16, np.int32)
    for k in range(4):
        for m in range(4):
            p = edge_points[k][m]
            s = filled[p]
            edge_of[s, p] = k
            spot_of[s, p] = m
            weight_of[s, p] = 1.0
            filled[p] = s + 1
    return (edge_of, spot_of, weight_of)


def gll_derivative():
    gll_nodes = np.array([-1.0, -1.0 / np.sqrt(5.0), 1.0 / np.sqrt(5.0), 1.0])
    factors = np.array(
        [np.prod([gll_nodes[i] - gll_nodes[k] for k in range(4) if k != i]) for i in range(4)]
    )
    derivative = np.zeros((4, 4))
    for i in range(4):
        for k in range(4):
            if i != k:
                derivative[i, k] = factors[i] / (factors[k] * (gll_nodes[i] - gll_nodes[k]))
            else:
                derivative[i, k] = sum(
                    (1.0 / (gll_nodes[i] - gll_nodes[j]) for j in range(4) if j != i)
                )
    return derivative


def derivative_matrix():
    derivative = gll_derivative()
    eye_block = np.eye(8)
    both = np.concatenate(
        [
            np.kron(eye_block, np.kron(derivative, np.eye(4)).T),
            np.kron(eye_block, np.kron(np.eye(4), derivative).T),
        ],
        axis=1,
    )
    high = both.astype(jnp.bfloat16)
    low = (both - high.astype(np.float64)).astype(jnp.bfloat16)
    return np.concatenate([high, low], axis=0)


def hermite(substep):
    instant = (substep + 1.0) / SUBSTEPS
    square = instant * instant
    cube = square * instant
    h00 = 2.0 * cube - 3.0 * square + 1.0
    h01 = -2.0 * cube + 3.0 * square
    slope = cube - 2.0 * square + instant + (cube - square)
    return (h00 - slope, h01 + slope)


def lane_ids(rows=1):
    return lax.broadcasted_iota(jnp.int32, (rows, LANES), 1)


def point_sets():
    point = lane_ids() % 16
    across = (point // 4 == 0) | (point // 4 == 3)
    along = (point % 4 == 0) | (point % 4 == 3)
    slots = (across | along, across & along)
    share = jnp.where(slots[1], 1.0 / 3.0, jnp.where(slots[0], 0.5, 1.0)).astype(jnp.float32)
    return slots, share


def edge_targets(links_ref, first_elem, element_count):
    edge_of, spot_of, _ = point_tables()
    elements = links_ref.shape[2]
    own = first_elem + lax.broadcasted_iota(jnp.int32, (4, elements), 1)
    apart = links_ref[0] - own
    half = element_count // 2
    apart = jnp.where(apart > half, apart - element_count, apart)
    apart = jnp.where(apart < -half, apart + element_count, apart) + 2
    both = jnp.concatenate([apart, links_ref[1]], axis=0).astype(jnp.float32)
    spread = lax.broadcasted_iota(jnp.int32, (elements, LANES), 0)
    spread = (spread == lax.broadcasted_iota(jnp.int32, (elements, LANES), 1) // 16).astype(jnp.float32)
    both = jnp.dot(both, spread, preferred_element_type=jnp.float32)
    both = (both + 0.5).astype(jnp.int32)
    lane = lane_ids()
    point = lane % 16
    rows = []
    for s in range(2):
        edge = jnp.zeros((1, LANES), jnp.int32)
        spot = edge
        for p in range(16):
            edge = jnp.where(point == p, int(edge_of[s, p]), edge)
            spot = jnp.where(point == p, int(spot_of[s, p]), spot)
        away, far = both[0:1], both[4:5]
        for k in range(1, 4):
            away = jnp.where(edge == k, both[k : k + 1], away)
            far = jnp.where(edge == k, both[4 + k : 5 + k], far)
        place = jnp.where(far == 2, 12 + spot, 4 * spot)
        place = jnp.where(far == 1, 15 - 4 * spot, place)
        place = jnp.where(far == 0, 3 - spot, place)
        rows.append(lane - point + 16 * away + place)
    rows = jnp.concatenate(rows + [jnp.zeros((6, LANES), jnp.int32)], axis=0)
    return rows.astype(jnp.float32)


def packed_halves(value, low):
    away = [pltpu.roll(value[k + 2], 64, 1) for k in range(2)]
    upper = [jnp.where(low, away[k], value[k]) for k in range(2)]
    lower = [jnp.where(low, value[k], away[k]) for k in range(2)]
    return upper, lower


def whole_halves(left, right, low):
    count, rows = left.shape[0], left.shape[1]
    direct = jnp.where(low, right, left).reshape(count * rows, LANES)
    turned = jnp.where(low, left, right).reshape(count * rows, LANES)
    return jnp.concatenate([direct, pltpu.roll(turned, 64, 1)], axis=0)


def pack_kernel(state_ref, prev_ref, wind_ref, links_ref, right_ref, left_ref, target_ref):
    step = pl.program_id(0)
    rows = state_ref.shape[1]
    at = pl.ds(pl.multiple_of(step * rows, 16), rows)
    low = lane_ids() < 64
    upper, lower = packed_halves([state_ref[k] for k in range(PARTS)], low)
    for k in range(2):
        right_ref[k, at] = upper[k].astype(jnp.bfloat16)
        left_ref[k, at] = lower[k].astype(jnp.bfloat16)
    quarter = lane_ids() // 32
    to_right = jnp.zeros((rows, LANES), jnp.float32)
    to_left = to_right
    for k in range(PARTS):
        turned = prev_ref[k].astype(jnp.float32)
        turned = pltpu.roll(turned, 32 * k, 1) if k else turned
        to_right = jnp.where(quarter == (3 + k) % 4, turned, to_right)
        to_left = jnp.where(quarter == k, turned, to_left)
    right_ref[2, at] = to_right.astype(jnp.bfloat16)
    left_ref[2, at] = to_left.astype(jnp.bfloat16)

    @pl.when(step == 0)
    def _():
        devices = lax.axis_size(AXES)
        elements = links_ref.shape[2]
        targets = edge_targets(links_ref, lax.axis_index(AXES) * elements, elements * devices)
        target_ref[...] = targets
        end = right_ref.shape[1]
        blank = jnp.zeros((24, LANES), jnp.float32)
        for k in range(3):
            piece = wind_ref[pl.ds(48 * k, 48), :]
            piece = jnp.concatenate([piece, targets, blank], axis=0).astype(jnp.bfloat16)
            right_ref[k, end - 80 : end] = piece
            left_ref[k, end - 80 : end] = piece


def chosen_products(matrices, state_ref, group, first, emit):
    lev = 72
    group = jnp.concatenate([group, group], axis=1)
    picks = [jnp.broadcast_to(group == first + c, (lev, 2 * LANES)) for c in range(8)]
    matrices = jnp.concatenate([matrices, matrices], axis=1)
    blank = jnp.zeros((LANES - lev, 2 * LANES), jnp.float32)
    for k in range(PARTS):
        pair = state_ref[k]
        pair = jnp.concatenate([pair[:lev], pair[lev:]], axis=1)
        high = pair.astype(jnp.bfloat16).astype(jnp.float32)
        column = jnp.concatenate([high, blank, pair - high, blank], axis=0).astype(jnp.bfloat16)
        product = jnp.dot(matrices, column, preferred_element_type=jnp.float32)
        chosen = jnp.zeros((lev, 2 * LANES), jnp.float32)
        for c in range(8):
            chosen = jnp.where(picks[c], product[c * lev : (c + 1) * lev], chosen)
        emit(k, jnp.concatenate([chosen[:, :LANES], chosen[:, LANES:]], axis=0))


def column_group(slot_ref):
    slot = slot_ref[...]
    return jnp.where(slot // LANES == lax.axis_index(AXES), 0, 8) + slot % LANES // 16


def moved(value, slope, blow_x, blow_y):
    rows, lev = value.shape[0], blow_x.shape[0]
    value = value.astype(jnp.bfloat16)
    both = jnp.dot(jnp.concatenate([value, value], axis=1), slope, preferred_element_type=jnp.float32)
    both = both.reshape(rows // lev, lev, 2 * LANES)
    motion = both[..., :LANES] * blow_x + both[..., LANES:] * blow_y
    return motion.reshape(rows, LANES).astype(jnp.bfloat16)


def sum_block(source, targets, slots, own):
    row = lax.broadcasted_iota(jnp.int32, (LANES, LANES), 0)
    total = jnp.zeros((LANES, LANES), jnp.float32)
    if own:
        total = (row == lax.broadcasted_iota(jnp.int32, (LANES, LANES), 1)).astype(jnp.float32)
    place = {
        "own": row,
        "near": jnp.where(row < 64, row + LANES, row - LANES),
        "outer": jnp.where(row < 64, row - LANES, row + LANES),
    }[source]
    for s in range(2):
        total = total + ((place == targets[s : s + 1]) & slots[s]).astype(jnp.float32)
    return total.astype(jnp.bfloat16)


def own_kernel(
    state_ref, prev_ref, wind_ref, target_ref, slope_ref, slot_ref, own_ref, part_ref, next_ref, sum_ref
):
    slots, share = point_sets()

    @pl.when(pl.program_id(0) == 0)
    def _():
        targets = target_ref[...].astype(jnp.int32) - 32
        sum_ref[...] = sum_block("own", targets, slots, True)

    def emit(k, chosen):
        part_ref[k] = chosen

    chosen_products(own_ref[...], state_ref, column_group(slot_ref), 0, emit)
    early = time_step * hermite(0)[0]
    pairs, rows = state_ref.shape[0], state_ref.shape[1]
    state = state_ref[...].reshape(pairs * rows, LANES)
    motion = moved(state, slope_ref[...], -time_step * wind_ref[0], -time_step * wind_ref[1])
    total = jnp.dot(motion, sum_ref[...], preferred_element_type=jnp.float32)
    ahead = state + total * share + early * prev_ref[...].astype(jnp.float32).reshape(state.shape)
    next_ref[...] = ahead.reshape(pairs, rows, LANES)


def far_kernel(
    state_ref, prev_ref, slot_ref, far_ref, part_ref, next_ref, tend_ref, ahead_ref, right_ref, left_ref
):
    group = column_group(slot_ref)
    here = group < 8
    quarter = lane_ids() // 32
    inner = (quarter == 1) | (quarter == 2)
    low = lane_ids() < 64
    late = time_step * hermite(0)[1]
    early_1, late_1 = (time_step * w for w in hermite(1))
    ahead, force = [], []

    def emit(k, chosen):
        tend = jnp.where(here, part_ref[k], chosen).astype(jnp.bfloat16)
        tend_ref[k] = tend
        tend = tend.astype(jnp.float32)
        ahead.append(next_ref[k] + late * tend)
        ahead_ref[k] = ahead[k]
        forced = early_1 * prev_ref[k].astype(jnp.float32) + late_1 * tend
        force.append(jnp.where(inner, forced, tend))

    chosen_products(far_ref[...], state_ref, group, 8, emit)
    upper, lower = packed_halves(force, low)
    for k in range(2):
        middle = jnp.where(inner, ahead[k], pltpu.roll(ahead[k + 2], 64, 1)).astype(jnp.bfloat16)
        right_ref[k] = middle
        left_ref[k] = middle
        right_ref[2 + k] = upper[k].astype(jnp.bfloat16)
        left_ref[2 + k] = lower[k].astype(jnp.bfloat16)


def near_kernel(
    state_ref,
    wind_ref,
    target_ref,
    slope_ref,
    left_ref,
    right_ref,
    left_extra_ref,
    right_extra_ref,
    add_ref,
    near_ref,
    force_ref,
    sum_ref,
    outer_sum_ref,
    blow_ref,
):
    lev = wind_ref.shape[1]
    slots, share = point_sets()
    low = lane_ids() < 64

    @pl.when(pl.program_id(0) == 0)
    def _():
        def winds(ref):
            whole = jnp.concatenate([ref[k].astype(jnp.float32)[:48] for k in range(3)], axis=0)
            return whole[:lev], whole[lev:]

        def targets(ref):
            return ref[0].astype(jnp.float32)[48:56].astype(jnp.int32) - 32

        own_t = target_ref[...].astype(jnp.int32) - 32
        left_t, right_t = targets(left_extra_ref) - LANES, targets(right_extra_ref) + LANES
        near_t = jnp.where(low, right_t, left_t)
        sum_ref[:LANES, :LANES] = sum_block("own", own_t, slots, True)
        sum_ref[LANES:, :LANES] = sum_block("near", own_t, slots, False)
        sum_ref[:LANES, LANES:] = sum_block("own", near_t, slots, False)
        sum_ref[LANES:, LANES:] = sum_block("near", near_t, slots, True)
        outer_sum_ref[...] = sum_block("outer", near_t, slots, False)
        left_w, right_w = winds(left_extra_ref), winds(right_extra_ref)
        for d in range(2):
            blow_ref[0, d] = -time_step * wind_ref[d]
            blow_ref[1, d] = -time_step * jnp.where(low, right_w[d], left_w[d])
            blow_ref[2, d] = -time_step * jnp.where(low, left_w[d], right_w[d])

    pairs, rows = state_ref.shape[0], state_ref.shape[1]
    slope = slope_ref[...]
    own = state_ref[...].reshape(pairs * rows, LANES)
    left, right = left_ref[...].astype(jnp.float32), right_ref[...].astype(jnp.float32)
    near = whole_halves(left[:2], right[:2], low)
    own_move = moved(own, slope, blow_ref[0, 0], blow_ref[0, 1])
    near_move = moved(near, slope, blow_ref[1, 0], blow_ref[1, 1])
    total = jnp.dot(near_move, sum_ref[LANES:], preferred_element_type=jnp.float32)
    near_total = total[:, LANES:] + jnp.dot(
        own_move, sum_ref[:LANES, LANES:], preferred_element_type=jnp.float32
    )
    add_ref[...] = (total[:, :LANES] * share).reshape(pairs, rows, LANES)
    prev = jnp.concatenate(
        [
            jnp.where(low, right[2], left[2])
            if k == 0
            else jnp.where(
                low, pltpu.roll(right[2], LANES - 32 * k, 1), pltpu.roll(left[2], LANES - 32 * k, 1)
            )
            for k in range(PARTS)
        ],
        axis=0,
    )
    early = time_step * hermite(0)[0]
    near_ref[...] = (near + near_total * share + early * prev).reshape(pairs, rows, LANES)
    force_ref[...] = prev.astype(jnp.bfloat16).reshape(pairs, rows, LANES)


def advance_kernel(
    ahead_ref,
    add_ref,
    near_ref,
    near_prev_ref,
    prev_ref,
    tend_ref,
    left_ref,
    right_ref,
    slope_ref,
    sum_ref,
    outer_sum_ref,
    blow_ref,
    out_ref,
):
    pairs, pair = ahead_ref.shape[0], ahead_ref.shape[1]
    rows = pairs * pair
    _, share = point_sets()
    quarter = lane_ids() // 32
    inner = (quarter == 1) | (quarter == 2)
    low = lane_ids() < 64
    slope, sums = slope_ref[...], sum_ref[...]
    weights = [tuple(time_step * w for w in hermite(s)) for s in range(SUBSTEPS)]

    def flat(ref):
        return ref[...].astype(jnp.float32).reshape(rows, LANES)

    def advect(value, unit):
        return moved(value, slope, blow_ref[unit, 0], blow_ref[unit, 1])

    def gather(pieces, matrix):
        return jnp.dot(jnp.concatenate(pieces, axis=1), matrix, preferred_element_type=jnp.float32)

    left, right = left_ref[...].astype(jnp.float32), right_ref[...].astype(jnp.float32)

    def middle(value):
        value = value.reshape(2 * pair, LANES)
        return jnp.concatenate([value, pltpu.roll(value, 64, 1)], axis=0)

    left_mid, right_mid = middle(left[:2]), middle(right[:2])
    received = whole_halves(left[2:], right[2:], low)
    own_prev, own_tend, near_prev = flat(prev_ref), flat(tend_ref), flat(near_prev_ref)
    own = flat(ahead_ref) + flat(add_ref)
    near = flat(near_ref) + weights[0][1] * received
    near = jnp.where(inner, jnp.where(low, right_mid, left_mid), near)
    outer = jnp.where(low, left_mid, right_mid)
    for s in range(1, SUBSTEPS):
        early, late = weights[s]
        own_force = early * own_prev + late * own_tend
        own_move, near_move = advect(own, 0), advect(near, 1)
        if s == SUBSTEPS - 1:
            total = gather([own_move, near_move], sums[:, :LANES])
            out_ref[...] = (own + total * share + own_force).reshape(pairs, pair, LANES)
            break
        near_force = early * near_prev + late * received
        total = gather([own_move, near_move], sums)
        own = own + total[:, :LANES] * share + own_force
        near_total = total[:, LANES:]
        if s == 1:
            near_force = jnp.where(inner, received, near_force)
            near_total = near_total + jnp.dot(
                advect(outer, 2), outer_sum_ref[...], preferred_element_type=jnp.float32
            )
        near = near + near_total * share + near_force


def shifted(value, by):
    count = lax.axis_size(AXES)
    return lax.ppermute(value, AXES, [(i, (i + by) % count) for i in range(count)])


def per_device(state, prev_tendency, wind, edge_links, swap_slot, inverse):
    devices = lax.axis_size(AXES)
    shape = state.shape
    lev = shape[1]
    pair = 2 * lev
    rows = shape[0] * lev // PARTS
    steps = rows // pair
    params = pltpu.CompilerParams(vmem_limit_bytes=VMEM)
    bf16, f32 = jnp.bfloat16, jnp.float32

    def like(count, kind, length=rows):
        return jax.ShapeDtypeStruct((count, length, LANES), kind)

    def chunk(count):
        return pl.BlockSpec((count, pair, LANES), lambda j: (0, j, 0))

    def whole(array):
        return pl.BlockSpec(array.shape, lambda j, n=len(array.shape): (0,) * n)

    def call(body, ins, outs, name, passes):
        size = sum(math.prod(array.shape) * array.dtype.itemsize for array, _ in ins)
        cost = pl.CostEstimate(
            flops=passes * 2 * PARTS * rows * 256 * 256, bytes_accessed=2 * size, transcendentals=0
        )
        return pl.pallas_call(
            body,
            grid=(steps,),
            in_specs=[spec for _, spec in ins],
            out_specs=tuple(spec for _, spec in outs),
            out_shape=tuple(kind for kind, _ in outs),
            compiler_params=params,
            cost_estimate=cost,
            name=name,
        )(*[array for array, _ in ins])

    matrices = (inverse - jnp.eye(lev, dtype=f32)).astype(bf16)
    matrices = jnp.pad(matrices, ((0, 0), (0, 0), (0, LANES - lev))).reshape(-1, LANES)
    far_matrices = lax.ppermute(matrices, AXES, [(i, i ^ (devices // 2)) for i in range(devices)])

    state4 = state.reshape(PARTS, rows, LANES)
    prev4 = prev_tendency.reshape(PARTS, rows, LANES)
    slot = swap_slot.reshape(1, LANES)
    flat_wind = wind.reshape(pair, LANES)
    slope = jnp.asarray(derivative_matrix())
    message = like(3, bf16, rows + 80)
    target_kind = jax.ShapeDtypeStruct((8, LANES), f32)
    to_right, to_left, targets = call(
        pack_kernel,
        [(state4, chunk(4)), (prev4, chunk(4)), (flat_wind, whole(flat_wind)), (edge_links, whole(edge_links))],
        [(message, whole(message)), (message, whole(message)), (target_kind, whole(target_kind))],
        "pack",
        2,
    )
    from_left, from_right = shifted(to_right, 1), shifted(to_left, -1)

    sum_kind = jax.ShapeDtypeStruct((LANES, LANES), bf16)
    part, ahead, _ = call(
        own_kernel,
        [
            (state4, chunk(4)),
            (prev4, chunk(4)),
            (wind, whole(wind)),
            (targets, whole(targets)),
            (slope, whole(slope)),
            (slot, whole(slot)),
            (matrices, whole(matrices)),
        ],
        [(like(4, f32), chunk(4)), (like(4, f32), chunk(4)), (sum_kind, whole(sum_kind))],
        "own",
        10,
    )
    tend4, ahead, mid_right, mid_left = call(
        far_kernel,
        [
            (state4, chunk(4)),
            (prev4, chunk(4)),
            (slot, whole(slot)),
            (far_matrices, whole(far_matrices)),
            (part, chunk(4)),
            (ahead, chunk(4)),
        ],
        [(like(4, bf16), chunk(4)), (like(4, f32), chunk(4)), (like(4, bf16), chunk(4)), (like(4, bf16), chunk(4))],
        "far",
        10,
    )
    mid_from_left, mid_from_right = shifted(mid_right, 1), shifted(mid_left, -1)

    extra = pl.BlockSpec((3, 80, LANES), lambda j: (0, rows // 80, 0))
    both_kind = jax.ShapeDtypeStruct((2 * LANES, 2 * LANES), bf16)
    blow_kind = jax.ShapeDtypeStruct((3, 2, lev, LANES), f32)
    add, near, near_prev, sums, outer_sums, blow = call(
        near_kernel,
        [
            (state4, chunk(4)),
            (wind, whole(wind)),
            (targets, whole(targets)),
            (slope, whole(slope)),
            (from_left, chunk(3)),
            (from_right, chunk(3)),
            (from_left, extra),
            (from_right, extra),
        ],
        [
            (like(4, f32), chunk(4)),
            (like(4, f32), chunk(4)),
            (like(4, bf16), chunk(4)),
            (both_kind, whole(both_kind)),
            (sum_kind, whole(sum_kind)),
            (blow_kind, whole(blow_kind)),
        ],
        "near",
        8,
    )
    (out4,) = call(
        advance_kernel,
        [
            (ahead, chunk(4)),
            (add, chunk(4)),
            (near, chunk(4)),
            (near_prev, chunk(4)),
            (prev4, chunk(4)),
            (tend4, chunk(4)),
            (mid_from_left, chunk(4)),
            (mid_from_right, chunk(4)),
            (slope, whole(slope)),
            (sums, whole(sums)),
            (outer_sums, whole(outer_sums)),
            (blow, whole(blow)),
        ],
        [(like(4, f32), chunk(4))],
        "advance",
        24,
    )
    return (out4.reshape(shape), tend4.reshape(shape))


def solution(mesh):
    columns = P(None, None, AXES)
    return jax.shard_map(
        per_device,
        mesh=mesh,
        in_specs=(columns, columns, columns, columns, P(AXES), P(AXES, None, None)),
        out_specs=(columns, columns),
        check_vma=False,
    )
```

```python
import math

import jax
import jax.numpy as jnp
import numpy as np
from jax import lax
from jax.experimental import pallas as pl
from jax.experimental.pallas import tpu as pltpu
from jax.sharding import PartitionSpec as P

SUBSTEPS = 4
AXES = ("gx", "gy")
LANES = 128
CHUNK = 144
PARTS = 4
VMEM = 16 * 1024 * 1024

time_step = 0.2
edge_points = ((0, 1, 2, 3), (3, 7, 11, 15), (15, 14, 13, 12), (12, 8, 4, 0))


def point_tables():
    edge_of = np.zeros((2, 16), np.int32)
    spot_of = np.zeros((2, 16), np.int32)
    weight_of = np.zeros((2, 16), np.float32)
    filled = np.zeros(16, np.int32)
    for k in range(4):
        for m in range(4):
            p = edge_points[k][m]
            s = filled[p]
            edge_of[s, p] = k
            spot_of[s, p] = m
            weight_of[s, p] = 1.0
            filled[p] = s + 1
    return (edge_of, spot_of, weight_of)


def gll_derivative():
    gll_nodes = np.array([-1.0, -1.0 / np.sqrt(5.0), 1.0 / np.sqrt(5.0), 1.0])
    factors = np.array(
        [np.prod([gll_nodes[i] - gll_nodes[k] for k in range(4) if k != i]) for i in range(4)]
    )
    derivative = np.zeros((4, 4))
    for i in range(4):
        for k in range(4):
            if i != k:
                derivative[i, k] = factors[i] / (factors[k] * (gll_nodes[i] - gll_nodes[k]))
            else:
                derivative[i, k] = sum(
                    (1.0 / (gll_nodes[i] - gll_nodes[j]) for j in range(4) if j != i)
                )
    return derivative


def derivative_matrix():
    derivative = gll_derivative()
    eye_block = np.eye(8)
    both = np.concatenate(
        [
            np.kron(eye_block, np.kron(derivative, np.eye(4)).T),
            np.kron(eye_block, np.kron(np.eye(4), derivative).T),
        ],
        axis=1,
    )
    high = both.astype(jnp.bfloat16)
    low = (both - high.astype(np.float64)).astype(jnp.bfloat16)
    return np.concatenate([high, low], axis=0)


def hermite(substep):
    instant = (substep + 1.0) / SUBSTEPS
    square = instant * instant
    cube = square * instant
    h00 = 2.0 * cube - 3.0 * square + 1.0
    h01 = -2.0 * cube + 3.0 * square
    slope = cube - 2.0 * square + instant + (cube - square)
    return (h00 - slope, h01 + slope)


def lane_ids(rows=1):
    return lax.broadcasted_iota(jnp.int32, (rows, LANES), 1)


def point_sets():
    point = lane_ids() % 16
    across = (point // 4 == 0) | (point // 4 == 3)
    along = (point % 4 == 0) | (point % 4 == 3)
    slots = (across | along, across & along)
    share = jnp.where(slots[1], 1.0 / 3.0, jnp.where(slots[0], 0.5, 1.0)).astype(jnp.float32)
    return slots, share


def edge_targets(links_ref, first_elem, element_count):
    edge_of, spot_of, _ = point_tables()
    elements = links_ref.shape[2]
    own = first_elem + lax.broadcasted_iota(jnp.int32, (4, elements), 1)
    apart = links_ref[0] - own
    half = element_count // 2
    apart = jnp.where(apart > half, apart - element_count, apart)
    apart = jnp.where(apart < -half, apart + element_count, apart) + 2
    both = jnp.concatenate([apart, links_ref[1]], axis=0).astype(jnp.float32)
    spread = lax.broadcasted_iota(jnp.int32, (elements, LANES), 0)
    spread = (spread == lax.broadcasted_iota(jnp.int32, (elements, LANES), 1) // 16).astype(jnp.float32)
    both = jnp.dot(both, spread, preferred_element_type=jnp.float32)
    both = (both + 0.5).astype(jnp.int32)
    lane = lane_ids()
    point = lane % 16
    rows = []
    for s in range(2):
        edge = jnp.zeros((1, LANES), jnp.int32)
        spot = edge
        for p in range(16):
            edge = jnp.where(point == p, int(edge_of[s, p]), edge)
            spot = jnp.where(point == p, int(spot_of[s, p]), spot)
        away, far = both[0:1], both[4:5]
        for k in range(1, 4):
            away = jnp.where(edge == k, both[k : k + 1], away)
            far = jnp.where(edge == k, both[4 + k : 5 + k], far)
        place = jnp.where(far == 2, 12 + spot, 4 * spot)
        place = jnp.where(far == 1, 15 - 4 * spot, place)
        place = jnp.where(far == 0, 3 - spot, place)
        rows.append(lane - point + 16 * away + place)
    rows = jnp.concatenate(rows + [jnp.zeros((6, LANES), jnp.int32)], axis=0)
    return rows.astype(jnp.float32)


def on_odd():
    return lax.axis_index(AXES) % 2 == 1


def sides():
    return (lane_ids() < 64) == on_odd()


def packed_halves(value, chosen):
    away = [pltpu.roll(value[k + 2], 64, 1) for k in range(2)]
    off = [jnp.where(chosen, away[k], value[k]) for k in range(2)]
    on = [jnp.where(chosen, value[k], away[k]) for k in range(2)]
    return off, on


def whole_halves(off, on, chosen):
    count, rows = off.shape[0], off.shape[1]
    direct = jnp.where(chosen, off, on).reshape(count * rows, LANES)
    turned = jnp.where(chosen, on, off).reshape(count * rows, LANES)
    return jnp.concatenate([direct, pltpu.roll(turned, 64, 1)], axis=0)


def pack_kernel(
    inverse_hbm,
    wind_hbm,
    links_hbm,
    state_hbm,
    prev_hbm,
    matrix_ref,
    off_ref,
    on_ref,
    target_ref,
    wind_ref,
    state_ref,
    prev_ref,
    inverse_ref,
    links_ref,
    sems,
):
    pairs = [(inverse_hbm, inverse_ref), (wind_hbm, wind_ref), (links_hbm, links_ref)]
    for k in range(PARTS):
        pairs += [(state_hbm.at[k], state_ref.at[k]), (prev_hbm.at[k], prev_ref.at[k])]
    copies = [pltpu.make_async_copy(a, b, sems.at[i]) for i, (a, b) in enumerate(pairs)]
    for copy in copies:
        copy.start()
    groups, lev = inverse_ref.shape[0], inverse_ref.shape[1]
    copies[0].wait()
    eye = lax.broadcasted_iota(jnp.int32, (lev, lev), 0) == lax.broadcasted_iota(jnp.int32, (lev, lev), 1)
    eye = eye.astype(jnp.float32)
    blank = jnp.zeros((lev, LANES - lev), jnp.float32)
    matrix = [jnp.concatenate([inverse_ref[c] - eye, blank], axis=1) for c in range(groups)]
    matrix_ref[...] = jnp.concatenate(matrix, axis=0).astype(jnp.bfloat16)
    copies[1].wait()
    copies[2].wait()
    devices = lax.axis_size(AXES)
    elements = links_ref.shape[2]
    targets = edge_targets(links_ref, lax.axis_index(AXES) * elements, elements * devices)
    target_ref[...] = targets
    end = off_ref.shape[1]
    filler = jnp.zeros((24, LANES), jnp.float32)
    flat_wind = wind_ref[...].reshape(2 * lev, LANES)
    for k in range(3):
        piece = jnp.concatenate([flat_wind[48 * k : 48 * k + 48], targets, filler], axis=0)
        piece = piece.astype(jnp.bfloat16)
        off_ref[k, end - 80 : end] = piece
        on_ref[k, end - 80 : end] = piece
    chosen = sides()
    odd = jnp.where(on_odd(), 3, 0)
    quarter = lane_ids() // 32
    for copy in copies[3:]:
        copy.wait()
    for at in chunks(state_ref):
        off, on = packed_halves([state_ref[k, at] for k in range(PARTS)], chosen)
        for k in range(2):
            off_ref[k, at] = off[k].astype(jnp.bfloat16)
            on_ref[k, at] = on[k].astype(jnp.bfloat16)
        to_off = jnp.zeros((CHUNK, LANES), jnp.float32)
        to_on = to_off
        for k in range(PARTS):
            turned = prev_ref[k, at].astype(jnp.float32)
            turned = pltpu.roll(turned, 32 * k, 1) if k else turned
            to_off = jnp.where(quarter == (odd + k) % 4, turned, to_off)
            to_on = jnp.where(quarter == (3 - odd + k) % 4, turned, to_on)
        off_ref[2, at] = to_off.astype(jnp.bfloat16)
        on_ref[2, at] = to_on.astype(jnp.bfloat16)


def chunks(ref):
    return [pl.ds(start, CHUNK) for start in range(0, ref.shape[1], CHUNK)]


def each_chunk(ref, body):
    def step(j, carry):
        body(pl.ds(pl.multiple_of(j * CHUNK, CHUNK), CHUNK))
        return carry

    lax.fori_loop(0, ref.shape[1] // CHUNK, step, 0)


def product_tables(matrices, group, first):
    lev = 72
    group = jnp.concatenate([group, group], axis=1)
    picks = [jnp.broadcast_to(group == first + c, (lev, 2 * LANES)) for c in range(8)]
    return jnp.concatenate([matrices, matrices], axis=1), picks


def chosen_product(tables, pair):
    matrices, picks = tables
    lev = pair.shape[0] // 2
    blank = jnp.zeros((LANES - lev, 2 * LANES), jnp.float32)
    pair = jnp.concatenate([pair[:lev], pair[lev:]], axis=1)
    high = pair.astype(jnp.bfloat16).astype(jnp.float32)
    column = jnp.concatenate([high, blank, pair - high, blank], axis=0).astype(jnp.bfloat16)
    product = jnp.dot(matrices, column, preferred_element_type=jnp.float32)
    chosen = jnp.zeros((lev, 2 * LANES), jnp.float32)
    for c in range(8):
        chosen = jnp.where(picks[c], product[c * lev : (c + 1) * lev], chosen)
    return jnp.concatenate([chosen[:, :LANES], chosen[:, LANES:]], axis=0)


def column_group(slot_ref):
    slot = slot_ref[...]
    return jnp.where(slot // LANES == lax.axis_index(AXES), 0, 8) + slot % LANES // 16


def flat(value):
    return value.astype(jnp.float32).reshape(-1, LANES)


def moved(value, slope, blow_x, blow_y):
    rows, lev = value.shape[0], blow_x.shape[0]
    value = value.astype(jnp.bfloat16)
    both = jnp.dot(jnp.concatenate([value, value], axis=1), slope, preferred_element_type=jnp.float32)
    both = both.reshape(rows // lev, lev, 2 * LANES)
    motion = both[..., :LANES] * blow_x + both[..., LANES:] * blow_y
    return motion.reshape(rows, LANES).astype(jnp.bfloat16)


def sum_block(source, targets, slots, own):
    row = lax.broadcasted_iota(jnp.int32, (LANES, LANES), 0)
    total = jnp.zeros((LANES, LANES), jnp.float32)
    if own:
        total = (row == lax.broadcasted_iota(jnp.int32, (LANES, LANES), 1)).astype(jnp.float32)
    place = {
        "own": row,
        "near": jnp.where(row < 64, row + LANES, row - LANES),
        "outer": jnp.where(row < 64, row - LANES, row + LANES),
    }[source]
    for s in range(2):
        total = total + ((place == targets[s : s + 1]) & slots[s]).astype(jnp.float32)
    return total.astype(jnp.bfloat16)


def own_kernel(state_ref, prev_ref, wind_ref, target_ref, slope_ref, slot_ref, own_ref, part_ref, next_ref):
    slots, share = point_sets()
    sums = sum_block("own", target_ref[...].astype(jnp.int32) - 32, slots, True)
    tables = product_tables(own_ref[...], column_group(slot_ref), 0)
    early = time_step * hermite(0)[0]
    blow = [-time_step * wind_ref[d] for d in range(2)]
    slope = slope_ref[...]

    def body(at):
        for k in range(PARTS):
            part_ref[k, at] = chosen_product(tables, state_ref[k, at])
        state = flat(state_ref[:, at])
        motion = moved(state, slope, *blow)
        total = jnp.dot(motion, sums, preferred_element_type=jnp.float32)
        ahead = state + total * share + early * flat(prev_ref[:, at])
        next_ref[:, at] = ahead.reshape(PARTS, CHUNK, LANES)

    each_chunk(state_ref, body)


def far_kernel(
    state_ref, prev_ref, slot_ref, far_ref, part_ref, next_ref, tend_ref, ahead_ref, off_ref, on_ref
):
    group = column_group(slot_ref)
    here = group < 8
    tables = product_tables(far_ref[...], group, 8)
    quarter = lane_ids() // 32
    inner = (quarter == 1) | (quarter == 2)
    chosen = sides()
    late = time_step * hermite(0)[1]
    early_1, late_1 = (time_step * w for w in hermite(1))

    def body(at):
        ahead, force = [], []
        for k in range(PARTS):
            tend = jnp.where(here, part_ref[k, at], chosen_product(tables, state_ref[k, at]))
            tend = tend.astype(jnp.bfloat16)
            tend_ref[k, at] = tend
            tend = tend.astype(jnp.float32)
            ahead.append(next_ref[k, at] + late * tend)
            ahead_ref[k, at] = ahead[k]
            forced = early_1 * prev_ref[k, at].astype(jnp.float32) + late_1 * tend
            force.append(jnp.where(inner, forced, tend))
        off, on = packed_halves(force, chosen)
        for k in range(2):
            middle = jnp.where(inner, ahead[k], pltpu.roll(ahead[k + 2], 64, 1)).astype(jnp.bfloat16)
            off_ref[k, at] = middle
            on_ref[k, at] = middle
            off_ref[2 + k, at] = off[k].astype(jnp.bfloat16)
            on_ref[2 + k, at] = on[k].astype(jnp.bfloat16)

    each_chunk(state_ref, body)


def near_kernel(
    state_ref,
    wind_ref,
    target_ref,
    slope_ref,
    off_ref,
    on_ref,
    add_ref,
    near_ref,
    force_ref,
    sum_ref,
    outer_sum_ref,
    blow_ref,
):
    lev = wind_ref.shape[1]
    slots, share = point_sets()
    chosen = sides()
    end = off_ref.shape[1]

    def extra(ref, k):
        return ref[k, end - 80 : end].astype(jnp.float32)

    def winds(ref):
        whole = jnp.concatenate([extra(ref, k)[:48] for k in range(3)], axis=0)
        return whole[:lev], whole[lev:]

    def targets(ref):
        return extra(ref, 0)[48:56].astype(jnp.int32) - 32

    own_t = target_ref[...].astype(jnp.int32) - 32
    near_t = jnp.where(chosen, targets(off_ref), targets(on_ref))
    near_t = near_t + jnp.where(lane_ids() < 64, LANES, -LANES)
    sum_ref[:LANES, :LANES] = sum_block("own", own_t, slots, True)
    sum_ref[LANES:, :LANES] = sum_block("near", own_t, slots, False)
    sum_ref[:LANES, LANES:] = sum_block("own", near_t, slots, False)
    sum_ref[LANES:, LANES:] = sum_block("near", near_t, slots, True)
    outer_sum_ref[...] = sum_block("outer", near_t, slots, False)
    off_w, on_w = winds(off_ref), winds(on_ref)
    for d in range(2):
        blow_ref[0, d] = -time_step * wind_ref[d]
        blow_ref[1, d] = -time_step * jnp.where(chosen, off_w[d], on_w[d])
        blow_ref[2, d] = -time_step * jnp.where(chosen, on_w[d], off_w[d])

    slope = slope_ref[...]
    early = time_step * hermite(0)[0]

    def body(at):
        off, on = off_ref[:, at].astype(jnp.float32), on_ref[:, at].astype(jnp.float32)
        near = whole_halves(off[:2], on[:2], chosen)
        own_move = moved(flat(state_ref[:, at]), slope, blow_ref[0, 0], blow_ref[0, 1])
        near_move = moved(near, slope, blow_ref[1, 0], blow_ref[1, 1])
        total = jnp.dot(near_move, sum_ref[LANES:], preferred_element_type=jnp.float32)
        near_total = total[:, LANES:] + jnp.dot(
            own_move, sum_ref[:LANES, LANES:], preferred_element_type=jnp.float32
        )
        add_ref[:, at] = (total[:, :LANES] * share).reshape(PARTS, CHUNK, LANES)
        prev = [jnp.where(chosen, off[2], on[2])]
        for k in range(1, PARTS):
            turned = [pltpu.roll(side[2], LANES - 32 * k, 1) for side in (off, on)]
            prev.append(jnp.where(chosen, *turned))
        prev = jnp.concatenate(prev, axis=0)
        near = near + near_total * share + early * prev
        near_ref[:, at] = near.reshape(PARTS, CHUNK, LANES)
        force_ref[:, at] = prev.astype(jnp.bfloat16).reshape(PARTS, CHUNK, LANES)

    each_chunk(state_ref, body)


def advance_kernel(
    ahead_ref,
    add_ref,
    near_ref,
    near_prev_ref,
    prev_ref,
    tend_ref,
    off_ref,
    on_ref,
    slope_ref,
    sum_ref,
    outer_sum_ref,
    blow_ref,
    out_hbm,
    tend_hbm,
    out_ref,
    sems,
):
    tend_copy = pltpu.make_async_copy(tend_ref, tend_hbm, sems.at[0])
    tend_copy.start()
    _, share = point_sets()
    quarter = lane_ids() // 32
    inner = (quarter == 1) | (quarter == 2)
    chosen = sides()
    slope, sums = slope_ref[...], sum_ref[...]
    weights = [tuple(time_step * w for w in hermite(s)) for s in range(SUBSTEPS)]

    def advect(value, unit):
        return moved(value, slope, blow_ref[unit, 0], blow_ref[unit, 1])

    def gather(pieces, matrix):
        return jnp.dot(jnp.concatenate(pieces, axis=1), matrix, preferred_element_type=jnp.float32)

    def middle(value):
        value = value.reshape(2 * CHUNK, LANES)
        return jnp.concatenate([value, pltpu.roll(value, 64, 1)], axis=0)

    def body(at):
        off, on = off_ref[:, at].astype(jnp.float32), on_ref[:, at].astype(jnp.float32)
        off_mid, on_mid = middle(off[:2]), middle(on[:2])
        received = whole_halves(off[2:], on[2:], chosen)
        own_prev, own_tend = flat(prev_ref[:, at]), flat(tend_ref[:, at])
        near_prev = flat(near_prev_ref[:, at])
        own = flat(ahead_ref[:, at]) + flat(add_ref[:, at])
        near = flat(near_ref[:, at]) + weights[0][1] * received
        near = jnp.where(inner, jnp.where(chosen, off_mid, on_mid), near)
        outer = jnp.where(chosen, on_mid, off_mid)
        for s in range(1, SUBSTEPS):
            early, late = weights[s]
            own_force = early * own_prev + late * own_tend
            own_move, near_move = advect(own, 0), advect(near, 1)
            if s == SUBSTEPS - 1:
                total = gather([own_move, near_move], sums[:, :LANES])
                out = own + total * share + own_force
                out_ref[:, at] = out.reshape(PARTS, CHUNK, LANES)
                break
            near_force = early * near_prev + late * received
            total = gather([own_move, near_move], sums)
            own = own + total[:, :LANES] * share + own_force
            near_total = total[:, LANES:]
            if s == 1:
                near_force = jnp.where(inner, received, near_force)
                near_total = near_total + jnp.dot(
                    advect(outer, 2), outer_sum_ref[...], preferred_element_type=jnp.float32
                )
            near = near + near_total * share + near_force

    copies = []
    for j, at in enumerate(chunks(out_ref)):
        body(at)
        copies.append(pltpu.make_async_copy(out_ref.at[:, at], out_hbm.at[:, at], sems.at[1 + j]))
        copies[j].start()
    for copy in copies:
        copy.wait()
    tend_copy.wait()


def exchanged(off, on):
    count = lax.axis_size(AXES)
    across = [(i, (i + 1) % count if i % 2 else (i - 1) % count) for i in range(count)]
    inside = [(i, i ^ 1) for i in range(count)]
    return lax.ppermute(off, AXES, across), lax.ppermute(on, AXES, inside)


def per_device(state, prev_tendency, wind, edge_links, swap_slot, inverse):
    devices = lax.axis_size(AXES)
    shape = state.shape
    lev = shape[1]
    rows = shape[0] * lev // PARTS
    params = pltpu.CompilerParams(vmem_limit_bytes=VMEM)
    bf16, f32 = jnp.bfloat16, jnp.float32
    inner = pl.BlockSpec(memory_space=pltpu.VMEM)
    outer = pl.BlockSpec(memory_space=pltpu.HBM)

    def like(count, kind, length=rows):
        return pltpu.VMEM((count, length, LANES), kind)

    def table(kind, *size):
        return pltpu.VMEM(size, kind)

    def call(body, ins, outs, name, passes, **more):
        size = sum(math.prod(array.shape) * array.dtype.itemsize for array in ins)
        cost = pl.CostEstimate(
            flops=passes * 2 * PARTS * rows * 256 * 256, bytes_accessed=2 * size, transcendentals=0
        )
        more = {"in_specs": [inner] * len(ins), "out_specs": (inner,) * len(outs)} | more
        return pl.pallas_call(
            body, out_shape=outs, compiler_params=params, cost_estimate=cost, name=name, **more
        )(*ins)

    slot = swap_slot.reshape(1, LANES)
    slope = jnp.asarray(derivative_matrix())
    message = like(3, bf16, rows + 80)
    inputs = (
        inverse,
        wind,
        edge_links,
        state.reshape(PARTS, rows, LANES),
        prev_tendency.reshape(PARTS, rows, LANES),
    )
    inputs = tuple(pltpu.with_memory_space_constraint(array, pltpu.HBM) for array in inputs)
    matrices, to_off, to_on, targets, wind, state, prev = call(
        pack_kernel,
        inputs,
        (
            table(bf16, inverse.shape[0] * lev, LANES),
            message,
            message,
            table(f32, 8, LANES),
            table(f32, *wind.shape),
            like(4, f32),
            like(4, bf16),
        ),
        "pack",
        2,
        in_specs=[outer] * len(inputs),
        scratch_shapes=[
            pltpu.VMEM(inverse.shape, f32),
            pltpu.VMEM(edge_links.shape, jnp.int32),
            pltpu.SemaphoreType.DMA((3 + 2 * PARTS,)),
        ],
    )
    far_matrices = lax.ppermute(matrices, AXES, [(i, i ^ (devices // 2)) for i in range(devices)])
    off, on = exchanged(to_off, to_on)
    part, ahead = call(
        own_kernel,
        (state, prev, wind, targets, slope, slot, matrices),
        (like(4, f32), like(4, f32)),
        "own",
        10,
    )
    tend, ahead, mid_off, mid_on = call(
        far_kernel,
        (state, prev, slot, far_matrices, part, ahead),
        (like(4, bf16), like(4, f32), like(4, bf16), like(4, bf16)),
        "far",
        10,
    )
    mid_off, mid_on = exchanged(mid_off, mid_on)
    add, near, near_prev, sums, outer_sums, blow = call(
        near_kernel,
        (state, wind, targets, slope, off, on),
        (
            like(4, f32),
            like(4, f32),
            like(4, bf16),
            table(bf16, 2 * LANES, 2 * LANES),
            table(bf16, LANES, LANES),
            table(f32, 3, 2, lev, LANES),
        ),
        "near",
        8,
    )
    out, tend = call(
        advance_kernel,
        (ahead, add, near, near_prev, prev, tend, mid_off, mid_on, slope, sums, outer_sums, blow),
        (
            jax.ShapeDtypeStruct((PARTS, rows, LANES), f32),
            jax.ShapeDtypeStruct((PARTS, rows, LANES), bf16),
        ),
        "advance",
        24,
        out_specs=(outer, outer),
        scratch_shapes=[
            pltpu.VMEM((PARTS, rows, LANES), f32),
            pltpu.SemaphoreType.DMA((1 + rows // CHUNK,)),
        ],
    )
    return (out.reshape(shape), tend.reshape(shape))


def solution(mesh):
    columns = P(None, None, AXES)
    return jax.shard_map(
        per_device,
        mesh=mesh,
        in_specs=(columns, columns, columns, columns, P(AXES), P(AXES, None, None)),
        out_specs=(columns, columns),
        check_vma=False,
    )
```

```python
import functools
import math

import jax
import jax.numpy as jnp
import numpy as np
from jax import lax
from jax.experimental import pallas as pl
from jax.experimental.pallas import tpu as pltpu
from jax.sharding import PartitionSpec as P

SUBSTEPS = 4
AXES = ("gx", "gy")
LANES = 128
CHUNK = 144
SPLIT = (3, 2)
PARTS = 4
VMEM = 16 * 1024 * 1024

time_step = 0.2
edge_points = ((0, 1, 2, 3), (3, 7, 11, 15), (15, 14, 13, 12), (12, 8, 4, 0))


def point_tables():
    edge_of = np.zeros((2, 16), np.int32)
    spot_of = np.zeros((2, 16), np.int32)
    weight_of = np.zeros((2, 16), np.float32)
    filled = np.zeros(16, np.int32)
    for k in range(4):
        for m in range(4):
            p = edge_points[k][m]
            s = filled[p]
            edge_of[s, p] = k
            spot_of[s, p] = m
            weight_of[s, p] = 1.0
            filled[p] = s + 1
    return (edge_of, spot_of, weight_of)


def gll_derivative():
    gll_nodes = np.array([-1.0, -1.0 / np.sqrt(5.0), 1.0 / np.sqrt(5.0), 1.0])
    factors = np.array(
        [np.prod([gll_nodes[i] - gll_nodes[k] for k in range(4) if k != i]) for i in range(4)]
    )
    derivative = np.zeros((4, 4))
    for i in range(4):
        for k in range(4):
            if i != k:
                derivative[i, k] = factors[i] / (factors[k] * (gll_nodes[i] - gll_nodes[k]))
            else:
                derivative[i, k] = sum(
                    (1.0 / (gll_nodes[i] - gll_nodes[j]) for j in range(4) if j != i)
                )
    return derivative


def derivative_matrix():
    derivative = gll_derivative()
    eye_block = np.eye(8)
    both = np.concatenate(
        [
            np.kron(eye_block, np.kron(derivative, np.eye(4)).T),
            np.kron(eye_block, np.kron(np.eye(4), derivative).T),
        ],
        axis=1,
    )
    high = both.astype(jnp.bfloat16)
    low = (both - high.astype(np.float64)).astype(jnp.bfloat16)
    return np.concatenate([high, low], axis=0)


def hermite(substep):
    instant = (substep + 1.0) / SUBSTEPS
    square = instant * instant
    cube = square * instant
    h00 = 2.0 * cube - 3.0 * square + 1.0
    h01 = -2.0 * cube + 3.0 * square
    slope = cube - 2.0 * square + instant + (cube - square)
    return (h00 - slope, h01 + slope)


def lane_ids(rows=1):
    return lax.broadcasted_iota(jnp.int32, (rows, LANES), 1)


def point_sets():
    point = lane_ids() % 16
    across = (point // 4 == 0) | (point // 4 == 3)
    along = (point % 4 == 0) | (point % 4 == 3)
    slots = (across | along, across & along)
    share = jnp.where(slots[1], 1.0 / 3.0, jnp.where(slots[0], 0.5, 1.0)).astype(jnp.float32)
    return slots, share


def edge_targets(links_ref, first_elem, element_count):
    edge_of, spot_of, _ = point_tables()
    elements = links_ref.shape[2]
    own = first_elem + lax.broadcasted_iota(jnp.int32, (4, elements), 1)
    apart = links_ref[0] - own
    half = element_count // 2
    apart = jnp.where(apart > half, apart - element_count, apart)
    apart = jnp.where(apart < -half, apart + element_count, apart) + 2
    both = jnp.concatenate([apart, links_ref[1]], axis=0).astype(jnp.float32)
    spread = lax.broadcasted_iota(jnp.int32, (elements, LANES), 0)
    spread = (spread == lax.broadcasted_iota(jnp.int32, (elements, LANES), 1) // 16).astype(jnp.float32)
    both = jnp.dot(both, spread, preferred_element_type=jnp.float32)
    both = (both + 0.5).astype(jnp.int32)
    lane = lane_ids()
    point = lane % 16
    rows = []
    for s in range(2):
        edge = jnp.zeros((1, LANES), jnp.int32)
        spot = edge
        for p in range(16):
            edge = jnp.where(point == p, int(edge_of[s, p]), edge)
            spot = jnp.where(point == p, int(spot_of[s, p]), spot)
        away, far = both[0:1], both[4:5]
        for k in range(1, 4):
            away = jnp.where(edge == k, both[k : k + 1], away)
            far = jnp.where(edge == k, both[4 + k : 5 + k], far)
        place = jnp.where(far == 2, 12 + spot, 4 * spot)
        place = jnp.where(far == 1, 15 - 4 * spot, place)
        place = jnp.where(far == 0, 3 - spot, place)
        rows.append(lane - point + 16 * away + place)
    rows = jnp.concatenate(rows + [jnp.zeros((6, LANES), jnp.int32)], axis=0)
    return rows.astype(jnp.float32)


def on_odd():
    return lax.axis_index(AXES) % 2 == 1


def sides():
    return (lane_ids() < 64) == on_odd()


def packed_halves(value, chosen):
    away = [pltpu.roll(value[k + 2], 64, 1) for k in range(2)]
    off = [jnp.where(chosen, away[k], value[k]) for k in range(2)]
    on = [jnp.where(chosen, value[k], away[k]) for k in range(2)]
    return off, on


def whole_halves(off, on, chosen):
    count, rows = off.shape[0], off.shape[1]
    direct = jnp.where(chosen, off, on).reshape(count * rows, LANES)
    turned = jnp.where(chosen, on, off).reshape(count * rows, LANES)
    return jnp.concatenate([direct, pltpu.roll(turned, 64, 1)], axis=0)


def pack_kernel(
    inverse_hbm,
    wind_hbm,
    links_hbm,
    state_hbm,
    prev_hbm,
    matrix_ref,
    off_ref,
    on_ref,
    target_ref,
    wind_ref,
    state_ref,
    prev_ref,
    inverse_ref,
    links_ref,
    sems,
):
    pairs = [(inverse_hbm, inverse_ref), (wind_hbm, wind_ref), (links_hbm, links_ref)]
    for k in range(PARTS):
        pairs += [(state_hbm.at[k], state_ref.at[k]), (prev_hbm.at[k], prev_ref.at[k])]
    copies = [pltpu.make_async_copy(a, b, sems.at[i]) for i, (a, b) in enumerate(pairs)]
    for copy in copies:
        copy.start()
    groups, lev = inverse_ref.shape[0], inverse_ref.shape[1]
    copies[0].wait()
    eye = lax.broadcasted_iota(jnp.int32, (lev, lev), 0) == lax.broadcasted_iota(jnp.int32, (lev, lev), 1)
    eye = eye.astype(jnp.float32)
    blank = jnp.zeros((lev, LANES - lev), jnp.float32)
    matrix = [jnp.concatenate([inverse_ref[c] - eye, blank], axis=1) for c in range(groups)]
    matrix_ref[...] = jnp.concatenate(matrix, axis=0).astype(jnp.bfloat16)
    copies[1].wait()
    copies[2].wait()
    devices = lax.axis_size(AXES)
    elements = links_ref.shape[2]
    targets = edge_targets(links_ref, lax.axis_index(AXES) * elements, elements * devices)
    target_ref[...] = targets
    end = off_ref.shape[1]
    filler = jnp.zeros((24, LANES), jnp.float32)
    flat_wind = wind_ref[...].reshape(2 * lev, LANES)
    for k in range(3):
        piece = jnp.concatenate([flat_wind[48 * k : 48 * k + 48], targets, filler], axis=0)
        piece = piece.astype(jnp.bfloat16)
        off_ref[k, end - 80 : end] = piece
        on_ref[k, end - 80 : end] = piece
    chosen = sides()
    odd = jnp.where(on_odd(), 3, 0)
    quarter = lane_ids() // 32
    for copy in copies[3:]:
        copy.wait()
    for at in chunks(state_ref):
        off, on = packed_halves([state_ref[k, at] for k in range(PARTS)], chosen)
        for k in range(2):
            off_ref[k, at] = off[k].astype(jnp.bfloat16)
            on_ref[k, at] = on[k].astype(jnp.bfloat16)
        to_off = jnp.zeros((CHUNK, LANES), jnp.float32)
        to_on = to_off
        for k in range(PARTS):
            turned = prev_ref[k, at].astype(jnp.float32)
            turned = pltpu.roll(turned, 32 * k, 1) if k else turned
            to_off = jnp.where(quarter == (odd + k) % 4, turned, to_off)
            to_on = jnp.where(quarter == (3 - odd + k) % 4, turned, to_on)
        off_ref[2, at] = to_off.astype(jnp.bfloat16)
        on_ref[2, at] = to_on.astype(jnp.bfloat16)


def chunks(ref):
    return [pl.ds(start, CHUNK) for start in range(0, ref.shape[1], CHUNK)]


def each_chunk(first, count, body):
    def step(j, carry):
        near, whole = j * CHUNK, (first + j) * CHUNK
        body(pl.ds(pl.multiple_of(whole, CHUNK), CHUNK), pl.ds(pl.multiple_of(near, CHUNK), CHUNK))
        return carry

    lax.fori_loop(0, count, step, 0)


def product_tables(matrices, group, first):
    lev = 72
    group = jnp.concatenate([group, group], axis=1)
    picks = [jnp.broadcast_to(group == first + c, (lev, 2 * LANES)) for c in range(8)]
    return jnp.concatenate([matrices, matrices], axis=1), picks


def chosen_product(tables, pair):
    matrices, picks = tables
    lev = pair.shape[0] // 2
    blank = jnp.zeros((LANES - lev, 2 * LANES), jnp.float32)
    pair = jnp.concatenate([pair[:lev], pair[lev:]], axis=1)
    high = pair.astype(jnp.bfloat16).astype(jnp.float32)
    column = jnp.concatenate([high, blank, pair - high, blank], axis=0).astype(jnp.bfloat16)
    product = jnp.dot(matrices, column, preferred_element_type=jnp.float32)
    chosen = jnp.zeros((lev, 2 * LANES), jnp.float32)
    for c in range(8):
        chosen = jnp.where(picks[c], product[c * lev : (c + 1) * lev], chosen)
    return jnp.concatenate([chosen[:, :LANES], chosen[:, LANES:]], axis=0)


def column_group(slot_ref):
    slot = slot_ref[...]
    return jnp.where(slot // LANES == lax.axis_index(AXES), 0, 8) + slot % LANES // 16


def flat(value):
    return value.astype(jnp.float32).reshape(-1, LANES)


def moved(value, slope, blow_x, blow_y):
    rows, lev = value.shape[0], blow_x.shape[0]
    value = value.astype(jnp.bfloat16)
    both = jnp.dot(jnp.concatenate([value, value], axis=1), slope, preferred_element_type=jnp.float32)
    both = both.reshape(rows // lev, lev, 2 * LANES)
    motion = both[..., :LANES] * blow_x + both[..., LANES:] * blow_y
    return motion.reshape(rows, LANES).astype(jnp.bfloat16)


def sum_block(source, targets, slots, own):
    row = lax.broadcasted_iota(jnp.int32, (LANES, LANES), 0)
    total = jnp.zeros((LANES, LANES), jnp.float32)
    if own:
        total = (row == lax.broadcasted_iota(jnp.int32, (LANES, LANES), 1)).astype(jnp.float32)
    place = {
        "own": row,
        "near": jnp.where(row < 64, row + LANES, row - LANES),
        "outer": jnp.where(row < 64, row - LANES, row + LANES),
    }[source]
    for s in range(2):
        total = total + ((place == targets[s : s + 1]) & slots[s]).astype(jnp.float32)
    return total.astype(jnp.bfloat16)


def own_kernel(state_ref, prev_ref, wind_ref, target_ref, slope_ref, slot_ref, own_ref, part_ref, next_ref):
    slots, share = point_sets()
    sums = sum_block("own", target_ref[...].astype(jnp.int32) - 32, slots, True)
    tables = product_tables(own_ref[...], column_group(slot_ref), 0)
    early = time_step * hermite(0)[0]
    blow = [-time_step * wind_ref[d] for d in range(2)]
    slope = slope_ref[...]

    def body(at, _):
        for k in range(PARTS):
            part_ref[k, at] = chosen_product(tables, state_ref[k, at])
        state = flat(state_ref[:, at])
        motion = moved(state, slope, *blow)
        total = jnp.dot(motion, sums, preferred_element_type=jnp.float32)
        ahead = state + total * share + early * flat(prev_ref[:, at])
        next_ref[:, at] = ahead.reshape(PARTS, CHUNK, LANES)

    each_chunk(0, state_ref.shape[1] // CHUNK, body)


def far_kernel(
    first, count, state_ref, prev_ref, slot_ref, far_ref, part_ref, next_ref, tend_ref, ahead_ref, off_ref, on_ref
):
    group = column_group(slot_ref)
    here = group < 8
    tables = product_tables(far_ref[...], group, 8)
    quarter = lane_ids() // 32
    inner = (quarter == 1) | (quarter == 2)
    chosen = sides()
    late = time_step * hermite(0)[1]
    early_1, late_1 = (time_step * w for w in hermite(1))

    def body(at, here_at):
        ahead, force = [], []
        for k in range(PARTS):
            tend = jnp.where(here, part_ref[k, at], chosen_product(tables, state_ref[k, at]))
            tend = tend.astype(jnp.bfloat16)
            tend_ref[k, here_at] = tend
            tend = tend.astype(jnp.float32)
            ahead.append(next_ref[k, at] + late * tend)
            ahead_ref[k, here_at] = ahead[k]
            forced = early_1 * prev_ref[k, at].astype(jnp.float32) + late_1 * tend
            force.append(jnp.where(inner, forced, tend))
        off, on = packed_halves(force, chosen)
        for k in range(2):
            middle = jnp.where(inner, ahead[k], pltpu.roll(ahead[k + 2], 64, 1)).astype(jnp.bfloat16)
            off_ref[k, here_at] = middle
            on_ref[k, here_at] = middle
            off_ref[2 + k, here_at] = off[k].astype(jnp.bfloat16)
            on_ref[2 + k, here_at] = on[k].astype(jnp.bfloat16)

    each_chunk(first, count, body)


def near_kernel(
    state_ref,
    wind_ref,
    target_ref,
    slope_ref,
    off_ref,
    on_ref,
    add_ref,
    near_ref,
    force_ref,
    sum_ref,
    outer_sum_ref,
    blow_ref,
):
    lev = wind_ref.shape[1]
    slots, share = point_sets()
    chosen = sides()
    end = off_ref.shape[1]

    def extra(ref, k):
        return ref[k, end - 80 : end].astype(jnp.float32)

    def winds(ref):
        whole = jnp.concatenate([extra(ref, k)[:48] for k in range(3)], axis=0)
        return whole[:lev], whole[lev:]

    def targets(ref):
        return extra(ref, 0)[48:56].astype(jnp.int32) - 32

    own_t = target_ref[...].astype(jnp.int32) - 32
    near_t = jnp.where(chosen, targets(off_ref), targets(on_ref))
    near_t = near_t + jnp.where(lane_ids() < 64, LANES, -LANES)
    sum_ref[:LANES, :LANES] = sum_block("own", own_t, slots, True)
    sum_ref[LANES:, :LANES] = sum_block("near", own_t, slots, False)
    sum_ref[:LANES, LANES:] = sum_block("own", near_t, slots, False)
    sum_ref[LANES:, LANES:] = sum_block("near", near_t, slots, True)
    outer_sum_ref[...] = sum_block("outer", near_t, slots, False)
    off_w, on_w = winds(off_ref), winds(on_ref)
    for d in range(2):
        blow_ref[0, d] = -time_step * wind_ref[d]
        blow_ref[1, d] = -time_step * jnp.where(chosen, off_w[d], on_w[d])
        blow_ref[2, d] = -time_step * jnp.where(chosen, on_w[d], off_w[d])

    slope = slope_ref[...]
    early = time_step * hermite(0)[0]

    def body(at, _):
        off, on = off_ref[:, at].astype(jnp.float32), on_ref[:, at].astype(jnp.float32)
        near = whole_halves(off[:2], on[:2], chosen)
        own_move = moved(flat(state_ref[:, at]), slope, blow_ref[0, 0], blow_ref[0, 1])
        near_move = moved(near, slope, blow_ref[1, 0], blow_ref[1, 1])
        total = jnp.dot(near_move, sum_ref[LANES:], preferred_element_type=jnp.float32)
        near_total = total[:, LANES:] + jnp.dot(
            own_move, sum_ref[:LANES, LANES:], preferred_element_type=jnp.float32
        )
        add_ref[:, at] = (total[:, :LANES] * share).reshape(PARTS, CHUNK, LANES)
        prev = [jnp.where(chosen, off[2], on[2])]
        for k in range(1, PARTS):
            turned = [pltpu.roll(side[2], LANES - 32 * k, 1) for side in (off, on)]
            prev.append(jnp.where(chosen, *turned))
        prev = jnp.concatenate(prev, axis=0)
        near = near + near_total * share + early * prev
        near_ref[:, at] = near.reshape(PARTS, CHUNK, LANES)
        force_ref[:, at] = prev.astype(jnp.bfloat16).reshape(PARTS, CHUNK, LANES)

    each_chunk(0, state_ref.shape[1] // CHUNK, body)


def advance_kernel(
    first,
    ahead_ref,
    add_ref,
    near_ref,
    near_prev_ref,
    prev_ref,
    tend_ref,
    off_ref,
    on_ref,
    slope_ref,
    sum_ref,
    outer_sum_ref,
    blow_ref,
    *rest,
):
    out_hbm, tend_hbm, out_ref, sems = rest[-4:]
    count = tend_ref.shape[1]
    tend_copy = pltpu.make_async_copy(tend_ref, tend_hbm.at[:, pl.ds(first * CHUNK, count)], sems.at[0])
    tend_copy.start()
    _, share = point_sets()
    quarter = lane_ids() // 32
    inner = (quarter == 1) | (quarter == 2)
    chosen = sides()
    slope, sums = slope_ref[...], sum_ref[...]
    weights = [tuple(time_step * w for w in hermite(s)) for s in range(SUBSTEPS)]

    def advect(value, unit):
        return moved(value, slope, blow_ref[unit, 0], blow_ref[unit, 1])

    def gather(pieces, matrix):
        return jnp.dot(jnp.concatenate(pieces, axis=1), matrix, preferred_element_type=jnp.float32)

    def middle(value):
        value = value.reshape(2 * CHUNK, LANES)
        return jnp.concatenate([value, pltpu.roll(value, 64, 1)], axis=0)

    def body(at, here_at):
        off, on = off_ref[:, here_at].astype(jnp.float32), on_ref[:, here_at].astype(jnp.float32)
        off_mid, on_mid = middle(off[:2]), middle(on[:2])
        received = whole_halves(off[2:], on[2:], chosen)
        own_prev, own_tend = flat(prev_ref[:, at]), flat(tend_ref[:, here_at])
        near_prev = flat(near_prev_ref[:, at])
        own = flat(ahead_ref[:, here_at]) + flat(add_ref[:, at])
        near = flat(near_ref[:, at]) + weights[0][1] * received
        near = jnp.where(inner, jnp.where(chosen, off_mid, on_mid), near)
        outer = jnp.where(chosen, on_mid, off_mid)
        for s in range(1, SUBSTEPS):
            early, late = weights[s]
            own_force = early * own_prev + late * own_tend
            own_move, near_move = advect(own, 0), advect(near, 1)
            if s == SUBSTEPS - 1:
                total = gather([own_move, near_move], sums[:, :LANES])
                out = own + total * share + own_force
                out_ref[:, here_at] = out.reshape(PARTS, CHUNK, LANES)
                break
            near_force = early * near_prev + late * received
            total = gather([own_move, near_move], sums)
            own = own + total[:, :LANES] * share + own_force
            near_total = total[:, LANES:]
            if s == 1:
                near_force = jnp.where(inner, received, near_force)
                near_total = near_total + jnp.dot(
                    advect(outer, 2), outer_sum_ref[...], preferred_element_type=jnp.float32
                )
            near = near + near_total * share + near_force

    copies = []
    for j, here_at in enumerate(chunks(out_ref)):
        at = pl.ds((first + j) * CHUNK, CHUNK)
        body(at, here_at)
        copies.append(pltpu.make_async_copy(out_ref.at[:, here_at], out_hbm.at[:, at], sems.at[1 + j]))
        copies[j].start()
    for copy in copies:
        copy.wait()
    tend_copy.wait()


def exchanged(off, on):
    count = lax.axis_size(AXES)
    across = [(i, (i + 1) % count if i % 2 else (i - 1) % count) for i in range(count)]
    inside = [(i, i ^ 1) for i in range(count)]
    return lax.ppermute(off, AXES, across), lax.ppermute(on, AXES, inside)


def per_device(state, prev_tendency, wind, edge_links, swap_slot, inverse):
    devices = lax.axis_size(AXES)
    shape = state.shape
    lev = shape[1]
    rows = shape[0] * lev // PARTS
    params = pltpu.CompilerParams(vmem_limit_bytes=VMEM)
    bf16, f32 = jnp.bfloat16, jnp.float32
    inner = pl.BlockSpec(memory_space=pltpu.VMEM)
    outer = pl.BlockSpec(memory_space=pltpu.HBM)

    def like(count, kind, length=rows):
        return pltpu.VMEM((count, length, LANES), kind)

    def table(kind, *size):
        return pltpu.VMEM(size, kind)

    def call(body, ins, outs, name, passes, **more):
        size = sum(math.prod(array.shape) * array.dtype.itemsize for array in ins)
        cost = pl.CostEstimate(
            flops=passes * 2 * PARTS * rows * 256 * 256, bytes_accessed=2 * size, transcendentals=0
        )
        more = {"in_specs": [inner] * len(ins), "out_specs": (inner,) * len(outs)} | more
        return pl.pallas_call(
            body, out_shape=outs, compiler_params=params, cost_estimate=cost, name=name, **more
        )(*ins)

    slot = swap_slot.reshape(1, LANES)
    slope = jnp.asarray(derivative_matrix())
    message = like(3, bf16, rows + 80)
    inputs = (
        inverse,
        wind,
        edge_links,
        state.reshape(PARTS, rows, LANES),
        prev_tendency.reshape(PARTS, rows, LANES),
    )
    inputs = tuple(pltpu.with_memory_space_constraint(array, pltpu.HBM) for array in inputs)
    matrices, to_off, to_on, targets, wind, state, prev = call(
        pack_kernel,
        inputs,
        (
            table(bf16, inverse.shape[0] * lev, LANES),
            message,
            message,
            table(f32, 8, LANES),
            table(f32, *wind.shape),
            like(4, f32),
            like(4, bf16),
        ),
        "pack",
        2,
        in_specs=[outer] * len(inputs),
        scratch_shapes=[
            pltpu.VMEM(inverse.shape, f32),
            pltpu.VMEM(edge_links.shape, jnp.int32),
            pltpu.SemaphoreType.DMA((3 + 2 * PARTS,)),
        ],
    )
    far_matrices = lax.ppermute(matrices, AXES, [(i, i ^ (devices // 2)) for i in range(devices)])
    off, on = exchanged(to_off, to_on)
    part, next_state = call(
        own_kernel,
        (state, prev, wind, targets, slope, slot, matrices),
        (like(4, f32), like(4, f32)),
        "own",
        10,
    )
    halves = []
    first = 0
    for count in SPLIT:
        size = count * CHUNK
        tend, ahead, to_off, to_on = call(
            functools.partial(far_kernel, first, count),
            (state, prev, slot, far_matrices, part, next_state),
            (like(4, bf16, size), like(4, f32, size), like(4, bf16, size), like(4, bf16, size)),
            "far",
            2 * count,
        )
        halves.append((first, count, tend, ahead, exchanged(to_off, to_on)))
        first += count
    add, near, near_prev, sums, outer_sums, blow = call(
        near_kernel,
        (state, wind, targets, slope, off, on),
        (
            like(4, f32),
            like(4, f32),
            like(4, bf16),
            table(bf16, 2 * LANES, 2 * LANES),
            table(bf16, LANES, LANES),
            table(f32, 3, 2, lev, LANES),
        ),
        "near",
        8,
    )
    done = ()
    for first, count, tend, ahead, (off, on) in halves:
        ins = (ahead, add, near, near_prev, prev, tend, off, on, slope, sums, outer_sums, blow)
        done = call(
            functools.partial(advance_kernel, first),
            ins + done,
            (
                jax.ShapeDtypeStruct((PARTS, rows, LANES), f32),
                jax.ShapeDtypeStruct((PARTS, rows, LANES), bf16),
            ),
            "advance",
            5 * count,
            in_specs=[inner] * len(ins) + [outer] * len(done),
            out_specs=(outer, outer),
            scratch_shapes=[
                pltpu.VMEM((PARTS, count * CHUNK, LANES), f32),
                pltpu.SemaphoreType.DMA((1 + count,)),
            ],
            input_output_aliases={len(ins) + i: i for i in range(len(done))},
        )
    out, tend = done
    return (out.reshape(shape), tend.reshape(shape))


def solution(mesh):
    columns = P(None, None, AXES)
    return jax.shard_map(
        per_device,
        mesh=mesh,
        in_specs=(columns, columns, columns, columns, P(AXES), P(AXES, None, None)),
        out_specs=(columns, columns),
        check_vma=False,
    )
```

```python
import functools
import math

import jax
import jax.numpy as jnp
import numpy as np
from jax import lax
from jax.experimental import pallas as pl
from jax.experimental.pallas import tpu as pltpu
from jax.sharding import PartitionSpec as P

SUBSTEPS = 4
AXES = ("gx", "gy")
LANES = 128
CHUNK = 144
SPLIT = (3, 2)
PARTS = 4
VMEM = 16 * 1024 * 1024

time_step = 0.2
edge_points = ((0, 1, 2, 3), (3, 7, 11, 15), (15, 14, 13, 12), (12, 8, 4, 0))


def point_tables():
    edge_of = np.zeros((2, 16), np.int32)
    spot_of = np.zeros((2, 16), np.int32)
    weight_of = np.zeros((2, 16), np.float32)
    filled = np.zeros(16, np.int32)
    for k in range(4):
        for m in range(4):
            p = edge_points[k][m]
            s = filled[p]
            edge_of[s, p] = k
            spot_of[s, p] = m
            weight_of[s, p] = 1.0
            filled[p] = s + 1
    return (edge_of, spot_of, weight_of)


def gll_derivative():
    gll_nodes = np.array([-1.0, -1.0 / np.sqrt(5.0), 1.0 / np.sqrt(5.0), 1.0])
    factors = np.array(
        [np.prod([gll_nodes[i] - gll_nodes[k] for k in range(4) if k != i]) for i in range(4)]
    )
    derivative = np.zeros((4, 4))
    for i in range(4):
        for k in range(4):
            if i != k:
                derivative[i, k] = factors[i] / (factors[k] * (gll_nodes[i] - gll_nodes[k]))
            else:
                derivative[i, k] = sum(
                    (1.0 / (gll_nodes[i] - gll_nodes[j]) for j in range(4) if j != i)
                )
    return derivative


def derivative_matrix():
    derivative = gll_derivative()
    eye_block = np.eye(8)
    both = np.concatenate(
        [
            np.kron(eye_block, np.kron(derivative, np.eye(4)).T),
            np.kron(eye_block, np.kron(np.eye(4), derivative).T),
        ],
        axis=1,
    )
    high = both.astype(jnp.bfloat16)
    low = (both - high.astype(np.float64)).astype(jnp.bfloat16)
    return np.concatenate([high, low], axis=0)


def hermite(substep):
    instant = (substep + 1.0) / SUBSTEPS
    square = instant * instant
    cube = square * instant
    h00 = 2.0 * cube - 3.0 * square + 1.0
    h01 = -2.0 * cube + 3.0 * square
    slope = cube - 2.0 * square + instant + (cube - square)
    return (h00 - slope, h01 + slope)


def lane_ids(rows=1):
    return lax.broadcasted_iota(jnp.int32, (rows, LANES), 1)


def point_sets():
    point = lane_ids() % 16
    across = (point // 4 == 0) | (point // 4 == 3)
    along = (point % 4 == 0) | (point % 4 == 3)
    slots = (across | along, across & along)
    share = jnp.where(slots[1], 1.0 / 3.0, jnp.where(slots[0], 0.5, 1.0)).astype(jnp.float32)
    return slots, share


def edge_targets(links_ref, first_elem, element_count):
    edge_of, spot_of, _ = point_tables()
    elements = links_ref.shape[2]
    own = first_elem + lax.broadcasted_iota(jnp.int32, (4, elements), 1)
    apart = links_ref[0] - own
    half = element_count // 2
    apart = jnp.where(apart > half, apart - element_count, apart)
    apart = jnp.where(apart < -half, apart + element_count, apart) + 2
    both = jnp.concatenate([apart, links_ref[1]], axis=0).astype(jnp.float32)
    spread = lax.broadcasted_iota(jnp.int32, (elements, LANES), 0)
    spread = (spread == lax.broadcasted_iota(jnp.int32, (elements, LANES), 1) // 16).astype(jnp.float32)
    both = jnp.dot(both, spread, preferred_element_type=jnp.float32)
    both = (both + 0.5).astype(jnp.int32)
    lane = lane_ids()
    point = lane % 16
    rows = []
    for s in range(2):
        edge = jnp.zeros((1, LANES), jnp.int32)
        spot = edge
        for p in range(16):
            edge = jnp.where(point == p, int(edge_of[s, p]), edge)
            spot = jnp.where(point == p, int(spot_of[s, p]), spot)
        away, far = both[0:1], both[4:5]
        for k in range(1, 4):
            away = jnp.where(edge == k, both[k : k + 1], away)
            far = jnp.where(edge == k, both[4 + k : 5 + k], far)
        place = jnp.where(far == 2, 12 + spot, 4 * spot)
        place = jnp.where(far == 1, 15 - 4 * spot, place)
        place = jnp.where(far == 0, 3 - spot, place)
        rows.append(lane - point + 16 * away + place)
    rows = jnp.concatenate(rows + [jnp.zeros((6, LANES), jnp.int32)], axis=0)
    return rows.astype(jnp.float32)


def on_odd():
    return lax.axis_index(AXES) % 2 == 1


def sides():
    return (lane_ids() < 64) == on_odd()


def packed_halves(value, chosen):
    away = [pltpu.roll(value[k + 2], 64, 1) for k in range(2)]
    off = [jnp.where(chosen, away[k], value[k]) for k in range(2)]
    on = [jnp.where(chosen, value[k], away[k]) for k in range(2)]
    return off, on


def whole_halves(off, on, chosen):
    count, rows = off.shape[0], off.shape[1]
    direct = jnp.where(chosen, off, on).reshape(count * rows, LANES)
    turned = jnp.where(chosen, on, off).reshape(count * rows, LANES)
    return jnp.concatenate([direct, pltpu.roll(turned, 64, 1)], axis=0)


def pack_kernel(
    inverse_hbm,
    wind_hbm,
    links_hbm,
    state_hbm,
    prev_hbm,
    matrix_ref,
    off_ref,
    on_ref,
    target_ref,
    wind_ref,
    state_ref,
    prev_ref,
    inverse_ref,
    links_ref,
    sems,
):
    pairs = [(inverse_hbm, inverse_ref), (wind_hbm, wind_ref), (links_hbm, links_ref)]
    for k in range(PARTS):
        pairs += [(state_hbm.at[k], state_ref.at[k]), (prev_hbm.at[k], prev_ref.at[k])]
    copies = [pltpu.make_async_copy(a, b, sems.at[i]) for i, (a, b) in enumerate(pairs)]
    for copy in copies:
        copy.start()
    groups, lev = inverse_ref.shape[0], inverse_ref.shape[1]
    copies[0].wait()
    eye = lax.broadcasted_iota(jnp.int32, (lev, lev), 0) == lax.broadcasted_iota(jnp.int32, (lev, lev), 1)
    eye = eye.astype(jnp.float32)
    blank = jnp.zeros((lev, LANES - lev), jnp.float32)
    matrix = [jnp.concatenate([inverse_ref[c] - eye, blank], axis=1) for c in range(groups)]
    matrix_ref[...] = jnp.concatenate(matrix, axis=0).astype(jnp.bfloat16)
    copies[1].wait()
    copies[2].wait()
    devices = lax.axis_size(AXES)
    elements = links_ref.shape[2]
    targets = edge_targets(links_ref, lax.axis_index(AXES) * elements, elements * devices)
    target_ref[...] = targets
    end = off_ref.shape[1]
    filler = jnp.zeros((24, LANES), jnp.float32)
    flat_wind = wind_ref[...].reshape(2 * lev, LANES)
    for k in range(3):
        piece = jnp.concatenate([flat_wind[48 * k : 48 * k + 48], targets, filler], axis=0)
        piece = piece.astype(jnp.bfloat16)
        off_ref[k, end - 80 : end] = piece
        on_ref[k, end - 80 : end] = piece
    chosen = sides()
    odd = jnp.where(on_odd(), 3, 0)
    quarter = lane_ids() // 32
    for copy in copies[3:]:
        copy.wait()
    for at in chunks(state_ref):
        off, on = packed_halves([state_ref[k, at] for k in range(PARTS)], chosen)
        for k in range(2):
            off_ref[k, at] = off[k].astype(jnp.bfloat16)
            on_ref[k, at] = on[k].astype(jnp.bfloat16)
        to_off = jnp.zeros((CHUNK, LANES), jnp.float32)
        to_on = to_off
        for k in range(PARTS):
            turned = prev_ref[k, at].astype(jnp.float32)
            turned = pltpu.roll(turned, 32 * k, 1) if k else turned
            to_off = jnp.where(quarter == (odd + k) % 4, turned, to_off)
            to_on = jnp.where(quarter == (3 - odd + k) % 4, turned, to_on)
        off_ref[2, at] = to_off.astype(jnp.bfloat16)
        on_ref[2, at] = to_on.astype(jnp.bfloat16)


def chunks(ref):
    return [pl.ds(start, CHUNK) for start in range(0, ref.shape[1], CHUNK)]


def each_chunk(first, count, body):
    def step(j, carry):
        near, whole = j * CHUNK, (first + j) * CHUNK
        body(pl.ds(pl.multiple_of(whole, CHUNK), CHUNK), pl.ds(pl.multiple_of(near, CHUNK), CHUNK))
        return carry

    lax.fori_loop(0, count, step, 0, unroll=True)


def chosen_product(matrices, group, pair):
    lev = pair.shape[0] // 2
    blank = jnp.zeros((LANES - lev, 2 * LANES), jnp.float32)
    pair = jnp.concatenate([pair[:lev], pair[lev:]], axis=1)
    high = pair.astype(jnp.bfloat16).astype(jnp.float32)
    column = jnp.concatenate([high, blank, pair - high, blank], axis=0).astype(jnp.bfloat16)
    product = jnp.dot(matrices, column, preferred_element_type=jnp.float32)
    chosen = product[:lev]
    for c in range(1, matrices.shape[0] // lev):
        chosen = jnp.where(group == c, product[c * lev : (c + 1) * lev], chosen)
    return jnp.concatenate([chosen[:, :LANES], chosen[:, LANES:]], axis=0)


def column_group(slot_ref):
    slot = slot_ref[...]
    return jnp.where(slot // LANES == lax.axis_index(AXES), 0, 8) + slot % LANES // 16


def flat(value):
    return value.astype(jnp.float32).reshape(-1, LANES)


def moved(value, slope, blow_x, blow_y):
    rows, lev = value.shape[0], blow_x.shape[0]
    value = value.astype(jnp.bfloat16)
    both = jnp.dot(jnp.concatenate([value, value], axis=1), slope, preferred_element_type=jnp.float32)
    both = both.reshape(rows // lev, lev, 2 * LANES)
    motion = both[..., :LANES] * blow_x + both[..., LANES:] * blow_y
    return motion.reshape(rows, LANES).astype(jnp.bfloat16)


def sum_block(source, targets, slots, own):
    row = lax.broadcasted_iota(jnp.int32, (LANES, LANES), 0)
    total = jnp.zeros((LANES, LANES), jnp.float32)
    if own:
        total = (row == lax.broadcasted_iota(jnp.int32, (LANES, LANES), 1)).astype(jnp.float32)
    place = {
        "own": row,
        "near": jnp.where(row < 64, row + LANES, row - LANES),
        "near turned": jnp.where(row < 64, row - 64, row + 64),
        "outer": jnp.where(row < 64, row - LANES, row + LANES),
        "outer turned": jnp.where(row < 64, row + LANES + 64, row - LANES - 64),
    }[source]
    for s in range(2):
        total = total + ((place == targets[s : s + 1]) & slots[s]).astype(jnp.float32)
    return total.astype(jnp.bfloat16)


def inner_lanes():
    quarter = lane_ids() // 32
    return (quarter == 1) | (quarter == 2)


def physics_kernel(
    first,
    count,
    state_ref,
    prev_ref,
    wind_ref,
    target_ref,
    slope_ref,
    slot_ref,
    own_ref,
    far_ref,
    tend_ref,
    ahead_ref,
    off_ref,
    on_ref,
):
    slots, share = point_sets()
    sums = sum_block("own", target_ref[...].astype(jnp.int32) - 32, slots, True)
    matrices = jnp.concatenate([own_ref[...], far_ref[...]], axis=0)
    matrices = jnp.concatenate([matrices, matrices], axis=1)
    group = column_group(slot_ref)
    group = jnp.concatenate([group, group], axis=1)
    inner = inner_lanes()
    chosen = sides()
    early, late = (time_step * w for w in hermite(0))
    early_1, late_1 = (time_step * w for w in hermite(1))
    blow = [-time_step * wind_ref[d] for d in range(2)]
    slope = slope_ref[...]

    def body(at, here_at):
        state, prev = flat(state_ref[:, at]), flat(prev_ref[:, at])
        motion = moved(state, slope, *blow)
        total = jnp.dot(motion, sums, preferred_element_type=jnp.float32)
        start = state + total * share + early * prev
        ahead, force = [], []
        for k in range(PARTS):
            rows = slice(k * CHUNK, (k + 1) * CHUNK)
            tend = chosen_product(matrices, group, state_ref[k, at]).astype(jnp.bfloat16)
            tend_ref[k, here_at] = tend
            tend = tend.astype(jnp.float32)
            ahead.append(start[rows] + late * tend)
            ahead_ref[k, here_at] = ahead[k]
            force.append(jnp.where(inner, early_1 * prev[rows] + late_1 * tend, tend))
        off, on = packed_halves(force, chosen)
        for k in range(2):
            middle = jnp.where(inner, ahead[k], pltpu.roll(ahead[k + 2], 64, 1)).astype(jnp.bfloat16)
            off_ref[k, here_at] = middle
            on_ref[k, here_at] = middle
            off_ref[2 + k, here_at] = off[k].astype(jnp.bfloat16)
            on_ref[2 + k, here_at] = on[k].astype(jnp.bfloat16)

    each_chunk(first, count, body)


def near_kernel(
    state_ref,
    wind_ref,
    target_ref,
    slope_ref,
    off_ref,
    on_ref,
    add_ref,
    near_ref,
    force_ref,
    sum_ref,
    edge_sum_ref,
    blow_ref,
):
    lev = wind_ref.shape[1]
    slots, share = point_sets()
    chosen = sides()
    end = off_ref.shape[1]

    def extra(ref, k):
        return ref[k, end - 80 : end].astype(jnp.float32)

    def winds(ref):
        whole = jnp.concatenate([extra(ref, k)[:48] for k in range(3)], axis=0)
        return whole[:lev], whole[lev:]

    def targets(ref):
        return extra(ref, 0)[48:56].astype(jnp.int32) - 32

    own_t = target_ref[...].astype(jnp.int32) - 32
    near_t = jnp.where(chosen, targets(off_ref), targets(on_ref))
    near_t = near_t + jnp.where(lane_ids() < 64, LANES, -LANES)
    sum_ref[:LANES, :LANES] = sum_block("own", own_t, slots, True)
    sum_ref[LANES:, :LANES] = sum_block("near", own_t, slots, False)
    sum_ref[:LANES, LANES:] = sum_block("own", near_t, slots, False)
    sum_ref[LANES:, LANES:] = sum_block("near", near_t, slots, True)
    edge_sum_ref[0, :, :LANES] = sum_block("outer", near_t, slots, False)
    edge_sum_ref[0, :, LANES:] = sum_block("outer turned", near_t, slots, False)
    edge_sum_ref[1, :, :LANES] = sum_block("near", own_t, slots, False)
    edge_sum_ref[1, :, LANES:] = sum_block("near turned", own_t, slots, False)
    inner = inner_lanes()
    off_w, on_w = winds(off_ref), winds(on_ref)
    for d in range(2):
        blow_ref[0, d] = -time_step * wind_ref[d]
        near_w = -time_step * jnp.where(chosen, off_w[d], on_w[d])
        outer_w = -time_step * jnp.where(chosen, on_w[d], off_w[d])
        blow_ref[1, d] = near_w
        blow_ref[2, d] = jnp.where(inner, outer_w, pltpu.roll(outer_w, 64, 1))
        blow_ref[3, d] = jnp.where(inner, pltpu.roll(near_w, 64, 1), near_w)

    slope = slope_ref[...]
    early = time_step * hermite(0)[0]

    def body(at, _):
        off, on = off_ref[:, at].astype(jnp.float32), on_ref[:, at].astype(jnp.float32)
        near = whole_halves(off[:2], on[:2], chosen)
        own_move = moved(flat(state_ref[:, at]), slope, blow_ref[0, 0], blow_ref[0, 1])
        near_move = moved(near, slope, blow_ref[1, 0], blow_ref[1, 1])
        total = jnp.dot(near_move, sum_ref[LANES:], preferred_element_type=jnp.float32)
        near_total = total[:, LANES:] + jnp.dot(
            own_move, sum_ref[:LANES, LANES:], preferred_element_type=jnp.float32
        )
        add_ref[:, at] = (total[:, :LANES] * share).reshape(PARTS, CHUNK, LANES)
        prev = [jnp.where(chosen, off[2], on[2])]
        for k in range(1, PARTS):
            turned = [pltpu.roll(side[2], LANES - 32 * k, 1) for side in (off, on)]
            prev.append(jnp.where(chosen, *turned))
        prev = jnp.concatenate(prev, axis=0)
        near = near + near_total * share + early * prev
        near_ref[:, at] = near.reshape(PARTS, CHUNK, LANES)
        force_ref[:, at] = prev.astype(jnp.bfloat16).reshape(PARTS, CHUNK, LANES)

    each_chunk(0, state_ref.shape[1] // CHUNK, body)


def advance_kernel(
    first,
    ahead_ref,
    add_ref,
    near_ref,
    near_prev_ref,
    prev_ref,
    tend_ref,
    off_ref,
    on_ref,
    slope_ref,
    sum_ref,
    edge_sum_ref,
    blow_ref,
    *rest,
):
    out_hbm, tend_hbm, out_ref, sems = rest[-4:]
    count = tend_ref.shape[1]
    tend_copy = pltpu.make_async_copy(tend_ref, tend_hbm.at[:, pl.ds(first * CHUNK, count)], sems.at[0])
    tend_copy.start()
    _, share = point_sets()
    inner = inner_lanes()
    chosen = sides()
    slope, sums = slope_ref[...], sum_ref[...]
    weights = [tuple(time_step * w for w in hermite(s)) for s in range(SUBSTEPS)]

    def advect(value, unit):
        return moved(value, slope, blow_ref[unit, 0], blow_ref[unit, 1])

    def gather(pieces, matrix):
        return jnp.dot(jnp.concatenate(pieces, axis=1), matrix, preferred_element_type=jnp.float32)

    def shared(value, which):
        total = jnp.dot(value, edge_sum_ref[which], preferred_element_type=jnp.float32)
        return jnp.concatenate([total[:, :LANES], total[:, LANES:]], axis=0)

    def body(at, here_at):
        off, on = off_ref[:, here_at].astype(jnp.float32), on_ref[:, here_at].astype(jnp.float32)
        off_mid, on_mid = flat(off[:2]), flat(on[:2])
        middle = [jnp.where(chosen, off_mid, on_mid), jnp.where(chosen, on_mid, off_mid)]
        middle = jnp.concatenate([middle[0], pltpu.roll(middle[1], 64, 1)], axis=0)
        outer = jnp.where(chosen == inner, on_mid, off_mid)
        received = whole_halves(off[2:], on[2:], chosen)
        own_prev, own_tend = flat(prev_ref[:, at]), flat(tend_ref[:, here_at])
        near_prev = flat(near_prev_ref[:, at])
        own = flat(ahead_ref[:, here_at]) + flat(add_ref[:, at])
        near = flat(near_ref[:, at]) + weights[0][1] * received
        near = jnp.where(inner, middle, near)
        for s in range(1, SUBSTEPS):
            early, late = weights[s]
            own_force = early * own_prev + late * own_tend
            own_move = advect(own, 0)
            if s == SUBSTEPS - 1:
                half = near.shape[0] // 2
                near = jnp.where(inner, pltpu.roll(near[half:], 64, 1), near[:half])
                total = jnp.dot(own_move, sums[:LANES, :LANES], preferred_element_type=jnp.float32)
                total = total + shared(advect(near, 3), 1)
                out = own + total * share + own_force
                out_ref[:, here_at] = out.reshape(PARTS, CHUNK, LANES)
                break
            near_force = early * near_prev + late * received
            total = gather([own_move, advect(near, 1)], sums)
            own = own + total[:, :LANES] * share + own_force
            near_total = total[:, LANES:]
            if s == 1:
                near_force = jnp.where(inner, received, near_force)
                near_total = near_total + shared(advect(outer, 2), 0)
            near = near + near_total * share + near_force

    copies = []
    for j, here_at in enumerate(chunks(out_ref)):
        at = pl.ds((first + j) * CHUNK, CHUNK)
        body(at, here_at)
        copies.append(pltpu.make_async_copy(out_ref.at[:, here_at], out_hbm.at[:, at], sems.at[1 + j]))
        copies[j].start()
    for copy in copies:
        copy.wait()
    tend_copy.wait()


def exchanged(off, on):
    count = lax.axis_size(AXES)
    across = [(i, (i + 1) % count if i % 2 else (i - 1) % count) for i in range(count)]
    inside = [(i, i ^ 1) for i in range(count)]
    return lax.ppermute(off, AXES, across), lax.ppermute(on, AXES, inside)


def per_device(state, prev_tendency, wind, edge_links, swap_slot, inverse):
    devices = lax.axis_size(AXES)
    shape = state.shape
    lev = shape[1]
    rows = shape[0] * lev // PARTS
    params = pltpu.CompilerParams(vmem_limit_bytes=VMEM)
    bf16, f32 = jnp.bfloat16, jnp.float32
    inner = pl.BlockSpec(memory_space=pltpu.VMEM)
    outer = pl.BlockSpec(memory_space=pltpu.HBM)

    def like(count, kind, length=rows):
        return pltpu.VMEM((count, length, LANES), kind)

    def table(kind, *size):
        return pltpu.VMEM(size, kind)

    def call(body, ins, outs, name, passes, **more):
        size = sum(math.prod(array.shape) * array.dtype.itemsize for array in ins)
        cost = pl.CostEstimate(
            flops=passes * 2 * PARTS * rows * 256 * 256, bytes_accessed=2 * size, transcendentals=0
        )
        more = {"in_specs": [inner] * len(ins), "out_specs": (inner,) * len(outs)} | more
        return pl.pallas_call(
            body, out_shape=outs, compiler_params=params, cost_estimate=cost, name=name, **more
        )(*ins)

    slot = swap_slot.reshape(1, LANES)
    slope = jnp.asarray(derivative_matrix())
    message = like(3, bf16, rows + 80)
    inputs = (
        inverse,
        wind,
        edge_links,
        state.reshape(PARTS, rows, LANES),
        prev_tendency.reshape(PARTS, rows, LANES),
    )
    inputs = tuple(pltpu.with_memory_space_constraint(array, pltpu.HBM) for array in inputs)
    matrices, to_off, to_on, targets, wind, state, prev = call(
        pack_kernel,
        inputs,
        (
            table(bf16, inverse.shape[0] * lev, LANES),
            message,
            message,
            table(f32, 8, LANES),
            table(f32, *wind.shape),
            like(4, f32),
            like(4, bf16),
        ),
        "pack",
        2,
        in_specs=[outer] * len(inputs),
        scratch_shapes=[
            pltpu.VMEM(inverse.shape, f32),
            pltpu.VMEM(edge_links.shape, jnp.int32),
            pltpu.SemaphoreType.DMA((3 + 2 * PARTS,)),
        ],
    )
    far_matrices = lax.ppermute(matrices, AXES, [(i, i ^ (devices // 2)) for i in range(devices)])
    off, on = exchanged(to_off, to_on)
    halves = []
    first = 0
    for count in SPLIT:
        size = count * CHUNK
        tend, ahead, to_off, to_on = call(
            functools.partial(physics_kernel, first, count),
            (state, prev, wind, targets, slope, slot, matrices, far_matrices),
            (like(4, bf16, size), like(4, f32, size), like(4, bf16, size), like(4, bf16, size)),
            "physics",
            5 * count,
        )
        halves.append((first, count, tend, ahead, exchanged(to_off, to_on)))
        first += count
    add, near, near_prev, sums, edge_sums, blow = call(
        near_kernel,
        (state, wind, targets, slope, off, on),
        (
            like(4, f32),
            like(4, f32),
            like(4, bf16),
            table(bf16, 2 * LANES, 2 * LANES),
            table(bf16, 2, LANES, 2 * LANES),
            table(f32, 4, 2, lev, LANES),
        ),
        "near",
        8,
    )
    done = ()
    for first, count, tend, ahead, (off, on) in halves:
        ins = (ahead, add, near, near_prev, prev, tend, off, on, slope, sums, edge_sums, blow)
        done = call(
            functools.partial(advance_kernel, first),
            ins + done,
            (
                jax.ShapeDtypeStruct((PARTS, rows, LANES), f32),
                jax.ShapeDtypeStruct((PARTS, rows, LANES), bf16),
            ),
            "advance",
            5 * count,
            in_specs=[inner] * len(ins) + [outer] * len(done),
            out_specs=(outer, outer),
            scratch_shapes=[
                pltpu.VMEM((PARTS, count * CHUNK, LANES), f32),
                pltpu.SemaphoreType.DMA((1 + count,)),
            ],
            input_output_aliases={len(ins) + i: i for i in range(len(done))},
        )
    out, tend = done
    return (out.reshape(shape), tend.reshape(shape))


def solution(mesh):
    columns = P(None, None, AXES)
    return jax.shard_map(
        per_device,
        mesh=mesh,
        in_specs=(columns, columns, columns, columns, P(AXES), P(AXES, None, None)),
        out_specs=(columns, columns),
        check_vma=False,
    )
```

```python
import functools
import math

import jax
import jax.numpy as jnp
import numpy as np
from jax import lax
from jax.experimental import pallas as pl
from jax.experimental.pallas import tpu as pltpu
from jax.sharding import PartitionSpec as P

SUBSTEPS = 4
AXES = ("gx", "gy")
LANES = 128
CHUNK = 144
SPLIT = (3, 2)
PARTS = 4
VMEM = 16 * 1024 * 1024

time_step = 0.2
edge_points = ((0, 1, 2, 3), (3, 7, 11, 15), (15, 14, 13, 12), (12, 8, 4, 0))


def point_tables():
    edge_of = np.zeros((2, 16), np.int32)
    spot_of = np.zeros((2, 16), np.int32)
    weight_of = np.zeros((2, 16), np.float32)
    filled = np.zeros(16, np.int32)
    for k in range(4):
        for m in range(4):
            p = edge_points[k][m]
            s = filled[p]
            edge_of[s, p] = k
            spot_of[s, p] = m
            weight_of[s, p] = 1.0
            filled[p] = s + 1
    return (edge_of, spot_of, weight_of)


def gll_derivative():
    gll_nodes = np.array([-1.0, -1.0 / np.sqrt(5.0), 1.0 / np.sqrt(5.0), 1.0])
    factors = np.array(
        [np.prod([gll_nodes[i] - gll_nodes[k] for k in range(4) if k != i]) for i in range(4)]
    )
    derivative = np.zeros((4, 4))
    for i in range(4):
        for k in range(4):
            if i != k:
                derivative[i, k] = factors[i] / (factors[k] * (gll_nodes[i] - gll_nodes[k]))
            else:
                derivative[i, k] = sum(
                    (1.0 / (gll_nodes[i] - gll_nodes[j]) for j in range(4) if j != i)
                )
    return derivative


def derivative_matrix():
    derivative = gll_derivative()
    eye_block = np.eye(8)
    both = np.concatenate(
        [
            np.kron(eye_block, np.kron(derivative, np.eye(4)).T),
            np.kron(eye_block, np.kron(np.eye(4), derivative).T),
        ],
        axis=1,
    )
    high = both.astype(jnp.bfloat16)
    low = (both - high.astype(np.float64)).astype(jnp.bfloat16)
    return np.concatenate([high, low], axis=0)


def hermite(substep):
    instant = (substep + 1.0) / SUBSTEPS
    square = instant * instant
    cube = square * instant
    h00 = 2.0 * cube - 3.0 * square + 1.0
    h01 = -2.0 * cube + 3.0 * square
    slope = cube - 2.0 * square + instant + (cube - square)
    return (h00 - slope, h01 + slope)


def lane_ids(rows=1):
    return lax.broadcasted_iota(jnp.int32, (rows, LANES), 1)


def point_sets():
    point = lane_ids() % 16
    across = (point // 4 == 0) | (point // 4 == 3)
    along = (point % 4 == 0) | (point % 4 == 3)
    slots = (across | along, across & along)
    share = jnp.where(slots[1], 1.0 / 3.0, jnp.where(slots[0], 0.5, 1.0)).astype(jnp.float32)
    return slots, share


def edge_targets(links_ref, first_elem, element_count):
    edge_of, spot_of, _ = point_tables()
    elements = links_ref.shape[2]
    own = first_elem + lax.broadcasted_iota(jnp.int32, (4, elements), 1)
    apart = links_ref[0] - own
    half = element_count // 2
    apart = jnp.where(apart > half, apart - element_count, apart)
    apart = jnp.where(apart < -half, apart + element_count, apart) + 2
    both = jnp.concatenate([apart, links_ref[1]], axis=0).astype(jnp.float32)
    spread = lax.broadcasted_iota(jnp.int32, (elements, LANES), 0)
    spread = (spread == lax.broadcasted_iota(jnp.int32, (elements, LANES), 1) // 16).astype(jnp.float32)
    both = jnp.dot(both, spread, preferred_element_type=jnp.float32)
    both = (both + 0.5).astype(jnp.int32)
    lane = lane_ids()
    point = lane % 16
    rows = []
    for s in range(2):
        edge = jnp.zeros((1, LANES), jnp.int32)
        spot = edge
        for p in range(16):
            edge = jnp.where(point == p, int(edge_of[s, p]), edge)
            spot = jnp.where(point == p, int(spot_of[s, p]), spot)
        away, far = both[0:1], both[4:5]
        for k in range(1, 4):
            away = jnp.where(edge == k, both[k : k + 1], away)
            far = jnp.where(edge == k, both[4 + k : 5 + k], far)
        place = jnp.where(far == 2, 12 + spot, 4 * spot)
        place = jnp.where(far == 1, 15 - 4 * spot, place)
        place = jnp.where(far == 0, 3 - spot, place)
        rows.append(lane - point + 16 * away + place)
    rows = jnp.concatenate(rows + [jnp.zeros((6, LANES), jnp.int32)], axis=0)
    return rows.astype(jnp.float32)


def on_odd():
    return lax.axis_index(AXES) % 2 == 1


def sides():
    return (lane_ids() < 64) == on_odd()


def packed_halves(value, chosen):
    away = [pltpu.roll(value[k + 2], 64, 1) for k in range(2)]
    off = [jnp.where(chosen, away[k], value[k]) for k in range(2)]
    on = [jnp.where(chosen, value[k], away[k]) for k in range(2)]
    return off, on


def whole_halves(off, on, chosen):
    count, rows = off.shape[0], off.shape[1]
    direct = jnp.where(chosen, off, on).reshape(count * rows, LANES)
    turned = jnp.where(chosen, on, off).reshape(count * rows, LANES)
    return jnp.concatenate([direct, pltpu.roll(turned, 64, 1)], axis=0)


def pack_kernel(
    inverse_hbm,
    wind_hbm,
    links_hbm,
    state_hbm,
    prev_hbm,
    matrix_ref,
    off_ref,
    on_ref,
    target_ref,
    wind_ref,
    state_ref,
    prev_ref,
    inverse_ref,
    links_ref,
    sems,
):
    pairs = [(inverse_hbm, inverse_ref), (wind_hbm, wind_ref), (links_hbm, links_ref)]
    for k in range(PARTS):
        pairs += [(state_hbm.at[k], state_ref.at[k]), (prev_hbm.at[k], prev_ref.at[k])]
    copies = [pltpu.make_async_copy(a, b, sems.at[i]) for i, (a, b) in enumerate(pairs)]
    for copy in copies:
        copy.start()
    groups, lev = inverse_ref.shape[0], inverse_ref.shape[1]
    copies[0].wait()
    eye = lax.broadcasted_iota(jnp.int32, (lev, lev), 0) == lax.broadcasted_iota(jnp.int32, (lev, lev), 1)
    eye = eye.astype(jnp.float32)
    blank = jnp.zeros((lev, LANES - lev), jnp.float32)
    matrix = [jnp.concatenate([inverse_ref[c] - eye, blank], axis=1) for c in range(groups)]
    matrix_ref[...] = jnp.concatenate(matrix, axis=0).astype(jnp.bfloat16)
    copies[1].wait()
    copies[2].wait()
    devices = lax.axis_size(AXES)
    elements = links_ref.shape[2]
    targets = edge_targets(links_ref, lax.axis_index(AXES) * elements, elements * devices)
    target_ref[...] = targets
    end = off_ref.shape[1]
    filler = jnp.zeros((24, LANES), jnp.float32)
    flat_wind = wind_ref[...].reshape(2 * lev, LANES)
    for k in range(3):
        piece = jnp.concatenate([flat_wind[48 * k : 48 * k + 48], targets, filler], axis=0)
        piece = piece.astype(jnp.bfloat16)
        off_ref[k, end - 80 : end] = piece
        on_ref[k, end - 80 : end] = piece
    chosen = sides()
    odd = jnp.where(on_odd(), 3, 0)
    quarter = lane_ids() // 32
    for copy in copies[3:]:
        copy.wait()
    for at in chunks(state_ref):
        off, on = packed_halves([state_ref[k, at] for k in range(PARTS)], chosen)
        for k in range(2):
            off_ref[k, at] = off[k].astype(jnp.bfloat16)
            on_ref[k, at] = on[k].astype(jnp.bfloat16)
        to_off = jnp.zeros((CHUNK, LANES), jnp.float32)
        to_on = to_off
        for k in range(PARTS):
            turned = prev_ref[k, at].astype(jnp.float32)
            turned = pltpu.roll(turned, 32 * k, 1) if k else turned
            to_off = jnp.where(quarter == (odd + k) % 4, turned, to_off)
            to_on = jnp.where(quarter == (3 - odd + k) % 4, turned, to_on)
        off_ref[2, at] = to_off.astype(jnp.bfloat16)
        on_ref[2, at] = to_on.astype(jnp.bfloat16)


def chunks(ref):
    return [pl.ds(start, CHUNK) for start in range(0, ref.shape[1], CHUNK)]


def each_chunk(first, count, body):
    def step(j, carry):
        near, whole = j * CHUNK, (first + j) * CHUNK
        body(pl.ds(pl.multiple_of(whole, CHUNK), CHUNK), pl.ds(pl.multiple_of(near, CHUNK), CHUNK))
        return carry

    lax.fori_loop(0, count, step, 0, unroll=True)


def chosen_product(matrices, group, pair, chosen=None, first=0):
    lev = pair.shape[0] // 2
    blank = jnp.zeros((LANES - lev, 2 * LANES), jnp.float32)
    pair = jnp.concatenate([pair[:lev], pair[lev:]], axis=1)
    high = pair.astype(jnp.bfloat16).astype(jnp.float32)
    column = jnp.concatenate([high, blank, pair - high, blank], axis=0).astype(jnp.bfloat16)
    product = jnp.dot(matrices, column, preferred_element_type=jnp.float32)
    for c in range(matrices.shape[0] // lev):
        part = product[c * lev : (c + 1) * lev]
        chosen = part if chosen is None else jnp.where(group == first + c, part, chosen)
    return chosen


def as_rows(pair):
    return jnp.concatenate([pair[:, :LANES], pair[:, LANES:]], axis=0)


def column_group(slot_ref):
    slot = slot_ref[...]
    return jnp.where(slot // LANES == lax.axis_index(AXES), 0, 8) + slot % LANES // 16


def flat(value):
    return value.astype(jnp.float32).reshape(-1, LANES)


def moved(value, slope, blow_x, blow_y):
    rows, lev = value.shape[0], blow_x.shape[0]
    value = value.astype(jnp.bfloat16)
    both = jnp.dot(jnp.concatenate([value, value], axis=1), slope, preferred_element_type=jnp.float32)
    both = both.reshape(rows // lev, lev, 2 * LANES)
    motion = both[..., :LANES] * blow_x + both[..., LANES:] * blow_y
    return motion.reshape(rows, LANES).astype(jnp.bfloat16)


def sum_block(source, targets, slots, own):
    row = lax.broadcasted_iota(jnp.int32, (LANES, LANES), 0)
    total = jnp.zeros((LANES, LANES), jnp.float32)
    if own:
        total = (row == lax.broadcasted_iota(jnp.int32, (LANES, LANES), 1)).astype(jnp.float32)
    place = {
        "own": row,
        "near": jnp.where(row < 64, row + LANES, row - LANES),
        "near turned": jnp.where(row < 64, row - 64, row + 64),
        "outer": jnp.where(row < 64, row - LANES, row + LANES),
        "outer turned": jnp.where(row < 64, row + LANES + 64, row - LANES - 64),
    }[source]
    for s in range(2):
        total = total + ((place == targets[s : s + 1]) & slots[s]).astype(jnp.float32)
    return total.astype(jnp.bfloat16)


def inner_lanes():
    quarter = lane_ids() // 32
    return (quarter == 1) | (quarter == 2)


class Physics:
    def __init__(self, slot_ref, matrix_refs):
        matrices = jnp.concatenate([ref[...] for ref in matrix_refs], axis=0)
        self.matrices = jnp.concatenate([matrices, matrices], axis=1)
        group = column_group(slot_ref)
        self.group = jnp.concatenate([group, group], axis=1)
        self.inner = inner_lanes()
        self.chosen = sides()

    def begin(self, wind_ref, target_ref, slope_ref):
        slots, self.share = point_sets()
        self.sums = sum_block("own", target_ref[...].astype(jnp.int32) - 32, slots, True)
        self.blow = [-time_step * wind_ref[d] for d in range(2)]
        self.slope = slope_ref[...]

    def start(self, state, prev):
        motion = moved(state, self.slope, *self.blow)
        total = jnp.dot(motion, self.sums, preferred_element_type=jnp.float32)
        return state + total * self.share + time_step * hermite(0)[0] * prev

    def finish(self, start, prev, tends, here_at, tend_ref, ahead_ref, off_ref, on_ref):
        late = time_step * hermite(0)[1]
        early_1, late_1 = (time_step * w for w in hermite(1))
        ahead, force = [], []
        for k, tend in enumerate(tends):
            tend = tend.astype(jnp.bfloat16)
            tend_ref[k, here_at] = tend
            tend = tend.astype(jnp.float32)
            ahead.append(start[k] + late * tend)
            ahead_ref[k, here_at] = ahead[k]
            force.append(jnp.where(self.inner, early_1 * prev[k] + late_1 * tend, tend))
        off, on = packed_halves(force, self.chosen)
        for k in range(2):
            middle = jnp.where(self.inner, ahead[k], pltpu.roll(ahead[k + 2], 64, 1))
            middle = middle.astype(jnp.bfloat16)
            off_ref[k, here_at] = middle
            on_ref[k, here_at] = middle
            off_ref[2 + k, here_at] = off[k].astype(jnp.bfloat16)
            on_ref[2 + k, here_at] = on[k].astype(jnp.bfloat16)


def own_kernel(
    first, count, state_ref, prev_ref, wind_ref, target_ref, slope_ref, slot_ref, own_ref, part_ref, start_ref
):
    physics = Physics(slot_ref, [own_ref])
    physics.begin(wind_ref, target_ref, slope_ref)
    def body(at, here_at):
        start = physics.start(flat(state_ref[:, at]), flat(prev_ref[:, at]))
        start_ref[:, here_at] = start.reshape(PARTS, CHUNK, LANES)
        for k in range(PARTS):
            chosen = chosen_product(physics.matrices, physics.group, state_ref[k, at])
            part_ref[k, here_at] = as_rows(chosen)

    each_chunk(first, count, body)


def far_kernel(
    first, count, state_ref, prev_ref, slot_ref, far_ref, part_ref, start_ref, tend_ref, ahead_ref, off_ref, on_ref
):
    physics = Physics(slot_ref, [far_ref])

    def body(at, here_at):
        tends = []
        for k in range(PARTS):
            pair = part_ref[k, here_at]
            lev = pair.shape[0] // 2
            pair = jnp.concatenate([pair[:lev], pair[lev:]], axis=1)
            tends.append(as_rows(chosen_product(physics.matrices, physics.group, state_ref[k, at], pair, 8)))
        start = [start_ref[k, here_at] for k in range(PARTS)]
        prev = [prev_ref[k, at].astype(jnp.float32) for k in range(PARTS)]
        physics.finish(start, prev, tends, here_at, tend_ref, ahead_ref, off_ref, on_ref)

    each_chunk(first, count, body)


def physics_kernel(
    first,
    count,
    state_ref,
    prev_ref,
    wind_ref,
    target_ref,
    slope_ref,
    slot_ref,
    own_ref,
    far_ref,
    tend_ref,
    ahead_ref,
    off_ref,
    on_ref,
):
    physics = Physics(slot_ref, [own_ref, far_ref])
    physics.begin(wind_ref, target_ref, slope_ref)

    def body(at, here_at):
        start = physics.start(flat(state_ref[:, at]), flat(prev_ref[:, at]))
        start = [start[k * CHUNK : (k + 1) * CHUNK] for k in range(PARTS)]
        prev = [prev_ref[k, at].astype(jnp.float32) for k in range(PARTS)]
        tends = [
            as_rows(chosen_product(physics.matrices, physics.group, state_ref[k, at]))
            for k in range(PARTS)
        ]
        physics.finish(start, prev, tends, here_at, tend_ref, ahead_ref, off_ref, on_ref)

    each_chunk(first, count, body)


def near_kernel(
    state_ref,
    wind_ref,
    target_ref,
    slope_ref,
    off_ref,
    on_ref,
    add_ref,
    near_ref,
    force_ref,
    sum_ref,
    edge_sum_ref,
    blow_ref,
):
    lev = wind_ref.shape[1]
    slots, share = point_sets()
    chosen = sides()
    end = off_ref.shape[1]

    def extra(ref, k):
        return ref[k, end - 80 : end].astype(jnp.float32)

    def winds(ref):
        whole = jnp.concatenate([extra(ref, k)[:48] for k in range(3)], axis=0)
        return whole[:lev], whole[lev:]

    def targets(ref):
        return extra(ref, 0)[48:56].astype(jnp.int32) - 32

    own_t = target_ref[...].astype(jnp.int32) - 32
    near_t = jnp.where(chosen, targets(off_ref), targets(on_ref))
    near_t = near_t + jnp.where(lane_ids() < 64, LANES, -LANES)
    sum_ref[:LANES, :LANES] = sum_block("own", own_t, slots, True)
    sum_ref[LANES:, :LANES] = sum_block("near", own_t, slots, False)
    sum_ref[:LANES, LANES:] = sum_block("own", near_t, slots, False)
    sum_ref[LANES:, LANES:] = sum_block("near", near_t, slots, True)
    edge_sum_ref[0, :, :LANES] = sum_block("outer", near_t, slots, False)
    edge_sum_ref[0, :, LANES:] = sum_block("outer turned", near_t, slots, False)
    edge_sum_ref[1, :, :LANES] = sum_block("near", own_t, slots, False)
    edge_sum_ref[1, :, LANES:] = sum_block("near turned", own_t, slots, False)
    inner = inner_lanes()
    off_w, on_w = winds(off_ref), winds(on_ref)
    for d in range(2):
        blow_ref[0, d] = -time_step * wind_ref[d]
        near_w = -time_step * jnp.where(chosen, off_w[d], on_w[d])
        outer_w = -time_step * jnp.where(chosen, on_w[d], off_w[d])
        blow_ref[1, d] = near_w
        blow_ref[2, d] = jnp.where(inner, outer_w, pltpu.roll(outer_w, 64, 1))
        blow_ref[3, d] = jnp.where(inner, pltpu.roll(near_w, 64, 1), near_w)

    slope = slope_ref[...]
    early = time_step * hermite(0)[0]

    def body(at, _):
        off, on = off_ref[:, at].astype(jnp.float32), on_ref[:, at].astype(jnp.float32)
        near = whole_halves(off[:2], on[:2], chosen)
        own_move = moved(flat(state_ref[:, at]), slope, blow_ref[0, 0], blow_ref[0, 1])
        near_move = moved(near, slope, blow_ref[1, 0], blow_ref[1, 1])
        total = jnp.dot(near_move, sum_ref[LANES:], preferred_element_type=jnp.float32)
        near_total = total[:, LANES:] + jnp.dot(
            own_move, sum_ref[:LANES, LANES:], preferred_element_type=jnp.float32
        )
        add_ref[:, at] = (total[:, :LANES] * share).reshape(PARTS, CHUNK, LANES)
        prev = [jnp.where(chosen, off[2], on[2])]
        for k in range(1, PARTS):
            turned = [pltpu.roll(side[2], LANES - 32 * k, 1) for side in (off, on)]
            prev.append(jnp.where(chosen, *turned))
        prev = jnp.concatenate(prev, axis=0)
        near = near + near_total * share + early * prev
        near_ref[:, at] = near.reshape(PARTS, CHUNK, LANES)
        force_ref[:, at] = prev.astype(jnp.bfloat16).reshape(PARTS, CHUNK, LANES)

    each_chunk(0, state_ref.shape[1] // CHUNK, body)


def advance_kernel(
    first,
    ahead_ref,
    add_ref,
    near_ref,
    near_prev_ref,
    prev_ref,
    tend_ref,
    off_ref,
    on_ref,
    slope_ref,
    sum_ref,
    edge_sum_ref,
    blow_ref,
    *rest,
):
    out_hbm, tend_hbm, out_ref, sems = rest[-4:]
    count = tend_ref.shape[1]
    tend_copy = pltpu.make_async_copy(tend_ref, tend_hbm.at[:, pl.ds(first * CHUNK, count)], sems.at[0])
    tend_copy.start()
    _, share = point_sets()
    inner = inner_lanes()
    chosen = sides()
    slope, sums = slope_ref[...], sum_ref[...]
    weights = [tuple(time_step * w for w in hermite(s)) for s in range(SUBSTEPS)]

    def advect(value, unit):
        return moved(value, slope, blow_ref[unit, 0], blow_ref[unit, 1])

    def gather(pieces, matrix):
        return jnp.dot(jnp.concatenate(pieces, axis=1), matrix, preferred_element_type=jnp.float32)

    def shared(value, which):
        total = jnp.dot(value, edge_sum_ref[which], preferred_element_type=jnp.float32)
        return jnp.concatenate([total[:, :LANES], total[:, LANES:]], axis=0)

    def body(at, here_at):
        off, on = off_ref[:, here_at].astype(jnp.float32), on_ref[:, here_at].astype(jnp.float32)
        off_mid, on_mid = flat(off[:2]), flat(on[:2])
        middle = [jnp.where(chosen, off_mid, on_mid), jnp.where(chosen, on_mid, off_mid)]
        middle = jnp.concatenate([middle[0], pltpu.roll(middle[1], 64, 1)], axis=0)
        outer = jnp.where(chosen == inner, on_mid, off_mid)
        received = whole_halves(off[2:], on[2:], chosen)
        own_prev, own_tend = flat(prev_ref[:, at]), flat(tend_ref[:, here_at])
        near_prev = flat(near_prev_ref[:, at])
        own = flat(ahead_ref[:, here_at]) + flat(add_ref[:, at])
        near = flat(near_ref[:, at]) + weights[0][1] * received
        near = jnp.where(inner, middle, near)
        for s in range(1, SUBSTEPS):
            early, late = weights[s]
            own_force = early * own_prev + late * own_tend
            own_move = advect(own, 0)
            if s == SUBSTEPS - 1:
                half = near.shape[0] // 2
                near = jnp.where(inner, pltpu.roll(near[half:], 64, 1), near[:half])
                total = jnp.dot(own_move, sums[:LANES, :LANES], preferred_element_type=jnp.float32)
                total = total + shared(advect(near, 3), 1)
                out = own + total * share + own_force
                out_ref[:, here_at] = out.reshape(PARTS, CHUNK, LANES)
                break
            near_force = early * near_prev + late * received
            total = gather([own_move, advect(near, 1)], sums)
            own = own + total[:, :LANES] * share + own_force
            near_total = total[:, LANES:]
            if s == 1:
                near_force = jnp.where(inner, received, near_force)
                near_total = near_total + shared(advect(outer, 2), 0)
            near = near + near_total * share + near_force

    copies = []
    for j, here_at in enumerate(chunks(out_ref)):
        at = pl.ds((first + j) * CHUNK, CHUNK)
        body(at, here_at)
        copies.append(pltpu.make_async_copy(out_ref.at[:, here_at], out_hbm.at[:, at], sems.at[1 + j]))
        copies[j].start()
    for copy in copies:
        copy.wait()
    tend_copy.wait()


def exchanged(off, on):
    count = lax.axis_size(AXES)
    across = [(i, (i + 1) % count if i % 2 else (i - 1) % count) for i in range(count)]
    inside = [(i, i ^ 1) for i in range(count)]
    return lax.ppermute(off, AXES, across), lax.ppermute(on, AXES, inside)


def per_device(state, prev_tendency, wind, edge_links, swap_slot, inverse):
    devices = lax.axis_size(AXES)
    shape = state.shape
    lev = shape[1]
    rows = shape[0] * lev // PARTS
    params = pltpu.CompilerParams(vmem_limit_bytes=VMEM)
    bf16, f32 = jnp.bfloat16, jnp.float32
    inner = pl.BlockSpec(memory_space=pltpu.VMEM)
    outer = pl.BlockSpec(memory_space=pltpu.HBM)

    def like(count, kind, length=rows):
        return pltpu.VMEM((count, length, LANES), kind)

    def table(kind, *size):
        return pltpu.VMEM(size, kind)

    def call(body, ins, outs, name, passes, **more):
        size = sum(math.prod(array.shape) * array.dtype.itemsize for array in ins)
        cost = pl.CostEstimate(
            flops=passes * 2 * PARTS * rows * 256 * 256, bytes_accessed=2 * size, transcendentals=0
        )
        more = {"in_specs": [inner] * len(ins), "out_specs": (inner,) * len(outs)} | more
        return pl.pallas_call(
            body, out_shape=outs, compiler_params=params, cost_estimate=cost, name=name, **more
        )(*ins)

    slot = swap_slot.reshape(1, LANES)
    slope = jnp.asarray(derivative_matrix())
    message = like(3, bf16, rows + 80)
    inputs = (
        inverse,
        wind,
        edge_links,
        state.reshape(PARTS, rows, LANES),
        prev_tendency.reshape(PARTS, rows, LANES),
    )
    inputs = tuple(pltpu.with_memory_space_constraint(array, pltpu.HBM) for array in inputs)
    matrices, to_off, to_on, targets, wind, state, prev = call(
        pack_kernel,
        inputs,
        (
            table(bf16, inverse.shape[0] * lev, LANES),
            message,
            message,
            table(f32, 8, LANES),
            table(f32, *wind.shape),
            like(4, f32),
            like(4, bf16),
        ),
        "pack",
        2,
        in_specs=[outer] * len(inputs),
        scratch_shapes=[
            pltpu.VMEM(inverse.shape, f32),
            pltpu.VMEM(edge_links.shape, jnp.int32),
            pltpu.SemaphoreType.DMA((3 + 2 * PARTS,)),
        ],
    )
    far_matrices = lax.ppermute(matrices, AXES, [(i, i ^ (devices // 2)) for i in range(devices)])
    off, on = exchanged(to_off, to_on)
    halves = []
    first = 0
    shared = (wind, targets, slope, slot, matrices)
    for count in SPLIT:
        size = count * CHUNK
        outs = (like(4, bf16, size), like(4, f32, size), like(4, bf16, size), like(4, bf16, size))
        if first == 0:
            part, start = call(
                functools.partial(own_kernel, first, count),
                (state, prev) + shared,
                (like(4, f32, size), like(4, f32, size)),
                "own",
                3 * count,
            )
            ins = (state, prev, slot, far_matrices, part, start)
            body, name = far_kernel, "far"
        else:
            ins = (state, prev) + shared + (far_matrices,)
            body, name = physics_kernel, "physics"
        tend, ahead, to_off, to_on = call(
            functools.partial(body, first, count), ins, outs, name, 5 * count
        )
        halves.append((first, count, tend, ahead, exchanged(to_off, to_on)))
        first += count
    add, near, near_prev, sums, edge_sums, blow = call(
        near_kernel,
        (state, wind, targets, slope, off, on),
        (
            like(4, f32),
            like(4, f32),
            like(4, bf16),
            table(bf16, 2 * LANES, 2 * LANES),
            table(bf16, 2, LANES, 2 * LANES),
            table(f32, 4, 2, lev, LANES),
        ),
        "near",
        8,
    )
    done = ()
    for first, count, tend, ahead, (off, on) in halves:
        ins = (ahead, add, near, near_prev, prev, tend, off, on, slope, sums, edge_sums, blow)
        done = call(
            functools.partial(advance_kernel, first),
            ins + done,
            (
                jax.ShapeDtypeStruct((PARTS, rows, LANES), f32),
                jax.ShapeDtypeStruct((PARTS, rows, LANES), bf16),
            ),
            "advance",
            5 * count,
            in_specs=[inner] * len(ins) + [outer] * len(done),
            out_specs=(outer, outer),
            scratch_shapes=[
                pltpu.VMEM((PARTS, count * CHUNK, LANES), f32),
                pltpu.SemaphoreType.DMA((1 + count,)),
            ],
            input_output_aliases={len(ins) + i: i for i in range(len(done))},
        )
    out, tend = done
    return (out.reshape(shape), tend.reshape(shape))


def solution(mesh):
    columns = P(None, None, AXES)
    return jax.shard_map(
        per_device,
        mesh=mesh,
        in_specs=(columns, columns, columns, columns, P(AXES), P(AXES, None, None)),
        out_specs=(columns, columns),
        check_vma=False,
    )
```

```python
import functools
import math

import jax
import jax.numpy as jnp
import numpy as np
from jax import lax
from jax.experimental import pallas as pl
from jax.experimental.pallas import tpu as pltpu
from jax.sharding import PartitionSpec as P

SUBSTEPS = 4
AXES = ("gx", "gy")
LANES = 128
CHUNK = 144
SPLIT = (3, 2)
PARTS = 4
VMEM = 16 * 1024 * 1024

time_step = 0.2
edge_points = ((0, 1, 2, 3), (3, 7, 11, 15), (15, 14, 13, 12), (12, 8, 4, 0))


def point_tables():
    edge_of = np.zeros((2, 16), np.int32)
    spot_of = np.zeros((2, 16), np.int32)
    weight_of = np.zeros((2, 16), np.float32)
    filled = np.zeros(16, np.int32)
    for k in range(4):
        for m in range(4):
            p = edge_points[k][m]
            s = filled[p]
            edge_of[s, p] = k
            spot_of[s, p] = m
            weight_of[s, p] = 1.0
            filled[p] = s + 1
    return (edge_of, spot_of, weight_of)


def gll_derivative():
    gll_nodes = np.array([-1.0, -1.0 / np.sqrt(5.0), 1.0 / np.sqrt(5.0), 1.0])
    factors = np.array(
        [np.prod([gll_nodes[i] - gll_nodes[k] for k in range(4) if k != i]) for i in range(4)]
    )
    derivative = np.zeros((4, 4))
    for i in range(4):
        for k in range(4):
            if i != k:
                derivative[i, k] = factors[i] / (factors[k] * (gll_nodes[i] - gll_nodes[k]))
            else:
                derivative[i, k] = sum(
                    (1.0 / (gll_nodes[i] - gll_nodes[j]) for j in range(4) if j != i)
                )
    return derivative


def derivative_matrix():
    derivative = gll_derivative()
    eye_block = np.eye(8)
    both = np.concatenate(
        [
            np.kron(eye_block, np.kron(derivative, np.eye(4)).T),
            np.kron(eye_block, np.kron(np.eye(4), derivative).T),
        ],
        axis=1,
    )
    high = both.astype(jnp.bfloat16)
    low = (both - high.astype(np.float64)).astype(jnp.bfloat16)
    return np.concatenate([high, low], axis=0)


def hermite(substep):
    instant = (substep + 1.0) / SUBSTEPS
    square = instant * instant
    cube = square * instant
    h00 = 2.0 * cube - 3.0 * square + 1.0
    h01 = -2.0 * cube + 3.0 * square
    slope = cube - 2.0 * square + instant + (cube - square)
    return (h00 - slope, h01 + slope)


def lane_ids(rows=1):
    return lax.broadcasted_iota(jnp.int32, (rows, LANES), 1)


def point_sets():
    point = lane_ids() % 16
    across = (point // 4 == 0) | (point // 4 == 3)
    along = (point % 4 == 0) | (point % 4 == 3)
    slots = (across | along, across & along)
    share = jnp.where(slots[1], 1.0 / 3.0, jnp.where(slots[0], 0.5, 1.0)).astype(jnp.float32)
    return slots, share


def edge_targets(links_ref, first_elem, element_count):
    edge_of, spot_of, _ = point_tables()
    elements = links_ref.shape[2]
    own = first_elem + lax.broadcasted_iota(jnp.int32, (4, elements), 1)
    apart = links_ref[0] - own
    half = element_count // 2
    apart = jnp.where(apart > half, apart - element_count, apart)
    apart = jnp.where(apart < -half, apart + element_count, apart) + 2
    both = jnp.concatenate([apart, links_ref[1]], axis=0).astype(jnp.float32)
    spread = lax.broadcasted_iota(jnp.int32, (elements, LANES), 0)
    spread = (spread == lax.broadcasted_iota(jnp.int32, (elements, LANES), 1) // 16).astype(jnp.float32)
    both = jnp.dot(both, spread, preferred_element_type=jnp.float32)
    both = (both + 0.5).astype(jnp.int32)
    lane = lane_ids()
    point = lane % 16
    rows = []
    for s in range(2):
        edge = jnp.zeros((1, LANES), jnp.int32)
        spot = edge
        for p in range(16):
            edge = jnp.where(point == p, int(edge_of[s, p]), edge)
            spot = jnp.where(point == p, int(spot_of[s, p]), spot)
        away, far = both[0:1], both[4:5]
        for k in range(1, 4):
            away = jnp.where(edge == k, both[k : k + 1], away)
            far = jnp.where(edge == k, both[4 + k : 5 + k], far)
        place = jnp.where(far == 2, 12 + spot, 4 * spot)
        place = jnp.where(far == 1, 15 - 4 * spot, place)
        place = jnp.where(far == 0, 3 - spot, place)
        rows.append(lane - point + 16 * away + place)
    rows = jnp.concatenate(rows + [jnp.zeros((6, LANES), jnp.int32)], axis=0)
    return rows.astype(jnp.float32)


def on_odd():
    return lax.axis_index(AXES) % 2 == 1


def sides():
    return (lane_ids() < 64) == on_odd()


def packed_halves(value, chosen):
    away = [pltpu.roll(value[k + 2], 64, 1) for k in range(2)]
    off = [jnp.where(chosen, away[k], value[k]) for k in range(2)]
    on = [jnp.where(chosen, value[k], away[k]) for k in range(2)]
    return off, on


def whole_halves(off, on, chosen):
    count, rows = off.shape[0], off.shape[1]
    direct = jnp.where(chosen, off, on).reshape(count * rows, LANES)
    turned = jnp.where(chosen, on, off).reshape(count * rows, LANES)
    return jnp.concatenate([direct, pltpu.roll(turned, 64, 1)], axis=0)


def packed_matrices(matrix):
    lane = lane_ids()
    half = len(matrix) // 2
    rows = [jnp.where(lane < 64, matrix[c], pltpu.roll(matrix[c + half], 64, 1)) for c in range(half)]
    rest = jnp.zeros_like(matrix[0])
    for c, value in enumerate(matrix):
        rest = jnp.where(lane // 8 == c, pltpu.roll(value, (8 * c - 64) % LANES, 1), rest)
    return jnp.concatenate(rows + [rest, jnp.zeros((8, LANES), jnp.float32)], axis=0)


def unpacked_matrices(packed):
    lane = lane_ids()
    lev, half = 72, 4
    rest = packed[half * lev : (half + 1) * lev]
    rows = []
    for c in range(2 * half):
        main = packed[c % half * lev : (c % half + 1) * lev]
        main = main if c < half else pltpu.roll(main, 64, 1)
        tail = jnp.where(lane < lev, pltpu.roll(rest, (64 - 8 * c) % LANES, 1), 0.0)
        rows.append(jnp.where(lane < 64, main, tail))
    return jnp.concatenate(rows, axis=0)


def pack_kernel(
    inverse_hbm,
    wind_hbm,
    links_hbm,
    state_hbm,
    prev_hbm,
    matrix_ref,
    packed_ref,
    off_ref,
    on_ref,
    target_ref,
    wind_ref,
    state_ref,
    prev_ref,
    inverse_ref,
    links_ref,
    sems,
):
    pairs = [(inverse_hbm, inverse_ref), (wind_hbm, wind_ref), (links_hbm, links_ref)]
    for k in range(PARTS):
        pairs += [(state_hbm.at[k], state_ref.at[k]), (prev_hbm.at[k], prev_ref.at[k])]
    copies = [pltpu.make_async_copy(a, b, sems.at[i]) for i, (a, b) in enumerate(pairs)]
    for copy in copies:
        copy.start()
    groups, lev = inverse_ref.shape[0], inverse_ref.shape[1]
    copies[0].wait()
    eye = lax.broadcasted_iota(jnp.int32, (lev, lev), 0) == lax.broadcasted_iota(jnp.int32, (lev, lev), 1)
    eye = eye.astype(jnp.float32)
    blank = jnp.zeros((lev, LANES - lev), jnp.float32)
    matrix = [jnp.concatenate([inverse_ref[c] - eye, blank], axis=1) for c in range(groups)]
    matrix_ref[...] = jnp.concatenate(matrix, axis=0).astype(jnp.bfloat16)
    packed_ref[...] = packed_matrices(matrix).astype(jnp.bfloat16)
    copies[1].wait()
    copies[2].wait()
    devices = lax.axis_size(AXES)
    elements = links_ref.shape[2]
    targets = edge_targets(links_ref, lax.axis_index(AXES) * elements, elements * devices)
    target_ref[...] = targets
    end = off_ref.shape[1]
    filler = jnp.zeros((8, LANES), jnp.float32)
    flat_wind = wind_ref[...].reshape(2 * lev, LANES)
    for k in range(3):
        piece = jnp.concatenate([flat_wind[48 * k : 48 * k + 48], targets, filler], axis=0)
        piece = piece.astype(jnp.bfloat16)
        off_ref[k, end - 64 : end] = piece
        on_ref[k, end - 64 : end] = piece
    chosen = sides()
    odd = jnp.where(on_odd(), 3, 0)
    quarter = lane_ids() // 32
    for copy in copies[3:]:
        copy.wait()
    for at in chunks(state_ref):
        off, on = packed_halves([state_ref[k, at] for k in range(PARTS)], chosen)
        for k in range(2):
            off_ref[k, at] = off[k].astype(jnp.bfloat16)
            on_ref[k, at] = on[k].astype(jnp.bfloat16)
        to_off = jnp.zeros((CHUNK, LANES), jnp.float32)
        to_on = to_off
        for k in range(PARTS):
            turned = prev_ref[k, at].astype(jnp.float32)
            turned = pltpu.roll(turned, 32 * k, 1) if k else turned
            to_off = jnp.where(quarter == (odd + k) % 4, turned, to_off)
            to_on = jnp.where(quarter == (3 - odd + k) % 4, turned, to_on)
        off_ref[2, at] = to_off.astype(jnp.bfloat16)
        on_ref[2, at] = to_on.astype(jnp.bfloat16)


def chunks(ref):
    return [pl.ds(start, CHUNK) for start in range(0, ref.shape[1], CHUNK)]


def each_chunk(first, count, body):
    def step(j, carry):
        near, whole = j * CHUNK, (first + j) * CHUNK
        body(pl.ds(pl.multiple_of(whole, CHUNK), CHUNK), pl.ds(pl.multiple_of(near, CHUNK), CHUNK))
        return carry

    lax.fori_loop(0, count, step, 0, unroll=True)


def chosen_product(matrices, group, pair, chosen=None, first=0):
    lev = pair.shape[0] // 2
    blank = jnp.zeros((LANES - lev, 2 * LANES), jnp.float32)
    pair = jnp.concatenate([pair[:lev], pair[lev:]], axis=1)
    high = pair.astype(jnp.bfloat16).astype(jnp.float32)
    column = jnp.concatenate([high, blank, pair - high, blank], axis=0).astype(jnp.bfloat16)
    product = jnp.dot(matrices, column, preferred_element_type=jnp.float32)
    for c in range(matrices.shape[0] // lev):
        part = product[c * lev : (c + 1) * lev]
        chosen = part if chosen is None else jnp.where(group == first + c, part, chosen)
    return chosen


def as_rows(pair):
    return jnp.concatenate([pair[:, :LANES], pair[:, LANES:]], axis=0)


def column_group(slot_ref):
    slot = slot_ref[...]
    return jnp.where(slot // LANES == lax.axis_index(AXES), 0, 8) + slot % LANES // 16


def flat(value):
    return value.astype(jnp.float32).reshape(-1, LANES)


def moved(value, slope, blow_x, blow_y):
    rows, lev = value.shape[0], blow_x.shape[0]
    value = value.astype(jnp.bfloat16)
    both = jnp.dot(jnp.concatenate([value, value], axis=1), slope, preferred_element_type=jnp.float32)
    both = both.reshape(rows // lev, lev, 2 * LANES)
    motion = both[..., :LANES] * blow_x + both[..., LANES:] * blow_y
    return motion.reshape(rows, LANES).astype(jnp.bfloat16)


def sum_block(source, targets, slots, own):
    row = lax.broadcasted_iota(jnp.int32, (LANES, LANES), 0)
    total = jnp.zeros((LANES, LANES), jnp.float32)
    if own:
        total = (row == lax.broadcasted_iota(jnp.int32, (LANES, LANES), 1)).astype(jnp.float32)
    place = {
        "own": row,
        "near": jnp.where(row < 64, row + LANES, row - LANES),
        "near turned": jnp.where(row < 64, row - 64, row + 64),
        "outer": jnp.where(row < 64, row - LANES, row + LANES),
        "outer turned": jnp.where(row < 64, row + LANES + 64, row - LANES - 64),
    }[source]
    for s in range(2):
        total = total + ((place == targets[s : s + 1]) & slots[s]).astype(jnp.float32)
    return total.astype(jnp.bfloat16)


def inner_lanes():
    quarter = lane_ids() // 32
    return (quarter == 1) | (quarter == 2)


class Physics:
    def __init__(self, slot_ref, matrix_refs):
        self.take(jnp.concatenate([ref[...] for ref in matrix_refs], axis=0) if matrix_refs else None)
        group = column_group(slot_ref)
        self.group = jnp.concatenate([group, group], axis=1)
        self.inner = inner_lanes()
        self.chosen = sides()

    def take(self, matrices):
        if matrices is not None:
            self.matrices = jnp.concatenate([matrices, matrices], axis=1)

    def begin(self, wind_ref, target_ref, slope_ref):
        slots, self.share = point_sets()
        self.sums = sum_block("own", target_ref[...].astype(jnp.int32) - 32, slots, True)
        self.blow = [-time_step * wind_ref[d] for d in range(2)]
        self.slope = slope_ref[...]

    def start(self, state, prev):
        motion = moved(state, self.slope, *self.blow)
        total = jnp.dot(motion, self.sums, preferred_element_type=jnp.float32)
        return state + total * self.share + time_step * hermite(0)[0] * prev

    def finish(self, start, prev, tends, here_at, tend_ref, ahead_ref, off_ref, on_ref):
        late = time_step * hermite(0)[1]
        early_1, late_1 = (time_step * w for w in hermite(1))
        ahead, force = [], []
        for k, tend in enumerate(tends):
            tend = tend.astype(jnp.bfloat16)
            tend_ref[k, here_at] = tend
            tend = tend.astype(jnp.float32)
            ahead.append(start[k] + late * tend)
            ahead_ref[k, here_at] = ahead[k]
            force.append(jnp.where(self.inner, early_1 * prev[k] + late_1 * tend, tend))
        off, on = packed_halves(force, self.chosen)
        for k in range(2):
            middle = jnp.where(self.inner, ahead[k], pltpu.roll(ahead[k + 2], 64, 1))
            middle = middle.astype(jnp.bfloat16)
            off_ref[k, here_at] = middle
            on_ref[k, here_at] = middle
            off_ref[2 + k, here_at] = off[k].astype(jnp.bfloat16)
            on_ref[2 + k, here_at] = on[k].astype(jnp.bfloat16)


def own_kernel(
    first, count, state_ref, prev_ref, wind_ref, target_ref, slope_ref, slot_ref, own_ref, part_ref, start_ref
):
    physics = Physics(slot_ref, [own_ref])
    physics.begin(wind_ref, target_ref, slope_ref)
    def body(at, here_at):
        start = physics.start(flat(state_ref[:, at]), flat(prev_ref[:, at]))
        start_ref[:, here_at] = start.reshape(PARTS, CHUNK, LANES)
        for k in range(PARTS):
            chosen = chosen_product(physics.matrices, physics.group, state_ref[k, at])
            part_ref[k, here_at] = as_rows(chosen)

    each_chunk(first, count, body)


def far_kernel(
    first,
    count,
    state_ref,
    prev_ref,
    slot_ref,
    packed_ref,
    part_ref,
    start_ref,
    tend_ref,
    ahead_ref,
    off_ref,
    on_ref,
    far_ref,
):
    physics = Physics(slot_ref, [])
    matrices = unpacked_matrices(packed_ref[...].astype(jnp.float32)).astype(jnp.bfloat16)
    far_ref[...] = matrices
    physics.take(matrices)

    def body(at, here_at):
        tends = []
        for k in range(PARTS):
            pair = part_ref[k, here_at]
            lev = pair.shape[0] // 2
            pair = jnp.concatenate([pair[:lev], pair[lev:]], axis=1)
            tends.append(as_rows(chosen_product(physics.matrices, physics.group, state_ref[k, at], pair, 8)))
        start = [start_ref[k, here_at] for k in range(PARTS)]
        prev = [prev_ref[k, at].astype(jnp.float32) for k in range(PARTS)]
        physics.finish(start, prev, tends, here_at, tend_ref, ahead_ref, off_ref, on_ref)

    each_chunk(first, count, body)


def physics_kernel(
    first,
    count,
    state_ref,
    prev_ref,
    wind_ref,
    target_ref,
    slope_ref,
    slot_ref,
    own_ref,
    far_ref,
    tend_ref,
    ahead_ref,
    off_ref,
    on_ref,
):
    physics = Physics(slot_ref, [own_ref, far_ref])
    physics.begin(wind_ref, target_ref, slope_ref)

    def body(at, here_at):
        start = physics.start(flat(state_ref[:, at]), flat(prev_ref[:, at]))
        start = [start[k * CHUNK : (k + 1) * CHUNK] for k in range(PARTS)]
        prev = [prev_ref[k, at].astype(jnp.float32) for k in range(PARTS)]
        tends = [
            as_rows(chosen_product(physics.matrices, physics.group, state_ref[k, at]))
            for k in range(PARTS)
        ]
        physics.finish(start, prev, tends, here_at, tend_ref, ahead_ref, off_ref, on_ref)

    each_chunk(first, count, body)


def near_kernel(
    state_ref,
    wind_ref,
    target_ref,
    slope_ref,
    off_ref,
    on_ref,
    prev_ref,
    *rest,
):
    parts, (own_ref, near_ref, near_add_ref, force_ref, sum_ref, edge_sum_ref, blow_ref) = rest[:-7], rest[-7:]
    lev = wind_ref.shape[1]
    slots, share = point_sets()
    chosen = sides()
    end = off_ref.shape[1]

    def extra(ref, k):
        return ref[k, end - 64 : end].astype(jnp.float32)

    def winds(ref):
        whole = jnp.concatenate([extra(ref, k)[:48] for k in range(3)], axis=0)
        return whole[:lev], whole[lev:]

    def targets(ref):
        return extra(ref, 0)[48:56].astype(jnp.int32) - 32

    own_t = target_ref[...].astype(jnp.int32) - 32
    near_t = jnp.where(chosen, targets(off_ref), targets(on_ref))
    near_t = near_t + jnp.where(lane_ids() < 64, LANES, -LANES)
    own_sums = jnp.concatenate(
        [sum_block("own", own_t, slots, True), sum_block("own", near_t, slots, False)], axis=1
    )
    near_sums = jnp.concatenate(
        [sum_block("near", own_t, slots, False), sum_block("near", near_t, slots, True)], axis=1
    )
    sum_ref[:LANES] = own_sums
    sum_ref[LANES:] = near_sums
    nothing = jnp.zeros((LANES, LANES), jnp.bfloat16)
    for k, turn in enumerate(("", " turned")):
        edge_sum_ref[k, :LANES] = near_sums
        edge_sum_ref[k, LANES:, :LANES] = nothing
        edge_sum_ref[k, LANES:, LANES:] = sum_block("outer" + turn, near_t, slots, False)
        edge_sum_ref[2 + k, :LANES, :LANES] = own_sums[:, :LANES]
        edge_sum_ref[2 + k, LANES:, :LANES] = sum_block("near" + turn, own_t, slots, False)
    inner = inner_lanes()
    off_w, on_w = winds(off_ref), winds(on_ref)
    for d in range(2):
        blow_ref[0, d] = -time_step * wind_ref[d]
        near_w = -time_step * jnp.where(chosen, off_w[d], on_w[d])
        outer_w = -time_step * jnp.where(chosen, on_w[d], off_w[d])
        blow_ref[1, d] = near_w
        blow_ref[2, d] = jnp.where(inner, outer_w, pltpu.roll(outer_w, 64, 1))
        blow_ref[3, d] = jnp.where(inner, pltpu.roll(near_w, 64, 1), near_w)

    slope = slope_ref[...]
    early = time_step * hermite(0)[0]
    early_1, late_1 = (time_step * w for w in hermite(1))
    own_blow = (blow_ref[0, 0], blow_ref[0, 1])
    near_blow = (blow_ref[1, 0], blow_ref[1, 1])

    def body(at, here_at, tend_ref, ahead_ref):
        off, on = off_ref[:, at].astype(jnp.float32), on_ref[:, at].astype(jnp.float32)
        near = whole_halves(off[:2], on[:2], chosen)
        own_move = moved(flat(state_ref[:, at]), slope, *own_blow)
        near_move = moved(near, slope, *near_blow)
        total = jnp.dot(near_move, near_sums, preferred_element_type=jnp.float32)
        near_total = total[:, LANES:] + jnp.dot(
            own_move, own_sums[:, LANES:], preferred_element_type=jnp.float32
        )
        kept = [jnp.where(chosen, off[2], on[2])]
        for k in range(1, PARTS):
            turned = [pltpu.roll(side[2], LANES - 32 * k, 1) for side in (off, on)]
            kept.append(jnp.where(chosen, *turned))
        kept = jnp.concatenate(kept, axis=0)
        near = near + near_total * share + early * kept
        near_ref[:, at] = near.reshape(PARTS, CHUNK, LANES)
        force_ref[:, at] = kept.astype(jnp.bfloat16).reshape(PARTS, CHUNK, LANES)
        own = flat(ahead_ref[:, here_at]) + total[:, :LANES] * share
        total = jnp.dot(moved(own, slope, *own_blow), own_sums, preferred_element_type=jnp.float32)
        force = early_1 * flat(prev_ref[:, at]) + late_1 * flat(tend_ref[:, here_at])
        own = own + total[:, :LANES] * share + force
        own_ref[:, at] = own.reshape(PARTS, CHUNK, LANES)
        near_add_ref[:, at] = (total[:, LANES:] * share).reshape(PARTS, CHUNK, LANES)

    first = 0
    for tend_ref, ahead_ref in zip(parts[::2], parts[1::2]):
        for j, here_at in enumerate(chunks(tend_ref)):
            body(pl.ds((first + j) * CHUNK, CHUNK), here_at, tend_ref, ahead_ref)
        first += tend_ref.shape[1] // CHUNK


def advance_kernel(
    first,
    last,
    own_ref,
    near_ref,
    near_add_ref,
    near_prev_ref,
    prev_ref,
    off_ref,
    on_ref,
    slope_ref,
    sum_ref,
    edge_sum_ref,
    blow_ref,
    *rest,
):
    if last:
        tend_ref, done_ref, out_hbm, out_ref, sems = rest
        copies = [pltpu.make_async_copy(done_ref, out_hbm.at[:, pl.ds(0, done_ref.shape[1])], sems.at[0])]
    else:
        *tend_refs, out_ref, tend_hbm, sems = rest
        tend_ref = tend_refs[0]
        copies, row = [], 0
        for k, ref in enumerate(tend_refs):
            copies.append(pltpu.make_async_copy(ref, tend_hbm.at[:, pl.ds(row, ref.shape[1])], sems.at[k]))
            row += ref.shape[1]
    for copy in copies:
        copy.start()
    _, share = point_sets()
    inner = inner_lanes()
    chosen = sides()
    slope = slope_ref[...]
    weights = [tuple(time_step * w for w in hermite(s)) for s in range(SUBSTEPS)]

    def advect(value, unit):
        return moved(value, slope, blow_ref[unit, 0], blow_ref[unit, 1])

    def gather(pieces, matrix):
        return jnp.dot(jnp.concatenate(pieces, axis=1), matrix, preferred_element_type=jnp.float32)

    def gather_shared(whole, packed, which, width):
        half = packed.shape[0]
        parts = [
            gather([whole[k * half : (k + 1) * half], packed], edge_sum_ref[which + k, :, :width])
            for k in range(2)
        ]
        return jnp.concatenate(parts, axis=0)

    def body(at, here_at):
        off, on = off_ref[:, here_at].astype(jnp.float32), on_ref[:, here_at].astype(jnp.float32)
        off_mid, on_mid = flat(off[:2]), flat(on[:2])
        middle = [jnp.where(chosen, off_mid, on_mid), jnp.where(chosen, on_mid, off_mid)]
        middle = jnp.concatenate([middle[0], pltpu.roll(middle[1], 64, 1)], axis=0)
        outer = jnp.where(chosen == inner, on_mid, off_mid)
        received = whole_halves(off[2:], on[2:], chosen)
        own_prev, own_tend = flat(prev_ref[:, at]), flat(tend_ref[:, here_at])
        near_prev = flat(near_prev_ref[:, at])
        early, late = weights[1]
        near = jnp.where(inner, middle, flat(near_ref[:, at]) + weights[0][1] * received)
        total = gather_shared(advect(near, 1), advect(outer, 2), 0, 2 * LANES)
        own = flat(own_ref[:, at]) + total[:, :LANES] * share
        force = jnp.where(inner, received, early * near_prev + late * received)
        near = near + total[:, LANES:] * share + flat(near_add_ref[:, at]) + force
        early, late = weights[2]
        total = gather([advect(own, 0), advect(near, 1)], sum_ref[...])
        own = own + total[:, :LANES] * share + (early * own_prev + late * own_tend)
        near = near + total[:, LANES:] * share + (early * near_prev + late * received)
        early, late = weights[3]
        half = near.shape[0] // 2
        near = jnp.where(inner, pltpu.roll(near[half:], 64, 1), near[:half])
        total = gather_shared(advect(own, 0), advect(near, 3), 2, LANES)
        out = own + total * share + (early * own_prev + late * own_tend)
        out_ref[:, here_at] = out.reshape(PARTS, CHUNK, LANES)

    for j, here_at in enumerate(chunks(out_ref)):
        at = pl.ds((first + j) * CHUNK, CHUNK)
        body(at, here_at)
        if last:
            copies.append(pltpu.make_async_copy(out_ref.at[:, here_at], out_hbm.at[:, at], sems.at[1 + j]))
            copies[-1].start()
    for copy in copies:
        copy.wait()


def exchanged(off, on):
    count = lax.axis_size(AXES)
    across = [(i, (i + 1) % count if i % 2 else (i - 1) % count) for i in range(count)]
    inside = [(i, i ^ 1) for i in range(count)]
    return lax.ppermute(off, AXES, across), lax.ppermute(on, AXES, inside)


def per_device(state, prev_tendency, wind, edge_links, swap_slot, inverse):
    devices = lax.axis_size(AXES)
    shape = state.shape
    lev = shape[1]
    rows = shape[0] * lev // PARTS
    params = pltpu.CompilerParams(vmem_limit_bytes=VMEM)
    bf16, f32 = jnp.bfloat16, jnp.float32
    inner = pl.BlockSpec(memory_space=pltpu.VMEM)
    outer = pl.BlockSpec(memory_space=pltpu.HBM)

    def like(count, kind, length=rows):
        return pltpu.VMEM((count, length, LANES), kind)

    def table(kind, *size):
        return pltpu.VMEM(size, kind)

    def call(body, ins, outs, name, passes, **more):
        size = sum(math.prod(array.shape) * array.dtype.itemsize for array in ins)
        cost = pl.CostEstimate(
            flops=passes * 2 * PARTS * rows * 256 * 256, bytes_accessed=2 * size, transcendentals=0
        )
        more = {"in_specs": [inner] * len(ins), "out_specs": (inner,) * len(outs)} | more
        return pl.pallas_call(
            body, out_shape=outs, compiler_params=params, cost_estimate=cost, name=name, **more
        )(*ins)

    slot = swap_slot.reshape(1, LANES)
    slope = jnp.asarray(derivative_matrix())
    message = like(3, bf16, rows + 64)
    inputs = (
        inverse,
        wind,
        edge_links,
        state.reshape(PARTS, rows, LANES),
        prev_tendency.reshape(PARTS, rows, LANES),
    )
    inputs = tuple(pltpu.with_memory_space_constraint(array, pltpu.HBM) for array in inputs)
    matrices, packed, to_off, to_on, targets, wind, state, prev = call(
        pack_kernel,
        inputs,
        (
            table(bf16, inverse.shape[0] * lev, LANES),
            table(bf16, 368, LANES),
            message,
            message,
            table(f32, 8, LANES),
            table(f32, *wind.shape),
            like(4, f32),
            like(4, bf16),
        ),
        "pack",
        2,
        in_specs=[outer] * len(inputs),
        scratch_shapes=[
            pltpu.VMEM(inverse.shape, f32),
            pltpu.VMEM(edge_links.shape, jnp.int32),
            pltpu.SemaphoreType.DMA((3 + 2 * PARTS,)),
        ],
    )
    far_packed = lax.ppermute(packed, AXES, [(i, i ^ (devices // 2)) for i in range(devices)])
    off, on = exchanged(to_off, to_on)
    halves = []
    first = 0
    shared = (wind, targets, slope, slot, matrices)
    for count in SPLIT:
        size = count * CHUNK
        outs = (like(4, bf16, size), like(4, f32, size), like(4, bf16, size), like(4, bf16, size))
        if first == 0:
            part, start = call(
                functools.partial(own_kernel, first, count),
                (state, prev) + shared,
                (like(4, f32, size), like(4, f32, size)),
                "own",
                3 * count,
            )
            ins = (state, prev, slot, far_packed, part, start)
            body, name = far_kernel, "far"
            outs += (table(bf16, *matrices.shape),)
        else:
            ins = (state, prev) + shared + (far_matrices,)
            body, name = physics_kernel, "physics"
        tend, ahead, to_off, to_on, *more = call(
            functools.partial(body, first, count), ins, outs, name, 5 * count
        )
        far_matrices = more[0] if more else far_matrices
        halves.append((first, count, tend, ahead, exchanged(to_off, to_on)))
        first += count
    parts = sum(((tend, ahead) for _, _, tend, ahead, _ in halves), ())
    own, near, near_add, near_prev, sums, edge_sums, blow = call(
        near_kernel,
        (state, wind, targets, slope, off, on, prev) + parts,
        (
            like(4, f32),
            like(4, f32),
            like(4, f32),
            like(4, bf16),
            table(bf16, 2 * LANES, 2 * LANES),
            table(bf16, 4, 2 * LANES, 2 * LANES),
            table(f32, 4, 2, lev, LANES),
        ),
        "near",
        16,
    )
    tends = tuple(tend for _, _, tend, _, _ in halves)
    out_spec = jax.ShapeDtypeStruct((PARTS, rows, LANES), f32)
    tend_spec = jax.ShapeDtypeStruct((PARTS, rows, LANES), bf16)
    for part, (first, count, tend, _, (off, on)) in enumerate(halves):
        ins = (own, near, near_add, near_prev, prev, off, on, slope, sums, edge_sums, blow)
        size = count * CHUNK
        if part == 0:
            done, tend_out = call(
                functools.partial(advance_kernel, first, False),
                ins + tends,
                (like(4, f32, size), tend_spec),
                "advance",
                5 * count,
                out_specs=(inner, outer),
                scratch_shapes=[pltpu.SemaphoreType.DMA((len(tends),))],
            )
        else:
            (out,) = call(
                functools.partial(advance_kernel, first, True),
                ins + (tend, done),
                (out_spec,),
                "advance",
                5 * count,
                out_specs=(outer,),
                scratch_shapes=[pltpu.VMEM((PARTS, size, LANES), f32), pltpu.SemaphoreType.DMA((1 + count,))],
            )
    tend = tend_out
    return (out.reshape(shape), tend.reshape(shape))


def solution(mesh):
    columns = P(None, None, AXES)
    return jax.shard_map(
        per_device,
        mesh=mesh,
        in_specs=(columns, columns, columns, columns, P(AXES), P(AXES, None, None)),
        out_specs=(columns, columns),
        check_vma=False,
    )
```

```python
import functools
import math

import jax
import jax.numpy as jnp
import numpy as np
from jax import lax
from jax.experimental import pallas as pl
from jax.experimental.pallas import tpu as pltpu
from jax.sharding import PartitionSpec as P

SUBSTEPS = 4
AXES = ("gx", "gy")
LANES = 128
CHUNK = 144
SPLIT = (3, 2)
PARTS = 4
VMEM = 16 * 1024 * 1024

time_step = 0.2
edge_points = ((0, 1, 2, 3), (3, 7, 11, 15), (15, 14, 13, 12), (12, 8, 4, 0))


def point_tables():
    edge_of = np.zeros((2, 16), np.int32)
    spot_of = np.zeros((2, 16), np.int32)
    weight_of = np.zeros((2, 16), np.float32)
    filled = np.zeros(16, np.int32)
    for k in range(4):
        for m in range(4):
            p = edge_points[k][m]
            s = filled[p]
            edge_of[s, p] = k
            spot_of[s, p] = m
            weight_of[s, p] = 1.0
            filled[p] = s + 1
    return (edge_of, spot_of, weight_of)


def gll_derivative():
    gll_nodes = np.array([-1.0, -1.0 / np.sqrt(5.0), 1.0 / np.sqrt(5.0), 1.0])
    factors = np.array(
        [np.prod([gll_nodes[i] - gll_nodes[k] for k in range(4) if k != i]) for i in range(4)]
    )
    derivative = np.zeros((4, 4))
    for i in range(4):
        for k in range(4):
            if i != k:
                derivative[i, k] = factors[i] / (factors[k] * (gll_nodes[i] - gll_nodes[k]))
            else:
                derivative[i, k] = sum(
                    (1.0 / (gll_nodes[i] - gll_nodes[j]) for j in range(4) if j != i)
                )
    return derivative


def derivative_matrix():
    derivative = gll_derivative()
    eye_block = np.eye(8)
    both = np.concatenate(
        [
            np.kron(eye_block, np.kron(derivative, np.eye(4)).T),
            np.kron(eye_block, np.kron(np.eye(4), derivative).T),
        ],
        axis=1,
    )
    high = both.astype(jnp.bfloat16)
    low = (both - high.astype(np.float64)).astype(jnp.bfloat16)
    return np.concatenate([high, low], axis=0)


def hermite(substep):
    instant = (substep + 1.0) / SUBSTEPS
    square = instant * instant
    cube = square * instant
    h00 = 2.0 * cube - 3.0 * square + 1.0
    h01 = -2.0 * cube + 3.0 * square
    slope = cube - 2.0 * square + instant + (cube - square)
    return (h00 - slope, h01 + slope)


def lane_ids(rows=1):
    return lax.broadcasted_iota(jnp.int32, (rows, LANES), 1)


def point_sets():
    point = lane_ids() % 16
    across = (point // 4 == 0) | (point // 4 == 3)
    along = (point % 4 == 0) | (point % 4 == 3)
    slots = (across | along, across & along)
    share = jnp.where(slots[1], 1.0 / 3.0, jnp.where(slots[0], 0.5, 1.0)).astype(jnp.float32)
    return slots, share


def edge_targets(links_ref, first_elem, element_count):
    edge_of, spot_of, _ = point_tables()
    elements = links_ref.shape[2]
    own = first_elem + lax.broadcasted_iota(jnp.int32, (4, elements), 1)
    apart = links_ref[0] - own
    half = element_count // 2
    apart = jnp.where(apart > half, apart - element_count, apart)
    apart = jnp.where(apart < -half, apart + element_count, apart) + 2
    both = jnp.concatenate([apart, links_ref[1]], axis=0).astype(jnp.float32)
    spread = lax.broadcasted_iota(jnp.int32, (elements, LANES), 0)
    spread = (spread == lax.broadcasted_iota(jnp.int32, (elements, LANES), 1) // 16).astype(jnp.float32)
    both = jnp.dot(both, spread, preferred_element_type=jnp.float32)
    both = (both + 0.5).astype(jnp.int32)
    lane = lane_ids()
    point = lane % 16
    rows = []
    for s in range(2):
        edge = jnp.zeros((1, LANES), jnp.int32)
        spot = edge
        for p in range(16):
            edge = jnp.where(point == p, int(edge_of[s, p]), edge)
            spot = jnp.where(point == p, int(spot_of[s, p]), spot)
        away, far = both[0:1], both[4:5]
        for k in range(1, 4):
            away = jnp.where(edge == k, both[k : k + 1], away)
            far = jnp.where(edge == k, both[4 + k : 5 + k], far)
        place = jnp.where(far == 2, 12 + spot, 4 * spot)
        place = jnp.where(far == 1, 15 - 4 * spot, place)
        place = jnp.where(far == 0, 3 - spot, place)
        rows.append(lane - point + 16 * away + place)
    rows = jnp.concatenate(rows + [jnp.zeros((6, LANES), jnp.int32)], axis=0)
    return rows.astype(jnp.float32)


def on_odd():
    return lax.axis_index(AXES) % 2 == 1


def sides():
    return (lane_ids() < 64) == on_odd()


def packed_halves(value, chosen):
    away = [pltpu.roll(value[k + 2], 64, 1) for k in range(2)]
    off = [jnp.where(chosen, away[k], value[k]) for k in range(2)]
    on = [jnp.where(chosen, value[k], away[k]) for k in range(2)]
    return off, on


def whole_halves(off, on, chosen):
    count, rows = off.shape[0], off.shape[1]
    direct = jnp.where(chosen, off, on).reshape(count * rows, LANES)
    turned = jnp.where(chosen, on, off).reshape(count * rows, LANES)
    return jnp.concatenate([direct, pltpu.roll(turned, 64, 1)], axis=0)


def packed_matrices(matrix):
    lane = lane_ids()
    half = len(matrix) // 2
    rows = [jnp.where(lane < 64, matrix[c], pltpu.roll(matrix[c + half], 64, 1)) for c in range(half)]
    rest = jnp.zeros_like(matrix[0])
    for c, value in enumerate(matrix):
        rest = jnp.where(lane // 8 == c, pltpu.roll(value, (8 * c - 64) % LANES, 1), rest)
    return jnp.concatenate(rows + [rest, jnp.zeros((8, LANES), jnp.float32)], axis=0)


def unpacked_matrices(packed):
    lane = lane_ids()
    lev, half = 72, 4
    rest = packed[half * lev : (half + 1) * lev]
    rows = []
    for c in range(2 * half):
        main = packed[c % half * lev : (c % half + 1) * lev]
        main = main if c < half else pltpu.roll(main, 64, 1)
        tail = jnp.where(lane < lev, pltpu.roll(rest, (64 - 8 * c) % LANES, 1), 0.0)
        rows.append(jnp.where(lane < 64, main, tail))
    return jnp.concatenate(rows, axis=0)


def pack_kernel(
    inverse_hbm,
    wind_hbm,
    links_hbm,
    state_hbm,
    prev_hbm,
    matrix_ref,
    packed_ref,
    off_ref,
    on_ref,
    target_ref,
    wind_ref,
    state_ref,
    prev_ref,
    inverse_ref,
    links_ref,
    sems,
):
    pairs = [(inverse_hbm, inverse_ref), (wind_hbm, wind_ref), (links_hbm, links_ref)]
    for at in chunks(state_ref):
        pairs += [(state_hbm.at[:, at], state_ref.at[:, at]), (prev_hbm.at[:, at], prev_ref.at[:, at])]
    copies = [pltpu.make_async_copy(a, b, sems.at[i]) for i, (a, b) in enumerate(pairs)]
    for copy in copies:
        copy.start()
    groups, lev = inverse_ref.shape[0], inverse_ref.shape[1]
    copies[0].wait()
    eye = lax.broadcasted_iota(jnp.int32, (lev, lev), 0) == lax.broadcasted_iota(jnp.int32, (lev, lev), 1)
    eye = eye.astype(jnp.float32)
    blank = jnp.zeros((lev, LANES - lev), jnp.float32)
    matrix = [jnp.concatenate([inverse_ref[c] - eye, blank], axis=1) for c in range(groups)]
    matrix_ref[...] = jnp.concatenate(matrix, axis=0).astype(jnp.bfloat16)
    packed_ref[...] = packed_matrices(matrix).astype(jnp.bfloat16)
    copies[1].wait()
    copies[2].wait()
    devices = lax.axis_size(AXES)
    elements = links_ref.shape[2]
    targets = edge_targets(links_ref, lax.axis_index(AXES) * elements, elements * devices)
    target_ref[...] = targets
    end = off_ref.shape[1]
    filler = jnp.zeros((8, LANES), jnp.float32)
    flat_wind = wind_ref[...].reshape(2 * lev, LANES)
    for k in range(3):
        piece = jnp.concatenate([flat_wind[48 * k : 48 * k + 48], targets, filler], axis=0)
        piece = piece.astype(jnp.bfloat16)
        off_ref[k, end - 64 : end] = piece
        on_ref[k, end - 64 : end] = piece
    chosen = sides()
    odd = jnp.where(on_odd(), 3, 0)
    quarter = lane_ids() // 32
    for j, at in enumerate(chunks(state_ref)):
        copies[3 + 2 * j].wait()
        copies[4 + 2 * j].wait()
        off, on = packed_halves([state_ref[k, at] for k in range(PARTS)], chosen)
        for k in range(2):
            off_ref[k, at] = off[k].astype(jnp.bfloat16)
            on_ref[k, at] = on[k].astype(jnp.bfloat16)
        to_off = jnp.zeros((CHUNK, LANES), jnp.float32)
        to_on = to_off
        for k in range(PARTS):
            turned = prev_ref[k, at].astype(jnp.float32)
            turned = pltpu.roll(turned, 32 * k, 1) if k else turned
            to_off = jnp.where(quarter == (odd + k) % 4, turned, to_off)
            to_on = jnp.where(quarter == (3 - odd + k) % 4, turned, to_on)
        off_ref[2, at] = to_off.astype(jnp.bfloat16)
        on_ref[2, at] = to_on.astype(jnp.bfloat16)


def chunks(ref):
    return [pl.ds(start, CHUNK) for start in range(0, ref.shape[1], CHUNK)]


def each_chunk(first, count, body):
    def step(j, carry):
        near, whole = j * CHUNK, (first + j) * CHUNK
        body(pl.ds(pl.multiple_of(whole, CHUNK), CHUNK), pl.ds(pl.multiple_of(near, CHUNK), CHUNK))
        return carry

    lax.fori_loop(0, count, step, 0, unroll=True)


def chosen_product(matrices, group, pair, chosen=None, first=0):
    lev = pair.shape[0] // 2
    blank = jnp.zeros((LANES - lev, 2 * LANES), jnp.float32)
    pair = jnp.concatenate([pair[:lev], pair[lev:]], axis=1)
    high = pair.astype(jnp.bfloat16).astype(jnp.float32)
    column = jnp.concatenate([high, blank, pair - high, blank], axis=0).astype(jnp.bfloat16)
    product = jnp.dot(matrices, column, preferred_element_type=jnp.float32)
    for c in range(matrices.shape[0] // lev):
        part = product[c * lev : (c + 1) * lev]
        chosen = part if chosen is None else jnp.where(group == first + c, part, chosen)
    return chosen


def as_rows(pair):
    return jnp.concatenate([pair[:, :LANES], pair[:, LANES:]], axis=0)


def column_group(slot_ref):
    slot = slot_ref[...]
    return jnp.where(slot // LANES == lax.axis_index(AXES), 0, 8) + slot % LANES // 16


def flat(value):
    return value.astype(jnp.float32).reshape(-1, LANES)


def moved(value, slope, blow_x, blow_y):
    rows, lev = value.shape[0], blow_x.shape[0]
    value = value.astype(jnp.bfloat16)
    both = jnp.dot(jnp.concatenate([value, value], axis=1), slope, preferred_element_type=jnp.float32)
    both = both.reshape(rows // lev, lev, 2 * LANES)
    motion = both[..., :LANES] * blow_x + both[..., LANES:] * blow_y
    return motion.reshape(rows, LANES).astype(jnp.bfloat16)


def sum_block(source, targets, slots, own):
    row = lax.broadcasted_iota(jnp.int32, (LANES, LANES), 0)
    total = jnp.zeros((LANES, LANES), jnp.float32)
    if own:
        total = (row == lax.broadcasted_iota(jnp.int32, (LANES, LANES), 1)).astype(jnp.float32)
    place = {
        "own": row,
        "near": jnp.where(row < 64, row + LANES, row - LANES),
        "near turned": jnp.where(row < 64, row - 64, row + 64),
        "outer": jnp.where(row < 64, row - LANES, row + LANES),
        "outer turned": jnp.where(row < 64, row + LANES + 64, row - LANES - 64),
    }[source]
    for s in range(2):
        total = total + ((place == targets[s : s + 1]) & slots[s]).astype(jnp.float32)
    return total.astype(jnp.bfloat16)


def inner_lanes():
    quarter = lane_ids() // 32
    return (quarter == 1) | (quarter == 2)


class Physics:
    def __init__(self, slot_ref, matrix_refs):
        self.take(jnp.concatenate([ref[...] for ref in matrix_refs], axis=0) if matrix_refs else None)
        group = column_group(slot_ref)
        self.group = jnp.concatenate([group, group], axis=1)
        self.inner = inner_lanes()
        self.chosen = sides()

    def take(self, matrices):
        if matrices is not None:
            self.matrices = jnp.concatenate([matrices, matrices], axis=1)

    def begin(self, wind_ref, target_ref, slope_ref):
        slots, self.share = point_sets()
        self.sums = sum_block("own", target_ref[...].astype(jnp.int32) - 32, slots, True)
        self.blow = [-time_step * wind_ref[d] for d in range(2)]
        self.slope = slope_ref[...]

    def start(self, state, prev):
        motion = moved(state, self.slope, *self.blow)
        total = jnp.dot(motion, self.sums, preferred_element_type=jnp.float32)
        return state + total * self.share + time_step * hermite(0)[0] * prev

    def finish(self, start, prev, tends, here_at, tend_ref, ahead_ref, off_ref, on_ref):
        late = time_step * hermite(0)[1]
        early_1, late_1 = (time_step * w for w in hermite(1))
        ahead, force = [], []
        for k, tend in enumerate(tends):
            tend = tend.astype(jnp.bfloat16)
            tend_ref[k, here_at] = tend
            tend = tend.astype(jnp.float32)
            ahead.append(start[k] + late * tend)
            ahead_ref[k, here_at] = ahead[k]
            force.append(jnp.where(self.inner, early_1 * prev[k] + late_1 * tend, tend))
        off, on = packed_halves(force, self.chosen)
        for k in range(2):
            middle = jnp.where(self.inner, ahead[k], pltpu.roll(ahead[k + 2], 64, 1))
            middle = middle.astype(jnp.bfloat16)
            off_ref[k, here_at] = middle
            on_ref[k, here_at] = middle
            off_ref[2 + k, here_at] = off[k].astype(jnp.bfloat16)
            on_ref[2 + k, here_at] = on[k].astype(jnp.bfloat16)


def own_kernel(
    first, count, state_ref, prev_ref, wind_ref, target_ref, slope_ref, slot_ref, own_ref, part_ref, start_ref
):
    physics = Physics(slot_ref, [own_ref])
    physics.begin(wind_ref, target_ref, slope_ref)
    def body(at, here_at):
        start = physics.start(flat(state_ref[:, at]), flat(prev_ref[:, at]))
        start_ref[:, here_at] = start.reshape(PARTS, CHUNK, LANES)
        for k in range(PARTS):
            chosen = chosen_product(physics.matrices, physics.group, state_ref[k, at])
            part_ref[k, here_at] = as_rows(chosen)

    each_chunk(first, count, body)


def far_kernel(
    first,
    count,
    state_ref,
    prev_ref,
    slot_ref,
    packed_ref,
    part_ref,
    start_ref,
    tend_ref,
    ahead_ref,
    off_ref,
    on_ref,
    far_ref,
):
    physics = Physics(slot_ref, [])
    matrices = unpacked_matrices(packed_ref[...].astype(jnp.float32)).astype(jnp.bfloat16)
    far_ref[...] = matrices
    physics.take(matrices)

    def body(at, here_at):
        tends = []
        for k in range(PARTS):
            pair = part_ref[k, here_at]
            lev = pair.shape[0] // 2
            pair = jnp.concatenate([pair[:lev], pair[lev:]], axis=1)
            tends.append(as_rows(chosen_product(physics.matrices, physics.group, state_ref[k, at], pair, 8)))
        start = [start_ref[k, here_at] for k in range(PARTS)]
        prev = [prev_ref[k, at].astype(jnp.float32) for k in range(PARTS)]
        physics.finish(start, prev, tends, here_at, tend_ref, ahead_ref, off_ref, on_ref)

    each_chunk(first, count, body)


def physics_kernel(
    first,
    count,
    state_ref,
    prev_ref,
    wind_ref,
    target_ref,
    slope_ref,
    slot_ref,
    own_ref,
    far_ref,
    tend_ref,
    ahead_ref,
    off_ref,
    on_ref,
):
    physics = Physics(slot_ref, [own_ref, far_ref])
    physics.begin(wind_ref, target_ref, slope_ref)

    def body(at, here_at):
        start = physics.start(flat(state_ref[:, at]), flat(prev_ref[:, at]))
        start = [start[k * CHUNK : (k + 1) * CHUNK] for k in range(PARTS)]
        prev = [prev_ref[k, at].astype(jnp.float32) for k in range(PARTS)]
        tends = [
            as_rows(chosen_product(physics.matrices, physics.group, state_ref[k, at]))
            for k in range(PARTS)
        ]
        physics.finish(start, prev, tends, here_at, tend_ref, ahead_ref, off_ref, on_ref)

    each_chunk(first, count, body)


def near_kernel(
    state_ref,
    wind_ref,
    target_ref,
    slope_ref,
    on_ref,
    off_ref,
    prev_ref,
    *rest,
):
    parts, (own_ref, near_ref, near_add_ref, force_ref, sum_ref, edge_sum_ref, blow_ref) = rest[:-7], rest[-7:]
    lev = wind_ref.shape[1]
    slots, share = point_sets()
    chosen = sides()
    end = off_ref.shape[1]

    def extra(ref, k):
        return ref[k, end - 64 : end].astype(jnp.float32)

    def winds(ref):
        whole = jnp.concatenate([extra(ref, k)[:48] for k in range(3)], axis=0)
        return whole[:lev], whole[lev:]

    def targets(ref):
        return extra(ref, 0)[48:56].astype(jnp.int32) - 32

    own_t = target_ref[...].astype(jnp.int32) - 32
    near_t = jnp.where(chosen, targets(off_ref), targets(on_ref))
    near_t = near_t + jnp.where(lane_ids() < 64, LANES, -LANES)
    own_sums = jnp.concatenate(
        [sum_block("own", own_t, slots, True), sum_block("own", near_t, slots, False)], axis=1
    )
    near_sums = jnp.concatenate(
        [sum_block("near", own_t, slots, False), sum_block("near", near_t, slots, True)], axis=1
    )
    sum_ref[:LANES] = own_sums
    sum_ref[LANES:] = near_sums
    nothing = jnp.zeros((LANES, LANES), jnp.bfloat16)
    for k, turn in enumerate(("", " turned")):
        edge_sum_ref[k, :LANES] = near_sums
        edge_sum_ref[k, LANES:, :LANES] = nothing
        edge_sum_ref[k, LANES:, LANES:] = sum_block("outer" + turn, near_t, slots, False)
        edge_sum_ref[2 + k, :LANES, :LANES] = own_sums[:, :LANES]
        edge_sum_ref[2 + k, LANES:, :LANES] = sum_block("near" + turn, own_t, slots, False)
    inner = inner_lanes()
    off_w, on_w = winds(off_ref), winds(on_ref)
    for d in range(2):
        blow_ref[0, d] = -time_step * wind_ref[d]
        near_w = -time_step * jnp.where(chosen, off_w[d], on_w[d])
        outer_w = -time_step * jnp.where(chosen, on_w[d], off_w[d])
        blow_ref[1, d] = near_w
        blow_ref[2, d] = jnp.where(inner, outer_w, pltpu.roll(outer_w, 64, 1))
        blow_ref[3, d] = jnp.where(inner, pltpu.roll(near_w, 64, 1), near_w)

    slope = slope_ref[...]
    early = time_step * hermite(0)[0]
    early_1, late_1 = (time_step * w for w in hermite(1))
    own_blow = (blow_ref[0, 0], blow_ref[0, 1])
    near_blow = (blow_ref[1, 0], blow_ref[1, 1])

    def body(at, here_at, tend_ref, ahead_ref):
        off, on = off_ref[:, at].astype(jnp.float32), on_ref[:, at].astype(jnp.float32)
        near = whole_halves(off[:2], on[:2], chosen)
        own_move = moved(flat(state_ref[:, at]), slope, *own_blow)
        near_move = moved(near, slope, *near_blow)
        total = jnp.dot(near_move, near_sums, preferred_element_type=jnp.float32)
        near_total = total[:, LANES:] + jnp.dot(
            own_move, own_sums[:, LANES:], preferred_element_type=jnp.float32
        )
        kept = [jnp.where(chosen, off[2], on[2])]
        for k in range(1, PARTS):
            turned = [pltpu.roll(side[2], LANES - 32 * k, 1) for side in (off, on)]
            kept.append(jnp.where(chosen, *turned))
        kept = jnp.concatenate(kept, axis=0)
        near = near + near_total * share + early * kept
        near_ref[:, at] = near.reshape(PARTS, CHUNK, LANES)
        force_ref[:, at] = kept.astype(jnp.bfloat16).reshape(PARTS, CHUNK, LANES)
        own = flat(ahead_ref[:, here_at]) + total[:, :LANES] * share
        total = jnp.dot(moved(own, slope, *own_blow), own_sums, preferred_element_type=jnp.float32)
        force = early_1 * flat(prev_ref[:, at]) + late_1 * flat(tend_ref[:, here_at])
        own = own + total[:, :LANES] * share + force
        own_ref[:, at] = own.reshape(PARTS, CHUNK, LANES)
        near_add_ref[:, at] = (total[:, LANES:] * share).reshape(PARTS, CHUNK, LANES)

    first = 0
    for tend_ref, ahead_ref in zip(parts[::2], parts[1::2]):
        for j, here_at in enumerate(chunks(tend_ref)):
            body(pl.ds((first + j) * CHUNK, CHUNK), here_at, tend_ref, ahead_ref)
        first += tend_ref.shape[1] // CHUNK


def advance_kernel(
    first,
    last,
    own_ref,
    near_ref,
    near_add_ref,
    near_prev_ref,
    prev_ref,
    on_ref,
    off_ref,
    slope_ref,
    sum_ref,
    edge_sum_ref,
    blow_ref,
    *rest,
):
    if last:
        tend_ref, done_ref, out_hbm, out_ref, sems = rest
        copies = [pltpu.make_async_copy(done_ref, out_hbm.at[:, pl.ds(0, done_ref.shape[1])], sems.at[0])]
    else:
        *tend_refs, out_ref, tend_hbm, sems = rest
        tend_ref = tend_refs[0]
        copies, row = [], 0
        for k, ref in enumerate(tend_refs):
            copies.append(pltpu.make_async_copy(ref, tend_hbm.at[:, pl.ds(row, ref.shape[1])], sems.at[k]))
            row += ref.shape[1]
    for copy in copies:
        copy.start()
    _, share = point_sets()
    inner = inner_lanes()
    chosen = sides()
    slope = slope_ref[...]
    weights = [tuple(time_step * w for w in hermite(s)) for s in range(SUBSTEPS)]

    def advect(value, unit):
        return moved(value, slope, blow_ref[unit, 0], blow_ref[unit, 1])

    def gather(pieces, matrix):
        return jnp.dot(jnp.concatenate(pieces, axis=1), matrix, preferred_element_type=jnp.float32)

    def gather_shared(whole, packed, which, width):
        half = packed.shape[0]
        parts = [
            gather([whole[k * half : (k + 1) * half], packed], edge_sum_ref[which + k, :, :width])
            for k in range(2)
        ]
        return jnp.concatenate(parts, axis=0)

    def body(at, here_at):
        off, on = off_ref[:, here_at].astype(jnp.float32), on_ref[:, here_at].astype(jnp.float32)
        off_mid, on_mid = flat(off[:2]), flat(on[:2])
        middle = [jnp.where(chosen, off_mid, on_mid), jnp.where(chosen, on_mid, off_mid)]
        middle = jnp.concatenate([middle[0], pltpu.roll(middle[1], 64, 1)], axis=0)
        outer = jnp.where(chosen == inner, on_mid, off_mid)
        received = whole_halves(off[2:], on[2:], chosen)
        own_prev, own_tend = flat(prev_ref[:, at]), flat(tend_ref[:, here_at])
        near_prev = flat(near_prev_ref[:, at])
        early, late = weights[1]
        near = jnp.where(inner, middle, flat(near_ref[:, at]) + weights[0][1] * received)
        total = gather_shared(advect(near, 1), advect(outer, 2), 0, 2 * LANES)
        own = flat(own_ref[:, at]) + total[:, :LANES] * share
        force = jnp.where(inner, received, early * near_prev + late * received)
        near = near + total[:, LANES:] * share + flat(near_add_ref[:, at]) + force
        early, late = weights[2]
        total = gather([advect(own, 0), advect(near, 1)], sum_ref[...])
        own = own + total[:, :LANES] * share + (early * own_prev + late * own_tend)
        near = near + total[:, LANES:] * share + (early * near_prev + late * received)
        early, late = weights[3]
        half = near.shape[0] // 2
        near = jnp.where(inner, pltpu.roll(near[half:], 64, 1), near[:half])
        total = gather_shared(advect(own, 0), advect(near, 3), 2, LANES)
        out = own + total * share + (early * own_prev + late * own_tend)
        out_ref[:, here_at] = out.reshape(PARTS, CHUNK, LANES)

    for j, here_at in enumerate(chunks(out_ref)):
        at = pl.ds((first + j) * CHUNK, CHUNK)
        body(at, here_at)
        if last:
            for k in range(PARTS):
                copies.append(
                    pltpu.make_async_copy(
                        out_ref.at[k, here_at], out_hbm.at[k, at], sems.at[1 + PARTS * j + k]
                    )
                )
                copies[-1].start()
    for copy in copies:
        copy.wait()


def exchanged(off, on):
    count = lax.axis_size(AXES)
    across = [(i, (i + 1) % count if i % 2 else (i - 1) % count) for i in range(count)]
    inside = [(i, i ^ 1) for i in range(count)]
    on = lax.ppermute(on, AXES, inside)
    return lax.ppermute(off, AXES, across), on


def per_device(state, prev_tendency, wind, edge_links, swap_slot, inverse):
    devices = lax.axis_size(AXES)
    shape = state.shape
    lev = shape[1]
    rows = shape[0] * lev // PARTS
    params = pltpu.CompilerParams(vmem_limit_bytes=VMEM)
    bf16, f32 = jnp.bfloat16, jnp.float32
    inner = pl.BlockSpec(memory_space=pltpu.VMEM)
    outer = pl.BlockSpec(memory_space=pltpu.HBM)

    def like(count, kind, length=rows):
        return pltpu.VMEM((count, length, LANES), kind)

    def table(kind, *size):
        return pltpu.VMEM(size, kind)

    def call(body, ins, outs, name, passes, **more):
        size = sum(math.prod(array.shape) * array.dtype.itemsize for array in ins)
        cost = pl.CostEstimate(
            flops=passes * 2 * PARTS * rows * 256 * 256, bytes_accessed=2 * size, transcendentals=0
        )
        more = {"in_specs": [inner] * len(ins), "out_specs": (inner,) * len(outs)} | more
        return pl.pallas_call(
            body, out_shape=outs, compiler_params=params, cost_estimate=cost, name=name, **more
        )(*ins)

    slot = swap_slot.reshape(1, LANES)
    slope = jnp.asarray(derivative_matrix())
    message = like(3, bf16, rows + 64)
    inputs = (
        inverse,
        wind,
        edge_links,
        state.reshape(PARTS, rows, LANES),
        prev_tendency.reshape(PARTS, rows, LANES),
    )
    inputs = tuple(pltpu.with_memory_space_constraint(array, pltpu.HBM) for array in inputs)
    matrices, packed, to_off, to_on, targets, wind, state, prev = call(
        pack_kernel,
        inputs,
        (
            table(bf16, inverse.shape[0] * lev, LANES),
            table(bf16, 368, LANES),
            message,
            message,
            table(f32, 8, LANES),
            table(f32, *wind.shape),
            like(4, f32),
            like(4, bf16),
        ),
        "pack",
        2,
        in_specs=[outer] * len(inputs),
        scratch_shapes=[
            pltpu.VMEM(inverse.shape, f32),
            pltpu.VMEM(edge_links.shape, jnp.int32),
            pltpu.SemaphoreType.DMA((3 + 2 * (rows // CHUNK),)),
        ],
    )
    far_packed = lax.ppermute(packed, AXES, [(i, i ^ (devices // 2)) for i in range(devices)])
    off, on = exchanged(to_off, to_on)
    halves = []
    first = 0
    shared = (wind, targets, slope, slot, matrices)
    for count in SPLIT:
        size = count * CHUNK
        outs = (like(4, bf16, size), like(4, f32, size), like(4, bf16, size), like(4, bf16, size))
        if first == 0:
            part, start = call(
                functools.partial(own_kernel, first, count),
                (state, prev) + shared,
                (like(4, f32, size), like(4, f32, size)),
                "own",
                3 * count,
            )
            ins = (state, prev, slot, far_packed, part, start)
            body, name = far_kernel, "far"
            outs += (table(bf16, *matrices.shape),)
        else:
            ins = (state, prev) + shared + (far_matrices,)
            body, name = physics_kernel, "physics"
        tend, ahead, to_off, to_on, *more = call(
            functools.partial(body, first, count), ins, outs, name, 5 * count
        )
        far_matrices = more[0] if more else far_matrices
        halves.append((first, count, tend, ahead, exchanged(to_off, to_on)))
        first += count
    parts = sum(((tend, ahead) for _, _, tend, ahead, _ in halves), ())
    own, near, near_add, near_prev, sums, edge_sums, blow = call(
        near_kernel,
        (state, wind, targets, slope, on, off, prev) + parts,
        (
            like(4, f32),
            like(4, f32),
            like(4, f32),
            like(4, bf16),
            table(bf16, 2 * LANES, 2 * LANES),
            table(bf16, 4, 2 * LANES, 2 * LANES),
            table(f32, 4, 2, lev, LANES),
        ),
        "near",
        16,
    )
    tends = tuple(tend for _, _, tend, _, _ in halves)
    out_spec = jax.ShapeDtypeStruct((PARTS, rows, LANES), f32)
    tend_spec = jax.ShapeDtypeStruct((PARTS, rows, LANES), bf16)
    for part, (first, count, tend, _, (off, on)) in enumerate(halves):
        ins = (own, near, near_add, near_prev, prev, on, off, slope, sums, edge_sums, blow)
        size = count * CHUNK
        if part == 0:
            done, tend_out = call(
                functools.partial(advance_kernel, first, False),
                ins + tends,
                (like(4, f32, size), tend_spec),
                "advance",
                5 * count,
                out_specs=(inner, outer),
                scratch_shapes=[pltpu.SemaphoreType.DMA((len(tends),))],
            )
        else:
            (out,) = call(
                functools.partial(advance_kernel, first, True),
                ins + (tend, done),
                (out_spec,),
                "advance",
                5 * count,
                out_specs=(outer,),
                scratch_shapes=[pltpu.VMEM((PARTS, size, LANES), f32), pltpu.SemaphoreType.DMA((1 + PARTS * count,))],
            )
    tend = tend_out
    return (out.reshape(shape), tend.reshape(shape))


def solution(mesh):
    columns = P(None, None, AXES)
    return jax.shard_map(
        per_device,
        mesh=mesh,
        in_specs=(columns, columns, columns, columns, P(AXES), P(AXES, None, None)),
        out_specs=(columns, columns),
        check_vma=False,
    )
```

```python
import functools
import math

import jax
import jax.numpy as jnp
import numpy as np
from jax import lax
from jax.experimental import pallas as pl
from jax.experimental.pallas import tpu as pltpu
from jax.sharding import PartitionSpec as P

SUBSTEPS = 4
AXES = ("gx", "gy")
LANES = 128
CHUNK = 144
SPLIT = (3, 2)
PARTS = 4
VMEM = 16 * 1024 * 1024

time_step = 0.2
edge_points = ((0, 1, 2, 3), (3, 7, 11, 15), (15, 14, 13, 12), (12, 8, 4, 0))


def point_tables():
    edge_of = np.zeros((2, 16), np.int32)
    spot_of = np.zeros((2, 16), np.int32)
    weight_of = np.zeros((2, 16), np.float32)
    filled = np.zeros(16, np.int32)
    for k in range(4):
        for m in range(4):
            p = edge_points[k][m]
            s = filled[p]
            edge_of[s, p] = k
            spot_of[s, p] = m
            weight_of[s, p] = 1.0
            filled[p] = s + 1
    return (edge_of, spot_of, weight_of)


def gll_derivative():
    gll_nodes = np.array([-1.0, -1.0 / np.sqrt(5.0), 1.0 / np.sqrt(5.0), 1.0])
    factors = np.array(
        [np.prod([gll_nodes[i] - gll_nodes[k] for k in range(4) if k != i]) for i in range(4)]
    )
    derivative = np.zeros((4, 4))
    for i in range(4):
        for k in range(4):
            if i != k:
                derivative[i, k] = factors[i] / (factors[k] * (gll_nodes[i] - gll_nodes[k]))
            else:
                derivative[i, k] = sum(
                    (1.0 / (gll_nodes[i] - gll_nodes[j]) for j in range(4) if j != i)
                )
    return derivative


def derivative_matrix():
    derivative = gll_derivative()
    eye_block = np.eye(8)
    both = np.concatenate(
        [
            np.kron(eye_block, np.kron(derivative, np.eye(4)).T),
            np.kron(eye_block, np.kron(np.eye(4), derivative).T),
        ],
        axis=1,
    )
    high = both.astype(jnp.bfloat16)
    low = (both - high.astype(np.float64)).astype(jnp.bfloat16)
    return np.concatenate([high, low], axis=0)


def hermite(substep):
    instant = (substep + 1.0) / SUBSTEPS
    square = instant * instant
    cube = square * instant
    h00 = 2.0 * cube - 3.0 * square + 1.0
    h01 = -2.0 * cube + 3.0 * square
    slope = cube - 2.0 * square + instant + (cube - square)
    return (h00 - slope, h01 + slope)


def lane_ids(rows=1):
    return lax.broadcasted_iota(jnp.int32, (rows, LANES), 1)


def point_sets():
    point = lane_ids() % 16
    across = (point // 4 == 0) | (point // 4 == 3)
    along = (point % 4 == 0) | (point % 4 == 3)
    slots = (across | along, across & along)
    share = jnp.where(slots[1], 1.0 / 3.0, jnp.where(slots[0], 0.5, 1.0)).astype(jnp.float32)
    return slots, share


def edge_targets(links_ref, first_elem, element_count):
    edge_of, spot_of, _ = point_tables()
    elements = links_ref.shape[2]
    own = first_elem + lax.broadcasted_iota(jnp.int32, (4, elements), 1)
    apart = links_ref[0] - own
    half = element_count // 2
    apart = jnp.where(apart > half, apart - element_count, apart)
    apart = jnp.where(apart < -half, apart + element_count, apart) + 2
    both = jnp.concatenate([apart, links_ref[1]], axis=0).astype(jnp.float32)
    spread = lax.broadcasted_iota(jnp.int32, (elements, LANES), 0)
    spread = (spread == lax.broadcasted_iota(jnp.int32, (elements, LANES), 1) // 16).astype(jnp.float32)
    both = jnp.dot(both, spread, preferred_element_type=jnp.float32)
    both = (both + 0.5).astype(jnp.int32)
    lane = lane_ids()
    point = lane % 16
    rows = []
    for s in range(2):
        edge = jnp.zeros((1, LANES), jnp.int32)
        spot = edge
        for p in range(16):
            edge = jnp.where(point == p, int(edge_of[s, p]), edge)
            spot = jnp.where(point == p, int(spot_of[s, p]), spot)
        away, far = both[0:1], both[4:5]
        for k in range(1, 4):
            away = jnp.where(edge == k, both[k : k + 1], away)
            far = jnp.where(edge == k, both[4 + k : 5 + k], far)
        place = jnp.where(far == 2, 12 + spot, 4 * spot)
        place = jnp.where(far == 1, 15 - 4 * spot, place)
        place = jnp.where(far == 0, 3 - spot, place)
        rows.append(lane - point + 16 * away + place)
    rows = jnp.concatenate(rows + [jnp.zeros((6, LANES), jnp.int32)], axis=0)
    return rows.astype(jnp.float32)


def on_odd():
    return lax.axis_index(AXES) % 2 == 1


def sides():
    return (lane_ids() < 64) == on_odd()


def packed_halves(value, chosen):
    away = [pltpu.roll(value[k + 2], 64, 1) for k in range(2)]
    off = [jnp.where(chosen, away[k], value[k]) for k in range(2)]
    on = [jnp.where(chosen, value[k], away[k]) for k in range(2)]
    return off, on


def whole_halves(off, on, chosen):
    count, rows = off.shape[0], off.shape[1]
    direct = jnp.where(chosen, off, on).reshape(count * rows, LANES)
    turned = jnp.where(chosen, on, off).reshape(count * rows, LANES)
    return jnp.concatenate([direct, pltpu.roll(turned, 64, 1)], axis=0)


def packed_matrices(matrix):
    lane = lane_ids()
    half = len(matrix) // 2
    rows = [jnp.where(lane < 64, matrix[c], pltpu.roll(matrix[c + half], 64, 1)) for c in range(half)]
    rest = jnp.zeros_like(matrix[0])
    for c, value in enumerate(matrix):
        rest = jnp.where(lane // 8 == c, pltpu.roll(value, (8 * c - 64) % LANES, 1), rest)
    return jnp.concatenate(rows + [rest, jnp.zeros((8, LANES), jnp.float32)], axis=0)


def unpacked_matrices(packed):
    lane = lane_ids()
    lev, half = 72, 4
    rest = packed[half * lev : (half + 1) * lev]
    rows = []
    for c in range(2 * half):
        main = packed[c % half * lev : (c % half + 1) * lev]
        main = main if c < half else pltpu.roll(main, 64, 1)
        tail = jnp.where(lane < lev, pltpu.roll(rest, (64 - 8 * c) % LANES, 1), 0.0)
        rows.append(jnp.where(lane < 64, main, tail))
    return jnp.concatenate(rows, axis=0)


def pack_kernel(
    inverse_hbm,
    wind_hbm,
    links_hbm,
    state_hbm,
    prev_hbm,
    matrix_ref,
    packed_ref,
    off_ref,
    on_ref,
    target_ref,
    wind_ref,
    state_ref,
    prev_ref,
    inverse_ref,
    links_ref,
    sems,
):
    pairs = [(inverse_hbm, inverse_ref), (wind_hbm, wind_ref), (links_hbm, links_ref)]
    for at in chunks(state_ref):
        pairs += [(state_hbm.at[:, at], state_ref.at[:, at]), (prev_hbm.at[:, at], prev_ref.at[:, at])]
    copies = [pltpu.make_async_copy(a, b, sems.at[i]) for i, (a, b) in enumerate(pairs)]
    for copy in copies:
        copy.start()
    groups, lev = inverse_ref.shape[0], inverse_ref.shape[1]
    copies[0].wait()
    eye = lax.broadcasted_iota(jnp.int32, (lev, lev), 0) == lax.broadcasted_iota(jnp.int32, (lev, lev), 1)
    eye = eye.astype(jnp.float32)
    blank = jnp.zeros((lev, LANES - lev), jnp.float32)
    matrix = [jnp.concatenate([inverse_ref[c] - eye, blank], axis=1) for c in range(groups)]
    matrix_ref[...] = jnp.concatenate(matrix, axis=0).astype(jnp.bfloat16)
    packed_ref[...] = packed_matrices(matrix).astype(jnp.bfloat16)
    copies[1].wait()
    copies[2].wait()
    devices = lax.axis_size(AXES)
    elements = links_ref.shape[2]
    targets = edge_targets(links_ref, lax.axis_index(AXES) * elements, elements * devices)
    target_ref[...] = targets
    end = off_ref.shape[1]
    filler = jnp.zeros((8, LANES), jnp.float32)
    flat_wind = wind_ref[...].reshape(2 * lev, LANES)
    for k in range(3):
        piece = jnp.concatenate([flat_wind[48 * k : 48 * k + 48], targets, filler], axis=0)
        piece = piece.astype(jnp.bfloat16)
        off_ref[k, end - 64 : end] = piece
        on_ref[k, end - 64 : end] = piece
    chosen = sides()
    odd = jnp.where(on_odd(), 3, 0)
    quarter = lane_ids() // 32
    for j, at in enumerate(chunks(state_ref)):
        copies[3 + 2 * j].wait()
        copies[4 + 2 * j].wait()
        off, on = packed_halves([state_ref[k, at] for k in range(PARTS)], chosen)
        for k in range(2):
            off_ref[k, at] = off[k].astype(jnp.bfloat16)
            on_ref[k, at] = on[k].astype(jnp.bfloat16)
        to_off = jnp.zeros((CHUNK, LANES), jnp.float32)
        to_on = to_off
        for k in range(PARTS):
            turned = prev_ref[k, at].astype(jnp.float32)
            turned = pltpu.roll(turned, 32 * k, 1) if k else turned
            to_off = jnp.where(quarter == (odd + k) % 4, turned, to_off)
            to_on = jnp.where(quarter == (3 - odd + k) % 4, turned, to_on)
        off_ref[2, at] = to_off.astype(jnp.bfloat16)
        on_ref[2, at] = to_on.astype(jnp.bfloat16)


def chunks(ref):
    return [pl.ds(start, CHUNK) for start in range(0, ref.shape[1], CHUNK)]


def in_turns(first, count, stages):
    running = []
    for j in range(count):
        running.append(stages(pl.ds((first + j) * CHUNK, CHUNK), pl.ds(j * CHUNK, CHUNK), j))
    waiting, started = list(running), []
    while waiting or started:
        if waiting:
            started.append(waiting.pop(0))
        started = [one for one in started if next(one, started) is not started]


def column_pair(pair):
    lev = pair.shape[0] // 2
    blank = jnp.zeros((LANES - lev, 2 * LANES), jnp.float32)
    pair = jnp.concatenate([pair[:lev], pair[lev:]], axis=1)
    high = pair.astype(jnp.bfloat16).astype(jnp.float32)
    return jnp.concatenate([high, blank, pair - high, blank], axis=0).astype(jnp.bfloat16)


def chosen_rows(product, group, chosen=None, first=0):
    lev = 72
    for c in range(product.shape[0] // lev):
        part = product[c * lev : (c + 1) * lev]
        chosen = part if chosen is None else jnp.where(group == first + c, part, chosen)
    return chosen


def as_rows(pair):
    return jnp.concatenate([pair[:, :LANES], pair[:, LANES:]], axis=0)


def column_group(slot_ref):
    slot = slot_ref[...]
    return jnp.where(slot // LANES == lax.axis_index(AXES), 0, 8) + slot % LANES // 16


def flat(value):
    return value.astype(jnp.float32).reshape(-1, LANES)


def moved(value, slope, blow_x, blow_y):
    rows, lev = value.shape[0], blow_x.shape[0]
    value = value.astype(jnp.bfloat16)
    both = jnp.dot(jnp.concatenate([value, value], axis=1), slope, preferred_element_type=jnp.float32)
    both = both.reshape(rows // lev, lev, 2 * LANES)
    motion = both[..., :LANES] * blow_x + both[..., LANES:] * blow_y
    return motion.reshape(rows, LANES).astype(jnp.bfloat16)


def sum_block(source, targets, slots, own):
    row = lax.broadcasted_iota(jnp.int32, (LANES, LANES), 0)
    total = jnp.zeros((LANES, LANES), jnp.float32)
    if own:
        total = (row == lax.broadcasted_iota(jnp.int32, (LANES, LANES), 1)).astype(jnp.float32)
    place = {
        "own": row,
        "near": jnp.where(row < 64, row + LANES, row - LANES),
        "near turned": jnp.where(row < 64, row - 64, row + 64),
        "outer": jnp.where(row < 64, row - LANES, row + LANES),
        "outer turned": jnp.where(row < 64, row + LANES + 64, row - LANES - 64),
    }[source]
    for s in range(2):
        total = total + ((place == targets[s : s + 1]) & slots[s]).astype(jnp.float32)
    return (total * point_sets()[1]).astype(jnp.bfloat16)


def inner_lanes():
    quarter = lane_ids() // 32
    return (quarter == 1) | (quarter == 2)


class Physics:
    def __init__(self, slot_ref, matrix_refs):
        self.take(jnp.concatenate([ref[...] for ref in matrix_refs], axis=0) if matrix_refs else None)
        group = column_group(slot_ref)
        self.group = jnp.concatenate([group, group], axis=1)
        self.inner = inner_lanes()
        self.chosen = sides()

    def take(self, matrices):
        if matrices is not None:
            self.matrices = jnp.concatenate([matrices, matrices], axis=1)

    def begin(self, wind_ref, target_ref, slope_ref):
        slots, _ = point_sets()
        self.sums = sum_block("own", target_ref[...].astype(jnp.int32) - 32, slots, True)
        self.blow = [-time_step * wind_ref[d] for d in range(2)]
        self.slope = slope_ref[...]

    def motion(self, state):
        return moved(state, self.slope, *self.blow)

    def start(self, state, prev, motion):
        total = jnp.dot(motion, self.sums, preferred_element_type=jnp.float32)
        return state + total + time_step * hermite(0)[0] * prev

    def products(self, pairs, others=None, first=0):
        ahead, rows = None, []

        def choose(k):
            other = None
            if others:
                lev = others[k].shape[0] // 2
                other = jnp.concatenate([others[k][:lev], others[k][lev:]], axis=1)
            return as_rows(chosen_rows(ahead, self.group, other, first))

        for k, pair in enumerate(pairs):
            product = jnp.dot(self.matrices, column_pair(pair), preferred_element_type=jnp.float32)
            if k:
                rows.append(choose(k - 1))
            ahead = product
            yield
        rows.append(choose(len(pairs) - 1))
        return rows

    def finish(self, start, prev, tends, here_at, tend_ref, ahead_ref, off_ref, on_ref):
        late = time_step * hermite(0)[1]
        early_1, late_1 = (time_step * w for w in hermite(1))
        ahead, force = [], []
        for k, tend in enumerate(tends):
            tend = tend.astype(jnp.bfloat16)
            tend_ref[k, here_at] = tend
            tend = tend.astype(jnp.float32)
            ahead.append(start[k] + late * tend)
            ahead_ref[k, here_at] = ahead[k]
            force.append(jnp.where(self.inner, early_1 * prev[k] + late_1 * tend, tend))
        off, on = packed_halves(force, self.chosen)
        for k in range(2):
            middle = jnp.where(self.inner, ahead[k], pltpu.roll(ahead[k + 2], 64, 1))
            middle = middle.astype(jnp.bfloat16)
            off_ref[k, here_at] = middle
            on_ref[k, here_at] = middle
            off_ref[2 + k, here_at] = off[k].astype(jnp.bfloat16)
            on_ref[2 + k, here_at] = on[k].astype(jnp.bfloat16)


def own_kernel(
    first, count, state_ref, prev_ref, wind_ref, target_ref, slope_ref, slot_ref, own_ref, part_ref, start_ref
):
    physics = Physics(slot_ref, [own_ref])
    physics.begin(wind_ref, target_ref, slope_ref)
    def stages(at, here_at, _):
        state = flat(state_ref[:, at])
        motion = physics.motion(state)
        yield
        start = physics.start(state, flat(prev_ref[:, at]), motion)
        start_ref[:, here_at] = start.reshape(PARTS, CHUNK, LANES)
        yield
        parts = yield from physics.products([state_ref[k, at] for k in range(PARTS)])
        for k, part in enumerate(parts):
            part_ref[k, here_at] = part

    in_turns(first, count, stages)


def far_kernel(
    first,
    count,
    state_ref,
    prev_ref,
    slot_ref,
    packed_ref,
    part_ref,
    start_ref,
    tend_ref,
    ahead_ref,
    off_ref,
    on_ref,
    far_ref,
):
    physics = Physics(slot_ref, [])
    matrices = unpacked_matrices(packed_ref[...].astype(jnp.float32)).astype(jnp.bfloat16)
    far_ref[...] = matrices
    physics.take(matrices)

    def stages(at, here_at, _):
        tends = yield from physics.products(
            [state_ref[k, at] for k in range(PARTS)], [part_ref[k, here_at] for k in range(PARTS)], 8
        )
        start = [start_ref[k, here_at] for k in range(PARTS)]
        prev = [prev_ref[k, at].astype(jnp.float32) for k in range(PARTS)]
        physics.finish(start, prev, tends, here_at, tend_ref, ahead_ref, off_ref, on_ref)

    in_turns(first, count, stages)


def physics_kernel(
    first,
    count,
    state_ref,
    prev_ref,
    wind_ref,
    target_ref,
    slope_ref,
    slot_ref,
    own_ref,
    far_ref,
    tend_ref,
    ahead_ref,
    off_ref,
    on_ref,
):
    physics = Physics(slot_ref, [own_ref, far_ref])
    physics.begin(wind_ref, target_ref, slope_ref)

    def stages(at, here_at, _):
        state = flat(state_ref[:, at])
        motion = physics.motion(state)
        yield
        start = physics.start(state, flat(prev_ref[:, at]), motion)
        start = [start[k * CHUNK : (k + 1) * CHUNK] for k in range(PARTS)]
        yield
        tends = yield from physics.products([state_ref[k, at] for k in range(PARTS)])
        prev = [prev_ref[k, at].astype(jnp.float32) for k in range(PARTS)]
        physics.finish(start, prev, tends, here_at, tend_ref, ahead_ref, off_ref, on_ref)

    in_turns(first, count, stages)


def near_kernel(
    state_ref,
    wind_ref,
    target_ref,
    slope_ref,
    off_ref,
    on_ref,
    prev_ref,
    *rest,
):
    parts, outs = rest[:-8], rest[-8:]
    own_ref, near_ref, near_add_ref, own_force_ref, near_force_ref, sum_ref, edge_sum_ref, blow_ref = outs
    lev = wind_ref.shape[1]
    slots, _ = point_sets()
    chosen = sides()
    end = off_ref.shape[1]

    def extra(ref, k):
        return ref[k, end - 64 : end].astype(jnp.float32)

    def winds(ref):
        whole = jnp.concatenate([extra(ref, k)[:48] for k in range(3)], axis=0)
        return whole[:lev], whole[lev:]

    def targets(ref):
        return extra(ref, 0)[48:56].astype(jnp.int32) - 32

    own_t = target_ref[...].astype(jnp.int32) - 32
    near_t = jnp.where(chosen, targets(off_ref), targets(on_ref))
    near_t = near_t + jnp.where(lane_ids() < 64, LANES, -LANES)
    own_sums = jnp.concatenate(
        [sum_block("own", own_t, slots, True), sum_block("own", near_t, slots, False)], axis=1
    )
    near_sums = jnp.concatenate(
        [sum_block("near", own_t, slots, False), sum_block("near", near_t, slots, True)], axis=1
    )
    sum_ref[:LANES] = own_sums
    sum_ref[LANES:] = near_sums
    nothing = jnp.zeros((LANES, LANES), jnp.bfloat16)
    for k, turn in enumerate(("", " turned")):
        edge_sum_ref[k, :LANES] = near_sums
        edge_sum_ref[k, LANES:, :LANES] = nothing
        edge_sum_ref[k, LANES:, LANES:] = sum_block("outer" + turn, near_t, slots, False)
        edge_sum_ref[2 + k, :LANES, :LANES] = own_sums[:, :LANES]
        edge_sum_ref[2 + k, LANES:, :LANES] = sum_block("near" + turn, own_t, slots, False)
    inner = inner_lanes()
    off_w, on_w = winds(off_ref), winds(on_ref)
    for d in range(2):
        blow_ref[0, d] = -time_step * wind_ref[d]
        near_w = -time_step * jnp.where(chosen, off_w[d], on_w[d])
        outer_w = -time_step * jnp.where(chosen, on_w[d], off_w[d])
        blow_ref[1, d] = near_w
        blow_ref[2, d] = jnp.where(inner, outer_w, pltpu.roll(outer_w, 64, 1))
        blow_ref[3, d] = jnp.where(inner, pltpu.roll(near_w, 64, 1), near_w)

    slope = slope_ref[...]
    early = time_step * hermite(0)[0]
    early_1, late_1 = (time_step * w for w in hermite(1))
    early_2, late_2 = (time_step * w for w in hermite(2))
    own_blow = (blow_ref[0, 0], blow_ref[0, 1])
    near_blow = (blow_ref[1, 0], blow_ref[1, 1])

    def stages(at, here_at, tend_ref, ahead_ref):
        off, on = off_ref[:, at].astype(jnp.float32), on_ref[:, at].astype(jnp.float32)
        near = whole_halves(off[:2], on[:2], chosen)
        own_move = moved(flat(state_ref[:, at]), slope, *own_blow)
        near_move = moved(near, slope, *near_blow)
        yield
        total = jnp.dot(near_move, near_sums, preferred_element_type=jnp.float32)
        near_total = total[:, LANES:] + jnp.dot(
            own_move, own_sums[:, LANES:], preferred_element_type=jnp.float32
        )
        kept = [jnp.where(chosen, off[2], on[2])]
        for k in range(1, PARTS):
            turned = [pltpu.roll(side[2], LANES - 32 * k, 1) for side in (off, on)]
            kept.append(jnp.where(chosen, *turned))
        kept = jnp.where(inner, 0.0, jnp.concatenate(kept, axis=0))
        near = near + near_total + early * kept
        near_ref[:, at] = near.reshape(PARTS, CHUNK, LANES)
        near_force_ref[:, at] = (early_2 * kept).reshape(PARTS, CHUNK, LANES)
        own = flat(ahead_ref[:, here_at]) + total[:, :LANES]
        yield
        own_move = moved(own, slope, *own_blow)
        yield
        total = jnp.dot(own_move, own_sums, preferred_element_type=jnp.float32)
        own_prev, own_tend = flat(prev_ref[:, at]), flat(tend_ref[:, here_at])
        own = own + total[:, :LANES] + (early_1 * own_prev + late_1 * own_tend)
        own_ref[:, at] = own.reshape(PARTS, CHUNK, LANES)
        own_force = early_2 * own_prev + late_2 * own_tend
        own_force_ref[:, at] = own_force.reshape(PARTS, CHUNK, LANES)
        near_add = total[:, LANES:] + early_1 * kept
        near_add_ref[:, at] = near_add.reshape(PARTS, CHUNK, LANES)

    places = []
    for tend_ref, ahead_ref in zip(parts[::2], parts[1::2]):
        places += [(here_at, tend_ref, ahead_ref) for here_at in chunks(tend_ref)]
    in_turns(0, len(places), lambda at, _, j: stages(at, *places[j]))


def advance_kernel(
    first,
    last,
    own_ref,
    near_ref,
    near_add_ref,
    own_force_ref,
    near_force_ref,
    off_ref,
    on_ref,
    slope_ref,
    sum_ref,
    edge_sum_ref,
    blow_ref,
    *rest,
):
    if last:
        tend_ref, done_ref, out_hbm, out_ref, sems = rest
        copies = [pltpu.make_async_copy(done_ref, out_hbm.at[:, pl.ds(0, done_ref.shape[1])], sems.at[0])]
    else:
        *tend_refs, out_ref, tend_hbm, sems = rest
        tend_ref = tend_refs[0]
        copies, row = [], 0
        for k, ref in enumerate(tend_refs):
            copies.append(pltpu.make_async_copy(ref, tend_hbm.at[:, pl.ds(row, ref.shape[1])], sems.at[k]))
            row += ref.shape[1]
    for copy in copies:
        copy.start()
    inner = inner_lanes()
    chosen = sides()
    slope = slope_ref[...]
    lates = [time_step * hermite(s)[1] for s in range(SUBSTEPS)]

    def advect(value, unit):
        return moved(value, slope, blow_ref[unit, 0], blow_ref[unit, 1])

    def gather(pieces, matrix):
        return jnp.dot(jnp.concatenate(pieces, axis=1), matrix, preferred_element_type=jnp.float32)

    def gather_shared(whole, packed, which, width):
        half = packed.shape[0]
        parts = [
            gather([whole[k * half : (k + 1) * half], packed], edge_sum_ref[which + k, :, :width])
            for k in range(2)
        ]
        return jnp.concatenate(parts, axis=0)

    def stages(at, here_at, j):
        off, on = off_ref[:, here_at].astype(jnp.float32), on_ref[:, here_at].astype(jnp.float32)
        off_mid, on_mid = flat(off[:2]), flat(on[:2])
        middle = [jnp.where(chosen, off_mid, on_mid), jnp.where(chosen, on_mid, off_mid)]
        middle = jnp.concatenate([middle[0], pltpu.roll(middle[1], 64, 1)], axis=0)
        outer = jnp.where(chosen == inner, on_mid, off_mid)
        received = whole_halves(off[2:], on[2:], chosen)
        near = jnp.where(inner, middle, flat(near_ref[:, at]) + lates[0] * received)
        moves = advect(near, 1), advect(outer, 2)
        yield
        total = gather_shared(*moves, 0, 2 * LANES)
        own = flat(own_ref[:, at]) + total[:, :LANES]
        force = received * jnp.where(inner, 1.0, lates[1])
        near = near + total[:, LANES:] + (flat(near_add_ref[:, at]) + force)
        yield
        moves = [advect(own, 0), advect(near, 1)]
        yield
        total = gather(moves, sum_ref[...])
        own = own + total[:, :LANES] + flat(own_force_ref[:, at])
        near = near + total[:, LANES:] + (flat(near_force_ref[:, at]) + lates[2] * received)
        yield
        half = near.shape[0] // 2
        near = jnp.where(inner, pltpu.roll(near[half:], 64, 1), near[:half])
        moves = advect(own, 0), advect(near, 3)
        yield
        total = gather_shared(*moves, 2, LANES)
        out = own + total + lates[3] * flat(tend_ref[:, here_at])
        out_ref[:, here_at] = out.reshape(PARTS, CHUNK, LANES)
        if last:
            for k in range(PARTS):
                copies.append(
                    pltpu.make_async_copy(
                        out_ref.at[k, here_at], out_hbm.at[k, at], sems.at[1 + PARTS * j + k]
                    )
                )
                copies[-1].start()

    in_turns(first, out_ref.shape[1] // CHUNK, stages)
    for copy in copies:
        copy.wait()


def exchanged(off, on):
    count = lax.axis_size(AXES)
    across = [(i, (i + 1) % count if i % 2 else (i - 1) % count) for i in range(count)]
    inside = [(i, i ^ 1) for i in range(count)]
    on = lax.ppermute(on, AXES, inside)
    return lax.ppermute(off, AXES, across), on


def per_device(state, prev_tendency, wind, edge_links, swap_slot, inverse):
    devices = lax.axis_size(AXES)
    shape = state.shape
    lev = shape[1]
    rows = shape[0] * lev // PARTS
    params = pltpu.CompilerParams(vmem_limit_bytes=VMEM)
    bf16, f32 = jnp.bfloat16, jnp.float32
    inner = pl.BlockSpec(memory_space=pltpu.VMEM)
    outer = pl.BlockSpec(memory_space=pltpu.HBM)

    def like(count, kind, length=rows):
        return pltpu.VMEM((count, length, LANES), kind)

    def table(kind, *size):
        return pltpu.VMEM(size, kind)

    def call(body, ins, outs, name, passes, **more):
        size = sum(math.prod(array.shape) * array.dtype.itemsize for array in ins)
        cost = pl.CostEstimate(
            flops=passes * 2 * PARTS * rows * 256 * 256, bytes_accessed=2 * size, transcendentals=0
        )
        more = {"in_specs": [inner] * len(ins), "out_specs": (inner,) * len(outs)} | more
        return pl.pallas_call(
            body, out_shape=outs, compiler_params=params, cost_estimate=cost, name=name, **more
        )(*ins)

    slot = swap_slot.reshape(1, LANES)
    slope = jnp.asarray(derivative_matrix())
    message = like(3, bf16, rows + 64)
    inputs = (
        inverse,
        wind,
        edge_links,
        state.reshape(PARTS, rows, LANES),
        prev_tendency.reshape(PARTS, rows, LANES),
    )
    inputs = tuple(pltpu.with_memory_space_constraint(array, pltpu.HBM) for array in inputs)
    matrices, packed, to_off, to_on, targets, wind, state, prev = call(
        pack_kernel,
        inputs,
        (
            table(bf16, inverse.shape[0] * lev, LANES),
            table(bf16, 368, LANES),
            message,
            message,
            table(f32, 8, LANES),
            table(f32, *wind.shape),
            like(4, f32),
            like(4, bf16),
        ),
        "pack",
        2,
        in_specs=[outer] * len(inputs),
        scratch_shapes=[
            pltpu.VMEM(inverse.shape, f32),
            pltpu.VMEM(edge_links.shape, jnp.int32),
            pltpu.SemaphoreType.DMA((3 + 2 * (rows // CHUNK),)),
        ],
    )
    far_packed = lax.ppermute(packed, AXES, [(i, i ^ (devices // 2)) for i in range(devices)])
    off, on = exchanged(to_off, to_on)
    halves = []
    first = 0
    shared = (wind, targets, slope, slot, matrices)
    for count in SPLIT:
        size = count * CHUNK
        outs = (like(4, bf16, size), like(4, f32, size), like(4, bf16, size), like(4, bf16, size))
        if first == 0:
            part, start = call(
                functools.partial(own_kernel, first, count),
                (state, prev) + shared,
                (like(4, f32, size), like(4, f32, size)),
                "own",
                3 * count,
            )
            ins = (state, prev, slot, far_packed, part, start)
            body, name = far_kernel, "far"
            outs += (table(bf16, *matrices.shape),)
        else:
            ins = (state, prev) + shared + (far_matrices,)
            body, name = physics_kernel, "physics"
        tend, ahead, to_off, to_on, *more = call(
            functools.partial(body, first, count), ins, outs, name, 5 * count
        )
        far_matrices = more[0] if more else far_matrices
        halves.append((first, count, tend, ahead, exchanged(to_off, to_on)))
        first += count
    parts = sum(((tend, ahead) for _, _, tend, ahead, _ in halves), ())
    own, near, near_add, own_force, near_force, sums, edge_sums, blow = call(
        near_kernel,
        (state, wind, targets, slope, off, on, prev) + parts,
        (
            like(4, f32),
            like(4, f32),
            like(4, f32),
            like(4, f32),
            like(4, f32),
            table(bf16, 2 * LANES, 2 * LANES),
            table(bf16, 4, 2 * LANES, 2 * LANES),
            table(f32, 4, 2, lev, LANES),
        ),
        "near",
        16,
    )
    tends = tuple(tend for _, _, tend, _, _ in halves)
    out_spec = jax.ShapeDtypeStruct((PARTS, rows, LANES), f32)
    tend_spec = jax.ShapeDtypeStruct((PARTS, rows, LANES), bf16)
    for part, (first, count, tend, _, (off, on)) in enumerate(halves):
        ins = (own, near, near_add, own_force, near_force, off, on, slope, sums, edge_sums, blow)
        size = count * CHUNK
        if part == 0:
            done, tend_out = call(
                functools.partial(advance_kernel, first, False),
                ins + tends,
                (like(4, f32, size), tend_spec),
                "advance",
                5 * count,
                out_specs=(inner, outer),
                scratch_shapes=[pltpu.SemaphoreType.DMA((len(tends),))],
            )
        else:
            (out,) = call(
                functools.partial(advance_kernel, first, True),
                ins + (tend, done),
                (out_spec,),
                "advance",
                5 * count,
                out_specs=(outer,),
                scratch_shapes=[pltpu.VMEM((PARTS, size, LANES), f32), pltpu.SemaphoreType.DMA((1 + PARTS * count,))],
            )
    tend = tend_out
    return (out.reshape(shape), tend.reshape(shape))


def solution(mesh):
    columns = P(None, None, AXES)
    return jax.shard_map(
        per_device,
        mesh=mesh,
        in_specs=(columns, columns, columns, columns, P(AXES), P(AXES, None, None)),
        out_specs=(columns, columns),
        check_vma=False,
    )
```

```python
import functools
import math

import jax
import jax.numpy as jnp
import numpy as np
from jax import lax
from jax.experimental import pallas as pl
from jax.experimental.pallas import tpu as pltpu
from jax.sharding import PartitionSpec as P

SUBSTEPS = 4
AXES = ("gx", "gy")
LANES = 128
CHUNK = 144
SPLIT = (3, 2)
PARTS = 4
VMEM = 16 * 1024 * 1024

time_step = 0.2
edge_points = ((0, 1, 2, 3), (3, 7, 11, 15), (15, 14, 13, 12), (12, 8, 4, 0))


def point_tables():
    edge_of = np.zeros((2, 16), np.int32)
    spot_of = np.zeros((2, 16), np.int32)
    weight_of = np.zeros((2, 16), np.float32)
    filled = np.zeros(16, np.int32)
    for k in range(4):
        for m in range(4):
            p = edge_points[k][m]
            s = filled[p]
            edge_of[s, p] = k
            spot_of[s, p] = m
            weight_of[s, p] = 1.0
            filled[p] = s + 1
    return (edge_of, spot_of, weight_of)


def gll_derivative():
    gll_nodes = np.array([-1.0, -1.0 / np.sqrt(5.0), 1.0 / np.sqrt(5.0), 1.0])
    factors = np.array(
        [np.prod([gll_nodes[i] - gll_nodes[k] for k in range(4) if k != i]) for i in range(4)]
    )
    derivative = np.zeros((4, 4))
    for i in range(4):
        for k in range(4):
            if i != k:
                derivative[i, k] = factors[i] / (factors[k] * (gll_nodes[i] - gll_nodes[k]))
            else:
                derivative[i, k] = sum(
                    (1.0 / (gll_nodes[i] - gll_nodes[j]) for j in range(4) if j != i)
                )
    return derivative


def derivative_matrix():
    derivative = gll_derivative()
    eye_block = np.eye(8)
    both = np.concatenate(
        [
            np.kron(eye_block, np.kron(derivative, np.eye(4)).T),
            np.kron(eye_block, np.kron(np.eye(4), derivative).T),
        ],
        axis=1,
    )
    high = both.astype(jnp.bfloat16)
    low = (both - high.astype(np.float64)).astype(jnp.bfloat16)
    return np.concatenate([high, low], axis=0)


def hermite(substep):
    instant = (substep + 1.0) / SUBSTEPS
    square = instant * instant
    cube = square * instant
    h00 = 2.0 * cube - 3.0 * square + 1.0
    h01 = -2.0 * cube + 3.0 * square
    slope = cube - 2.0 * square + instant + (cube - square)
    return (h00 - slope, h01 + slope)


def lane_ids(rows=1):
    return lax.broadcasted_iota(jnp.int32, (rows, LANES), 1)


def point_sets():
    point = lane_ids() % 16
    across = (point // 4 == 0) | (point // 4 == 3)
    along = (point % 4 == 0) | (point % 4 == 3)
    slots = (across | along, across & along)
    share = jnp.where(slots[1], 1.0 / 3.0, jnp.where(slots[0], 0.5, 1.0)).astype(jnp.float32)
    return slots, share


def edge_targets(links_ref, first_elem, element_count):
    edge_of, spot_of, _ = point_tables()
    elements = links_ref.shape[2]
    own = first_elem + lax.broadcasted_iota(jnp.int32, (4, elements), 1)
    apart = links_ref[0] - own
    half = element_count // 2
    apart = jnp.where(apart > half, apart - element_count, apart)
    apart = jnp.where(apart < -half, apart + element_count, apart) + 2
    both = jnp.concatenate([apart, links_ref[1]], axis=0).astype(jnp.float32)
    spread = lax.broadcasted_iota(jnp.int32, (elements, LANES), 0)
    spread = (spread == lax.broadcasted_iota(jnp.int32, (elements, LANES), 1) // 16).astype(jnp.float32)
    both = jnp.dot(both, spread, preferred_element_type=jnp.float32)
    both = (both + 0.5).astype(jnp.int32)
    lane = lane_ids()
    point = lane % 16
    rows = []
    for s in range(2):
        edge = jnp.zeros((1, LANES), jnp.int32)
        spot = edge
        for p in range(16):
            edge = jnp.where(point == p, int(edge_of[s, p]), edge)
            spot = jnp.where(point == p, int(spot_of[s, p]), spot)
        away, far = both[0:1], both[4:5]
        for k in range(1, 4):
            away = jnp.where(edge == k, both[k : k + 1], away)
            far = jnp.where(edge == k, both[4 + k : 5 + k], far)
        place = jnp.where(far == 2, 12 + spot, 4 * spot)
        place = jnp.where(far == 1, 15 - 4 * spot, place)
        place = jnp.where(far == 0, 3 - spot, place)
        rows.append(lane - point + 16 * away + place)
    rows = jnp.concatenate(rows + [jnp.zeros((6, LANES), jnp.int32)], axis=0)
    return rows.astype(jnp.float32)


def on_odd():
    return lax.axis_index(AXES) % 2 == 1


def sides():
    return (lane_ids() < 64) == on_odd()


def packed_halves(value, chosen):
    away = [pltpu.roll(value[k + 2], 64, 1) for k in range(2)]
    off = [jnp.where(chosen, away[k], value[k]) for k in range(2)]
    on = [jnp.where(chosen, value[k], away[k]) for k in range(2)]
    return off, on


def whole_halves(off, on, chosen):
    count, rows = off.shape[0], off.shape[1]
    direct = jnp.where(chosen, off, on).reshape(count * rows, LANES)
    turned = jnp.where(chosen, on, off).reshape(count * rows, LANES)
    return jnp.concatenate([direct, pltpu.roll(turned, 64, 1)], axis=0)


def mixed(*generators):
    values = {}
    while len(values) < len(generators):
        for i, one in enumerate(generators):
            if i not in values:
                try:
                    next(one)
                except StopIteration as end:
                    values[i] = end.value
        yield
    return [values[i] for i in range(len(generators))]


def packed_matrices(matrix):
    lane = lane_ids()
    half = len(matrix) // 2
    rows = [jnp.where(lane < 64, matrix[c], pltpu.roll(matrix[c + half], 64, 1)) for c in range(half)]
    rest = jnp.zeros_like(matrix[0])
    for c, value in enumerate(matrix):
        rest = jnp.where(lane // 8 == c, pltpu.roll(value, (8 * c - 64) % LANES, 1), rest)
    return jnp.concatenate(rows + [rest, jnp.zeros((8, LANES), jnp.float32)], axis=0)


def unpacked_matrices(packed):
    lane = lane_ids()
    lev, half = 72, 4
    rest = packed[half * lev : (half + 1) * lev]
    rows = []
    for c in range(2 * half):
        main = packed[c % half * lev : (c % half + 1) * lev]
        main = main if c < half else pltpu.roll(main, 64, 1)
        tail = jnp.where(lane < lev, pltpu.roll(rest, (64 - 8 * c) % LANES, 1), 0.0)
        rows.append(jnp.where(lane < 64, main, tail))
    return jnp.concatenate(rows, axis=0)


def leaving_tables(slot_ref, keep_ref, spread_ref, far_group_ref):
    slot = slot_ref[...]
    leaving = slot // LANES != lax.axis_index(AXES)
    row = lax.broadcasted_iota(jnp.int32, (LANES, LANES), 0)
    col = lax.broadcasted_iota(jnp.int32, (LANES, LANES), 1)
    ones = jnp.broadcast_to(leaving, (8, LANES)).astype(jnp.float32)
    rank = jnp.dot(ones, (row <= col).astype(jnp.float32), preferred_element_type=jnp.float32)
    yield
    rank = (rank[0:1] + 0.5).astype(jnp.int32) - 1
    spread = [(leaving & (rank + 64 * k == row)).astype(jnp.float32) for k in range(2)]
    yield
    keep = [jnp.transpose(half) for half in spread]
    yield
    for k in range(2):
        spread_ref[:, k * LANES : (k + 1) * LANES] = spread[k].astype(jnp.bfloat16)
        keep_ref[k * LANES : (k + 1) * LANES] = keep[k].astype(jnp.bfloat16)
    group = jnp.broadcast_to(slot % LANES // 16, (8, LANES)).astype(jnp.float32)
    far_group_ref[...] = jnp.dot(group, keep[0] + keep[1], preferred_element_type=jnp.float32)


def pack_kernel(
    inverse_hbm,
    wind_hbm,
    links_hbm,
    state_hbm,
    prev_hbm,
    matrix_ref,
    packed_ref,
    off_ref,
    on_ref,
    target_ref,
    wind_ref,
    state_ref,
    prev_ref,
    inverse_ref,
    links_ref,
    sems,
):
    pairs = [(links_hbm, links_ref), (inverse_hbm, inverse_ref), (wind_hbm, wind_ref)]
    for at in chunks(state_ref):
        pairs += [(state_hbm.at[:, at], state_ref.at[:, at]), (prev_hbm.at[:, at], prev_ref.at[:, at])]
    copies = [pltpu.make_async_copy(a, b, sems.at[i]) for i, (a, b) in enumerate(pairs)]
    for copy in copies:
        copy.start()
    copies[0].wait()
    devices = lax.axis_size(AXES)
    elements = links_ref.shape[2]
    targets = edge_targets(links_ref, lax.axis_index(AXES) * elements, elements * devices)
    groups, lev = inverse_ref.shape[0], inverse_ref.shape[1]
    copies[1].wait()
    eye = lax.broadcasted_iota(jnp.int32, (lev, lev), 0) == lax.broadcasted_iota(jnp.int32, (lev, lev), 1)
    eye = eye.astype(jnp.float32)
    blank = jnp.zeros((lev, LANES - lev), jnp.float32)
    matrix = [jnp.concatenate([inverse_ref[c] - eye, blank], axis=1) for c in range(groups)]
    matrix_ref[...] = jnp.concatenate(matrix, axis=0).astype(jnp.bfloat16)
    packed_ref[...] = packed_matrices(matrix).astype(jnp.bfloat16)
    copies[2].wait()
    target_ref[...] = targets
    end = off_ref.shape[1]
    filler = jnp.zeros((8, LANES), jnp.float32)
    flat_wind = wind_ref[...].reshape(2 * lev, LANES)
    for k in range(3):
        piece = jnp.concatenate([flat_wind[48 * k : 48 * k + 48], targets, filler], axis=0)
        piece = piece.astype(jnp.bfloat16)
        off_ref[k, end - 64 : end] = piece
        on_ref[k, end - 64 : end] = piece
    chosen = sides()
    odd = jnp.where(on_odd(), 3, 0)
    quarter = lane_ids() // 32
    for j, at in enumerate(chunks(state_ref)):
        copies[3 + 2 * j].wait()
        copies[4 + 2 * j].wait()
        off, on = packed_halves([state_ref[k, at] for k in range(PARTS)], chosen)
        for k in range(2):
            off_ref[k, at] = off[k].astype(jnp.bfloat16)
            on_ref[k, at] = on[k].astype(jnp.bfloat16)
        to_off = jnp.zeros((CHUNK, LANES), jnp.float32)
        to_on = to_off
        for k in range(PARTS):
            turned = prev_ref[k, at].astype(jnp.float32)
            turned = pltpu.roll(turned, 32 * k, 1) if k else turned
            to_off = jnp.where(quarter == (odd + k) % 4, turned, to_off)
            to_on = jnp.where(quarter == (3 - odd + k) % 4, turned, to_on)
        off_ref[2, at] = to_off.astype(jnp.bfloat16)
        on_ref[2, at] = to_on.astype(jnp.bfloat16)


def chunks(ref):
    return [pl.ds(start, CHUNK) for start in range(0, ref.shape[1], CHUNK)]


def in_turns(first, count, stages, together=False):
    running = []
    for j in range(count):
        running.append(stages(pl.ds((first + j) * CHUNK, CHUNK), pl.ds(j * CHUNK, CHUNK), j))
    waiting, started = list(running), []
    while waiting or started:
        while waiting:
            started.append(waiting.pop(0))
            if not together:
                break
        started = [one for one in started if next(one, started) is not started]


def column_pair(pair):
    lev = pair.shape[0] // 2
    blank = jnp.zeros((LANES - lev, 2 * LANES), jnp.float32)
    pair = jnp.concatenate([pair[:lev], pair[lev:]], axis=1)
    high = pair.astype(jnp.bfloat16).astype(jnp.float32)
    return jnp.concatenate([high, blank, pair - high, blank], axis=0).astype(jnp.bfloat16)


def chosen_rows(product, group, chosen=None, first=0):
    lev = 72
    for c in range(product.shape[0] // lev):
        part = product[c * lev : (c + 1) * lev]
        chosen = part if chosen is None else jnp.where(group == first + c, part, chosen)
    return chosen


def as_rows(pair):
    return jnp.concatenate([pair[:, :LANES], pair[:, LANES:]], axis=0)


def column_group(slot_ref):
    slot = slot_ref[...]
    return jnp.where(slot // LANES == lax.axis_index(AXES), 0, 8) + slot % LANES // 16


def flat(value):
    return value.astype(jnp.float32).reshape(-1, LANES)


def moved(value, slope, blow_x, blow_y):
    rows, lev = value.shape[0], blow_x.shape[0]
    value = value.astype(jnp.bfloat16)
    both = jnp.dot(jnp.concatenate([value, value], axis=1), slope, preferred_element_type=jnp.float32)
    both = both.reshape(rows // lev, lev, 2 * LANES)
    motion = both[..., :LANES] * blow_x + both[..., LANES:] * blow_y
    return motion.reshape(rows, LANES).astype(jnp.bfloat16)


def sum_block(source, targets, slots, own):
    row = lax.broadcasted_iota(jnp.int32, (LANES, LANES), 0)
    total = jnp.zeros((LANES, LANES), jnp.float32)
    if own:
        total = (row == lax.broadcasted_iota(jnp.int32, (LANES, LANES), 1)).astype(jnp.float32)
    place = {
        "own": row,
        "near": jnp.where(row < 64, row + LANES, row - LANES),
        "near turned": jnp.where(row < 64, row - 64, row + 64),
        "outer": jnp.where(row < 64, row - LANES, row + LANES),
        "outer turned": jnp.where(row < 64, row + LANES + 64, row - LANES - 64),
    }[source]
    for s in range(2):
        total = total + ((place == targets[s : s + 1]) & slots[s]).astype(jnp.float32)
    return (total * point_sets()[1]).astype(jnp.bfloat16)


def inner_lanes():
    quarter = lane_ids() // 32
    return (quarter == 1) | (quarter == 2)


class Physics:
    def __init__(self, slot_ref):
        group = column_group(slot_ref)
        self.here = group < 8
        self.group = jnp.concatenate([group, group], axis=1)
        self.inner = inner_lanes()
        self.chosen = sides()

    def take_own(self, own_ref):
        self.own = jnp.concatenate([own_ref[...], own_ref[...]], axis=1)

    def take_far(self, far, keep_ref, spread_ref, far_group_ref):
        self.far = far
        self.keep, self.spread = keep_ref[...], spread_ref[...]
        group = (far_group_ref[0:1, :] + 0.5).astype(jnp.int32)
        self.far_group = jnp.concatenate([group, group], axis=1)

    def begin(self, wind_ref, target_ref, slope_ref):
        slots, _ = point_sets()
        self.sums = sum_block("own", target_ref[...].astype(jnp.int32) - 32, slots, True)
        self.blow = [-time_step * wind_ref[d] for d in range(2)]
        self.slope = slope_ref[...]

    def motion(self, state):
        return moved(state, self.slope, *self.blow)

    def start(self, state, prev):
        motion = self.motion(state)
        yield
        total = jnp.dot(motion, self.sums, preferred_element_type=jnp.float32)
        return state + total + time_step * hermite(0)[0] * prev

    def own_products(self, pairs):
        ahead, rows = None, []
        for k, pair in enumerate(pairs):
            product = jnp.dot(self.own, column_pair(pair), preferred_element_type=jnp.float32)
            if k:
                rows.append(as_rows(chosen_rows(ahead, self.group)))
            ahead = product
            yield
        rows.append(as_rows(chosen_rows(ahead, self.group)))
        return rows

    def far_products(self, pairs):
        high = [pair.astype(jnp.bfloat16) for pair in pairs]
        both = [jnp.concatenate(high[k : k + 2], axis=1) for k in (0, 2)]
        few = jnp.dot(jnp.concatenate(both, axis=0), self.keep, preferred_element_type=jnp.float32)
        yield
        size = pairs[0].shape[0]
        lev = size // 2
        blank = jnp.zeros((LANES - lev, 2 * LANES), jnp.float32)
        products, rows = [], []
        for k in range(2):
            part = few[k * size : (k + 1) * size]
            part = jnp.concatenate([part[:lev], part[lev:]], axis=1)
            column = jnp.concatenate([part, blank], axis=0).astype(jnp.bfloat16)
            products.append(jnp.dot(self.far, column, preferred_element_type=jnp.float32))
            yield
        for k in range(2):
            rows.append(as_rows(chosen_rows(products[k], self.far_group)))
        rows = jnp.concatenate(rows, axis=0).astype(jnp.bfloat16)
        wide = jnp.dot(rows, self.spread, preferred_element_type=jnp.float32)
        yield
        return [wide[k * size : (k + 1) * size, c : c + LANES] for k in range(2) for c in (0, LANES)]

    def merged(self, own, far):
        return [jnp.where(self.here, a, b) for a, b in zip(own, far)]

    def finish(self, start, prev, tends, here_at, tend_ref, ahead_ref, off_ref, on_ref):
        late = time_step * hermite(0)[1]
        early_1, late_1 = (time_step * w for w in hermite(1))
        ahead, force = [], []
        for k, tend in enumerate(tends):
            tend = tend.astype(jnp.bfloat16)
            tend_ref[k, here_at] = tend
            tend = tend.astype(jnp.float32)
            ahead.append(start[k] + late * tend)
            ahead_ref[k, here_at] = ahead[k]
            force.append(jnp.where(self.inner, early_1 * prev[k] + late_1 * tend, tend))
        off, on = packed_halves(force, self.chosen)
        for k in range(2):
            middle = jnp.where(self.inner, ahead[k], pltpu.roll(ahead[k + 2], 64, 1))
            middle = middle.astype(jnp.bfloat16)
            off_ref[k, here_at] = middle
            on_ref[k, here_at] = middle
            off_ref[2 + k, here_at] = off[k].astype(jnp.bfloat16)
            on_ref[2 + k, here_at] = on[k].astype(jnp.bfloat16)


def own_kernel(
    first, count, state_ref, prev_ref, wind_ref, target_ref, slope_ref, slot_ref, own_ref, part_ref, start_ref, *tables
):
    physics = Physics(slot_ref)
    physics.take_own(own_ref)
    physics.begin(wind_ref, target_ref, slope_ref)

    def stages(at, here_at, j):
        parts, start, *_ = yield from mixed(
            physics.own_products([state_ref[k, at] for k in range(PARTS)]),
            physics.start(flat(state_ref[:, at]), flat(prev_ref[:, at])),
            *([leaving_tables(slot_ref, *tables)] if j == 0 else []),
        )
        start_ref[:, here_at] = start.reshape(PARTS, CHUNK, LANES)
        for k, part in enumerate(parts):
            part_ref[k, here_at] = part

    in_turns(first, count, stages, True)


def far_kernel(
    first,
    count,
    state_ref,
    prev_ref,
    slot_ref,
    packed_ref,
    keep_ref,
    spread_ref,
    far_group_ref,
    part_ref,
    start_ref,
    tend_ref,
    ahead_ref,
    off_ref,
    on_ref,
    far_ref,
):
    physics = Physics(slot_ref)
    matrices = unpacked_matrices(packed_ref[...].astype(jnp.float32)).astype(jnp.bfloat16)
    far_ref[...] = matrices
    physics.take_far(matrices, keep_ref, spread_ref, far_group_ref)

    def stages(at, here_at, _):
        far = yield from physics.far_products([state_ref[k, at] for k in range(PARTS)])
        tends = physics.merged([part_ref[k, here_at] for k in range(PARTS)], far)
        start = [start_ref[k, here_at] for k in range(PARTS)]
        prev = [prev_ref[k, at].astype(jnp.float32) for k in range(PARTS)]
        physics.finish(start, prev, tends, here_at, tend_ref, ahead_ref, off_ref, on_ref)

    in_turns(first, count, stages, True)


def physics_kernel(
    first,
    count,
    state_ref,
    prev_ref,
    wind_ref,
    target_ref,
    slope_ref,
    slot_ref,
    own_ref,
    far_ref,
    keep_ref,
    spread_ref,
    far_group_ref,
    tend_ref,
    ahead_ref,
    off_ref,
    on_ref,
):
    physics = Physics(slot_ref)
    physics.take_own(own_ref)
    physics.take_far(far_ref[...], keep_ref, spread_ref, far_group_ref)
    physics.begin(wind_ref, target_ref, slope_ref)

    def stages(at, here_at, _):
        pairs = [state_ref[k, at] for k in range(PARTS)]
        far, own, start = yield from mixed(
            physics.far_products(pairs),
            physics.own_products(pairs),
            physics.start(flat(state_ref[:, at]), flat(prev_ref[:, at])),
        )
        start = [start[k * CHUNK : (k + 1) * CHUNK] for k in range(PARTS)]
        tends = physics.merged(own, far)
        prev = [prev_ref[k, at].astype(jnp.float32) for k in range(PARTS)]
        physics.finish(start, prev, tends, here_at, tend_ref, ahead_ref, off_ref, on_ref)

    in_turns(first, count, stages, True)


def near_kernel(
    state_ref,
    wind_ref,
    target_ref,
    slope_ref,
    off_ref,
    on_ref,
    prev_ref,
    *rest,
):
    parts, outs = rest[:-8], rest[-8:]
    own_ref, near_ref, near_add_ref, own_force_ref, near_force_ref, sum_ref, edge_sum_ref, blow_ref = outs
    lev = wind_ref.shape[1]
    slots, _ = point_sets()
    chosen = sides()
    end = off_ref.shape[1]

    def extra(ref, k):
        return ref[k, end - 64 : end].astype(jnp.float32)

    def winds(ref):
        whole = jnp.concatenate([extra(ref, k)[:48] for k in range(3)], axis=0)
        return whole[:lev], whole[lev:]

    def targets(ref):
        return extra(ref, 0)[48:56].astype(jnp.int32) - 32

    own_t = target_ref[...].astype(jnp.int32) - 32
    near_t = jnp.where(chosen, targets(off_ref), targets(on_ref))
    near_t = near_t + jnp.where(lane_ids() < 64, LANES, -LANES)
    own_sums = jnp.concatenate(
        [sum_block("own", own_t, slots, True), sum_block("own", near_t, slots, False)], axis=1
    )
    near_sums = jnp.concatenate(
        [sum_block("near", own_t, slots, False), sum_block("near", near_t, slots, True)], axis=1
    )
    sum_ref[:LANES] = own_sums
    sum_ref[LANES:] = near_sums
    nothing = jnp.zeros((LANES, LANES), jnp.bfloat16)
    for k, turn in enumerate(("", " turned")):
        edge_sum_ref[k, :LANES] = near_sums
        edge_sum_ref[k, LANES:, :LANES] = nothing
        edge_sum_ref[k, LANES:, LANES:] = sum_block("outer" + turn, near_t, slots, False)
        edge_sum_ref[2 + k, :LANES, :LANES] = own_sums[:, :LANES]
        edge_sum_ref[2 + k, LANES:, :LANES] = sum_block("near" + turn, own_t, slots, False)
    inner = inner_lanes()
    off_w, on_w = winds(off_ref), winds(on_ref)
    for d in range(2):
        blow_ref[0, d] = -time_step * wind_ref[d]
        near_w = -time_step * jnp.where(chosen, off_w[d], on_w[d])
        outer_w = -time_step * jnp.where(chosen, on_w[d], off_w[d])
        blow_ref[1, d] = near_w
        blow_ref[2, d] = jnp.where(inner, outer_w, pltpu.roll(outer_w, 64, 1))
        blow_ref[3, d] = jnp.where(inner, pltpu.roll(near_w, 64, 1), near_w)

    slope = slope_ref[...]
    early = time_step * hermite(0)[0]
    early_1, late_1 = (time_step * w for w in hermite(1))
    early_2, late_2 = (time_step * w for w in hermite(2))
    own_blow = (blow_ref[0, 0], blow_ref[0, 1])
    near_blow = (blow_ref[1, 0], blow_ref[1, 1])

    def stages(at, here_at, tend_ref, ahead_ref):
        off, on = off_ref[:, at].astype(jnp.float32), on_ref[:, at].astype(jnp.float32)
        near = whole_halves(off[:2], on[:2], chosen)
        own_move = moved(flat(state_ref[:, at]), slope, *own_blow)
        near_move = moved(near, slope, *near_blow)
        yield
        total = jnp.dot(near_move, near_sums, preferred_element_type=jnp.float32)
        near_total = total[:, LANES:] + jnp.dot(
            own_move, own_sums[:, LANES:], preferred_element_type=jnp.float32
        )
        kept = [jnp.where(chosen, off[2], on[2])]
        for k in range(1, PARTS):
            turned = [pltpu.roll(side[2], LANES - 32 * k, 1) for side in (off, on)]
            kept.append(jnp.where(chosen, *turned))
        kept = jnp.where(inner, 0.0, jnp.concatenate(kept, axis=0))
        near = near + near_total + early * kept
        near_ref[:, at] = near.reshape(PARTS, CHUNK, LANES)
        near_force_ref[:, at] = (early_2 * kept).reshape(PARTS, CHUNK, LANES)
        own = flat(ahead_ref[:, here_at]) + total[:, :LANES]
        yield
        own_move = moved(own, slope, *own_blow)
        yield
        total = jnp.dot(own_move, own_sums, preferred_element_type=jnp.float32)
        own_prev, own_tend = flat(prev_ref[:, at]), flat(tend_ref[:, here_at])
        own = own + total[:, :LANES] + (early_1 * own_prev + late_1 * own_tend)
        own_ref[:, at] = own.reshape(PARTS, CHUNK, LANES)
        own_force = early_2 * own_prev + late_2 * own_tend
        own_force_ref[:, at] = own_force.reshape(PARTS, CHUNK, LANES)
        near_add = total[:, LANES:] + early_1 * kept
        near_add_ref[:, at] = near_add.reshape(PARTS, CHUNK, LANES)

    places = []
    for tend_ref, ahead_ref in zip(parts[::2], parts[1::2]):
        places += [(here_at, tend_ref, ahead_ref) for here_at in chunks(tend_ref)]
    in_turns(0, len(places), lambda at, _, j: stages(at, *places[j]))


def advance_kernel(
    first,
    last,
    own_ref,
    near_ref,
    near_add_ref,
    own_force_ref,
    near_force_ref,
    off_ref,
    on_ref,
    slope_ref,
    sum_ref,
    edge_sum_ref,
    blow_ref,
    *rest,
):
    if last:
        tend_ref, done_ref, out_hbm, out_ref, sems = rest
        copies = [pltpu.make_async_copy(done_ref, out_hbm.at[:, pl.ds(0, done_ref.shape[1])], sems.at[0])]
    else:
        *tend_refs, out_ref, tend_hbm, sems = rest
        tend_ref = tend_refs[0]
        copies, row = [], 0
        for k, ref in enumerate(tend_refs):
            copies.append(pltpu.make_async_copy(ref, tend_hbm.at[:, pl.ds(row, ref.shape[1])], sems.at[k]))
            row += ref.shape[1]
    for copy in copies:
        copy.start()
    inner = inner_lanes()
    chosen = sides()
    slope = slope_ref[...]
    lates = [time_step * hermite(s)[1] for s in range(SUBSTEPS)]

    def advect(value, unit):
        return moved(value, slope, blow_ref[unit, 0], blow_ref[unit, 1])

    def gather(pieces, matrix):
        return jnp.dot(jnp.concatenate(pieces, axis=1), matrix, preferred_element_type=jnp.float32)

    def gather_shared(whole, packed, which, width):
        half = packed.shape[0]
        parts = [
            gather([whole[k * half : (k + 1) * half], packed], edge_sum_ref[which + k, :, :width])
            for k in range(2)
        ]
        return jnp.concatenate(parts, axis=0)

    def stages(at, here_at, j):
        off, on = off_ref[:, here_at].astype(jnp.float32), on_ref[:, here_at].astype(jnp.float32)
        off_mid, on_mid = flat(off[:2]), flat(on[:2])
        middle = [jnp.where(chosen, off_mid, on_mid), jnp.where(chosen, on_mid, off_mid)]
        middle = jnp.concatenate([middle[0], pltpu.roll(middle[1], 64, 1)], axis=0)
        outer = jnp.where(chosen == inner, on_mid, off_mid)
        received = whole_halves(off[2:], on[2:], chosen)
        near = jnp.where(inner, middle, flat(near_ref[:, at]) + lates[0] * received)
        moves = advect(near, 1), advect(outer, 2)
        yield
        total = gather_shared(*moves, 0, 2 * LANES)
        own = flat(own_ref[:, at]) + total[:, :LANES]
        force = received * jnp.where(inner, 1.0, lates[1])
        near = near + total[:, LANES:] + (flat(near_add_ref[:, at]) + force)
        yield
        moves = [advect(own, 0), advect(near, 1)]
        yield
        total = gather(moves, sum_ref[...])
        own = own + total[:, :LANES] + flat(own_force_ref[:, at])
        near = near + total[:, LANES:] + (flat(near_force_ref[:, at]) + lates[2] * received)
        yield
        half = near.shape[0] // 2
        near = jnp.where(inner, pltpu.roll(near[half:], 64, 1), near[:half])
        moves = advect(own, 0), advect(near, 3)
        yield
        total = gather_shared(*moves, 2, LANES)
        out = own + total + lates[3] * flat(tend_ref[:, here_at])
        out_ref[:, here_at] = out.reshape(PARTS, CHUNK, LANES)
        if last:
            for k in range(PARTS):
                copies.append(
                    pltpu.make_async_copy(
                        out_ref.at[k, here_at], out_hbm.at[k, at], sems.at[1 + PARTS * j + k]
                    )
                )
                copies[-1].start()

    in_turns(first, out_ref.shape[1] // CHUNK, stages, last)
    for copy in copies:
        copy.wait()


def exchanged(off, on):
    count = lax.axis_size(AXES)
    across = [(i, (i + 1) % count if i % 2 else (i - 1) % count) for i in range(count)]
    inside = [(i, i ^ 1) for i in range(count)]
    on = lax.ppermute(on, AXES, inside)
    return lax.ppermute(off, AXES, across), on


def per_device(state, prev_tendency, wind, edge_links, swap_slot, inverse):
    devices = lax.axis_size(AXES)
    shape = state.shape
    lev = shape[1]
    rows = shape[0] * lev // PARTS
    params = pltpu.CompilerParams(vmem_limit_bytes=VMEM)
    bf16, f32 = jnp.bfloat16, jnp.float32
    inner = pl.BlockSpec(memory_space=pltpu.VMEM)
    outer = pl.BlockSpec(memory_space=pltpu.HBM)

    def like(count, kind, length=rows):
        return pltpu.VMEM((count, length, LANES), kind)

    def table(kind, *size):
        return pltpu.VMEM(size, kind)

    def call(body, ins, outs, name, passes, **more):
        size = sum(math.prod(array.shape) * array.dtype.itemsize for array in ins)
        cost = pl.CostEstimate(
            flops=passes * 2 * PARTS * rows * 256 * 256, bytes_accessed=2 * size, transcendentals=0
        )
        more = {"in_specs": [inner] * len(ins), "out_specs": (inner,) * len(outs)} | more
        return pl.pallas_call(
            body, out_shape=outs, compiler_params=params, cost_estimate=cost, name=name, **more
        )(*ins)

    slot = swap_slot.reshape(1, LANES)
    slope = jnp.asarray(derivative_matrix())
    message = like(3, bf16, rows + 64)
    inputs = (
        inverse,
        wind,
        edge_links,
        state.reshape(PARTS, rows, LANES),
        prev_tendency.reshape(PARTS, rows, LANES),
    )
    inputs = tuple(pltpu.with_memory_space_constraint(array, pltpu.HBM) for array in inputs)
    matrices, packed, to_off, to_on, targets, wind, state, prev = call(
        pack_kernel,
        inputs,
        (
            table(bf16, inverse.shape[0] * lev, LANES),
            table(bf16, 368, LANES),
            message,
            message,
            table(f32, 8, LANES),
            table(f32, *wind.shape),
            like(4, f32),
            like(4, bf16),
        ),
        "pack",
        2,
        in_specs=[outer] * len(inputs),
        scratch_shapes=[
            pltpu.VMEM(inverse.shape, f32),
            pltpu.VMEM(edge_links.shape, jnp.int32),
            pltpu.SemaphoreType.DMA((3 + 2 * (rows // CHUNK),)),
        ],
    )
    far_packed = lax.ppermute(packed, AXES, [(i, i ^ (devices // 2)) for i in range(devices)])
    off, on = exchanged(to_off, to_on)
    halves = []
    first = 0
    shared = (wind, targets, slope, slot, matrices)
    for count in SPLIT:
        size = count * CHUNK
        outs = (like(4, bf16, size), like(4, f32, size), like(4, bf16, size), like(4, bf16, size))
        if first == 0:
            part, start, *tables = call(
                functools.partial(own_kernel, first, count),
                (state, prev) + shared,
                (like(4, f32, size), like(4, f32, size))
                + (table(bf16, 2 * LANES, LANES), table(bf16, LANES, 2 * LANES), table(f32, 8, LANES)),
                "own",
                3 * count,
            )
            ins = (state, prev, slot, far_packed, *tables, part, start)
            body, name = far_kernel, "far"
            outs += (table(bf16, *matrices.shape),)
        else:
            ins = (state, prev) + shared + (far_matrices, *tables)
            body, name = physics_kernel, "physics"
        tend, ahead, to_off, to_on, *more = call(
            functools.partial(body, first, count), ins, outs, name, 5 * count
        )
        far_matrices = more[0] if more else far_matrices
        halves.append((first, count, tend, ahead, exchanged(to_off, to_on)))
        first += count
    parts = sum(((tend, ahead) for _, _, tend, ahead, _ in halves), ())
    own, near, near_add, own_force, near_force, sums, edge_sums, blow = call(
        near_kernel,
        (state, wind, targets, slope, off, on, prev) + parts,
        (
            like(4, f32),
            like(4, f32),
            like(4, f32),
            like(4, f32),
            like(4, f32),
            table(bf16, 2 * LANES, 2 * LANES),
            table(bf16, 4, 2 * LANES, 2 * LANES),
            table(f32, 4, 2, lev, LANES),
        ),
        "near",
        16,
    )
    tends = tuple(tend for _, _, tend, _, _ in halves)
    out_spec = jax.ShapeDtypeStruct((PARTS, rows, LANES), f32)
    tend_spec = jax.ShapeDtypeStruct((PARTS, rows, LANES), bf16)
    for part, (first, count, tend, _, (off, on)) in enumerate(halves):
        ins = (own, near, near_add, own_force, near_force, off, on, slope, sums, edge_sums, blow)
        size = count * CHUNK
        if part == 0:
            done, tend_out = call(
                functools.partial(advance_kernel, first, False),
                ins + tends,
                (like(4, f32, size), tend_spec),
                "advance",
                5 * count,
                out_specs=(inner, outer),
                scratch_shapes=[pltpu.SemaphoreType.DMA((len(tends),))],
            )
        else:
            (out,) = call(
                functools.partial(advance_kernel, first, True),
                ins + (tend, done),
                (out_spec,),
                "advance",
                5 * count,
                out_specs=(outer,),
                scratch_shapes=[pltpu.VMEM((PARTS, size, LANES), f32), pltpu.SemaphoreType.DMA((1 + PARTS * count,))],
            )
    tend = tend_out
    return (out.reshape(shape), tend.reshape(shape))


def solution(mesh):
    columns = P(None, None, AXES)
    return jax.shard_map(
        per_device,
        mesh=mesh,
        in_specs=(columns, columns, columns, columns, P(AXES), P(AXES, None, None)),
        out_specs=(columns, columns),
        check_vma=False,
    )
```

```python
import functools
import math

import jax
import jax.numpy as jnp
import numpy as np
from jax import lax
from jax.experimental import pallas as pl
from jax.experimental.pallas import tpu as pltpu
from jax.sharding import PartitionSpec as P

SUBSTEPS = 4
AXES = ("gx", "gy")
LANES = 128
CHUNK = 144
SPLIT = (3, 2)
PARTS = 4
VMEM = 16 * 1024 * 1024

time_step = 0.2
edge_points = ((0, 1, 2, 3), (3, 7, 11, 15), (15, 14, 13, 12), (12, 8, 4, 0))


def point_tables():
    edge_of = np.zeros((2, 16), np.int32)
    spot_of = np.zeros((2, 16), np.int32)
    weight_of = np.zeros((2, 16), np.float32)
    filled = np.zeros(16, np.int32)
    for k in range(4):
        for m in range(4):
            p = edge_points[k][m]
            s = filled[p]
            edge_of[s, p] = k
            spot_of[s, p] = m
            weight_of[s, p] = 1.0
            filled[p] = s + 1
    return (edge_of, spot_of, weight_of)


def gll_derivative():
    gll_nodes = np.array([-1.0, -1.0 / np.sqrt(5.0), 1.0 / np.sqrt(5.0), 1.0])
    factors = np.array(
        [np.prod([gll_nodes[i] - gll_nodes[k] for k in range(4) if k != i]) for i in range(4)]
    )
    derivative = np.zeros((4, 4))
    for i in range(4):
        for k in range(4):
            if i != k:
                derivative[i, k] = factors[i] / (factors[k] * (gll_nodes[i] - gll_nodes[k]))
            else:
                derivative[i, k] = sum(
                    (1.0 / (gll_nodes[i] - gll_nodes[j]) for j in range(4) if j != i)
                )
    return derivative


def derivative_matrix():
    derivative = gll_derivative()
    eye_block = np.eye(8)
    both = np.concatenate(
        [
            np.kron(eye_block, np.kron(derivative, np.eye(4)).T),
            np.kron(eye_block, np.kron(np.eye(4), derivative).T),
        ],
        axis=1,
    )
    high = both.astype(jnp.bfloat16)
    low = (both - high.astype(np.float64)).astype(jnp.bfloat16)
    return np.concatenate([high, low], axis=0)


def hermite(substep):
    instant = (substep + 1.0) / SUBSTEPS
    square = instant * instant
    cube = square * instant
    h00 = 2.0 * cube - 3.0 * square + 1.0
    h01 = -2.0 * cube + 3.0 * square
    slope = cube - 2.0 * square + instant + (cube - square)
    return (h00 - slope, h01 + slope)


def lane_ids(rows=1):
    return lax.broadcasted_iota(jnp.int32, (rows, LANES), 1)


def point_sets():
    point = lane_ids() % 16
    across = (point // 4 == 0) | (point // 4 == 3)
    along = (point % 4 == 0) | (point % 4 == 3)
    slots = (across | along, across & along)
    share = jnp.where(slots[1], 1.0 / 3.0, jnp.where(slots[0], 0.5, 1.0)).astype(jnp.float32)
    return slots, share


def edge_targets(links_ref, first_elem, element_count):
    edge_of, spot_of, _ = point_tables()
    elements = links_ref.shape[2]
    own = first_elem + lax.broadcasted_iota(jnp.int32, (4, elements), 1)
    apart = links_ref[0] - own
    half = element_count // 2
    apart = jnp.where(apart > half, apart - element_count, apart)
    apart = jnp.where(apart < -half, apart + element_count, apart) + 2
    both = jnp.concatenate([apart, links_ref[1]], axis=0).astype(jnp.float32)
    spread = lax.broadcasted_iota(jnp.int32, (elements, LANES), 0)
    spread = (spread == lax.broadcasted_iota(jnp.int32, (elements, LANES), 1) // 16).astype(jnp.float32)
    both = jnp.dot(both, spread, preferred_element_type=jnp.float32)
    both = (both + 0.5).astype(jnp.int32)
    lane = lane_ids()
    point = lane % 16
    rows = []
    for s in range(2):
        edge = jnp.zeros((1, LANES), jnp.int32)
        spot = edge
        for p in range(16):
            edge = jnp.where(point == p, int(edge_of[s, p]), edge)
            spot = jnp.where(point == p, int(spot_of[s, p]), spot)
        away, far = both[0:1], both[4:5]
        for k in range(1, 4):
            away = jnp.where(edge == k, both[k : k + 1], away)
            far = jnp.where(edge == k, both[4 + k : 5 + k], far)
        place = jnp.where(far == 2, 12 + spot, 4 * spot)
        place = jnp.where(far == 1, 15 - 4 * spot, place)
        place = jnp.where(far == 0, 3 - spot, place)
        rows.append(lane - point + 16 * away + place)
    rows = jnp.concatenate(rows + [jnp.zeros((6, LANES), jnp.int32)], axis=0)
    return rows.astype(jnp.float32)


def on_odd():
    return lax.axis_index(AXES) % 2 == 1


def sides():
    return (lane_ids() < 64) == on_odd()


def packed_halves(value, chosen):
    away = [pltpu.roll(value[k + 2], 64, 1) for k in range(2)]
    off = [jnp.where(chosen, away[k], value[k]) for k in range(2)]
    on = [jnp.where(chosen, value[k], away[k]) for k in range(2)]
    return off, on


def whole_halves(off, on, chosen):
    count, rows = off.shape[0], off.shape[1]
    direct = jnp.where(chosen, off, on).reshape(count * rows, LANES)
    turned = jnp.where(chosen, on, off).reshape(count * rows, LANES)
    return jnp.concatenate([direct, pltpu.roll(turned, 64, 1)], axis=0)


def mixed(*generators):
    values = {}
    while len(values) < len(generators):
        for i, one in enumerate(generators):
            if i not in values:
                try:
                    next(one)
                except StopIteration as end:
                    values[i] = end.value
        yield
    return [values[i] for i in range(len(generators))]


def packed_quarters(value, first_off, first_on):
    quarter = lane_ids() // 32
    to_off = to_on = jnp.zeros(value[0].shape, jnp.float32)
    for k, turned in enumerate(value):
        turned = pltpu.roll(turned, 32 * k, 1) if k else turned
        to_off = jnp.where(quarter == (first_off + k) % 4, turned, to_off)
        to_on = jnp.where(quarter == (first_on + k) % 4, turned, to_on)
    return to_off, to_on


def whole_quarters(off, on, chosen):
    kept = [jnp.where(chosen, off, on)]
    for k in range(1, PARTS):
        turned = [pltpu.roll(side, LANES - 32 * k, 1) for side in (off, on)]
        kept.append(jnp.where(chosen, *turned))
    return jnp.concatenate(kept, axis=0)


def packed_matrices(matrix):
    lane = lane_ids()
    half = len(matrix) // 2
    rows = [jnp.where(lane < 64, matrix[c], pltpu.roll(matrix[c + half], 64, 1)) for c in range(half)]
    rest = jnp.zeros_like(matrix[0])
    for c, value in enumerate(matrix):
        rest = jnp.where(lane // 8 == c, pltpu.roll(value, (8 * c - 64) % LANES, 1), rest)
    return jnp.concatenate(rows + [rest, jnp.zeros((8, LANES), jnp.float32)], axis=0)


def unpacked_matrices(packed):
    lane = lane_ids()
    lev, half = 72, 4
    rest = packed[half * lev : (half + 1) * lev]
    rows = []
    for c in range(2 * half):
        main = packed[c % half * lev : (c % half + 1) * lev]
        main = main if c < half else pltpu.roll(main, 64, 1)
        tail = jnp.where(lane < lev, pltpu.roll(rest, (64 - 8 * c) % LANES, 1), 0.0)
        rows.append(jnp.where(lane < 64, main, tail))
    return jnp.concatenate(rows, axis=0)


def leaving_tables(slot_ref, keep_ref, spread_ref, far_group_ref):
    slot = slot_ref[...]
    leaving = slot // LANES != lax.axis_index(AXES)
    row = lax.broadcasted_iota(jnp.int32, (LANES, LANES), 0)
    col = lax.broadcasted_iota(jnp.int32, (LANES, LANES), 1)
    ones = jnp.broadcast_to(leaving, (8, LANES)).astype(jnp.float32)
    rank = jnp.dot(ones, (row <= col).astype(jnp.float32), preferred_element_type=jnp.float32)
    yield
    rank = (rank[0:1] + 0.5).astype(jnp.int32) - 1
    spread = [(leaving & (rank + 64 * k == row)).astype(jnp.float32) for k in range(2)]
    yield
    keep = [jnp.transpose(half) for half in spread]
    yield
    for k in range(2):
        spread_ref[:, k * LANES : (k + 1) * LANES] = spread[k].astype(jnp.bfloat16)
        keep_ref[k * LANES : (k + 1) * LANES] = keep[k].astype(jnp.bfloat16)
    group = jnp.broadcast_to(slot % LANES // 16, (8, LANES)).astype(jnp.float32)
    far_group_ref[...] = jnp.dot(group, keep[0] + keep[1], preferred_element_type=jnp.float32)


def pack_kernel(
    inverse_hbm,
    wind_hbm,
    links_hbm,
    state_hbm,
    prev_hbm,
    matrix_ref,
    packed_ref,
    off_ref,
    on_ref,
    target_ref,
    wind_ref,
    state_ref,
    prev_ref,
    inverse_ref,
    links_ref,
    sems,
):
    pairs = [(links_hbm, links_ref), (inverse_hbm, inverse_ref), (wind_hbm, wind_ref)]
    for at in chunks(state_ref):
        pairs += [(state_hbm.at[:, at], state_ref.at[:, at]), (prev_hbm.at[:, at], prev_ref.at[:, at])]
    copies = [pltpu.make_async_copy(a, b, sems.at[i]) for i, (a, b) in enumerate(pairs)]
    for copy in copies:
        copy.start()
    copies[0].wait()
    devices = lax.axis_size(AXES)
    elements = links_ref.shape[2]
    targets = edge_targets(links_ref, lax.axis_index(AXES) * elements, elements * devices)
    groups, lev = inverse_ref.shape[0], inverse_ref.shape[1]
    copies[1].wait()
    eye = lax.broadcasted_iota(jnp.int32, (lev, lev), 0) == lax.broadcasted_iota(jnp.int32, (lev, lev), 1)
    eye = eye.astype(jnp.float32)
    blank = jnp.zeros((lev, LANES - lev), jnp.float32)
    matrix = [jnp.concatenate([inverse_ref[c] - eye, blank], axis=1) for c in range(groups)]
    matrix_ref[...] = jnp.concatenate(matrix, axis=0).astype(jnp.bfloat16)
    packed_ref[...] = packed_matrices(matrix).astype(jnp.bfloat16)
    copies[2].wait()
    target_ref[...] = targets
    end = off_ref.shape[1]
    filler = jnp.zeros((8, LANES), jnp.float32)
    flat_wind = wind_ref[...].reshape(2 * lev, LANES)
    for k in range(3):
        piece = jnp.concatenate([flat_wind[48 * k : 48 * k + 48], targets, filler], axis=0)
        piece = piece.astype(jnp.bfloat16)
        off_ref[k, end - 64 : end] = piece
        on_ref[k, end - 64 : end] = piece
    chosen = sides()
    odd = jnp.where(on_odd(), 3, 0)
    quarter = lane_ids() // 32
    for j, at in enumerate(chunks(state_ref)):
        copies[3 + 2 * j].wait()
        copies[4 + 2 * j].wait()
        off, on = packed_halves([state_ref[k, at] for k in range(PARTS)], chosen)
        for k in range(2):
            off_ref[k, at] = off[k].astype(jnp.bfloat16)
            on_ref[k, at] = on[k].astype(jnp.bfloat16)
        to_off = jnp.zeros((CHUNK, LANES), jnp.float32)
        to_on = to_off
        for k in range(PARTS):
            turned = prev_ref[k, at].astype(jnp.float32)
            turned = pltpu.roll(turned, 32 * k, 1) if k else turned
            to_off = jnp.where(quarter == (odd + k) % 4, turned, to_off)
            to_on = jnp.where(quarter == (3 - odd + k) % 4, turned, to_on)
        off_ref[2, at] = to_off.astype(jnp.bfloat16)
        on_ref[2, at] = to_on.astype(jnp.bfloat16)


def chunks(ref):
    return [pl.ds(start, CHUNK) for start in range(0, ref.shape[1], CHUNK)]


def in_turns(first, count, stages, together=False):
    running = []
    for j in range(count):
        running.append(stages(pl.ds((first + j) * CHUNK, CHUNK), pl.ds(j * CHUNK, CHUNK), j))
    waiting, started = list(running), []
    while waiting or started:
        while waiting:
            started.append(waiting.pop(0))
            if not together:
                break
        started = [one for one in started if next(one, started) is not started]


def column_pair(pair):
    lev = pair.shape[0] // 2
    blank = jnp.zeros((LANES - lev, 2 * LANES), jnp.float32)
    pair = jnp.concatenate([pair[:lev], pair[lev:]], axis=1)
    high = pair.astype(jnp.bfloat16).astype(jnp.float32)
    return jnp.concatenate([high, blank, pair - high, blank], axis=0).astype(jnp.bfloat16)


def chosen_rows(product, group, chosen=None, first=0):
    lev = 72
    for c in range(product.shape[0] // lev):
        part = product[c * lev : (c + 1) * lev]
        chosen = part if chosen is None else jnp.where(group == first + c, part, chosen)
    return chosen


def as_rows(pair):
    return jnp.concatenate([pair[:, :LANES], pair[:, LANES:]], axis=0)


def column_group(slot_ref):
    slot = slot_ref[...]
    return jnp.where(slot // LANES == lax.axis_index(AXES), 0, 8) + slot % LANES // 16


def flat(value):
    return value.astype(jnp.float32).reshape(-1, LANES)


def moved(value, slope, blow_x, blow_y):
    rows, lev = value.shape[0], blow_x.shape[0]
    value = value.astype(jnp.bfloat16)
    both = jnp.dot(jnp.concatenate([value, value], axis=1), slope, preferred_element_type=jnp.float32)
    both = both.reshape(rows // lev, lev, 2 * LANES)
    motion = both[..., :LANES] * blow_x + both[..., LANES:] * blow_y
    return motion.reshape(rows, LANES).astype(jnp.bfloat16)


def sum_block(source, targets, slots, own):
    row = lax.broadcasted_iota(jnp.int32, (LANES, LANES), 0)
    total = jnp.zeros((LANES, LANES), jnp.float32)
    if own:
        total = (row == lax.broadcasted_iota(jnp.int32, (LANES, LANES), 1)).astype(jnp.float32)
    place = {
        "own": row,
        "own turned": jnp.where(row < 64, row + 64, row - 64),
        "near": jnp.where(row < 64, row + LANES, row - LANES),
        "near turned": jnp.where(row < 64, row - 64, row + 64),
        "outer": jnp.where(row < 64, row - LANES, row + LANES),
        "outer turned": jnp.where(row < 64, row + LANES + 64, row - LANES - 64),
    }[source]
    for s in range(2):
        total = total + ((place == targets[s : s + 1]) & slots[s]).astype(jnp.float32)
    return (total * point_sets()[1]).astype(jnp.bfloat16)


def inner_lanes():
    quarter = lane_ids() // 32
    return (quarter == 1) | (quarter == 2)


class Physics:
    def __init__(self, slot_ref):
        group = column_group(slot_ref)
        self.here = group < 8
        self.group = jnp.concatenate([group, group], axis=1)
        self.inner = inner_lanes()
        self.chosen = sides()

    def take_own(self, own_ref):
        self.own = jnp.concatenate([own_ref[...], own_ref[...]], axis=1)

    def take_far(self, far, keep_ref, spread_ref, far_group_ref):
        self.far = far
        self.keep, self.spread = keep_ref[...], spread_ref[...]
        group = (far_group_ref[0:1, :] + 0.5).astype(jnp.int32)
        self.far_group = jnp.concatenate([group, group], axis=1)

    def begin(self, wind_ref, target_ref, slope_ref):
        slots, _ = point_sets()
        self.sums = sum_block("own", target_ref[...].astype(jnp.int32) - 32, slots, True)
        self.blow = [-time_step * wind_ref[d] for d in range(2)]
        self.slope = slope_ref[...]
        self.targets, self.slots = target_ref[...].astype(jnp.int32) - 32, slots

    def begin_cross(self):
        row = lax.broadcasted_iota(jnp.int32, (LANES, LANES), 0)
        col = lax.broadcasted_iota(jnp.int32, (LANES, LANES), 1) // 32
        blocks = []
        for turn in (0, 64):
            place = (row + turn) % LANES // 32
            crossing = ((place == 1) & (col == 2)) | ((place == 2) & (col == 1))
            block = sum_block("own turned" if turn else "own", self.targets, self.slots, False)
            blocks.append(jnp.where(crossing, block.astype(jnp.float32), 0.0).astype(jnp.bfloat16))
        self.cross = jnp.concatenate(blocks, axis=1)
        self.cross_blow = [jnp.where(self.inner, w, pltpu.roll(w, 64, 1)) for w in self.blow]

    def motion(self, state):
        return moved(state, self.slope, *self.blow)

    def start(self, state, prev):
        motion = self.motion(state)
        yield
        total = jnp.dot(motion, self.sums, preferred_element_type=jnp.float32)
        return state + total + time_step * hermite(0)[0] * prev

    def own_products(self, pairs):
        ahead, rows = None, []
        for k, pair in enumerate(pairs):
            product = jnp.dot(self.own, column_pair(pair), preferred_element_type=jnp.float32)
            if k:
                rows.append(as_rows(chosen_rows(ahead, self.group)))
            ahead = product
            yield
        rows.append(as_rows(chosen_rows(ahead, self.group)))
        return rows

    def far_products(self, pairs):
        high = [pair.astype(jnp.bfloat16) for pair in pairs]
        both = [jnp.concatenate(high[k : k + 2], axis=1) for k in (0, 2)]
        few = jnp.dot(jnp.concatenate(both, axis=0), self.keep, preferred_element_type=jnp.float32)
        yield
        size = pairs[0].shape[0]
        lev = size // 2
        blank = jnp.zeros((LANES - lev, 2 * LANES), jnp.float32)
        products, rows = [], []
        for k in range(2):
            part = few[k * size : (k + 1) * size]
            part = jnp.concatenate([part[:lev], part[lev:]], axis=1)
            column = jnp.concatenate([part, blank], axis=0).astype(jnp.bfloat16)
            products.append(jnp.dot(self.far, column, preferred_element_type=jnp.float32))
            yield
        for k in range(2):
            rows.append(as_rows(chosen_rows(products[k], self.far_group)))
        rows = jnp.concatenate(rows, axis=0).astype(jnp.bfloat16)
        wide = jnp.dot(rows, self.spread, preferred_element_type=jnp.float32)
        yield
        return [wide[k * size : (k + 1) * size, c : c + LANES] for k in range(2) for c in (0, LANES)]

    def merged(self, own, far):
        return [jnp.where(self.here, a, b) for a, b in zip(own, far)]

    def finish(self, start, prev, tends, here_at, tend_ref, ahead_ref, off_ref, on_ref, lean=False):
        late = time_step * hermite(0)[1]
        early_1, late_1 = (time_step * w for w in hermite(1))
        ahead, force = [], []
        for k, tend in enumerate(tends):
            tend = tend.astype(jnp.bfloat16)
            tend_ref[k, here_at] = tend
            tend = tend.astype(jnp.float32)
            ahead.append(start[k] + late * tend)
            ahead_ref[k, here_at] = ahead[k]
            force.append(jnp.where(self.inner, early_1 * prev[k] + late_1 * tend, tend))
        middle = [jnp.where(self.inner, ahead[k], pltpu.roll(ahead[k + 2], 64, 1)) for k in range(2)]
        if lean:
            motion = moved(jnp.concatenate(middle, axis=0), self.slope, *self.cross_blow)
            yield
            cross = jnp.dot(motion, self.cross, preferred_element_type=jnp.float32)
            yield
            for k in range(PARTS):
                rows = slice(k % 2 * CHUNK, (k % 2 + 1) * CHUNK)
                force[k] = force[k] + cross[rows, k // 2 * LANES : (k // 2 + 1) * LANES]
            to_off, to_on = packed_quarters(ahead, jnp.where(on_odd(), 2, 1), jnp.where(on_odd(), 1, 2))
            off_ref[0, here_at] = to_off.astype(jnp.bfloat16)
            on_ref[0, here_at] = to_on.astype(jnp.bfloat16)
        else:
            for k in range(2):
                off_ref[k, here_at] = middle[k].astype(jnp.bfloat16)
                on_ref[k, here_at] = middle[k].astype(jnp.bfloat16)
        off, on = packed_halves(force, self.chosen)
        at = off_ref.shape[0] - 2
        for k in range(2):
            off_ref[at + k, here_at] = off[k].astype(jnp.bfloat16)
            on_ref[at + k, here_at] = on[k].astype(jnp.bfloat16)


def own_kernel(
    first, count, state_ref, prev_ref, wind_ref, target_ref, slope_ref, slot_ref, own_ref, part_ref, start_ref, *tables
):
    physics = Physics(slot_ref)
    physics.take_own(own_ref)
    physics.begin(wind_ref, target_ref, slope_ref)

    def stages(at, here_at, j):
        parts, start, *_ = yield from mixed(
            physics.own_products([state_ref[k, at] for k in range(PARTS)]),
            physics.start(flat(state_ref[:, at]), flat(prev_ref[:, at])),
            *([leaving_tables(slot_ref, *tables)] if j == 0 else []),
        )
        start_ref[:, here_at] = start.reshape(PARTS, CHUNK, LANES)
        for k, part in enumerate(parts):
            part_ref[k, here_at] = part

    in_turns(first, count, stages, True)


def far_kernel(
    first,
    count,
    state_ref,
    prev_ref,
    slot_ref,
    packed_ref,
    keep_ref,
    spread_ref,
    far_group_ref,
    part_ref,
    start_ref,
    tend_ref,
    ahead_ref,
    off_ref,
    on_ref,
    far_ref,
):
    physics = Physics(slot_ref)
    matrices = unpacked_matrices(packed_ref[...].astype(jnp.float32)).astype(jnp.bfloat16)
    far_ref[...] = matrices
    physics.take_far(matrices, keep_ref, spread_ref, far_group_ref)

    def stages(at, here_at, _):
        far = yield from physics.far_products([state_ref[k, at] for k in range(PARTS)])
        tends = physics.merged([part_ref[k, here_at] for k in range(PARTS)], far)
        start = [start_ref[k, here_at] for k in range(PARTS)]
        prev = [prev_ref[k, at].astype(jnp.float32) for k in range(PARTS)]
        yield from physics.finish(start, prev, tends, here_at, tend_ref, ahead_ref, off_ref, on_ref)

    in_turns(first, count, stages, True)


def physics_kernel(
    first,
    count,
    state_ref,
    prev_ref,
    wind_ref,
    target_ref,
    slope_ref,
    slot_ref,
    own_ref,
    far_ref,
    keep_ref,
    spread_ref,
    far_group_ref,
    tend_ref,
    ahead_ref,
    off_ref,
    on_ref,
):
    physics = Physics(slot_ref)
    physics.take_own(own_ref)
    physics.take_far(far_ref[...], keep_ref, spread_ref, far_group_ref)
    physics.begin(wind_ref, target_ref, slope_ref)
    physics.begin_cross()

    def stages(at, here_at, _):
        pairs = [state_ref[k, at] for k in range(PARTS)]
        far, own, start = yield from mixed(
            physics.far_products(pairs),
            physics.own_products(pairs),
            physics.start(flat(state_ref[:, at]), flat(prev_ref[:, at])),
        )
        start = [start[k * CHUNK : (k + 1) * CHUNK] for k in range(PARTS)]
        tends = physics.merged(own, far)
        prev = [prev_ref[k, at].astype(jnp.float32) for k in range(PARTS)]
        yield from physics.finish(start, prev, tends, here_at, tend_ref, ahead_ref, off_ref, on_ref, True)

    in_turns(first, count, stages, True)


def near_kernel(
    state_ref,
    wind_ref,
    target_ref,
    slope_ref,
    off_ref,
    on_ref,
    prev_ref,
    *rest,
):
    parts, outs = rest[:-8], rest[-8:]
    own_ref, near_ref, near_add_ref, own_force_ref, near_force_ref, sum_ref, edge_sum_ref, blow_ref = outs
    lev = wind_ref.shape[1]
    slots, _ = point_sets()
    chosen = sides()
    end = off_ref.shape[1]

    def extra(ref, k):
        return ref[k, end - 64 : end].astype(jnp.float32)

    def winds(ref):
        whole = jnp.concatenate([extra(ref, k)[:48] for k in range(3)], axis=0)
        return whole[:lev], whole[lev:]

    def targets(ref):
        return extra(ref, 0)[48:56].astype(jnp.int32) - 32

    own_t = target_ref[...].astype(jnp.int32) - 32
    near_t = jnp.where(chosen, targets(off_ref), targets(on_ref))
    near_t = near_t + jnp.where(lane_ids() < 64, LANES, -LANES)
    own_sums = jnp.concatenate(
        [sum_block("own", own_t, slots, True), sum_block("own", near_t, slots, False)], axis=1
    )
    near_sums = jnp.concatenate(
        [sum_block("near", own_t, slots, False), sum_block("near", near_t, slots, True)], axis=1
    )
    sum_ref[:LANES] = own_sums
    sum_ref[LANES:] = near_sums
    nothing = jnp.zeros((LANES, LANES), jnp.bfloat16)
    first_sums = jnp.concatenate([nothing, own_sums[:, LANES:]], axis=1)
    first_sums = jnp.concatenate([near_sums, first_sums], axis=0)
    for k, turn in enumerate(("", " turned")):
        edge_sum_ref[k, :LANES] = near_sums
        edge_sum_ref[k, LANES:, :LANES] = nothing
        edge_sum_ref[k, LANES:, LANES:] = sum_block("outer" + turn, near_t, slots, False)
        edge_sum_ref[2 + k, :LANES, :LANES] = own_sums[:, :LANES]
        edge_sum_ref[2 + k, LANES:, :LANES] = sum_block("near" + turn, own_t, slots, False)
    inner = inner_lanes()
    off_w, on_w = winds(off_ref), winds(on_ref)
    for d in range(2):
        blow_ref[0, d] = -time_step * wind_ref[d]
        near_w = -time_step * jnp.where(chosen, off_w[d], on_w[d])
        outer_w = -time_step * jnp.where(chosen, on_w[d], off_w[d])
        blow_ref[1, d] = near_w
        blow_ref[2, d] = jnp.where(inner, outer_w, pltpu.roll(outer_w, 64, 1))
        blow_ref[3, d] = jnp.where(inner, pltpu.roll(near_w, 64, 1), near_w)

    slope = slope_ref[...]
    early = time_step * hermite(0)[0]
    early_1, late_1 = (time_step * w for w in hermite(1))
    early_2, late_2 = (time_step * w for w in hermite(2))
    own_blow = (blow_ref[0, 0], blow_ref[0, 1])
    near_blow = (blow_ref[1, 0], blow_ref[1, 1])

    def stages(at, here_at, tend_ref, ahead_ref):
        off, on = off_ref[:, at].astype(jnp.float32), on_ref[:, at].astype(jnp.float32)
        near = whole_halves(off[:2], on[:2], chosen)
        own_move = moved(flat(state_ref[:, at]), slope, *own_blow)
        near_move = moved(near, slope, *near_blow)
        yield
        total = jnp.concatenate([near_move, own_move], axis=1)
        total = jnp.dot(total, first_sums, preferred_element_type=jnp.float32)
        near_total = total[:, LANES:]
        kept = jnp.where(inner, 0.0, whole_quarters(off[2], on[2], chosen))
        near = near + near_total + early * kept
        near_ref[:, at] = near.reshape(PARTS, CHUNK, LANES)
        near_force_ref[:, at] = (early_2 * kept).reshape(PARTS, CHUNK, LANES)
        own = flat(ahead_ref[:, here_at]) + total[:, :LANES]
        yield
        own_move = moved(own, slope, *own_blow)
        yield
        total = jnp.dot(own_move, own_sums, preferred_element_type=jnp.float32)
        own_prev, own_tend = flat(prev_ref[:, at]), flat(tend_ref[:, here_at])
        own = own + total[:, :LANES] + (early_1 * own_prev + late_1 * own_tend)
        own_ref[:, at] = own.reshape(PARTS, CHUNK, LANES)
        own_force = early_2 * own_prev + late_2 * own_tend
        own_force_ref[:, at] = own_force.reshape(PARTS, CHUNK, LANES)
        near_add = total[:, LANES:] + early_1 * kept
        near_add_ref[:, at] = near_add.reshape(PARTS, CHUNK, LANES)

    places = []
    for tend_ref, ahead_ref in zip(parts[::2], parts[1::2]):
        places += [(here_at, tend_ref, ahead_ref) for here_at in chunks(tend_ref)]
    in_turns(0, len(places), lambda at, _, j: stages(at, *places[j]))


def advance_kernel(
    first,
    last,
    own_ref,
    near_ref,
    near_add_ref,
    own_force_ref,
    near_force_ref,
    off_ref,
    on_ref,
    slope_ref,
    sum_ref,
    edge_sum_ref,
    blow_ref,
    *rest,
):
    if last:
        tend_ref, done_ref, out_hbm, out_ref, sems = rest
        copies = [pltpu.make_async_copy(done_ref, out_hbm.at[:, pl.ds(0, done_ref.shape[1])], sems.at[0])]
    else:
        *tend_refs, out_ref, tend_hbm, sems = rest
        tend_ref = tend_refs[0]
        copies, row = [], 0
        for k, ref in enumerate(tend_refs):
            copies.append(pltpu.make_async_copy(ref, tend_hbm.at[:, pl.ds(row, ref.shape[1])], sems.at[k]))
            row += ref.shape[1]
    for copy in copies:
        copy.start()
    inner = inner_lanes()
    chosen = sides()
    slope = slope_ref[...]
    lates = [time_step * hermite(s)[1] for s in range(SUBSTEPS)]

    def advect(value, unit):
        return moved(value, slope, blow_ref[unit, 0], blow_ref[unit, 1])

    def gather(pieces, matrix):
        return jnp.dot(jnp.concatenate(pieces, axis=1), matrix, preferred_element_type=jnp.float32)

    def gather_shared(whole, packed, which, width):
        half = packed.shape[0]
        parts = [
            gather([whole[k * half : (k + 1) * half], packed], edge_sum_ref[which + k, :, :width])
            for k in range(2)
        ]
        return jnp.concatenate(parts, axis=0)

    def stages(at, here_at, j):
        off, on = off_ref[:, here_at].astype(jnp.float32), on_ref[:, here_at].astype(jnp.float32)
        if last:
            middle = whole_quarters(off[0], on[0], chosen)
        else:
            off_mid, on_mid = flat(off[:2]), flat(on[:2])
            middle = [jnp.where(chosen, off_mid, on_mid), jnp.where(chosen, on_mid, off_mid)]
            middle = jnp.concatenate([middle[0], pltpu.roll(middle[1], 64, 1)], axis=0)
            outer = jnp.where(chosen == inner, on_mid, off_mid)
        received = whole_halves(off[-2:], on[-2:], chosen)
        near = jnp.where(inner, middle, flat(near_ref[:, at]) + lates[0] * received)
        moves = [advect(near, 1)] if last else [advect(near, 1), advect(outer, 2)]
        yield
        if last:
            total = jnp.dot(moves[0], sum_ref[LANES:], preferred_element_type=jnp.float32)
        else:
            total = gather_shared(*moves, 0, 2 * LANES)
        own = flat(own_ref[:, at]) + total[:, :LANES]
        force = received * jnp.where(inner, 1.0, lates[1])
        near = near + total[:, LANES:] + (flat(near_add_ref[:, at]) + force)
        yield
        moves = [advect(own, 0), advect(near, 1)]
        yield
        total = gather(moves, sum_ref[...])
        own = own + total[:, :LANES] + flat(own_force_ref[:, at])
        near = near + total[:, LANES:] + (flat(near_force_ref[:, at]) + lates[2] * received)
        yield
        half = near.shape[0] // 2
        near = jnp.where(inner, pltpu.roll(near[half:], 64, 1), near[:half])
        moves = advect(own, 0), advect(near, 3)
        yield
        total = gather_shared(*moves, 2, LANES)
        out = own + total + lates[3] * flat(tend_ref[:, here_at])
        out_ref[:, here_at] = out.reshape(PARTS, CHUNK, LANES)
        if last:
            for k in range(PARTS):
                copies.append(
                    pltpu.make_async_copy(
                        out_ref.at[k, here_at], out_hbm.at[k, at], sems.at[1 + PARTS * j + k]
                    )
                )
                copies[-1].start()

    in_turns(first, out_ref.shape[1] // CHUNK, stages, last)
    for copy in copies:
        copy.wait()


def exchanged(off, on):
    count = lax.axis_size(AXES)
    across = [(i, (i + 1) % count if i % 2 else (i - 1) % count) for i in range(count)]
    inside = [(i, i ^ 1) for i in range(count)]
    on = lax.ppermute(on, AXES, inside)
    return lax.ppermute(off, AXES, across), on


def per_device(state, prev_tendency, wind, edge_links, swap_slot, inverse):
    devices = lax.axis_size(AXES)
    shape = state.shape
    lev = shape[1]
    rows = shape[0] * lev // PARTS
    params = pltpu.CompilerParams(vmem_limit_bytes=VMEM)
    bf16, f32 = jnp.bfloat16, jnp.float32
    inner = pl.BlockSpec(memory_space=pltpu.VMEM)
    outer = pl.BlockSpec(memory_space=pltpu.HBM)

    def like(count, kind, length=rows):
        return pltpu.VMEM((count, length, LANES), kind)

    def table(kind, *size):
        return pltpu.VMEM(size, kind)

    def call(body, ins, outs, name, passes, **more):
        size = sum(math.prod(array.shape) * array.dtype.itemsize for array in ins)
        cost = pl.CostEstimate(
            flops=passes * 2 * PARTS * rows * 256 * 256, bytes_accessed=2 * size, transcendentals=0
        )
        more = {"in_specs": [inner] * len(ins), "out_specs": (inner,) * len(outs)} | more
        return pl.pallas_call(
            body, out_shape=outs, compiler_params=params, cost_estimate=cost, name=name, **more
        )(*ins)

    slot = swap_slot.reshape(1, LANES)
    slope = jnp.asarray(derivative_matrix())
    message = like(3, bf16, rows + 64)
    inputs = (
        inverse,
        wind,
        edge_links,
        state.reshape(PARTS, rows, LANES),
        prev_tendency.reshape(PARTS, rows, LANES),
    )
    inputs = tuple(pltpu.with_memory_space_constraint(array, pltpu.HBM) for array in inputs)
    matrices, packed, to_off, to_on, targets, wind, state, prev = call(
        pack_kernel,
        inputs,
        (
            table(bf16, inverse.shape[0] * lev, LANES),
            table(bf16, 368, LANES),
            message,
            message,
            table(f32, 8, LANES),
            table(f32, *wind.shape),
            like(4, f32),
            like(4, bf16),
        ),
        "pack",
        2,
        in_specs=[outer] * len(inputs),
        scratch_shapes=[
            pltpu.VMEM(inverse.shape, f32),
            pltpu.VMEM(edge_links.shape, jnp.int32),
            pltpu.SemaphoreType.DMA((3 + 2 * (rows // CHUNK),)),
        ],
    )
    far_packed = lax.ppermute(packed, AXES, [(i, i ^ (devices // 2)) for i in range(devices)])
    off, on = exchanged(to_off, to_on)
    halves = []
    first = 0
    shared = (wind, targets, slope, slot, matrices)
    for count in SPLIT:
        size = count * CHUNK
        sent = like(3 if first else 4, bf16, size)
        outs = (like(4, bf16, size), like(4, f32, size), sent, sent)
        if first == 0:
            part, start, *tables = call(
                functools.partial(own_kernel, first, count),
                (state, prev) + shared,
                (like(4, f32, size), like(4, f32, size))
                + (table(bf16, 2 * LANES, LANES), table(bf16, LANES, 2 * LANES), table(f32, 8, LANES)),
                "own",
                3 * count,
            )
            ins = (state, prev, slot, far_packed, *tables, part, start)
            body, name = far_kernel, "far"
            outs += (table(bf16, *matrices.shape),)
        else:
            ins = (state, prev) + shared + (far_matrices, *tables)
            body, name = physics_kernel, "physics"
        tend, ahead, to_off, to_on, *more = call(
            functools.partial(body, first, count), ins, outs, name, 5 * count
        )
        far_matrices = more[0] if more else far_matrices
        halves.append((first, count, tend, ahead, exchanged(to_off, to_on)))
        first += count
    parts = sum(((tend, ahead) for _, _, tend, ahead, _ in halves), ())
    own, near, near_add, own_force, near_force, sums, edge_sums, blow = call(
        near_kernel,
        (state, wind, targets, slope, off, on, prev) + parts,
        (
            like(4, f32),
            like(4, f32),
            like(4, f32),
            like(4, f32),
            like(4, f32),
            table(bf16, 2 * LANES, 2 * LANES),
            table(bf16, 4, 2 * LANES, 2 * LANES),
            table(f32, 4, 2, lev, LANES),
        ),
        "near",
        16,
    )
    tends = tuple(tend for _, _, tend, _, _ in halves)
    out_spec = jax.ShapeDtypeStruct((PARTS, rows, LANES), f32)
    tend_spec = jax.ShapeDtypeStruct((PARTS, rows, LANES), bf16)
    for part, (first, count, tend, _, (off, on)) in enumerate(halves):
        ins = (own, near, near_add, own_force, near_force, off, on, slope, sums, edge_sums, blow)
        size = count * CHUNK
        if part == 0:
            done, tend_out = call(
                functools.partial(advance_kernel, first, False),
                ins + tends,
                (like(4, f32, size), tend_spec),
                "advance",
                5 * count,
                out_specs=(inner, outer),
                scratch_shapes=[pltpu.SemaphoreType.DMA((len(tends),))],
            )
        else:
            (out,) = call(
                functools.partial(advance_kernel, first, True),
                ins + (tend, done),
                (out_spec,),
                "advance",
                5 * count,
                out_specs=(outer,),
                scratch_shapes=[pltpu.VMEM((PARTS, size, LANES), f32), pltpu.SemaphoreType.DMA((1 + PARTS * count,))],
            )
    tend = tend_out
    return (out.reshape(shape), tend.reshape(shape))


def solution(mesh):
    columns = P(None, None, AXES)
    return jax.shard_map(
        per_device,
        mesh=mesh,
        in_specs=(columns, columns, columns, columns, P(AXES), P(AXES, None, None)),
        out_specs=(columns, columns),
        check_vma=False,
    )
```

```python
import functools
import math

import jax
import jax.numpy as jnp
import numpy as np
from jax import lax
from jax.experimental import pallas as pl
from jax.experimental.pallas import tpu as pltpu
from jax.sharding import PartitionSpec as P

SUBSTEPS = 4
AXES = ("gx", "gy")
LANES = 128
CHUNK = 144
SPLIT = (3, 2)
PARTS = 4
VMEM = 16 * 1024 * 1024

time_step = 0.2
edge_points = ((0, 1, 2, 3), (3, 7, 11, 15), (15, 14, 13, 12), (12, 8, 4, 0))


def point_tables():
    edge_of = np.zeros((2, 16), np.int32)
    spot_of = np.zeros((2, 16), np.int32)
    weight_of = np.zeros((2, 16), np.float32)
    filled = np.zeros(16, np.int32)
    for k in range(4):
        for m in range(4):
            p = edge_points[k][m]
            s = filled[p]
            edge_of[s, p] = k
            spot_of[s, p] = m
            weight_of[s, p] = 1.0
            filled[p] = s + 1
    return (edge_of, spot_of, weight_of)


def gll_derivative():
    gll_nodes = np.array([-1.0, -1.0 / np.sqrt(5.0), 1.0 / np.sqrt(5.0), 1.0])
    factors = np.array(
        [np.prod([gll_nodes[i] - gll_nodes[k] for k in range(4) if k != i]) for i in range(4)]
    )
    derivative = np.zeros((4, 4))
    for i in range(4):
        for k in range(4):
            if i != k:
                derivative[i, k] = factors[i] / (factors[k] * (gll_nodes[i] - gll_nodes[k]))
            else:
                derivative[i, k] = sum(
                    (1.0 / (gll_nodes[i] - gll_nodes[j]) for j in range(4) if j != i)
                )
    return derivative


def derivative_matrix():
    derivative = gll_derivative()
    eye_block = np.eye(8)
    both = np.concatenate(
        [
            np.kron(eye_block, np.kron(derivative, np.eye(4)).T),
            np.kron(eye_block, np.kron(np.eye(4), derivative).T),
        ],
        axis=1,
    )
    high = both.astype(jnp.bfloat16)
    low = (both - high.astype(np.float64)).astype(jnp.bfloat16)
    return np.concatenate([high, low], axis=0)


def hermite(substep):
    instant = (substep + 1.0) / SUBSTEPS
    square = instant * instant
    cube = square * instant
    h00 = 2.0 * cube - 3.0 * square + 1.0
    h01 = -2.0 * cube + 3.0 * square
    slope = cube - 2.0 * square + instant + (cube - square)
    return (h00 - slope, h01 + slope)


def lane_ids(rows=1):
    return lax.broadcasted_iota(jnp.int32, (rows, LANES), 1)


def point_sets():
    point = lane_ids() % 16
    across = (point // 4 == 0) | (point // 4 == 3)
    along = (point % 4 == 0) | (point % 4 == 3)
    slots = (across | along, across & along)
    share = jnp.where(slots[1], 1.0 / 3.0, jnp.where(slots[0], 0.5, 1.0)).astype(jnp.float32)
    return slots, share


def edge_targets(links_ref, first_elem, element_count):
    edge_of, spot_of, _ = point_tables()
    elements = links_ref.shape[2]
    own = first_elem + lax.broadcasted_iota(jnp.int32, (4, elements), 1)
    apart = links_ref[0] - own
    half = element_count // 2
    apart = jnp.where(apart > half, apart - element_count, apart)
    apart = jnp.where(apart < -half, apart + element_count, apart) + 2
    both = jnp.concatenate([apart, links_ref[1]], axis=0).astype(jnp.float32)
    spread = lax.broadcasted_iota(jnp.int32, (elements, LANES), 0)
    spread = (spread == lax.broadcasted_iota(jnp.int32, (elements, LANES), 1) // 16).astype(jnp.float32)
    both = jnp.dot(both, spread, preferred_element_type=jnp.float32)
    both = (both + 0.5).astype(jnp.int32)
    lane = lane_ids()
    point = lane % 16
    rows = []
    for s in range(2):
        edge = jnp.zeros((1, LANES), jnp.int32)
        spot = edge
        for p in range(16):
            edge = jnp.where(point == p, int(edge_of[s, p]), edge)
            spot = jnp.where(point == p, int(spot_of[s, p]), spot)
        away, far = both[0:1], both[4:5]
        for k in range(1, 4):
            away = jnp.where(edge == k, both[k : k + 1], away)
            far = jnp.where(edge == k, both[4 + k : 5 + k], far)
        place = jnp.where(far == 2, 12 + spot, 4 * spot)
        place = jnp.where(far == 1, 15 - 4 * spot, place)
        place = jnp.where(far == 0, 3 - spot, place)
        rows.append(lane - point + 16 * away + place)
    rows = jnp.concatenate(rows + [jnp.zeros((6, LANES), jnp.int32)], axis=0)
    return rows.astype(jnp.float32)


def on_odd():
    return lax.axis_index(AXES) % 2 == 1


def sides():
    return (lane_ids() < 64) == on_odd()


def packed_halves(value, chosen):
    away = [pltpu.roll(value[k + 2], 64, 1) for k in range(2)]
    off = [jnp.where(chosen, away[k], value[k]) for k in range(2)]
    on = [jnp.where(chosen, value[k], away[k]) for k in range(2)]
    return off, on


def whole_halves(off, on, chosen):
    count, rows = off.shape[0], off.shape[1]
    direct = jnp.where(chosen, off, on).reshape(count * rows, LANES)
    turned = jnp.where(chosen, on, off).reshape(count * rows, LANES)
    return jnp.concatenate([direct, pltpu.roll(turned, 64, 1)], axis=0)


def mixed(*generators):
    values = {}
    while len(values) < len(generators):
        for i, one in enumerate(generators):
            if i not in values:
                try:
                    next(one)
                except StopIteration as end:
                    values[i] = end.value
        yield
    return [values[i] for i in range(len(generators))]


def packed_quarters(value, first_off, first_on):
    quarter = lane_ids() // 32
    to_off = to_on = jnp.zeros(value[0].shape, jnp.float32)
    for k, turned in enumerate(value):
        turned = pltpu.roll(turned, 32 * k, 1) if k else turned
        to_off = jnp.where(quarter == (first_off + k) % 4, turned, to_off)
        to_on = jnp.where(quarter == (first_on + k) % 4, turned, to_on)
    return to_off, to_on


def whole_quarters(off, on, chosen):
    kept = [jnp.where(chosen, off, on)]
    for k in range(1, PARTS):
        turned = [pltpu.roll(side, LANES - 32 * k, 1) for side in (off, on)]
        kept.append(jnp.where(chosen, *turned))
    return jnp.concatenate(kept, axis=0)


def packed_matrices(matrix):
    lane = lane_ids()
    half = len(matrix) // 2
    rows = [jnp.where(lane < 64, matrix[c], pltpu.roll(matrix[c + half], 64, 1)) for c in range(half)]
    rest = jnp.zeros_like(matrix[0])
    for c, value in enumerate(matrix):
        rest = jnp.where(lane // 8 == c, pltpu.roll(value, (8 * c - 64) % LANES, 1), rest)
    return jnp.concatenate(rows + [rest, jnp.zeros((8, LANES), jnp.float32)], axis=0)


def unpacked_matrices(packed):
    lane = lane_ids()
    lev, half = 72, 4
    rest = packed[half * lev : (half + 1) * lev]
    rows = []
    for c in range(2 * half):
        main = packed[c % half * lev : (c % half + 1) * lev]
        main = main if c < half else pltpu.roll(main, 64, 1)
        tail = jnp.where(lane < lev, pltpu.roll(rest, (64 - 8 * c) % LANES, 1), 0.0)
        rows.append(jnp.where(lane < 64, main, tail))
    return jnp.concatenate(rows, axis=0)


def leaving_tables(slot_ref, keep_ref, spread_ref, far_group_ref):
    slot = slot_ref[...]
    leaving = slot // LANES != lax.axis_index(AXES)
    row = lax.broadcasted_iota(jnp.int32, (LANES, LANES), 0)
    col = lax.broadcasted_iota(jnp.int32, (LANES, LANES), 1)
    ones = jnp.broadcast_to(leaving, (8, LANES)).astype(jnp.float32)
    rank = jnp.dot(ones, (row <= col).astype(jnp.float32), preferred_element_type=jnp.float32)
    yield
    rank = (rank[0:1] + 0.5).astype(jnp.int32) - 1
    spread = [(leaving & (rank + 64 * k == row)).astype(jnp.float32) for k in range(2)]
    yield
    keep = [jnp.transpose(half) for half in spread]
    yield
    for k in range(2):
        spread_ref[:, k * LANES : (k + 1) * LANES] = spread[k].astype(jnp.bfloat16)
        keep_ref[k * LANES : (k + 1) * LANES] = keep[k].astype(jnp.bfloat16)
    group = jnp.broadcast_to(slot % LANES // 16, (8, LANES)).astype(jnp.float32)
    far_group_ref[...] = jnp.dot(group, keep[0] + keep[1], preferred_element_type=jnp.float32)


def pack_kernel(
    inverse_hbm,
    wind_hbm,
    links_hbm,
    state_hbm,
    prev_hbm,
    matrix_ref,
    packed_ref,
    off_ref,
    on_ref,
    target_ref,
    wind_ref,
    state_ref,
    prev_ref,
    inverse_ref,
    links_ref,
    sems,
):
    pairs = [(links_hbm, links_ref), (inverse_hbm, inverse_ref), (wind_hbm, wind_ref)]
    for at in chunks(state_ref):
        pairs += [(state_hbm.at[:, at], state_ref.at[:, at]), (prev_hbm.at[:, at], prev_ref.at[:, at])]
    copies = [pltpu.make_async_copy(a, b, sems.at[i]) for i, (a, b) in enumerate(pairs)]
    for copy in copies:
        copy.start()
    copies[0].wait()
    devices = lax.axis_size(AXES)
    elements = links_ref.shape[2]
    targets = edge_targets(links_ref, lax.axis_index(AXES) * elements, elements * devices)
    groups, lev = inverse_ref.shape[0], inverse_ref.shape[1]
    copies[1].wait()
    eye = lax.broadcasted_iota(jnp.int32, (lev, lev), 0) == lax.broadcasted_iota(jnp.int32, (lev, lev), 1)
    eye = eye.astype(jnp.float32)
    blank = jnp.zeros((lev, LANES - lev), jnp.float32)
    matrix = [jnp.concatenate([inverse_ref[c] - eye, blank], axis=1) for c in range(groups)]
    matrix_ref[...] = jnp.concatenate(matrix, axis=0).astype(jnp.bfloat16)
    packed_ref[...] = packed_matrices(matrix).astype(jnp.bfloat16)
    copies[2].wait()
    target_ref[...] = targets
    end = off_ref.shape[1]
    filler = jnp.zeros((8, LANES), jnp.float32)
    flat_wind = wind_ref[...].reshape(2 * lev, LANES)
    for k in range(3):
        piece = jnp.concatenate([flat_wind[48 * k : 48 * k + 48], targets, filler], axis=0)
        piece = piece.astype(jnp.bfloat16)
        off_ref[k, end - 64 : end] = piece
        on_ref[k, end - 64 : end] = piece
    chosen = sides()
    odd = jnp.where(on_odd(), 3, 0)
    quarter = lane_ids() // 32
    for j, at in enumerate(chunks(state_ref)):
        copies[3 + 2 * j].wait()
        copies[4 + 2 * j].wait()
        off, on = packed_halves([state_ref[k, at] for k in range(PARTS)], chosen)
        for k in range(2):
            off_ref[k, at] = off[k].astype(jnp.bfloat16)
            on_ref[k, at] = on[k].astype(jnp.bfloat16)
        to_off = jnp.zeros((CHUNK, LANES), jnp.float32)
        to_on = to_off
        for k in range(PARTS):
            turned = prev_ref[k, at].astype(jnp.float32)
            turned = pltpu.roll(turned, 32 * k, 1) if k else turned
            to_off = jnp.where(quarter == (odd + k) % 4, turned, to_off)
            to_on = jnp.where(quarter == (3 - odd + k) % 4, turned, to_on)
        off_ref[2, at] = to_off.astype(jnp.bfloat16)
        on_ref[2, at] = to_on.astype(jnp.bfloat16)


def chunks(ref):
    return [pl.ds(start, CHUNK) for start in range(0, ref.shape[1], CHUNK)]


def in_turns(first, count, stages, together=False):
    running = []
    for j in range(count):
        running.append(stages(pl.ds((first + j) * CHUNK, CHUNK), pl.ds(j * CHUNK, CHUNK), j))
    waiting, started = list(running), []
    while waiting or started:
        while waiting:
            started.append(waiting.pop(0))
            if not together:
                break
        started = [one for one in started if next(one, started) is not started]


def column_pair(pair):
    lev = pair.shape[0] // 2
    blank = jnp.zeros((LANES - lev, 2 * LANES), jnp.float32)
    pair = jnp.concatenate([pair[:lev], pair[lev:]], axis=1)
    high = pair.astype(jnp.bfloat16).astype(jnp.float32)
    return jnp.concatenate([high, blank, pair - high, blank], axis=0).astype(jnp.bfloat16)


def chosen_rows(product, group, chosen=None, first=0):
    lev = 72
    for c in range(product.shape[0] // lev):
        part = product[c * lev : (c + 1) * lev]
        chosen = part if chosen is None else jnp.where(group == first + c, part, chosen)
    return chosen


def as_rows(pair):
    return jnp.concatenate([pair[:, :LANES], pair[:, LANES:]], axis=0)


def column_group(slot_ref):
    slot = slot_ref[...]
    return jnp.where(slot // LANES == lax.axis_index(AXES), 0, 8) + slot % LANES // 16


def flat(value):
    return value.astype(jnp.float32).reshape(-1, LANES)


def moved(value, slope, blow_x, blow_y):
    rows, lev = value.shape[0], blow_x.shape[0]
    value = value.astype(jnp.bfloat16)
    both = jnp.dot(jnp.concatenate([value, value], axis=1), slope, preferred_element_type=jnp.float32)
    both = both.reshape(rows // lev, lev, 2 * LANES)
    motion = both[..., :LANES] * blow_x + both[..., LANES:] * blow_y
    return motion.reshape(rows, LANES).astype(jnp.bfloat16)


def sum_block(source, targets, slots, own):
    row = lax.broadcasted_iota(jnp.int32, (LANES, LANES), 0)
    total = jnp.zeros((LANES, LANES), jnp.float32)
    if own:
        total = (row == lax.broadcasted_iota(jnp.int32, (LANES, LANES), 1)).astype(jnp.float32)
    place = {
        "own": row,
        "own turned": jnp.where(row < 64, row + 64, row - 64),
        "near": jnp.where(row < 64, row + LANES, row - LANES),
        "near turned": jnp.where(row < 64, row - 64, row + 64),
        "outer": jnp.where(row < 64, row - LANES, row + LANES),
        "outer turned": jnp.where(row < 64, row + LANES + 64, row - LANES - 64),
    }[source]
    for s in range(2):
        total = total + ((place == targets[s : s + 1]) & slots[s]).astype(jnp.float32)
    return (total * point_sets()[1]).astype(jnp.bfloat16)


def inner_lanes():
    quarter = lane_ids() // 32
    return (quarter == 1) | (quarter == 2)


class Physics:
    def __init__(self, slot_ref):
        group = column_group(slot_ref)
        self.here = group < 8
        self.group = jnp.concatenate([group, group], axis=1)
        self.inner = inner_lanes()
        self.chosen = sides()

    def take_own(self, own_ref):
        self.own = jnp.concatenate([own_ref[...], own_ref[...]], axis=1)

    def take_far(self, far, keep_ref, spread_ref, far_group_ref):
        self.far = far
        self.keep, self.spread = keep_ref[...], spread_ref[...]
        group = (far_group_ref[0:1, :] + 0.5).astype(jnp.int32)
        self.far_group = jnp.concatenate([group, group], axis=1)

    def begin(self, wind_ref, target_ref, slope_ref):
        slots, _ = point_sets()
        self.sums = sum_block("own", target_ref[...].astype(jnp.int32) - 32, slots, True)
        self.blow = [-time_step * wind_ref[d] for d in range(2)]
        self.slope = slope_ref[...]
        self.targets, self.slots = target_ref[...].astype(jnp.int32) - 32, slots

    def begin_cross(self):
        row = lax.broadcasted_iota(jnp.int32, (LANES, LANES), 0)
        col = lax.broadcasted_iota(jnp.int32, (LANES, LANES), 1) // 32
        blocks = []
        for turn in (0, 64):
            place = (row + turn) % LANES // 32
            crossing = ((place == 1) & (col == 2)) | ((place == 2) & (col == 1))
            block = sum_block("own turned" if turn else "own", self.targets, self.slots, False)
            blocks.append(jnp.where(crossing, block.astype(jnp.float32), 0.0).astype(jnp.bfloat16))
        self.cross = jnp.concatenate(blocks, axis=1)
        self.cross_blow = [jnp.where(self.inner, w, pltpu.roll(w, 64, 1)) for w in self.blow]

    def motion(self, state):
        return moved(state, self.slope, *self.blow)

    def start(self, state, prev):
        motion = self.motion(state)
        yield
        total = jnp.dot(motion, self.sums, preferred_element_type=jnp.float32)
        return state + total + time_step * hermite(0)[0] * prev

    def own_products(self, pairs):
        ahead, rows = None, []
        for k, pair in enumerate(pairs):
            product = jnp.dot(self.own, column_pair(pair), preferred_element_type=jnp.float32)
            if k:
                rows.append(as_rows(chosen_rows(ahead, self.group)))
            ahead = product
            yield
        rows.append(as_rows(chosen_rows(ahead, self.group)))
        return rows

    def far_products(self, pairs):
        high = [pair.astype(jnp.bfloat16) for pair in pairs]
        both = [jnp.concatenate(high[k : k + 2], axis=1) for k in (0, 2)]
        few = jnp.dot(jnp.concatenate(both, axis=0), self.keep, preferred_element_type=jnp.float32)
        yield
        size = pairs[0].shape[0]
        lev = size // 2
        blank = jnp.zeros((LANES - lev, 2 * LANES), jnp.float32)
        products, rows = [], []
        for k in range(2):
            part = few[k * size : (k + 1) * size]
            part = jnp.concatenate([part[:lev], part[lev:]], axis=1)
            column = jnp.concatenate([part, blank], axis=0).astype(jnp.bfloat16)
            products.append(jnp.dot(self.far, column, preferred_element_type=jnp.float32))
            yield
        for k in range(2):
            rows.append(as_rows(chosen_rows(products[k], self.far_group)))
        rows = jnp.concatenate(rows, axis=0).astype(jnp.bfloat16)
        wide = jnp.dot(rows, self.spread, preferred_element_type=jnp.float32)
        yield
        return [wide[k * size : (k + 1) * size, c : c + LANES] for k in range(2) for c in (0, LANES)]

    def merged(self, own, far):
        return [jnp.where(self.here, a, b) for a, b in zip(own, far)]

    def finish(self, start, prev, tends, here_at, tend_ref, ahead_ref, off_ref, on_ref, lean=False):
        late = time_step * hermite(0)[1]
        early_1, late_1 = (time_step * w for w in hermite(1))
        ahead, force = [], []
        for k, tend in enumerate(tends):
            tend = tend.astype(jnp.bfloat16)
            tend_ref[k, here_at] = tend
            tend = tend.astype(jnp.float32)
            ahead.append(start[k] + late * tend)
            ahead_ref[k, here_at] = ahead[k]
            force.append(jnp.where(self.inner, early_1 * prev[k] + late_1 * tend, tend))
        middle = [jnp.where(self.inner, ahead[k], pltpu.roll(ahead[k + 2], 64, 1)) for k in range(2)]
        if lean:
            motion = moved(jnp.concatenate(middle, axis=0), self.slope, *self.cross_blow)
            yield
            cross = jnp.dot(motion, self.cross, preferred_element_type=jnp.float32)
            yield
            for k in range(PARTS):
                rows = slice(k % 2 * CHUNK, (k % 2 + 1) * CHUNK)
                force[k] = force[k] + cross[rows, k // 2 * LANES : (k // 2 + 1) * LANES]
            to_off, to_on = packed_quarters(ahead, jnp.where(on_odd(), 2, 1), jnp.where(on_odd(), 1, 2))
            off_ref[0, here_at] = to_off.astype(jnp.bfloat16)
            on_ref[0, here_at] = to_on.astype(jnp.bfloat16)
        else:
            for k in range(2):
                off_ref[k, here_at] = middle[k].astype(jnp.bfloat16)
                on_ref[k, here_at] = middle[k].astype(jnp.bfloat16)
        off, on = packed_halves(force, self.chosen)
        at = off_ref.shape[0] - 2
        for k in range(2):
            off_ref[at + k, here_at] = off[k].astype(jnp.bfloat16)
            on_ref[at + k, here_at] = on[k].astype(jnp.bfloat16)


def own_kernel(
    first, count, state_ref, prev_ref, wind_ref, target_ref, slope_ref, slot_ref, own_ref, part_ref, start_ref, *tables
):
    physics = Physics(slot_ref)
    physics.take_own(own_ref)
    physics.begin(wind_ref, target_ref, slope_ref)

    def stages(at, here_at, j):
        parts, start, *_ = yield from mixed(
            physics.own_products([state_ref[k, at] for k in range(PARTS)]),
            physics.start(flat(state_ref[:, at]), flat(prev_ref[:, at])),
            *([leaving_tables(slot_ref, *tables)] if j == 0 else []),
        )
        start_ref[:, here_at] = start.reshape(PARTS, CHUNK, LANES)
        for k, part in enumerate(parts):
            part_ref[k, here_at] = part

    in_turns(first, count, stages, True)


def far_kernel(
    first,
    count,
    state_ref,
    prev_ref,
    slot_ref,
    packed_ref,
    keep_ref,
    spread_ref,
    far_group_ref,
    part_ref,
    start_ref,
    tend_ref,
    ahead_ref,
    off_ref,
    on_ref,
    far_ref,
):
    physics = Physics(slot_ref)
    matrices = unpacked_matrices(packed_ref[...].astype(jnp.float32)).astype(jnp.bfloat16)
    far_ref[...] = matrices
    physics.take_far(matrices, keep_ref, spread_ref, far_group_ref)

    def stages(at, here_at, _):
        far = yield from physics.far_products([state_ref[k, at] for k in range(PARTS)])
        tends = physics.merged([part_ref[k, here_at] for k in range(PARTS)], far)
        start = [start_ref[k, here_at] for k in range(PARTS)]
        prev = [prev_ref[k, at].astype(jnp.float32) for k in range(PARTS)]
        yield from physics.finish(start, prev, tends, here_at, tend_ref, ahead_ref, off_ref, on_ref)

    in_turns(first, count, stages, True)


def physics_kernel(
    first,
    count,
    state_ref,
    prev_ref,
    wind_ref,
    target_ref,
    slope_ref,
    slot_ref,
    own_ref,
    far_ref,
    keep_ref,
    spread_ref,
    far_group_ref,
    tend_ref,
    ahead_ref,
    off_ref,
    on_ref,
):
    physics = Physics(slot_ref)
    physics.take_own(own_ref)
    physics.take_far(far_ref[...], keep_ref, spread_ref, far_group_ref)
    physics.begin(wind_ref, target_ref, slope_ref)
    physics.begin_cross()

    def stages(at, here_at, _):
        pairs = [state_ref[k, at] for k in range(PARTS)]
        far, own, start = yield from mixed(
            physics.far_products(pairs),
            physics.own_products(pairs),
            physics.start(flat(state_ref[:, at]), flat(prev_ref[:, at])),
        )
        start = [start[k * CHUNK : (k + 1) * CHUNK] for k in range(PARTS)]
        tends = physics.merged(own, far)
        prev = [prev_ref[k, at].astype(jnp.float32) for k in range(PARTS)]
        yield from physics.finish(start, prev, tends, here_at, tend_ref, ahead_ref, off_ref, on_ref, True)

    in_turns(first, count, stages, True)


def near_kernel(
    state_ref,
    wind_ref,
    target_ref,
    slope_ref,
    off_ref,
    on_ref,
    prev_ref,
    *rest,
):
    parts, outs = rest[:-10], rest[-9:-1]
    own_ref, near_ref, near_add_ref, own_force_ref, near_force_ref, sum_ref, edge_sum_ref, blow_ref = outs
    lev = wind_ref.shape[1]
    slots, _ = point_sets()
    chosen = sides()
    end = off_ref.shape[1]

    def extra(ref, k):
        return ref[k, end - 64 : end].astype(jnp.float32)

    def winds(ref):
        whole = jnp.concatenate([extra(ref, k)[:48] for k in range(3)], axis=0)
        return whole[:lev], whole[lev:]

    def targets(ref):
        return extra(ref, 0)[48:56].astype(jnp.int32) - 32

    own_t = target_ref[...].astype(jnp.int32) - 32
    near_t = jnp.where(chosen, targets(off_ref), targets(on_ref))
    near_t = near_t + jnp.where(lane_ids() < 64, LANES, -LANES)
    own_sums = jnp.concatenate(
        [sum_block("own", own_t, slots, True), sum_block("own", near_t, slots, False)], axis=1
    )
    near_sums = jnp.concatenate(
        [sum_block("near", own_t, slots, False), sum_block("near", near_t, slots, True)], axis=1
    )
    sum_ref[:LANES] = own_sums
    sum_ref[LANES:] = near_sums
    nothing = jnp.zeros((LANES, LANES), jnp.bfloat16)
    first_sums = jnp.concatenate([nothing, own_sums[:, LANES:]], axis=1)
    first_sums = jnp.concatenate([near_sums, first_sums], axis=0)
    for k, turn in enumerate(("", " turned")):
        edge_sum_ref[k, :LANES] = near_sums
        edge_sum_ref[k, LANES:, :LANES] = nothing
        edge_sum_ref[k, LANES:, LANES:] = sum_block("outer" + turn, near_t, slots, False)
        edge_sum_ref[2 + k, :LANES, :LANES] = own_sums[:, :LANES]
        edge_sum_ref[2 + k, LANES:, :LANES] = sum_block("near" + turn, own_t, slots, False)
    inner = inner_lanes()
    off_w, on_w = winds(off_ref), winds(on_ref)
    for d in range(2):
        blow_ref[0, d] = -time_step * wind_ref[d]
        near_w = -time_step * jnp.where(chosen, off_w[d], on_w[d])
        outer_w = -time_step * jnp.where(chosen, on_w[d], off_w[d])
        blow_ref[1, d] = near_w
        blow_ref[2, d] = jnp.where(inner, outer_w, pltpu.roll(outer_w, 64, 1))
        blow_ref[3, d] = jnp.where(inner, pltpu.roll(near_w, 64, 1), near_w)

    slope = slope_ref[...]
    early = time_step * hermite(0)[0]
    early_1, late_1 = (time_step * w for w in hermite(1))
    early_2, late_2 = (time_step * w for w in hermite(2))
    own_blow = (blow_ref[0, 0], blow_ref[0, 1])
    near_blow = (blow_ref[1, 0], blow_ref[1, 1])

    def stages(at, here_at, tend_ref, ahead_ref):
        off, on = off_ref[:, at].astype(jnp.float32), on_ref[:, at].astype(jnp.float32)
        near = whole_halves(off[:2], on[:2], chosen)
        own_move = moved(flat(state_ref[:, at]), slope, *own_blow)
        near_move = moved(near, slope, *near_blow)
        yield
        total = jnp.concatenate([near_move, own_move], axis=1)
        total = jnp.dot(total, first_sums, preferred_element_type=jnp.float32)
        near_total = total[:, LANES:]
        kept = jnp.where(inner, 0.0, whole_quarters(off[2], on[2], chosen))
        near = near + near_total + early * kept
        near_ref[:, at] = near.reshape(PARTS, CHUNK, LANES)
        near_force_ref[:, at] = (early_2 * kept).reshape(PARTS, CHUNK, LANES)
        own = flat(ahead_ref[:, here_at]) + total[:, :LANES]
        yield
        own_move = moved(own, slope, *own_blow)
        yield
        total = jnp.dot(own_move, own_sums, preferred_element_type=jnp.float32)
        own_prev, own_tend = flat(prev_ref[:, at]), flat(tend_ref[:, here_at])
        own = own + total[:, :LANES] + (early_1 * own_prev + late_1 * own_tend)
        own_ref[:, at] = own.reshape(PARTS, CHUNK, LANES)
        own_force = early_2 * own_prev + late_2 * own_tend
        own_force_ref[:, at] = own_force.reshape(PARTS, CHUNK, LANES)
        near_add = total[:, LANES:] + early_1 * kept
        near_add_ref[:, at] = near_add.reshape(PARTS, CHUNK, LANES)

    places = []
    for tend_ref, ahead_ref in zip(parts[::2], parts[1::2]):
        places += [(here_at, tend_ref, ahead_ref) for here_at in chunks(tend_ref)]
    in_turns(0, len(places), lambda at, _, j: stages(at, *places[j]))


def advance_kernel(
    first,
    last,
    own_ref,
    near_ref,
    near_add_ref,
    own_force_ref,
    near_force_ref,
    off_ref,
    on_ref,
    slope_ref,
    sum_ref,
    edge_sum_ref,
    blow_ref,
    *rest,
):
    if last:
        tend_ref, done_ref, out_hbm, out_ref, sems = rest
        copies = [pltpu.make_async_copy(done_ref, out_hbm.at[:, pl.ds(0, done_ref.shape[1])], sems.at[0])]
    else:
        *tend_refs, out_ref, tend_hbm, sems = rest
        tend_ref = tend_refs[0]
        copies, row = [], 0
        for k, ref in enumerate(tend_refs):
            copies.append(pltpu.make_async_copy(ref, tend_hbm.at[:, pl.ds(row, ref.shape[1])], sems.at[k]))
            row += ref.shape[1]
    for copy in copies:
        copy.start()
    inner = inner_lanes()
    chosen = sides()
    slope = slope_ref[...]
    lates = [time_step * hermite(s)[1] for s in range(SUBSTEPS)]

    def advect(value, unit):
        return moved(value, slope, blow_ref[unit, 0], blow_ref[unit, 1])

    def gather(pieces, matrix):
        return jnp.dot(jnp.concatenate(pieces, axis=1), matrix, preferred_element_type=jnp.float32)

    def gather_shared(whole, packed, which, width):
        half = packed.shape[0]
        parts = [
            gather([whole[k * half : (k + 1) * half], packed], edge_sum_ref[which + k, :, :width])
            for k in range(2)
        ]
        return jnp.concatenate(parts, axis=0)

    def stages(at, here_at, j):
        off, on = off_ref[:, here_at].astype(jnp.float32), on_ref[:, here_at].astype(jnp.float32)
        if last:
            middle = whole_quarters(off[0], on[0], chosen)
        else:
            off_mid, on_mid = flat(off[:2]), flat(on[:2])
            middle = [jnp.where(chosen, off_mid, on_mid), jnp.where(chosen, on_mid, off_mid)]
            middle = jnp.concatenate([middle[0], pltpu.roll(middle[1], 64, 1)], axis=0)
            outer = jnp.where(chosen == inner, on_mid, off_mid)
        received = whole_halves(off[-2:], on[-2:], chosen)
        near = jnp.where(inner, middle, flat(near_ref[:, at]) + lates[0] * received)
        moves = [advect(near, 1)] if last else [advect(near, 1), advect(outer, 2)]
        yield
        if last:
            total = jnp.dot(moves[0], sum_ref[LANES:], preferred_element_type=jnp.float32)
        else:
            total = gather_shared(*moves, 0, 2 * LANES)
        own = flat(own_ref[:, at]) + total[:, :LANES]
        force = received * jnp.where(inner, 1.0, lates[1])
        near = near + total[:, LANES:] + (flat(near_add_ref[:, at]) + force)
        yield
        moves = [advect(own, 0), advect(near, 1)]
        yield
        total = gather(moves, sum_ref[...])
        own = own + total[:, :LANES] + flat(own_force_ref[:, at])
        near = near + total[:, LANES:] + (flat(near_force_ref[:, at]) + lates[2] * received)
        yield
        half = near.shape[0] // 2
        near = jnp.where(inner, pltpu.roll(near[half:], 64, 1), near[:half])
        moves = advect(own, 0), advect(near, 3)
        yield
        total = gather_shared(*moves, 2, LANES)
        out = own + total + lates[3] * flat(tend_ref[:, here_at])
        out_ref[:, here_at] = out.reshape(PARTS, CHUNK, LANES)
        if last:
            for k in range(PARTS):
                copies.append(
                    pltpu.make_async_copy(
                        out_ref.at[k, here_at], out_hbm.at[k, at], sems.at[1 + PARTS * j + k]
                    )
                )
                copies[-1].start()

    in_turns(first, out_ref.shape[1] // CHUNK, stages, last)
    for copy in copies:
        copy.wait()


def across(value):
    count = lax.axis_size(AXES)
    return lax.ppermute(value, AXES, [(i, (i + 1) % count if i % 2 else (i - 1) % count) for i in range(count)])


def inside(value):
    return lax.ppermute(value, AXES, [(i, i ^ 1) for i in range(lax.axis_size(AXES))])


def per_device(state, prev_tendency, wind, edge_links, swap_slot, inverse):
    devices = lax.axis_size(AXES)
    shape = state.shape
    lev = shape[1]
    rows = shape[0] * lev // PARTS
    params = pltpu.CompilerParams(vmem_limit_bytes=VMEM)
    bf16, f32 = jnp.bfloat16, jnp.float32
    inner = pl.BlockSpec(memory_space=pltpu.VMEM)
    outer = pl.BlockSpec(memory_space=pltpu.HBM)

    def like(count, kind, length=rows):
        return pltpu.VMEM((count, length, LANES), kind)

    def table(kind, *size):
        return pltpu.VMEM(size, kind)

    def call(body, ins, outs, name, passes, **more):
        size = sum(math.prod(array.shape) * array.dtype.itemsize for array in ins)
        cost = pl.CostEstimate(
            flops=passes * 2 * PARTS * rows * 256 * 256, bytes_accessed=2 * size, transcendentals=0
        )
        more = {"in_specs": [inner] * len(ins), "out_specs": (inner,) * len(outs)} | more
        return pl.pallas_call(
            body, out_shape=outs, compiler_params=params, cost_estimate=cost, name=name, **more
        )(*ins)

    slot = swap_slot.reshape(1, LANES)
    slope = jnp.asarray(derivative_matrix())
    message = like(3, bf16, rows + 64)
    inputs = (
        inverse,
        wind,
        edge_links,
        state.reshape(PARTS, rows, LANES),
        prev_tendency.reshape(PARTS, rows, LANES),
    )
    inputs = tuple(pltpu.with_memory_space_constraint(array, pltpu.HBM) for array in inputs)
    matrices, packed, to_off, to_on, targets, wind, state, prev = call(
        pack_kernel,
        inputs,
        (
            table(bf16, inverse.shape[0] * lev, LANES),
            table(bf16, 368, LANES),
            message,
            message,
            table(f32, 8, LANES),
            table(f32, *wind.shape),
            like(4, f32),
            like(4, bf16),
        ),
        "pack",
        2,
        in_specs=[outer] * len(inputs),
        scratch_shapes=[
            pltpu.VMEM(inverse.shape, f32),
            pltpu.VMEM(edge_links.shape, jnp.int32),
            pltpu.SemaphoreType.DMA((3 + 2 * (rows // CHUNK),)),
        ],
    )
    far_packed = lax.ppermute(packed, AXES, [(i, i ^ (devices // 2)) for i in range(devices)])
    off, on = across(to_off), inside(to_on)
    halves = []
    first = 0
    shared = (wind, targets, slope, slot, matrices)
    for count in SPLIT:
        size = count * CHUNK
        sent = like(3 if first else 4, bf16, size)
        outs = (like(4, bf16, size), like(4, f32, size), sent, sent)
        if first == 0:
            part, start, *tables = call(
                functools.partial(own_kernel, first, count),
                (state, prev) + shared,
                (like(4, f32, size), like(4, f32, size))
                + (table(bf16, 2 * LANES, LANES), table(bf16, LANES, 2 * LANES), table(f32, 8, LANES)),
                "own",
                3 * count,
            )
            ins = (state, prev, slot, far_packed, *tables, part, start)
            body, name = far_kernel, "far"
            outs += (table(bf16, *matrices.shape),)
        else:
            ins = (state, prev) + shared + (far_matrices, *tables)
            body, name = physics_kernel, "physics"
        tend, ahead, to_off, to_on, *more = call(
            functools.partial(body, first, count), ins, outs, name, 5 * count
        )
        far_matrices = more[0] if more else far_matrices
        halves.append([first, count, tend, ahead, across(to_off), to_on if first else inside(to_on)])
        first += count
    parts = sum(((tend, ahead) for _, _, tend, ahead, _, _ in halves), ())
    passed = halves[-1][-1]
    ins = (state, wind, targets, slope, off, on, prev) + parts + (passed,)
    own, near, near_add, own_force, near_force, sums, edge_sums, blow, passed = call(
        near_kernel,
        ins,
        (
            like(4, f32),
            like(4, f32),
            like(4, f32),
            like(4, f32),
            like(4, f32),
            table(bf16, 2 * LANES, 2 * LANES),
            table(bf16, 4, 2 * LANES, 2 * LANES),
            table(f32, 4, 2, lev, LANES),
            like(3, bf16, passed.shape[1]),
        ),
        "near",
        16,
        input_output_aliases={len(ins) - 1: 8},
    )
    halves[-1][-1] = inside(passed)
    tends = tuple(tend for _, _, tend, _, _, _ in halves)
    out_spec = jax.ShapeDtypeStruct((PARTS, rows, LANES), f32)
    tend_spec = jax.ShapeDtypeStruct((PARTS, rows, LANES), bf16)
    for part, (first, count, tend, _, off, on) in enumerate(halves):
        ins = (own, near, near_add, own_force, near_force, off, on, slope, sums, edge_sums, blow)
        size = count * CHUNK
        if part == 0:
            done, tend_out = call(
                functools.partial(advance_kernel, first, False),
                ins + tends,
                (like(4, f32, size), tend_spec),
                "advance",
                5 * count,
                out_specs=(inner, outer),
                scratch_shapes=[pltpu.SemaphoreType.DMA((len(tends),))],
            )
        else:
            (out,) = call(
                functools.partial(advance_kernel, first, True),
                ins + (tend, done),
                (out_spec,),
                "advance",
                5 * count,
                out_specs=(outer,),
                scratch_shapes=[pltpu.VMEM((PARTS, size, LANES), f32), pltpu.SemaphoreType.DMA((1 + PARTS * count,))],
            )
    tend = tend_out
    return (out.reshape(shape), tend.reshape(shape))


def solution(mesh):
    columns = P(None, None, AXES)
    return jax.shard_map(
        per_device,
        mesh=mesh,
        in_specs=(columns, columns, columns, columns, P(AXES), P(AXES, None, None)),
        out_specs=(columns, columns),
        check_vma=False,
    )
```

```python
import functools
import math

import jax
import jax.numpy as jnp
import numpy as np
from jax import lax
from jax.experimental import pallas as pl
from jax.experimental.pallas import tpu as pltpu
from jax.sharding import PartitionSpec as P

SUBSTEPS = 4
AXES = ("gx", "gy")
LANES = 128
CHUNK = 144
SPLIT = (3, 2)
PARTS = 4
VMEM = 16 * 1024 * 1024

time_step = 0.2
edge_points = ((0, 1, 2, 3), (3, 7, 11, 15), (15, 14, 13, 12), (12, 8, 4, 0))


def point_tables():
    edge_of = np.zeros((2, 16), np.int32)
    spot_of = np.zeros((2, 16), np.int32)
    weight_of = np.zeros((2, 16), np.float32)
    filled = np.zeros(16, np.int32)
    for k in range(4):
        for m in range(4):
            p = edge_points[k][m]
            s = filled[p]
            edge_of[s, p] = k
            spot_of[s, p] = m
            weight_of[s, p] = 1.0
            filled[p] = s + 1
    return (edge_of, spot_of, weight_of)


def gll_derivative():
    gll_nodes = np.array([-1.0, -1.0 / np.sqrt(5.0), 1.0 / np.sqrt(5.0), 1.0])
    factors = np.array(
        [np.prod([gll_nodes[i] - gll_nodes[k] for k in range(4) if k != i]) for i in range(4)]
    )
    derivative = np.zeros((4, 4))
    for i in range(4):
        for k in range(4):
            if i != k:
                derivative[i, k] = factors[i] / (factors[k] * (gll_nodes[i] - gll_nodes[k]))
            else:
                derivative[i, k] = sum(
                    (1.0 / (gll_nodes[i] - gll_nodes[j]) for j in range(4) if j != i)
                )
    return derivative


def derivative_matrix():
    derivative = gll_derivative()
    eye_block = np.eye(8)
    both = np.concatenate(
        [
            np.kron(eye_block, np.kron(derivative, np.eye(4)).T),
            np.kron(eye_block, np.kron(np.eye(4), derivative).T),
        ],
        axis=1,
    )
    high = both.astype(jnp.bfloat16)
    low = (both - high.astype(np.float64)).astype(jnp.bfloat16)
    return np.concatenate([high, low], axis=0)


def hermite(substep):
    instant = (substep + 1.0) / SUBSTEPS
    square = instant * instant
    cube = square * instant
    h00 = 2.0 * cube - 3.0 * square + 1.0
    h01 = -2.0 * cube + 3.0 * square
    slope = cube - 2.0 * square + instant + (cube - square)
    return (h00 - slope, h01 + slope)


def lane_ids(rows=1):
    return lax.broadcasted_iota(jnp.int32, (rows, LANES), 1)


def point_sets():
    point = lane_ids() % 16
    across = (point // 4 == 0) | (point // 4 == 3)
    along = (point % 4 == 0) | (point % 4 == 3)
    slots = (across | along, across & along)
    share = jnp.where(slots[1], 1.0 / 3.0, jnp.where(slots[0], 0.5, 1.0)).astype(jnp.float32)
    return slots, share


def edge_targets(links_ref, first_elem, element_count):
    edge_of, spot_of, _ = point_tables()
    elements = links_ref.shape[2]
    own = first_elem + lax.broadcasted_iota(jnp.int32, (4, elements), 1)
    apart = links_ref[0] - own
    half = element_count // 2
    apart = jnp.where(apart > half, apart - element_count, apart)
    apart = jnp.where(apart < -half, apart + element_count, apart) + 2
    both = jnp.concatenate([apart, links_ref[1]], axis=0).astype(jnp.float32)
    spread = lax.broadcasted_iota(jnp.int32, (elements, LANES), 0)
    spread = (spread == lax.broadcasted_iota(jnp.int32, (elements, LANES), 1) // 16).astype(jnp.float32)
    both = jnp.dot(both, spread, preferred_element_type=jnp.float32)
    both = (both + 0.5).astype(jnp.int32)
    lane = lane_ids()
    point = lane % 16
    rows = []
    for s in range(2):
        edge = jnp.zeros((1, LANES), jnp.int32)
        spot = edge
        for p in range(16):
            edge = jnp.where(point == p, int(edge_of[s, p]), edge)
            spot = jnp.where(point == p, int(spot_of[s, p]), spot)
        away, far = both[0:1], both[4:5]
        for k in range(1, 4):
            away = jnp.where(edge == k, both[k : k + 1], away)
            far = jnp.where(edge == k, both[4 + k : 5 + k], far)
        place = jnp.where(far == 2, 12 + spot, 4 * spot)
        place = jnp.where(far == 1, 15 - 4 * spot, place)
        place = jnp.where(far == 0, 3 - spot, place)
        rows.append(lane - point + 16 * away + place)
    rows = jnp.concatenate(rows + [jnp.zeros((6, LANES), jnp.int32)], axis=0)
    return rows.astype(jnp.float32)


def on_odd():
    return lax.axis_index(AXES) % 2 == 1


def sides():
    return (lane_ids() < 64) == on_odd()


def packed_halves(value, chosen):
    away = [pltpu.roll(value[k + 2], 64, 1) for k in range(2)]
    off = [jnp.where(chosen, away[k], value[k]) for k in range(2)]
    on = [jnp.where(chosen, value[k], away[k]) for k in range(2)]
    return off, on


def whole_halves(off, on, chosen):
    count, rows = off.shape[0], off.shape[1]
    direct = jnp.where(chosen, off, on).reshape(count * rows, LANES)
    turned = jnp.where(chosen, on, off).reshape(count * rows, LANES)
    return jnp.concatenate([direct, pltpu.roll(turned, 64, 1)], axis=0)


def mixed(*generators):
    values = {}
    while len(values) < len(generators):
        for i, one in enumerate(generators):
            if i not in values:
                try:
                    next(one)
                except StopIteration as end:
                    values[i] = end.value
        yield
    return [values[i] for i in range(len(generators))]


def packed_quarters(value, first_off, first_on):
    quarter = lane_ids() // 32
    to_off = to_on = jnp.zeros(value[0].shape, jnp.float32)
    for k, turned in enumerate(value):
        turned = pltpu.roll(turned, 32 * k, 1) if k else turned
        to_off = jnp.where(quarter == (first_off + k) % 4, turned, to_off)
        to_on = jnp.where(quarter == (first_on + k) % 4, turned, to_on)
    return to_off, to_on


def whole_quarters(off, on, chosen):
    kept = [jnp.where(chosen, off, on)]
    for k in range(1, PARTS):
        turned = [pltpu.roll(side, LANES - 32 * k, 1) for side in (off, on)]
        kept.append(jnp.where(chosen, *turned))
    return jnp.concatenate(kept, axis=0)


def packed_matrices(matrix):
    lane = lane_ids()
    half = len(matrix) // 2
    rows = [jnp.where(lane < 64, matrix[c], pltpu.roll(matrix[c + half], 64, 1)) for c in range(half)]
    rest = jnp.zeros_like(matrix[0])
    for c, value in enumerate(matrix):
        rest = jnp.where(lane // 8 == c, pltpu.roll(value, (8 * c - 64) % LANES, 1), rest)
    return jnp.concatenate(rows + [rest, jnp.zeros((8, LANES), jnp.float32)], axis=0)


def unpacked_matrices(packed):
    lane = lane_ids()
    lev, half = 72, 4
    rest = packed[half * lev : (half + 1) * lev]
    rows = []
    for c in range(2 * half):
        main = packed[c % half * lev : (c % half + 1) * lev]
        main = main if c < half else pltpu.roll(main, 64, 1)
        tail = jnp.where(lane < lev, pltpu.roll(rest, (64 - 8 * c) % LANES, 1), 0.0)
        rows.append(jnp.where(lane < 64, main, tail))
    return jnp.concatenate(rows, axis=0)


def leaving_tables(slot_ref, keep_ref, spread_ref, far_group_ref):
    slot = slot_ref[...]
    leaving = slot // LANES != lax.axis_index(AXES)
    row = lax.broadcasted_iota(jnp.int32, (LANES, LANES), 0)
    col = lax.broadcasted_iota(jnp.int32, (LANES, LANES), 1)
    ones = jnp.broadcast_to(leaving, (8, LANES)).astype(jnp.float32)
    rank = jnp.dot(ones, (row <= col).astype(jnp.float32), preferred_element_type=jnp.float32)
    yield
    rank = (rank[0:1] + 0.5).astype(jnp.int32) - 1
    spread = [(leaving & (rank + 64 * k == row)).astype(jnp.float32) for k in range(2)]
    yield
    keep = [jnp.transpose(half) for half in spread]
    yield
    for k in range(2):
        spread_ref[:, k * LANES : (k + 1) * LANES] = spread[k].astype(jnp.bfloat16)
        keep_ref[k * LANES : (k + 1) * LANES] = keep[k].astype(jnp.bfloat16)
    group = jnp.broadcast_to(slot % LANES // 16, (8, LANES)).astype(jnp.float32)
    far_group_ref[...] = jnp.dot(group, keep[0] + keep[1], preferred_element_type=jnp.float32)


def pack_kernel(
    inverse_hbm,
    wind_hbm,
    links_hbm,
    state_hbm,
    prev_hbm,
    matrix_ref,
    packed_ref,
    off_ref,
    on_ref,
    target_ref,
    wind_ref,
    state_ref,
    prev_ref,
    inverse_ref,
    links_ref,
    sems,
):
    pairs = [(links_hbm, links_ref), (inverse_hbm, inverse_ref), (wind_hbm, wind_ref)]
    for at in chunks(state_ref):
        pairs += [(state_hbm.at[:, at], state_ref.at[:, at]), (prev_hbm.at[:, at], prev_ref.at[:, at])]
    copies = [pltpu.make_async_copy(a, b, sems.at[i]) for i, (a, b) in enumerate(pairs)]
    for copy in copies:
        copy.start()
    copies[0].wait()
    devices = lax.axis_size(AXES)
    elements = links_ref.shape[2]
    targets = edge_targets(links_ref, lax.axis_index(AXES) * elements, elements * devices)
    groups, lev = inverse_ref.shape[0], inverse_ref.shape[1]
    copies[1].wait()
    eye = lax.broadcasted_iota(jnp.int32, (lev, lev), 0) == lax.broadcasted_iota(jnp.int32, (lev, lev), 1)
    eye = eye.astype(jnp.float32)
    blank = jnp.zeros((lev, LANES - lev), jnp.float32)
    matrix = [jnp.concatenate([inverse_ref[c] - eye, blank], axis=1) for c in range(groups)]
    matrix_ref[...] = jnp.concatenate(matrix, axis=0).astype(jnp.bfloat16)
    packed_ref[...] = packed_matrices(matrix).astype(jnp.bfloat16)
    copies[2].wait()
    target_ref[...] = targets
    end = off_ref.shape[1]
    filler = jnp.zeros((8, LANES), jnp.float32)
    flat_wind = wind_ref[...].reshape(2 * lev, LANES)
    for k in range(3):
        piece = jnp.concatenate([flat_wind[48 * k : 48 * k + 48], targets, filler], axis=0)
        piece = piece.astype(jnp.bfloat16)
        off_ref[k, end - 64 : end] = piece
        on_ref[k, end - 64 : end] = piece
    chosen = sides()
    odd = jnp.where(on_odd(), 3, 0)
    quarter = lane_ids() // 32
    for j, at in enumerate(chunks(state_ref)):
        copies[3 + 2 * j].wait()
        copies[4 + 2 * j].wait()
        off, on = packed_halves([state_ref[k, at] for k in range(PARTS)], chosen)
        for k in range(2):
            off_ref[k, at] = off[k].astype(jnp.bfloat16)
            on_ref[k, at] = on[k].astype(jnp.bfloat16)
        to_off = jnp.zeros((CHUNK, LANES), jnp.float32)
        to_on = to_off
        for k in range(PARTS):
            turned = prev_ref[k, at].astype(jnp.float32)
            turned = pltpu.roll(turned, 32 * k, 1) if k else turned
            to_off = jnp.where(quarter == (odd + k) % 4, turned, to_off)
            to_on = jnp.where(quarter == (3 - odd + k) % 4, turned, to_on)
        off_ref[2, at] = to_off.astype(jnp.bfloat16)
        on_ref[2, at] = to_on.astype(jnp.bfloat16)


def chunks(ref):
    return [pl.ds(start, CHUNK) for start in range(0, ref.shape[1], CHUNK)]


def in_turns(first, count, stages, together=False):
    running = []
    for j in range(count):
        running.append(stages(pl.ds((first + j) * CHUNK, CHUNK), pl.ds(j * CHUNK, CHUNK), j))
    waiting, started = list(running), []
    while waiting or started:
        while waiting:
            started.append(waiting.pop(0))
            if not together:
                break
        started = [one for one in started if next(one, started) is not started]


def column_pair(pair):
    lev = pair.shape[0] // 2
    blank = jnp.zeros((LANES - lev, 2 * LANES), jnp.float32)
    pair = jnp.concatenate([pair[:lev], pair[lev:]], axis=1)
    high = pair.astype(jnp.bfloat16).astype(jnp.float32)
    return jnp.concatenate([high, blank, pair - high, blank], axis=0).astype(jnp.bfloat16)


def chosen_rows(product, group, chosen=None, first=0):
    lev = 72
    for c in range(product.shape[0] // lev):
        part = product[c * lev : (c + 1) * lev]
        chosen = part if chosen is None else jnp.where(group == first + c, part, chosen)
    return chosen


def as_rows(pair):
    return jnp.concatenate([pair[:, :LANES], pair[:, LANES:]], axis=0)


def column_group(slot_ref):
    slot = slot_ref[...]
    return jnp.where(slot // LANES == lax.axis_index(AXES), 0, 8) + slot % LANES // 16


def flat(value):
    return value.astype(jnp.float32).reshape(-1, LANES)


def moved(value, slope, blow_x, blow_y):
    rows, lev = value.shape[0], blow_x.shape[0]
    value = value.astype(jnp.bfloat16)
    both = jnp.dot(jnp.concatenate([value, value], axis=1), slope, preferred_element_type=jnp.float32)
    both = both.reshape(rows // lev, lev, 2 * LANES)
    motion = both[..., :LANES] * blow_x + both[..., LANES:] * blow_y
    return motion.reshape(rows, LANES).astype(jnp.bfloat16)


def sum_block(source, targets, slots, own):
    row = lax.broadcasted_iota(jnp.int32, (LANES, LANES), 0)
    total = jnp.zeros((LANES, LANES), jnp.float32)
    if own:
        total = (row == lax.broadcasted_iota(jnp.int32, (LANES, LANES), 1)).astype(jnp.float32)
    place = {
        "own": row,
        "own turned": jnp.where(row < 64, row + 64, row - 64),
        "near": jnp.where(row < 64, row + LANES, row - LANES),
        "near turned": jnp.where(row < 64, row - 64, row + 64),
        "outer": jnp.where(row < 64, row - LANES, row + LANES),
        "outer turned": jnp.where(row < 64, row + LANES + 64, row - LANES - 64),
    }[source]
    for s in range(2):
        total = total + ((place == targets[s : s + 1]) & slots[s]).astype(jnp.float32)
    return (total * point_sets()[1]).astype(jnp.bfloat16)


def inner_lanes():
    quarter = lane_ids() // 32
    return (quarter == 1) | (quarter == 2)


class Physics:
    def __init__(self, slot_ref):
        group = column_group(slot_ref)
        self.here = group < 8
        self.group = jnp.concatenate([group, group], axis=1)
        self.inner = inner_lanes()
        self.chosen = sides()

    def take_own(self, own_ref):
        self.own = jnp.concatenate([own_ref[...], own_ref[...]], axis=1)

    def take_far(self, far, keep_ref, spread_ref, far_group_ref):
        self.far = far
        self.keep, self.spread = keep_ref[...], spread_ref[...]
        group = (far_group_ref[0:1, :] + 0.5).astype(jnp.int32)
        self.far_group = jnp.concatenate([group, group], axis=1)

    def begin(self, wind_ref, target_ref, slope_ref):
        slots, _ = point_sets()
        self.sums = sum_block("own", target_ref[...].astype(jnp.int32) - 32, slots, True)
        self.blow = [-time_step * wind_ref[d] for d in range(2)]
        self.slope = slope_ref[...]
        self.targets, self.slots = target_ref[...].astype(jnp.int32) - 32, slots

    def begin_cross(self):
        row = lax.broadcasted_iota(jnp.int32, (LANES, LANES), 0)
        col = lax.broadcasted_iota(jnp.int32, (LANES, LANES), 1) // 32
        blocks = []
        for turn in (0, 64):
            place = (row + turn) % LANES // 32
            crossing = ((place == 1) & (col == 2)) | ((place == 2) & (col == 1))
            block = sum_block("own turned" if turn else "own", self.targets, self.slots, False)
            blocks.append(jnp.where(crossing, block.astype(jnp.float32), 0.0).astype(jnp.bfloat16))
        self.cross = jnp.concatenate(blocks, axis=1)
        self.cross_blow = [jnp.where(self.inner, w, pltpu.roll(w, 64, 1)) for w in self.blow]

    def motion(self, state):
        return moved(state, self.slope, *self.blow)

    def start(self, state, prev, move_ref, at):
        motion = self.motion(state)
        move_ref[:, at] = motion.reshape(PARTS, CHUNK, LANES)
        yield
        total = jnp.dot(motion, self.sums, preferred_element_type=jnp.float32)
        return state + total + time_step * hermite(0)[0] * prev

    def own_products(self, pairs):
        ahead, rows = None, []
        for k, pair in enumerate(pairs):
            product = jnp.dot(self.own, column_pair(pair), preferred_element_type=jnp.float32)
            if k:
                rows.append(as_rows(chosen_rows(ahead, self.group)))
            ahead = product
            yield
        rows.append(as_rows(chosen_rows(ahead, self.group)))
        return rows

    def far_products(self, pairs):
        high = [pair.astype(jnp.bfloat16) for pair in pairs]
        both = [jnp.concatenate(high[k : k + 2], axis=1) for k in (0, 2)]
        few = jnp.dot(jnp.concatenate(both, axis=0), self.keep, preferred_element_type=jnp.float32)
        yield
        size = pairs[0].shape[0]
        lev = size // 2
        blank = jnp.zeros((LANES - lev, 2 * LANES), jnp.float32)
        products, rows = [], []
        for k in range(2):
            part = few[k * size : (k + 1) * size]
            part = jnp.concatenate([part[:lev], part[lev:]], axis=1)
            column = jnp.concatenate([part, blank], axis=0).astype(jnp.bfloat16)
            products.append(jnp.dot(self.far, column, preferred_element_type=jnp.float32))
            yield
        for k in range(2):
            rows.append(as_rows(chosen_rows(products[k], self.far_group)))
        rows = jnp.concatenate(rows, axis=0).astype(jnp.bfloat16)
        wide = jnp.dot(rows, self.spread, preferred_element_type=jnp.float32)
        yield
        return [wide[k * size : (k + 1) * size, c : c + LANES] for k in range(2) for c in (0, LANES)]

    def merged(self, own, far):
        return [jnp.where(self.here, a, b) for a, b in zip(own, far)]

    def finish(self, start, prev, tends, here_at, tend_ref, ahead_ref, off_ref, on_ref, lean=False):
        late = time_step * hermite(0)[1]
        early_1, late_1 = (time_step * w for w in hermite(1))
        ahead, force = [], []
        for k, tend in enumerate(tends):
            tend = tend.astype(jnp.bfloat16)
            tend_ref[k, here_at] = tend
            tend = tend.astype(jnp.float32)
            ahead.append(start[k] + late * tend)
            ahead_ref[k, here_at] = ahead[k]
            force.append(jnp.where(self.inner, early_1 * prev[k] + late_1 * tend, tend))
        middle = [jnp.where(self.inner, ahead[k], pltpu.roll(ahead[k + 2], 64, 1)) for k in range(2)]
        if lean:
            motion = moved(jnp.concatenate(middle, axis=0), self.slope, *self.cross_blow)
            yield
            cross = jnp.dot(motion, self.cross, preferred_element_type=jnp.float32)
            yield
            for k in range(PARTS):
                rows = slice(k % 2 * CHUNK, (k % 2 + 1) * CHUNK)
                force[k] = force[k] + cross[rows, k // 2 * LANES : (k // 2 + 1) * LANES]
            to_off, to_on = packed_quarters(ahead, jnp.where(on_odd(), 2, 1), jnp.where(on_odd(), 1, 2))
            off_ref[0, here_at] = to_off.astype(jnp.bfloat16)
            on_ref[0, here_at] = to_on.astype(jnp.bfloat16)
        else:
            for k in range(2):
                off_ref[k, here_at] = middle[k].astype(jnp.bfloat16)
                on_ref[k, here_at] = middle[k].astype(jnp.bfloat16)
        off, on = packed_halves(force, self.chosen)
        at = off_ref.shape[0] - 2
        for k in range(2):
            off_ref[at + k, here_at] = off[k].astype(jnp.bfloat16)
            on_ref[at + k, here_at] = on[k].astype(jnp.bfloat16)


def own_kernel(
    first, count, state_ref, prev_ref, wind_ref, target_ref, slope_ref, slot_ref, own_ref, part_ref, start_ref, move_ref, *tables
):
    physics = Physics(slot_ref)
    physics.take_own(own_ref)
    physics.begin(wind_ref, target_ref, slope_ref)

    def stages(at, here_at, j):
        parts, start, *_ = yield from mixed(
            physics.own_products([state_ref[k, at] for k in range(PARTS)]),
            physics.start(flat(state_ref[:, at]), flat(prev_ref[:, at]), move_ref, here_at),
            *([leaving_tables(slot_ref, *tables)] if j == 0 else []),
        )
        start_ref[:, here_at] = start.reshape(PARTS, CHUNK, LANES)
        for k, part in enumerate(parts):
            part_ref[k, here_at] = part

    in_turns(first, count, stages, True)


def far_kernel(
    first,
    count,
    state_ref,
    prev_ref,
    slot_ref,
    packed_ref,
    keep_ref,
    spread_ref,
    far_group_ref,
    part_ref,
    start_ref,
    tend_ref,
    ahead_ref,
    off_ref,
    on_ref,
    far_ref,
):
    physics = Physics(slot_ref)
    matrices = unpacked_matrices(packed_ref[...].astype(jnp.float32)).astype(jnp.bfloat16)
    far_ref[...] = matrices
    physics.take_far(matrices, keep_ref, spread_ref, far_group_ref)

    def stages(at, here_at, _):
        far = yield from physics.far_products([state_ref[k, at] for k in range(PARTS)])
        tends = physics.merged([part_ref[k, here_at] for k in range(PARTS)], far)
        start = [start_ref[k, here_at] for k in range(PARTS)]
        prev = [prev_ref[k, at].astype(jnp.float32) for k in range(PARTS)]
        yield from physics.finish(start, prev, tends, here_at, tend_ref, ahead_ref, off_ref, on_ref)

    in_turns(first, count, stages, True)


def physics_kernel(
    first,
    count,
    state_ref,
    prev_ref,
    wind_ref,
    target_ref,
    slope_ref,
    slot_ref,
    own_ref,
    far_ref,
    keep_ref,
    spread_ref,
    far_group_ref,
    tend_ref,
    ahead_ref,
    off_ref,
    on_ref,
    move_ref,
):
    physics = Physics(slot_ref)
    physics.take_own(own_ref)
    physics.take_far(far_ref[...], keep_ref, spread_ref, far_group_ref)
    physics.begin(wind_ref, target_ref, slope_ref)
    physics.begin_cross()

    def stages(at, here_at, _):
        pairs = [state_ref[k, at] for k in range(PARTS)]
        far, own, start = yield from mixed(
            physics.far_products(pairs),
            physics.own_products(pairs),
            physics.start(flat(state_ref[:, at]), flat(prev_ref[:, at]), move_ref, here_at),
        )
        start = [start[k * CHUNK : (k + 1) * CHUNK] for k in range(PARTS)]
        tends = physics.merged(own, far)
        prev = [prev_ref[k, at].astype(jnp.float32) for k in range(PARTS)]
        yield from physics.finish(start, prev, tends, here_at, tend_ref, ahead_ref, off_ref, on_ref, True)

    in_turns(first, count, stages, True)


def near_kernel(
    state_ref,
    wind_ref,
    target_ref,
    slope_ref,
    off_ref,
    on_ref,
    prev_ref,
    *rest,
):
    parts, outs = rest[:-8], rest[-8:]
    own_ref, near_ref, near_add_ref, own_force_ref, near_force_ref, sum_ref, edge_sum_ref, blow_ref = outs
    lev = wind_ref.shape[1]
    slots, _ = point_sets()
    chosen = sides()
    end = off_ref.shape[1]

    def extra(ref, k):
        return ref[k, end - 64 : end].astype(jnp.float32)

    def winds(ref):
        whole = jnp.concatenate([extra(ref, k)[:48] for k in range(3)], axis=0)
        return whole[:lev], whole[lev:]

    def targets(ref):
        return extra(ref, 0)[48:56].astype(jnp.int32) - 32

    own_t = target_ref[...].astype(jnp.int32) - 32
    near_t = jnp.where(chosen, targets(off_ref), targets(on_ref))
    near_t = near_t + jnp.where(lane_ids() < 64, LANES, -LANES)
    own_sums = jnp.concatenate(
        [sum_block("own", own_t, slots, True), sum_block("own", near_t, slots, False)], axis=1
    )
    near_sums = jnp.concatenate(
        [sum_block("near", own_t, slots, False), sum_block("near", near_t, slots, True)], axis=1
    )
    sum_ref[:LANES] = own_sums
    sum_ref[LANES:] = near_sums
    nothing = jnp.zeros((LANES, LANES), jnp.bfloat16)
    first_sums = jnp.concatenate([nothing, own_sums[:, LANES:]], axis=1)
    first_sums = jnp.concatenate([near_sums, first_sums], axis=0)
    for k, turn in enumerate(("", " turned")):
        edge_sum_ref[k, :LANES] = near_sums
        edge_sum_ref[k, LANES:, :LANES] = nothing
        edge_sum_ref[k, LANES:, LANES:] = sum_block("outer" + turn, near_t, slots, False)
        edge_sum_ref[2 + k, :LANES, :LANES] = own_sums[:, :LANES]
        edge_sum_ref[2 + k, LANES:, :LANES] = sum_block("near" + turn, own_t, slots, False)
    inner = inner_lanes()
    off_w, on_w = winds(off_ref), winds(on_ref)
    for d in range(2):
        blow_ref[0, d] = -time_step * wind_ref[d]
        near_w = -time_step * jnp.where(chosen, off_w[d], on_w[d])
        outer_w = -time_step * jnp.where(chosen, on_w[d], off_w[d])
        blow_ref[1, d] = near_w
        blow_ref[2, d] = jnp.where(inner, outer_w, pltpu.roll(outer_w, 64, 1))
        blow_ref[3, d] = jnp.where(inner, pltpu.roll(near_w, 64, 1), near_w)

    slope = slope_ref[...]
    early = time_step * hermite(0)[0]
    early_1, late_1 = (time_step * w for w in hermite(1))
    early_2, late_2 = (time_step * w for w in hermite(2))
    own_blow = (blow_ref[0, 0], blow_ref[0, 1])
    near_blow = (blow_ref[1, 0], blow_ref[1, 1])

    def stages(at, here_at, tend_ref, ahead_ref, move_ref):
        off, on = off_ref[:, at].astype(jnp.float32), on_ref[:, at].astype(jnp.float32)
        near = whole_halves(off[:2], on[:2], chosen)
        own_move = move_ref[:, here_at].reshape(-1, LANES)
        near_move = moved(near, slope, *near_blow)
        yield
        total = jnp.concatenate([near_move, own_move], axis=1)
        total = jnp.dot(total, first_sums, preferred_element_type=jnp.float32)
        near_total = total[:, LANES:]
        kept = jnp.where(inner, 0.0, whole_quarters(off[2], on[2], chosen))
        near = near + near_total + early * kept
        near_ref[:, at] = near.reshape(PARTS, CHUNK, LANES)
        near_force_ref[:, at] = (early_2 * kept).reshape(PARTS, CHUNK, LANES)
        own = flat(ahead_ref[:, here_at]) + total[:, :LANES]
        yield
        own_move = moved(own, slope, *own_blow)
        yield
        total = jnp.dot(own_move, own_sums, preferred_element_type=jnp.float32)
        own_prev, own_tend = flat(prev_ref[:, at]), flat(tend_ref[:, here_at])
        own = own + total[:, :LANES] + (early_1 * own_prev + late_1 * own_tend)
        own_ref[:, at] = own.reshape(PARTS, CHUNK, LANES)
        own_force = early_2 * own_prev + late_2 * own_tend
        own_force_ref[:, at] = own_force.reshape(PARTS, CHUNK, LANES)
        near_add = total[:, LANES:] + early_1 * kept
        near_add_ref[:, at] = near_add.reshape(PARTS, CHUNK, LANES)

    places = []
    for refs in zip(parts[::3], parts[1::3], parts[2::3]):
        places += [(here_at, *refs) for here_at in chunks(refs[0])]
    in_turns(0, len(places), lambda at, _, j: stages(at, *places[j]))


def advance_kernel(
    first,
    last,
    own_ref,
    near_ref,
    near_add_ref,
    own_force_ref,
    near_force_ref,
    off_ref,
    on_ref,
    slope_ref,
    sum_ref,
    edge_sum_ref,
    blow_ref,
    *rest,
):
    if last:
        tend_ref, done_ref, out_hbm, out_ref, sems = rest
        copies = [pltpu.make_async_copy(done_ref, out_hbm.at[:, pl.ds(0, done_ref.shape[1])], sems.at[0])]
    else:
        *tend_refs, out_ref, tend_hbm, sems = rest
        tend_ref = tend_refs[0]
        copies, row = [], 0
        for k, ref in enumerate(tend_refs):
            copies.append(pltpu.make_async_copy(ref, tend_hbm.at[:, pl.ds(row, ref.shape[1])], sems.at[k]))
            row += ref.shape[1]
    for copy in copies:
        copy.start()
    inner = inner_lanes()
    chosen = sides()
    slope = slope_ref[...]
    lates = [time_step * hermite(s)[1] for s in range(SUBSTEPS)]

    def advect(value, unit):
        return moved(value, slope, blow_ref[unit, 0], blow_ref[unit, 1])

    def gather(pieces, matrix):
        return jnp.dot(jnp.concatenate(pieces, axis=1), matrix, preferred_element_type=jnp.float32)

    def gather_shared(whole, packed, which, width):
        half = packed.shape[0]
        parts = [
            gather([whole[k * half : (k + 1) * half], packed], edge_sum_ref[which + k, :, :width])
            for k in range(2)
        ]
        return jnp.concatenate(parts, axis=0)

    def stages(at, here_at, j):
        off, on = off_ref[:, here_at].astype(jnp.float32), on_ref[:, here_at].astype(jnp.float32)
        if last:
            middle = whole_quarters(off[0], on[0], chosen)
        else:
            off_mid, on_mid = flat(off[:2]), flat(on[:2])
            middle = [jnp.where(chosen, off_mid, on_mid), jnp.where(chosen, on_mid, off_mid)]
            middle = jnp.concatenate([middle[0], pltpu.roll(middle[1], 64, 1)], axis=0)
            outer = jnp.where(chosen == inner, on_mid, off_mid)
        received = whole_halves(off[-2:], on[-2:], chosen)
        near = jnp.where(inner, middle, flat(near_ref[:, at]) + lates[0] * received)
        moves = [advect(near, 1)] if last else [advect(near, 1), advect(outer, 2)]
        yield
        if last:
            total = jnp.dot(moves[0], sum_ref[LANES:], preferred_element_type=jnp.float32)
        else:
            total = gather_shared(*moves, 0, 2 * LANES)
        own = flat(own_ref[:, at]) + total[:, :LANES]
        force = received * jnp.where(inner, 1.0, lates[1])
        near = near + total[:, LANES:] + (flat(near_add_ref[:, at]) + force)
        yield
        moves = [advect(own, 0), advect(near, 1)]
        yield
        total = gather(moves, sum_ref[...])
        own = own + total[:, :LANES] + flat(own_force_ref[:, at])
        near = near + total[:, LANES:] + (flat(near_force_ref[:, at]) + lates[2] * received)
        yield
        half = near.shape[0] // 2
        near = jnp.where(inner, pltpu.roll(near[half:], 64, 1), near[:half])
        moves = advect(own, 0), advect(near, 3)
        yield
        total = gather_shared(*moves, 2, LANES)
        out = own + total + lates[3] * flat(tend_ref[:, here_at])
        out_ref[:, here_at] = out.reshape(PARTS, CHUNK, LANES)
        if last:
            for k in range(PARTS):
                copies.append(
                    pltpu.make_async_copy(
                        out_ref.at[k, here_at], out_hbm.at[k, at], sems.at[1 + PARTS * j + k]
                    )
                )
                copies[-1].start()

    in_turns(first, out_ref.shape[1] // CHUNK, stages, last)
    for copy in copies:
        copy.wait()


def exchanged(off, on):
    count = lax.axis_size(AXES)
    across = [(i, (i + 1) % count if i % 2 else (i - 1) % count) for i in range(count)]
    inside = [(i, i ^ 1) for i in range(count)]
    on = lax.ppermute(on, AXES, inside)
    return lax.ppermute(off, AXES, across), on


def per_device(state, prev_tendency, wind, edge_links, swap_slot, inverse):
    devices = lax.axis_size(AXES)
    shape = state.shape
    lev = shape[1]
    rows = shape[0] * lev // PARTS
    params = pltpu.CompilerParams(vmem_limit_bytes=VMEM)
    bf16, f32 = jnp.bfloat16, jnp.float32
    inner = pl.BlockSpec(memory_space=pltpu.VMEM)
    outer = pl.BlockSpec(memory_space=pltpu.HBM)

    def like(count, kind, length=rows):
        return pltpu.VMEM((count, length, LANES), kind)

    def table(kind, *size):
        return pltpu.VMEM(size, kind)

    def call(body, ins, outs, name, passes, **more):
        size = sum(math.prod(array.shape) * array.dtype.itemsize for array in ins)
        cost = pl.CostEstimate(
            flops=passes * 2 * PARTS * rows * 256 * 256, bytes_accessed=2 * size, transcendentals=0
        )
        more = {"in_specs": [inner] * len(ins), "out_specs": (inner,) * len(outs)} | more
        return pl.pallas_call(
            body, out_shape=outs, compiler_params=params, cost_estimate=cost, name=name, **more
        )(*ins)

    slot = swap_slot.reshape(1, LANES)
    slope = jnp.asarray(derivative_matrix())
    message = like(3, bf16, rows + 64)
    inputs = (
        inverse,
        wind,
        edge_links,
        state.reshape(PARTS, rows, LANES),
        prev_tendency.reshape(PARTS, rows, LANES),
    )
    inputs = tuple(pltpu.with_memory_space_constraint(array, pltpu.HBM) for array in inputs)
    matrices, packed, to_off, to_on, targets, wind, state, prev = call(
        pack_kernel,
        inputs,
        (
            table(bf16, inverse.shape[0] * lev, LANES),
            table(bf16, 368, LANES),
            message,
            message,
            table(f32, 8, LANES),
            table(f32, *wind.shape),
            like(4, f32),
            like(4, bf16),
        ),
        "pack",
        2,
        in_specs=[outer] * len(inputs),
        scratch_shapes=[
            pltpu.VMEM(inverse.shape, f32),
            pltpu.VMEM(edge_links.shape, jnp.int32),
            pltpu.SemaphoreType.DMA((3 + 2 * (rows // CHUNK),)),
        ],
    )
    far_packed = lax.ppermute(packed, AXES, [(i, i ^ (devices // 2)) for i in range(devices)])
    off, on = exchanged(to_off, to_on)
    halves = []
    first = 0
    shared = (wind, targets, slope, slot, matrices)
    for count in SPLIT:
        size = count * CHUNK
        sent = like(3 if first else 4, bf16, size)
        outs = (like(4, bf16, size), like(4, f32, size), sent, sent)
        if first == 0:
            part, start, move, *tables = call(
                functools.partial(own_kernel, first, count),
                (state, prev) + shared,
                (like(4, f32, size), like(4, f32, size), like(4, bf16, size))
                + (table(bf16, 2 * LANES, LANES), table(bf16, LANES, 2 * LANES), table(f32, 8, LANES)),
                "own",
                3 * count,
            )
            ins = (state, prev, slot, far_packed, *tables, part, start)
            body, name = far_kernel, "far"
            outs += (table(bf16, *matrices.shape),)
        else:
            ins = (state, prev) + shared + (far_matrices, *tables)
            body, name = physics_kernel, "physics"
            outs += (like(4, bf16, size),)
        tend, ahead, to_off, to_on, *more = call(
            functools.partial(body, first, count), ins, outs, name, 5 * count
        )
        if first:
            move = more[0]
        else:
            far_matrices = more[0]
        halves.append((first, count, tend, (tend, ahead, move), exchanged(to_off, to_on)))
        first += count
    parts = sum((part for _, _, _, part, _ in halves), ())
    own, near, near_add, own_force, near_force, sums, edge_sums, blow = call(
        near_kernel,
        (state, wind, targets, slope, off, on, prev) + parts,
        (
            like(4, f32),
            like(4, f32),
            like(4, f32),
            like(4, f32),
            like(4, f32),
            table(bf16, 2 * LANES, 2 * LANES),
            table(bf16, 4, 2 * LANES, 2 * LANES),
            table(f32, 4, 2, lev, LANES),
        ),
        "near",
        16,
    )
    tends = tuple(tend for _, _, tend, _, _ in halves)
    out_spec = jax.ShapeDtypeStruct((PARTS, rows, LANES), f32)
    tend_spec = jax.ShapeDtypeStruct((PARTS, rows, LANES), bf16)
    for part, (first, count, tend, _, (off, on)) in enumerate(halves):
        ins = (own, near, near_add, own_force, near_force, off, on, slope, sums, edge_sums, blow)
        size = count * CHUNK
        if part == 0:
            done, tend_out = call(
                functools.partial(advance_kernel, first, False),
                ins + tends,
                (like(4, f32, size), tend_spec),
                "advance",
                5 * count,
                out_specs=(inner, outer),
                scratch_shapes=[pltpu.SemaphoreType.DMA((len(tends),))],
            )
        else:
            (out,) = call(
                functools.partial(advance_kernel, first, True),
                ins + (tend, done),
                (out_spec,),
                "advance",
                5 * count,
                out_specs=(outer,),
                scratch_shapes=[pltpu.VMEM((PARTS, size, LANES), f32), pltpu.SemaphoreType.DMA((1 + PARTS * count,))],
            )
    tend = tend_out
    return (out.reshape(shape), tend.reshape(shape))


def solution(mesh):
    columns = P(None, None, AXES)
    return jax.shard_map(
        per_device,
        mesh=mesh,
        in_specs=(columns, columns, columns, columns, P(AXES), P(AXES, None, None)),
        out_specs=(columns, columns),
        check_vma=False,
    )
```

```python
import functools
import math

import jax
import jax.numpy as jnp
import numpy as np
from jax import lax
from jax.experimental import pallas as pl
from jax.experimental.pallas import tpu as pltpu
from jax.sharding import PartitionSpec as P

SUBSTEPS = 4
AXES = ("gx", "gy")
LANES = 128
CHUNK = 144
SPLIT = (3, 2)
PARTS = 4
VMEM = 16 * 1024 * 1024

time_step = 0.2
edge_points = ((0, 1, 2, 3), (3, 7, 11, 15), (15, 14, 13, 12), (12, 8, 4, 0))


def point_tables():
    edge_of = np.zeros((2, 16), np.int32)
    spot_of = np.zeros((2, 16), np.int32)
    weight_of = np.zeros((2, 16), np.float32)
    filled = np.zeros(16, np.int32)
    for k in range(4):
        for m in range(4):
            p = edge_points[k][m]
            s = filled[p]
            edge_of[s, p] = k
            spot_of[s, p] = m
            weight_of[s, p] = 1.0
            filled[p] = s + 1
    return (edge_of, spot_of, weight_of)


def gll_derivative():
    gll_nodes = np.array([-1.0, -1.0 / np.sqrt(5.0), 1.0 / np.sqrt(5.0), 1.0])
    factors = np.array(
        [np.prod([gll_nodes[i] - gll_nodes[k] for k in range(4) if k != i]) for i in range(4)]
    )
    derivative = np.zeros((4, 4))
    for i in range(4):
        for k in range(4):
            if i != k:
                derivative[i, k] = factors[i] / (factors[k] * (gll_nodes[i] - gll_nodes[k]))
            else:
                derivative[i, k] = sum(
                    (1.0 / (gll_nodes[i] - gll_nodes[j]) for j in range(4) if j != i)
                )
    return derivative


def derivative_matrix():
    derivative = gll_derivative()
    eye_block = np.eye(8)
    both = np.concatenate(
        [
            np.kron(eye_block, np.kron(derivative, np.eye(4)).T),
            np.kron(eye_block, np.kron(np.eye(4), derivative).T),
        ],
        axis=1,
    )
    high = both.astype(jnp.bfloat16)
    low = (both - high.astype(np.float64)).astype(jnp.bfloat16)
    return np.concatenate([high, low], axis=0)


def hermite(substep):
    instant = (substep + 1.0) / SUBSTEPS
    square = instant * instant
    cube = square * instant
    h00 = 2.0 * cube - 3.0 * square + 1.0
    h01 = -2.0 * cube + 3.0 * square
    slope = cube - 2.0 * square + instant + (cube - square)
    return (h00 - slope, h01 + slope)


def lane_ids(rows=1):
    return lax.broadcasted_iota(jnp.int32, (rows, LANES), 1)


def point_sets():
    point = lane_ids() % 16
    across = (point // 4 == 0) | (point // 4 == 3)
    along = (point % 4 == 0) | (point % 4 == 3)
    slots = (across | along, across & along)
    share = jnp.where(slots[1], 1.0 / 3.0, jnp.where(slots[0], 0.5, 1.0)).astype(jnp.float32)
    return slots, share


def edge_targets(links_ref, first_elem, element_count):
    edge_of, spot_of, _ = point_tables()
    elements = links_ref.shape[2]
    own = first_elem + lax.broadcasted_iota(jnp.int32, (4, elements), 1)
    apart = links_ref[0] - own
    half = element_count // 2
    apart = jnp.where(apart > half, apart - element_count, apart)
    apart = jnp.where(apart < -half, apart + element_count, apart) + 2
    both = jnp.concatenate([apart, links_ref[1]], axis=0).astype(jnp.float32)
    spread = lax.broadcasted_iota(jnp.int32, (elements, LANES), 0)
    spread = (spread == lax.broadcasted_iota(jnp.int32, (elements, LANES), 1) // 16).astype(jnp.float32)
    both = jnp.dot(both, spread, preferred_element_type=jnp.float32)
    both = (both + 0.5).astype(jnp.int32)
    lane = lane_ids()
    point = lane % 16
    rows = []
    for s in range(2):
        edge = jnp.zeros((1, LANES), jnp.int32)
        spot = edge
        for p in range(16):
            edge = jnp.where(point == p, int(edge_of[s, p]), edge)
            spot = jnp.where(point == p, int(spot_of[s, p]), spot)
        away, far = both[0:1], both[4:5]
        for k in range(1, 4):
            away = jnp.where(edge == k, both[k : k + 1], away)
            far = jnp.where(edge == k, both[4 + k : 5 + k], far)
        place = jnp.where(far == 2, 12 + spot, 4 * spot)
        place = jnp.where(far == 1, 15 - 4 * spot, place)
        place = jnp.where(far == 0, 3 - spot, place)
        rows.append(lane - point + 16 * away + place)
    rows = jnp.concatenate(rows + [jnp.zeros((6, LANES), jnp.int32)], axis=0)
    return rows.astype(jnp.float32)


def on_odd():
    return lax.axis_index(AXES) % 2 == 1


def sides():
    return (lane_ids() < 64) == on_odd()


def packed_halves(value, chosen):
    away = [pltpu.roll(value[k + 2], 64, 1) for k in range(2)]
    off = [jnp.where(chosen, away[k], value[k]) for k in range(2)]
    on = [jnp.where(chosen, value[k], away[k]) for k in range(2)]
    return off, on


def whole_halves(off, on, chosen):
    count, rows = off.shape[0], off.shape[1]
    direct = jnp.where(chosen, off, on).reshape(count * rows, LANES)
    turned = jnp.where(chosen, on, off).reshape(count * rows, LANES)
    return jnp.concatenate([direct, pltpu.roll(turned, 64, 1)], axis=0)


def mixed(*generators):
    values = {}
    while len(values) < len(generators):
        for i, one in enumerate(generators):
            if i not in values:
                try:
                    next(one)
                except StopIteration as end:
                    values[i] = end.value
        yield
    return [values[i] for i in range(len(generators))]


def packed_quarters(value, first_off, first_on):
    quarter = lane_ids() // 32
    to_off = to_on = jnp.zeros(value[0].shape, jnp.float32)
    for k, turned in enumerate(value):
        turned = pltpu.roll(turned, 32 * k, 1) if k else turned
        to_off = jnp.where(quarter == (first_off + k) % 4, turned, to_off)
        to_on = jnp.where(quarter == (first_on + k) % 4, turned, to_on)
    return to_off, to_on


def whole_quarters(off, on, chosen):
    kept = [jnp.where(chosen, off, on)]
    for k in range(1, PARTS):
        turned = [pltpu.roll(side, LANES - 32 * k, 1) for side in (off, on)]
        kept.append(jnp.where(chosen, *turned))
    return jnp.concatenate(kept, axis=0)


def packed_matrices(matrix):
    lane = lane_ids()
    half = len(matrix) // 2
    rows = [jnp.where(lane < 64, matrix[c], pltpu.roll(matrix[c + half], 64, 1)) for c in range(half)]
    rest = jnp.zeros_like(matrix[0])
    for c, value in enumerate(matrix):
        rest = jnp.where(lane // 8 == c, pltpu.roll(value, (8 * c - 64) % LANES, 1), rest)
    return jnp.concatenate(rows + [rest, jnp.zeros((8, LANES), jnp.float32)], axis=0)


def unpacked_matrices(packed):
    lane = lane_ids()
    lev, half = 72, 4
    rest = packed[half * lev : (half + 1) * lev]
    rows = []
    for c in range(2 * half):
        main = packed[c % half * lev : (c % half + 1) * lev]
        main = main if c < half else pltpu.roll(main, 64, 1)
        tail = jnp.where(lane < lev, pltpu.roll(rest, (64 - 8 * c) % LANES, 1), 0.0)
        rows.append(jnp.where(lane < 64, main, tail))
    return jnp.concatenate(rows, axis=0)


def leaving_tables(slot_ref, keep_ref, spread_ref, far_group_ref):
    slot = slot_ref[...]
    leaving = slot // LANES != lax.axis_index(AXES)
    row = lax.broadcasted_iota(jnp.int32, (LANES, LANES), 0)
    col = lax.broadcasted_iota(jnp.int32, (LANES, LANES), 1)
    ones = jnp.broadcast_to(leaving, (8, LANES)).astype(jnp.float32)
    rank = jnp.dot(ones, (row <= col).astype(jnp.float32), preferred_element_type=jnp.float32)
    yield
    rank = (rank[0:1] + 0.5).astype(jnp.int32) - 1
    spread = [(leaving & (rank + 64 * k == row)).astype(jnp.float32) for k in range(2)]
    yield
    keep = [jnp.transpose(half) for half in spread]
    yield
    for k in range(2):
        spread_ref[:, k * LANES : (k + 1) * LANES] = spread[k].astype(jnp.bfloat16)
        keep_ref[k * LANES : (k + 1) * LANES] = keep[k].astype(jnp.bfloat16)
    group = jnp.broadcast_to(slot % LANES // 16, (8, LANES)).astype(jnp.float32)
    far_group_ref[...] = jnp.dot(group, keep[0] + keep[1], preferred_element_type=jnp.float32)


def pack_kernel(
    inverse_hbm,
    wind_hbm,
    links_hbm,
    state_hbm,
    prev_hbm,
    matrix_ref,
    packed_ref,
    off_ref,
    on_ref,
    target_ref,
    wind_ref,
    state_ref,
    prev_ref,
    inverse_ref,
    links_ref,
    sems,
):
    pairs = [(links_hbm, links_ref), (inverse_hbm, inverse_ref), (wind_hbm, wind_ref)]
    for at in chunks(state_ref):
        pairs += [(state_hbm.at[:, at], state_ref.at[:, at]), (prev_hbm.at[:, at], prev_ref.at[:, at])]
    copies = [pltpu.make_async_copy(a, b, sems.at[i]) for i, (a, b) in enumerate(pairs)]
    for copy in copies:
        copy.start()
    copies[0].wait()
    devices = lax.axis_size(AXES)
    elements = links_ref.shape[2]
    targets = edge_targets(links_ref, lax.axis_index(AXES) * elements, elements * devices)
    groups, lev = inverse_ref.shape[0], inverse_ref.shape[1]
    copies[1].wait()
    eye = lax.broadcasted_iota(jnp.int32, (lev, lev), 0) == lax.broadcasted_iota(jnp.int32, (lev, lev), 1)
    eye = eye.astype(jnp.float32)
    blank = jnp.zeros((lev, LANES - lev), jnp.float32)
    matrix = [jnp.concatenate([inverse_ref[c] - eye, blank], axis=1) for c in range(groups)]
    matrix_ref[...] = jnp.concatenate(matrix, axis=0).astype(jnp.bfloat16)
    packed_ref[...] = packed_matrices(matrix).astype(jnp.bfloat16)
    copies[2].wait()
    target_ref[...] = targets
    end = off_ref.shape[1]
    filler = jnp.zeros((8, LANES), jnp.float32)
    flat_wind = wind_ref[...].reshape(2 * lev, LANES)
    for k in range(3):
        piece = jnp.concatenate([flat_wind[48 * k : 48 * k + 48], targets, filler], axis=0)
        piece = piece.astype(jnp.bfloat16)
        off_ref[k, end - 64 : end] = piece
        on_ref[k, end - 64 : end] = piece
    chosen = sides()
    odd = jnp.where(on_odd(), 3, 0)
    quarter = lane_ids() // 32
    for j, at in enumerate(chunks(state_ref)):
        copies[3 + 2 * j].wait()
        copies[4 + 2 * j].wait()
        off, on = packed_halves([state_ref[k, at] for k in range(PARTS)], chosen)
        for k in range(2):
            off_ref[k, at] = off[k].astype(jnp.bfloat16)
            on_ref[k, at] = on[k].astype(jnp.bfloat16)
        to_off = jnp.zeros((CHUNK, LANES), jnp.float32)
        to_on = to_off
        for k in range(PARTS):
            turned = prev_ref[k, at].astype(jnp.float32)
            turned = pltpu.roll(turned, 32 * k, 1) if k else turned
            to_off = jnp.where(quarter == (odd + k) % 4, turned, to_off)
            to_on = jnp.where(quarter == (3 - odd + k) % 4, turned, to_on)
        off_ref[2, at] = to_off.astype(jnp.bfloat16)
        on_ref[2, at] = to_on.astype(jnp.bfloat16)


def chunks(ref):
    return [pl.ds(start, CHUNK) for start in range(0, ref.shape[1], CHUNK)]


def in_turns(first, count, stages, together=False):
    running = []
    for j in range(count):
        running.append(stages(pl.ds((first + j) * CHUNK, CHUNK), pl.ds(j * CHUNK, CHUNK), j))
    waiting, started = list(running), []
    while waiting or started:
        while waiting:
            started.append(waiting.pop(0))
            if not together:
                break
        started = [one for one in started if next(one, started) is not started]


def column_pair(pair):
    lev = pair.shape[0] // 2
    blank = jnp.zeros((LANES - lev, 2 * LANES), jnp.float32)
    pair = jnp.concatenate([pair[:lev], pair[lev:]], axis=1)
    high = pair.astype(jnp.bfloat16).astype(jnp.float32)
    return jnp.concatenate([high, blank, pair - high, blank], axis=0).astype(jnp.bfloat16)


def chosen_rows(product, group, chosen=None, first=0):
    lev = 72
    for c in range(product.shape[0] // lev):
        part = product[c * lev : (c + 1) * lev]
        chosen = part if chosen is None else jnp.where(group == first + c, part, chosen)
    return chosen


def as_rows(pair):
    return jnp.concatenate([pair[:, :LANES], pair[:, LANES:]], axis=0)


def column_group(slot_ref):
    slot = slot_ref[...]
    return jnp.where(slot // LANES == lax.axis_index(AXES), 0, 8) + slot % LANES // 16


def flat(value):
    return value.astype(jnp.float32).reshape(-1, LANES)


def moved(value, slope, blow_x, blow_y):
    rows, lev = value.shape[0], blow_x.shape[0]
    value = value.astype(jnp.bfloat16)
    both = jnp.dot(jnp.concatenate([value, value], axis=1), slope, preferred_element_type=jnp.float32)
    both = both.reshape(rows // lev, lev, 2 * LANES)
    motion = both[..., :LANES] * blow_x + both[..., LANES:] * blow_y
    return motion.reshape(rows, LANES).astype(jnp.bfloat16)


def sum_block(source, targets, slots, own):
    row = lax.broadcasted_iota(jnp.int32, (LANES, LANES), 0)
    total = jnp.zeros((LANES, LANES), jnp.float32)
    if own:
        total = (row == lax.broadcasted_iota(jnp.int32, (LANES, LANES), 1)).astype(jnp.float32)
    place = {
        "own": row,
        "own turned": jnp.where(row < 64, row + 64, row - 64),
        "near": jnp.where(row < 64, row + LANES, row - LANES),
        "near turned": jnp.where(row < 64, row - 64, row + 64),
        "outer": jnp.where(row < 64, row - LANES, row + LANES),
        "outer turned": jnp.where(row < 64, row + LANES + 64, row - LANES - 64),
    }[source]
    for s in range(2):
        total = total + ((place == targets[s : s + 1]) & slots[s]).astype(jnp.float32)
    return (total * point_sets()[1]).astype(jnp.bfloat16)


def inner_lanes():
    quarter = lane_ids() // 32
    return (quarter == 1) | (quarter == 2)


class Physics:
    def __init__(self, slot_ref):
        group = column_group(slot_ref)
        self.here = group < 8
        self.group = jnp.concatenate([group, group], axis=1)
        self.inner = inner_lanes()
        self.chosen = sides()

    def take_own(self, own_ref):
        self.own = jnp.concatenate([own_ref[...], own_ref[...]], axis=1)

    def take_far(self, far, keep_ref, spread_ref, far_group_ref):
        self.far = far
        self.keep, self.spread = keep_ref[...], spread_ref[...]
        group = (far_group_ref[0:1, :] + 0.5).astype(jnp.int32)
        self.far_group = jnp.concatenate([group, group], axis=1)

    def begin(self, wind_ref, target_ref, slope_ref):
        slots, _ = point_sets()
        self.sums = sum_block("own", target_ref[...].astype(jnp.int32) - 32, slots, True)
        self.blow = [-time_step * wind_ref[d] for d in range(2)]
        self.slope = slope_ref[...]
        self.targets, self.slots = target_ref[...].astype(jnp.int32) - 32, slots

    def begin_cross(self):
        row = lax.broadcasted_iota(jnp.int32, (LANES, LANES), 0)
        col = lax.broadcasted_iota(jnp.int32, (LANES, LANES), 1) // 32
        blocks = []
        for turn in (0, 64):
            place = (row + turn) % LANES // 32
            crossing = ((place == 1) & (col == 2)) | ((place == 2) & (col == 1))
            block = sum_block("own turned" if turn else "own", self.targets, self.slots, False)
            blocks.append(jnp.where(crossing, block.astype(jnp.float32), 0.0).astype(jnp.bfloat16))
        self.cross = jnp.concatenate(blocks, axis=1)
        self.cross_blow = [jnp.where(self.inner, w, pltpu.roll(w, 64, 1)) for w in self.blow]

    def motion(self, state):
        return moved(state, self.slope, *self.blow)

    def start(self, state, prev, move_ref, at):
        motion = self.motion(state)
        move_ref[:, at] = motion.reshape(PARTS, CHUNK, LANES)
        yield
        total = jnp.dot(motion, self.sums, preferred_element_type=jnp.float32)
        return state + total + time_step * hermite(0)[0] * prev

    def own_products(self, pairs):
        ahead, rows = None, []
        for k, pair in enumerate(pairs):
            product = jnp.dot(self.own, column_pair(pair), preferred_element_type=jnp.float32)
            if k:
                rows.append(as_rows(chosen_rows(ahead, self.group)))
            ahead = product
            yield
        rows.append(as_rows(chosen_rows(ahead, self.group)))
        return rows

    def far_products(self, pairs):
        high = [pair.astype(jnp.bfloat16) for pair in pairs]
        both = [jnp.concatenate(high[k : k + 2], axis=1) for k in (0, 2)]
        few = jnp.dot(jnp.concatenate(both, axis=0), self.keep, preferred_element_type=jnp.float32)
        yield
        if self.far is None:
            self.far = self.unpack()
        size = pairs[0].shape[0]
        lev = size // 2
        blank = jnp.zeros((LANES - lev, 2 * LANES), jnp.float32)
        products, rows = [], []
        for k in range(2):
            part = few[k * size : (k + 1) * size]
            part = jnp.concatenate([part[:lev], part[lev:]], axis=1)
            column = jnp.concatenate([part, blank], axis=0).astype(jnp.bfloat16)
            products.append(jnp.dot(self.far, column, preferred_element_type=jnp.float32))
            if k:
                rows.append(as_rows(chosen_rows(products[0], self.far_group)))
            yield
        rows.append(as_rows(chosen_rows(products[1], self.far_group)))
        rows = jnp.concatenate(rows, axis=0).astype(jnp.bfloat16)
        wide = jnp.dot(rows, self.spread, preferred_element_type=jnp.float32)
        yield
        return [wide[k * size : (k + 1) * size, c : c + LANES] for k in range(2) for c in (0, LANES)]

    def merged(self, own, far):
        return [jnp.where(self.here, a, b) for a, b in zip(own, far)]

    def finish(self, start, prev, tends, here_at, tend_ref, ahead_ref, off_ref, on_ref, lean=False):
        late = time_step * hermite(0)[1]
        early_1, late_1 = (time_step * w for w in hermite(1))
        ahead, force = [], []
        for k, tend in enumerate(tends):
            tend = tend.astype(jnp.bfloat16)
            tend_ref[k, here_at] = tend
            tend = tend.astype(jnp.float32)
            ahead.append(start[k] + late * tend)
            ahead_ref[k, here_at] = ahead[k]
            force.append(jnp.where(self.inner, early_1 * prev[k] + late_1 * tend, tend))
        middle = [jnp.where(self.inner, ahead[k], pltpu.roll(ahead[k + 2], 64, 1)) for k in range(2)]
        if lean:
            motion = moved(jnp.concatenate(middle, axis=0), self.slope, *self.cross_blow)
            yield
            cross = jnp.dot(motion, self.cross, preferred_element_type=jnp.float32)
            yield
            for k in range(PARTS):
                rows = slice(k % 2 * CHUNK, (k % 2 + 1) * CHUNK)
                force[k] = force[k] + cross[rows, k // 2 * LANES : (k // 2 + 1) * LANES]
            to_off, to_on = packed_quarters(ahead, jnp.where(on_odd(), 2, 1), jnp.where(on_odd(), 1, 2))
            off_ref[0, here_at] = to_off.astype(jnp.bfloat16)
            on_ref[0, here_at] = to_on.astype(jnp.bfloat16)
        else:
            for k in range(2):
                off_ref[k, here_at] = middle[k].astype(jnp.bfloat16)
                on_ref[k, here_at] = middle[k].astype(jnp.bfloat16)
        off, on = packed_halves(force, self.chosen)
        at = off_ref.shape[0] - 2
        for k in range(2):
            off_ref[at + k, here_at] = off[k].astype(jnp.bfloat16)
            on_ref[at + k, here_at] = on[k].astype(jnp.bfloat16)


def own_kernel(
    first, count, state_ref, prev_ref, wind_ref, target_ref, slope_ref, slot_ref, own_ref, part_ref, start_ref, move_ref, *tables
):
    physics = Physics(slot_ref)
    physics.take_own(own_ref)
    physics.begin(wind_ref, target_ref, slope_ref)

    def stages(at, here_at, j):
        parts, start, *_ = yield from mixed(
            physics.own_products([state_ref[k, at] for k in range(PARTS)]),
            physics.start(flat(state_ref[:, at]), flat(prev_ref[:, at]), move_ref, here_at),
            *([leaving_tables(slot_ref, *tables)] if j == 0 else []),
        )
        start_ref[:, here_at] = start.reshape(PARTS, CHUNK, LANES)
        for k, part in enumerate(parts):
            part_ref[k, here_at] = part

    in_turns(first, count, stages, True)


def far_kernel(
    first,
    count,
    state_ref,
    prev_ref,
    slot_ref,
    packed_ref,
    keep_ref,
    spread_ref,
    far_group_ref,
    part_ref,
    start_ref,
    tend_ref,
    ahead_ref,
    off_ref,
    on_ref,
    far_ref,
):
    physics = Physics(slot_ref)
    physics.take_far(None, keep_ref, spread_ref, far_group_ref)

    def unpack():
        matrices = unpacked_matrices(packed_ref[...].astype(jnp.float32)).astype(jnp.bfloat16)
        far_ref[...] = matrices
        return matrices

    physics.unpack = unpack

    def stages(at, here_at, _):
        far = yield from physics.far_products([state_ref[k, at] for k in range(PARTS)])
        tends = physics.merged([part_ref[k, here_at] for k in range(PARTS)], far)
        start = [start_ref[k, here_at] for k in range(PARTS)]
        prev = [prev_ref[k, at].astype(jnp.float32) for k in range(PARTS)]
        yield from physics.finish(start, prev, tends, here_at, tend_ref, ahead_ref, off_ref, on_ref)

    in_turns(first, count, stages, True)


def physics_kernel(
    first,
    count,
    state_ref,
    prev_ref,
    wind_ref,
    target_ref,
    slope_ref,
    slot_ref,
    own_ref,
    far_ref,
    keep_ref,
    spread_ref,
    far_group_ref,
    tend_ref,
    ahead_ref,
    off_ref,
    on_ref,
    move_ref,
):
    physics = Physics(slot_ref)
    physics.take_own(own_ref)
    physics.take_far(far_ref[...], keep_ref, spread_ref, far_group_ref)
    physics.begin(wind_ref, target_ref, slope_ref)
    physics.begin_cross()

    def stages(at, here_at, _):
        pairs = [state_ref[k, at] for k in range(PARTS)]
        far, own, start = yield from mixed(
            physics.far_products(pairs),
            physics.own_products(pairs),
            physics.start(flat(state_ref[:, at]), flat(prev_ref[:, at]), move_ref, here_at),
        )
        start = [start[k * CHUNK : (k + 1) * CHUNK] for k in range(PARTS)]
        tends = physics.merged(own, far)
        prev = [prev_ref[k, at].astype(jnp.float32) for k in range(PARTS)]
        yield from physics.finish(start, prev, tends, here_at, tend_ref, ahead_ref, off_ref, on_ref, True)

    in_turns(first, count, stages, True)


def near_kernel(
    state_ref,
    wind_ref,
    target_ref,
    slope_ref,
    off_ref,
    on_ref,
    prev_ref,
    *rest,
):
    parts, outs = rest[:-8], rest[-8:]
    own_ref, near_ref, near_add_ref, own_force_ref, near_force_ref, sum_ref, edge_sum_ref, blow_ref = outs
    lev = wind_ref.shape[1]
    slots, _ = point_sets()
    chosen = sides()
    end = off_ref.shape[1]

    def extra(ref, k):
        return ref[k, end - 64 : end].astype(jnp.float32)

    def winds(ref):
        whole = jnp.concatenate([extra(ref, k)[:48] for k in range(3)], axis=0)
        return whole[:lev], whole[lev:]

    def targets(ref):
        return extra(ref, 0)[48:56].astype(jnp.int32) - 32

    own_t = target_ref[...].astype(jnp.int32) - 32
    near_t = jnp.where(chosen, targets(off_ref), targets(on_ref))
    near_t = near_t + jnp.where(lane_ids() < 64, LANES, -LANES)
    own_sums = jnp.concatenate(
        [sum_block("own", own_t, slots, True), sum_block("own", near_t, slots, False)], axis=1
    )
    near_sums = jnp.concatenate(
        [sum_block("near", own_t, slots, False), sum_block("near", near_t, slots, True)], axis=1
    )
    sum_ref[:LANES] = own_sums
    sum_ref[LANES:] = near_sums
    nothing = jnp.zeros((LANES, LANES), jnp.bfloat16)
    first_sums = jnp.concatenate([nothing, own_sums[:, LANES:]], axis=1)
    first_sums = jnp.concatenate([near_sums, first_sums], axis=0)
    for k, turn in enumerate(("", " turned")):
        edge_sum_ref[k, :LANES] = near_sums
        edge_sum_ref[k, LANES:, :LANES] = nothing
        edge_sum_ref[k, LANES:, LANES:] = sum_block("outer" + turn, near_t, slots, False)
        edge_sum_ref[2 + k, :LANES, :LANES] = own_sums[:, :LANES]
        edge_sum_ref[2 + k, LANES:, :LANES] = sum_block("near" + turn, own_t, slots, False)
    inner = inner_lanes()
    off_w, on_w = winds(off_ref), winds(on_ref)
    for d in range(2):
        blow_ref[0, d] = -time_step * wind_ref[d]
        near_w = -time_step * jnp.where(chosen, off_w[d], on_w[d])
        outer_w = -time_step * jnp.where(chosen, on_w[d], off_w[d])
        blow_ref[1, d] = near_w
        blow_ref[2, d] = jnp.where(inner, outer_w, pltpu.roll(outer_w, 64, 1))
        blow_ref[3, d] = jnp.where(inner, pltpu.roll(near_w, 64, 1), near_w)

    slope = slope_ref[...]
    early = time_step * hermite(0)[0]
    early_1, late_1 = (time_step * w for w in hermite(1))
    early_2, late_2 = (time_step * w for w in hermite(2))
    own_blow = (blow_ref[0, 0], blow_ref[0, 1])
    near_blow = (blow_ref[1, 0], blow_ref[1, 1])

    def stages(at, here_at, tend_ref, ahead_ref, move_ref):
        off, on = off_ref[:, at].astype(jnp.float32), on_ref[:, at].astype(jnp.float32)
        near = whole_halves(off[:2], on[:2], chosen)
        own_move = move_ref[:, here_at].reshape(-1, LANES)
        near_move = moved(near, slope, *near_blow)
        yield
        total = jnp.concatenate([near_move, own_move], axis=1)
        total = jnp.dot(total, first_sums, preferred_element_type=jnp.float32)
        near_total = total[:, LANES:]
        kept = jnp.where(inner, 0.0, whole_quarters(off[2], on[2], chosen))
        near = near + near_total + early * kept
        near_ref[:, at] = near.reshape(PARTS, CHUNK, LANES)
        near_force_ref[:, at] = (early_2 * kept).reshape(PARTS, CHUNK, LANES)
        own = flat(ahead_ref[:, here_at]) + total[:, :LANES]
        yield
        own_move = moved(own, slope, *own_blow)
        yield
        total = jnp.dot(own_move, own_sums, preferred_element_type=jnp.float32)
        own_prev, own_tend = flat(prev_ref[:, at]), flat(tend_ref[:, here_at])
        own = own + total[:, :LANES] + (early_1 * own_prev + late_1 * own_tend)
        own_ref[:, at] = own.reshape(PARTS, CHUNK, LANES)
        own_force = early_2 * own_prev + late_2 * own_tend
        own_force_ref[:, at] = own_force.reshape(PARTS, CHUNK, LANES)
        near_add = total[:, LANES:] + early_1 * kept
        near_add_ref[:, at] = near_add.reshape(PARTS, CHUNK, LANES)

    places = []
    for refs in zip(parts[::3], parts[1::3], parts[2::3]):
        places += [(here_at, *refs) for here_at in chunks(refs[0])]
    in_turns(0, len(places), lambda at, _, j: stages(at, *places[j]))


def advance_kernel(
    first,
    last,
    own_ref,
    near_ref,
    near_add_ref,
    own_force_ref,
    near_force_ref,
    off_ref,
    on_ref,
    slope_ref,
    sum_ref,
    edge_sum_ref,
    blow_ref,
    *rest,
):
    if last:
        tend_ref, done_ref, out_hbm, out_ref, sems = rest
        copies = [pltpu.make_async_copy(done_ref, out_hbm.at[:, pl.ds(0, done_ref.shape[1])], sems.at[0])]
    else:
        *tend_refs, out_ref, tend_hbm, sems = rest
        tend_ref = tend_refs[0]
        copies, row = [], 0
        for k, ref in enumerate(tend_refs):
            copies.append(pltpu.make_async_copy(ref, tend_hbm.at[:, pl.ds(row, ref.shape[1])], sems.at[k]))
            row += ref.shape[1]
    for copy in copies:
        copy.start()
    inner = inner_lanes()
    chosen = sides()
    slope = slope_ref[...]
    lates = [time_step * hermite(s)[1] for s in range(SUBSTEPS)]

    def advect(value, unit):
        return moved(value, slope, blow_ref[unit, 0], blow_ref[unit, 1])

    def gather(pieces, matrix):
        return jnp.dot(jnp.concatenate(pieces, axis=1), matrix, preferred_element_type=jnp.float32)

    def gather_shared(whole, packed, which, width):
        half = packed.shape[0]
        parts = [
            gather([whole[k * half : (k + 1) * half], packed], edge_sum_ref[which + k, :, :width])
            for k in range(2)
        ]
        return jnp.concatenate(parts, axis=0)

    def stages(at, here_at, j):
        off, on = off_ref[:, here_at].astype(jnp.float32), on_ref[:, here_at].astype(jnp.float32)
        if last:
            middle = whole_quarters(off[0], on[0], chosen)
        else:
            off_mid, on_mid = flat(off[:2]), flat(on[:2])
            middle = [jnp.where(chosen, off_mid, on_mid), jnp.where(chosen, on_mid, off_mid)]
            middle = jnp.concatenate([middle[0], pltpu.roll(middle[1], 64, 1)], axis=0)
            outer = jnp.where(chosen == inner, on_mid, off_mid)
        received = whole_halves(off[-2:], on[-2:], chosen)
        near = jnp.where(inner, middle, flat(near_ref[:, at]) + lates[0] * received)
        moves = [advect(near, 1)] if last else [advect(near, 1), advect(outer, 2)]
        yield
        if last:
            total = jnp.dot(moves[0], sum_ref[LANES:], preferred_element_type=jnp.float32)
        else:
            total = gather_shared(*moves, 0, 2 * LANES)
        own = flat(own_ref[:, at]) + total[:, :LANES]
        force = received * jnp.where(inner, 1.0, lates[1])
        near = near + total[:, LANES:] + (flat(near_add_ref[:, at]) + force)
        yield
        moves = [advect(own, 0), advect(near, 1)]
        yield
        total = gather(moves, sum_ref[...])
        own = own + total[:, :LANES] + flat(own_force_ref[:, at])
        near = near + total[:, LANES:] + (flat(near_force_ref[:, at]) + lates[2] * received)
        yield
        half = near.shape[0] // 2
        near = jnp.where(inner, pltpu.roll(near[half:], 64, 1), near[:half])
        moves = advect(own, 0), advect(near, 3)
        yield
        total = gather_shared(*moves, 2, LANES)
        out = own + total + lates[3] * flat(tend_ref[:, here_at])
        out_ref[:, here_at] = out.reshape(PARTS, CHUNK, LANES)
        if last:
            for k in range(PARTS):
                copies.append(
                    pltpu.make_async_copy(
                        out_ref.at[k, here_at], out_hbm.at[k, at], sems.at[1 + PARTS * j + k]
                    )
                )
                copies[-1].start()

    in_turns(first, out_ref.shape[1] // CHUNK, stages, last)
    for copy in copies:
        copy.wait()


def exchanged(off, on):
    count = lax.axis_size(AXES)
    across = [(i, (i + 1) % count if i % 2 else (i - 1) % count) for i in range(count)]
    inside = [(i, i ^ 1) for i in range(count)]
    on = lax.ppermute(on, AXES, inside)
    return lax.ppermute(off, AXES, across), on


def per_device(state, prev_tendency, wind, edge_links, swap_slot, inverse):
    devices = lax.axis_size(AXES)
    shape = state.shape
    lev = shape[1]
    rows = shape[0] * lev // PARTS
    params = pltpu.CompilerParams(vmem_limit_bytes=VMEM)
    bf16, f32 = jnp.bfloat16, jnp.float32
    inner = pl.BlockSpec(memory_space=pltpu.VMEM)
    outer = pl.BlockSpec(memory_space=pltpu.HBM)

    def like(count, kind, length=rows):
        return pltpu.VMEM((count, length, LANES), kind)

    def table(kind, *size):
        return pltpu.VMEM(size, kind)

    def call(body, ins, outs, name, passes, **more):
        size = sum(math.prod(array.shape) * array.dtype.itemsize for array in ins)
        cost = pl.CostEstimate(
            flops=passes * 2 * PARTS * rows * 256 * 256, bytes_accessed=2 * size, transcendentals=0
        )
        more = {"in_specs": [inner] * len(ins), "out_specs": (inner,) * len(outs)} | more
        return pl.pallas_call(
            body, out_shape=outs, compiler_params=params, cost_estimate=cost, name=name, **more
        )(*ins)

    slot = swap_slot.reshape(1, LANES)
    slope = jnp.asarray(derivative_matrix())
    message = like(3, bf16, rows + 64)
    inputs = (
        inverse,
        wind,
        edge_links,
        state.reshape(PARTS, rows, LANES),
        prev_tendency.reshape(PARTS, rows, LANES),
    )
    inputs = tuple(pltpu.with_memory_space_constraint(array, pltpu.HBM) for array in inputs)
    matrices, packed, to_off, to_on, targets, wind, state, prev = call(
        pack_kernel,
        inputs,
        (
            table(bf16, inverse.shape[0] * lev, LANES),
            table(bf16, 368, LANES),
            message,
            message,
            table(f32, 8, LANES),
            table(f32, *wind.shape),
            like(4, f32),
            like(4, bf16),
        ),
        "pack",
        2,
        in_specs=[outer] * len(inputs),
        scratch_shapes=[
            pltpu.VMEM(inverse.shape, f32),
            pltpu.VMEM(edge_links.shape, jnp.int32),
            pltpu.SemaphoreType.DMA((3 + 2 * (rows // CHUNK),)),
        ],
    )
    far_packed = lax.ppermute(packed, AXES, [(i, i ^ (devices // 2)) for i in range(devices)])
    off, on = exchanged(to_off, to_on)
    halves = []
    first = 0
    shared = (wind, targets, slope, slot, matrices)
    for count in SPLIT:
        size = count * CHUNK
        sent = like(3 if first else 4, bf16, size)
        outs = (like(4, bf16, size), like(4, f32, size), sent, sent)
        if first == 0:
            part, start, move, *tables = call(
                functools.partial(own_kernel, first, count),
                (state, prev) + shared,
                (like(4, f32, size), like(4, f32, size), like(4, bf16, size))
                + (table(bf16, 2 * LANES, LANES), table(bf16, LANES, 2 * LANES), table(f32, 8, LANES)),
                "own",
                3 * count,
            )
            ins = (state, prev, slot, far_packed, *tables, part, start)
            body, name = far_kernel, "far"
            outs += (table(bf16, *matrices.shape),)
        else:
            ins = (state, prev) + shared + (far_matrices, *tables)
            body, name = physics_kernel, "physics"
            outs += (like(4, bf16, size),)
        tend, ahead, to_off, to_on, *more = call(
            functools.partial(body, first, count), ins, outs, name, 5 * count
        )
        if first:
            move = more[0]
        else:
            far_matrices = more[0]
        halves.append((first, count, tend, (tend, ahead, move), exchanged(to_off, to_on)))
        first += count
    parts = sum((part for _, _, _, part, _ in halves), ())
    own, near, near_add, own_force, near_force, sums, edge_sums, blow = call(
        near_kernel,
        (state, wind, targets, slope, off, on, prev) + parts,
        (
            like(4, f32),
            like(4, f32),
            like(4, f32),
            like(4, f32),
            like(4, f32),
            table(bf16, 2 * LANES, 2 * LANES),
            table(bf16, 4, 2 * LANES, 2 * LANES),
            table(f32, 4, 2, lev, LANES),
        ),
        "near",
        16,
    )
    tends = tuple(tend for _, _, tend, _, _ in halves)
    out_spec = jax.ShapeDtypeStruct((PARTS, rows, LANES), f32)
    tend_spec = jax.ShapeDtypeStruct((PARTS, rows, LANES), bf16)
    for part, (first, count, tend, _, (off, on)) in enumerate(halves):
        ins = (own, near, near_add, own_force, near_force, off, on, slope, sums, edge_sums, blow)
        size = count * CHUNK
        if part == 0:
            done, tend_out = call(
                functools.partial(advance_kernel, first, False),
                ins + tends,
                (like(4, f32, size), tend_spec),
                "advance",
                5 * count,
                out_specs=(inner, outer),
                scratch_shapes=[pltpu.SemaphoreType.DMA((len(tends),))],
            )
        else:
            (out,) = call(
                functools.partial(advance_kernel, first, True),
                ins + (tend, done),
                (out_spec,),
                "advance",
                5 * count,
                out_specs=(outer,),
                scratch_shapes=[pltpu.VMEM((PARTS, size, LANES), f32), pltpu.SemaphoreType.DMA((1 + PARTS * count,))],
            )
    tend = tend_out
    return (out.reshape(shape), tend.reshape(shape))


def solution(mesh):
    columns = P(None, None, AXES)
    return jax.shard_map(
        per_device,
        mesh=mesh,
        in_specs=(columns, columns, columns, columns, P(AXES), P(AXES, None, None)),
        out_specs=(columns, columns),
        check_vma=False,
    )
```
